32 devices in a mesh: section: 4 (over y, core), dp: 4 (over z), tensor: 2 (over x).
Axes of the slice: x: 2, y: 2, z: 4, core: 2. Of those that a mesh axis runs over, the one named last changes fastest.
Arguments:
- layer_input: bfloat16 [4, 8, 512, 1024], P('dp', None, 'tensor'), may hold values from -6 to 6
- output_grad: bfloat16 [4, 8, 512, 1024], P('dp', None, 'tensor'), may hold values from -6 to 6
- seg_blocks: int32 [8], replicated, may hold values from 2 to 4, as said below
- seg_group: int32 [8], replicated, may hold values from 0 to 3, as said below
- gain_a: bfloat16 [1024], replicated, may hold values from 0.5 to 1.5
- wqkv_a: bfloat16 [1024, 3, 1024], P(None, None, 'tensor'), may hold values from -0.1875 to 0.1875
- wout_a: bfloat16 [1024, 1024], P('tensor'), may hold values from -0.75 to 0.75
- gain_b: bfloat16 [1024], replicated, may hold values from 0.5 to 1.5
- up_b: bfloat16 [1024, 4096], P(None, 'tensor'), may hold values from -0.1875 to 0.1875
- down_b: bfloat16 [4096, 1024], P('tensor'), may hold values from -0.09375 to 0.09375
- gain_c: bfloat16 [1024], replicated, may hold values from 0.5 to 1.5
- gain_s: bfloat16 [1024], replicated, may hold values from 0.5 to 1.5
- wqkv_c: bfloat16 [1024, 3, 1024], P(None, None, 'tensor'), may hold values from -0.1875 to 0.1875
- sqkv_c: bfloat16 [1024, 3, 1024], P(None, None, 'tensor'), may hold values from -0.1875 to 0.1875
- wout_c: bfloat16 [1024, 1024], P('tensor'), may hold values from -0.75 to 0.75
- sout_c: bfloat16 [1024, 1024], P('tensor'), may hold values from -0.75 to 0.75
- gate_bias: bfloat16 [1024], replicated, may hold values from -1 to 3
- init_states: bfloat16 [512, 1024], P('tensor'), may hold values from -6 to 6
- gain_d: bfloat16 [1024], replicated, may hold values from 0.5 to 1.5
- up_d: bfloat16 [1024, 4096], P(None, 'tensor'), may hold values from -0.1875 to 0.1875
- down_d: bfloat16 [4096, 1024], P('tensor'), may hold values from -0.09375 to 0.09375
Outputs:
- layer_output: bfloat16 [4, 8, 512, 1024], P('dp', None, 'tensor', 'section')
- final_states: float32 [4, 512, 3, 1024], P('dp', 'tensor', None, 'section')
- input_grad: float32 [4, 8, 512, 1024], P('dp', None, 'tensor', 'section')
- grad_gain_a: float32 [1024], P('section')
- grad_wqkv_a: float32 [1024, 3, 1024], P('section', None, 'tensor')
- grad_wout_a: float32 [1024, 1024], P('tensor', 'section')
- grad_gain_b: float32 [1024], P('section')
- grad_up_b: float32 [1024, 4096], P('section', 'tensor')
- grad_down_b: float32 [4096, 1024], P('tensor', 'section')
- grad_gain_c: float32 [1024], P('section')
- grad_gain_s: float32 [1024], P('section')
- grad_wqkv_c: float32 [1024, 3, 1024], P('section', None, 'tensor')
- grad_sqkv_c: float32 [1024, 3, 1024], P('section', None, 'tensor')
- grad_wout_c: float32 [1024, 1024], P('tensor', 'section')
- grad_sout_c: float32 [1024, 1024], P('tensor', 'section')
- grad_gate_bias: float32 [1024], P('section')
- grad_init_states: float32 [512, 1024], P('tensor', 'section')
- grad_gain_d: float32 [1024], P('section')
- grad_up_d: float32 [1024, 4096], P('section', 'tensor')
- grad_down_d: float32 [4096, 1024], P('tensor', 'section')
The draws below stay inside these ranges and needn't reach their ends.
Inputs may be any that keep to these rules, and one draw needn't show every extreme that they name: `seg_blocks`: every segment has 2 or 4 blocks, as many segments of each length. `seg_group`: each data group holds one segment of 4 blocks; half of the groups hold two segments of 2 blocks besides, so that a group holds at most 8 blocks and half of the groups are full.
All inputs are finite; a program needn't handle non-finite values.
Results may differ from the reference program's by a relative error of at most 0.034.
Values may be sent and summed in bfloat16 or wider, within the bound.
A program may use at most 576 MiB of HBM per device.

```python
import math
import jax
import jax.numpy as jnp
from jax import lax

D = 1024
HEADS = 8
HEAD_DIM = 128
FF = 4096
NSTATE = 512
BLOCK = 512
SLOTS = 3
SHORT_B = 2
CAP_BLOCKS = 8
SEGS = 8
N_DP = 4


def deal_segments(key):
    first_key, second_key, third_key = jax.random.split(key, 3)
    ordering = jax.random.permutation(first_key, SEGS)
    long_groups = jax.random.permutation(second_key, N_DP)
    short_groups = jax.random.permutation(third_key, N_DP)
    is_long = ordering < N_DP
    long_pick = jnp.take(long_groups, jnp.minimum(ordering, N_DP - 1))
    short_pick = jnp.take(short_groups, jnp.maximum(ordering - N_DP, 0) // 2)
    groups = jnp.where(is_long, long_pick, short_pick).astype(jnp.int32)
    lengths = jnp.where(is_long, 2 * SHORT_B, SHORT_B).astype(jnp.int32)
    return (lengths, groups)


def draw_seg_blocks(key, part):
    return deal_segments(key)[0]


def draw_seg_group(key, part):
    return deal_segments(key)[1]


def level_of(stream_key, shape, cuts, low, top_value):
    level = 1.0
    for axis_at, parts in cuts:
        heights = jax.random.uniform(jax.random.fold_in(jax.random.fold_in(stream_key, 6), axis_at), (parts,), jnp.float32, low / len(cuts), top_value / len(cuts))
        level = level * jnp.repeat(jnp.exp(heights), shape[axis_at] // parts).reshape((-1,) + (1,) * (len(shape) - 1 - axis_at))
    return level


def scatter_about(key, dims, width, bound, shards=(), kind=jnp.bfloat16):
    loudness = level_of(key, dims, shards, -0.22, 0.18) if shards else 1.0
    entries = jax.random.normal(key, dims, jnp.float32) * width * loudness
    return jnp.minimum(jnp.maximum(entries, -bound), bound).astype(kind)


def setup_inputs(seed: int = 0) -> dict:
    arg_keys = jax.random.split(jax.random.key(seed), 22)
    layer_input = scatter_about(arg_keys[0], (N_DP, CAP_BLOCKS, BLOCK, D), 1.0, 6.0, ((0, 4), (2, 2)))
    output_grad = scatter_about(arg_keys[1], (N_DP, CAP_BLOCKS, BLOCK, D), 1.0, 6.0, ((0, 4), (2, 2)))
    seg_blocks = draw_seg_blocks(jax.random.fold_in(arg_keys[21], 71), 0)
    seg_group = draw_seg_group(jax.random.fold_in(arg_keys[21], 71), 0)
    gain_a = jnp.clip(1.0 + 0.1 * jax.random.normal(arg_keys[4], (D,), jnp.float32), 0.5, 1.5).astype(jnp.bfloat16)
    wqkv_a = scatter_about(arg_keys[5], (D, 3, D), D ** -0.5, 0.1875, ((2, 2),))
    wout_a = scatter_about(arg_keys[6], (D, D), (D // 16) ** -0.5, 0.75, ((0, 2),))
    gain_b = jnp.clip(1.0 + 0.1 * jax.random.normal(arg_keys[7], (D,), jnp.float32), 0.5, 1.5).astype(jnp.bfloat16)
    up_b = scatter_about(arg_keys[8], (D, FF), D ** -0.5, 0.1875, ((1, 2),))
    down_b = scatter_about(arg_keys[9], (FF, D), FF ** -0.5, 0.09375, ((0, 2),))
    gain_c = jnp.clip(1.0 + 0.1 * jax.random.normal(arg_keys[10], (D,), jnp.float32), 0.5, 1.5).astype(jnp.bfloat16)
    gain_s = jnp.clip(1.0 + 0.1 * jax.random.normal(arg_keys[11], (D,), jnp.float32), 0.5, 1.5).astype(jnp.bfloat16)
    wqkv_c = scatter_about(arg_keys[12], (D, 3, D), D ** -0.5, 0.1875, ((2, 2),))
    sqkv_c = scatter_about(arg_keys[13], (D, 3, D), D ** -0.5, 0.1875, ((2, 2),))
    wout_c = scatter_about(arg_keys[14], (D, D), (D // 16) ** -0.5, 0.75, ((0, 2),))
    sout_c = scatter_about(arg_keys[15], (D, D), (D // 16) ** -0.5, 0.75, ((0, 2),))
    gate_bias = jnp.clip(jax.random.uniform(arg_keys[16], (D,), jnp.float32, -1.0, 3.0), -1.0, 3.0).astype(jnp.bfloat16)
    init_states = scatter_about(arg_keys[17], (NSTATE, D), 1.0, 6.0, ((0, 2),))
    gain_d = jnp.clip(1.0 + 0.1 * jax.random.normal(arg_keys[18], (D,), jnp.float32), 0.5, 1.5).astype(jnp.bfloat16)
    up_d = scatter_about(arg_keys[19], (D, FF), D ** -0.5, 0.1875, ((1, 2),))
    down_d = scatter_about(arg_keys[20], (FF, D), FF ** -0.5, 0.09375, ((0, 2),))
    return dict(layer_input=layer_input, output_grad=output_grad, seg_blocks=seg_blocks, seg_group=seg_group, gain_a=gain_a, wqkv_a=wqkv_a, wout_a=wout_a, gain_b=gain_b, up_b=up_b, down_b=down_b, gain_c=gain_c, gain_s=gain_s, wqkv_c=wqkv_c, sqkv_c=sqkv_c, wout_c=wout_c, sout_c=sout_c, gate_bias=gate_bias, init_states=init_states, gain_d=gain_d, up_d=up_d, down_d=down_d)


@jax.custom_vjp
def low(v):
    return lax.optimization_barrier(v.astype(jnp.bfloat16)).astype(jnp.float32)

@jax.custom_vjp
def lower_backward(v):
    return v

def low_keep(v):
    return (low(v), None)

def low_pass(kept, grad):
    return (grad,)

def back_keep(v):
    return (v, None)

def back_low(kept, grad):
    return (low(grad),)
low.defvjp(low_keep, low_pass)
lower_backward.defvjp(back_keep, back_low)
EPSILON = 1e-06
PRECISION_TOP = lax.Precision.HIGHEST

def bidirectional_pass(values):
    return low(lower_backward(values))

def normed(values, gain):
    return low(values * lax.rsqrt(lax.optimization_barrier(jnp.mean(values * values, axis=-1, keepdims=True)) + EPSILON) * gain)

def layout(seg_blocks, seg_group, group_index, block_count):
    mine = seg_group == group_index
    lengths = jnp.where(mine, seg_blocks, 0)
    offsets = jnp.cumsum(lengths) - lengths
    ranking = jnp.cumsum(mine.astype(jnp.int32)) - mine.astype(jnp.int32)
    blocks = jnp.arange(block_count, dtype=jnp.int32)[None, :]
    inside = mine[:, None] & (blocks >= offsets[:, None]) & (blocks < (offsets + lengths)[:, None])
    begins = jnp.any(inside & (blocks == offsets[:, None]), axis=0)
    closes = jnp.any(inside & (blocks == (offsets + lengths - 1)[:, None]), axis=0)
    lively = jnp.any(inside, axis=0)
    numbers = lax.optimization_barrier(jnp.sum(jnp.where(inside, ranking[:, None], 0), axis=0)).astype(jnp.int32)
    return (begins, closes, lively, numbers)

def split_heads(rows_in):
    return rows_in.reshape(rows_in.shape[0], HEADS, HEAD_DIM)

def attend(queries, key_rows, value_rows, allowed):
    scores = lower_backward(jnp.einsum('rhd,khd->hrk', queries, key_rows, precision=PRECISION_TOP) * (1.0 / math.sqrt(HEAD_DIM)))
    scores = jnp.where(allowed[None], scores, -1e+30)
    weights = jax.nn.softmax(scores, axis=-1)
    return jnp.einsum('hrk,khd->rhd', low(weights), value_rows, precision=PRECISION_TOP)

def window_masks(opening):
    later_keys = jnp.arange(BLOCK)[None, :] > jnp.arange(BLOCK)[:, None]
    return (later_keys & jnp.logical_not(opening), jnp.logical_not(later_keys))

def projections(residual_stream, gain, wqkv):
    hidden_rows = normed(residual_stream, gain)
    projected = bidirectional_pass(jnp.einsum('cbd,djn->cbjn', hidden_rows, wqkv, precision=PRECISION_TOP))
    queries = projected[:, :, 0]
    key_rows = projected[:, :, 1]
    value_rows = projected[:, :, 2]
    prior_keys = jnp.concatenate([jnp.zeros_like(key_rows[:1]), key_rows[:-1]], axis=0)
    prior_values = jnp.concatenate([jnp.zeros_like(value_rows[:1]), value_rows[:-1]], axis=0)
    return (queries, key_rows, value_rows, prior_keys, prior_values)

def plain_layer(residual_stream, gain, wqkv, output_weight, begins):
    queries, key_rows, value_rows, prior_keys, prior_values = projections(residual_stream, gain, wqkv)

    def one_block(pieces):
        asking, own_keys, own_values, old_keys, old_values, opening = pieces
        reach_prior, reach_current = window_masks(opening)
        allowed = jnp.concatenate([reach_prior, reach_current], axis=1)
        mixture_output = attend(split_heads(asking), split_heads(jnp.concatenate([old_keys, own_keys], axis=0)), split_heads(jnp.concatenate([old_values, own_values], axis=0)), allowed)
        return mixture_output.reshape(BLOCK, D)
    mixture_output = lax.map(jax.checkpoint(one_block), (queries, key_rows, value_rows, prior_keys, prior_values, begins))
    return residual_stream + lower_backward(jnp.einsum('urx,xt->urt', bidirectional_pass(mixture_output), output_weight, precision=PRECISION_TOP))

def feed_layer(residual_stream, gain, up_projection_weight, down_projection_weight):
    hidden_rows = normed(residual_stream, gain)
    inner_hidden_rows = lower_backward(jnp.einsum('nip,pu->niu', hidden_rows, up_projection_weight, precision=PRECISION_TOP))
    active_flags = low(jax.nn.gelu(inner_hidden_rows, approximate=True))
    return residual_stream + lower_backward(jnp.einsum('uov,vy->uoy', active_flags, down_projection_weight, precision=PRECISION_TOP))

def recurrent_layer(residual_stream, gain, state_gain, wqkv, sqkv, output_weight, sout, gate_bias, initial, begins):
    queries, key_rows, value_rows, prior_keys, prior_values = projections(residual_stream, gain, wqkv)
    retain = jax.nn.sigmoid(gate_bias)
    every_key = jnp.ones((NSTATE, BLOCK + NSTATE), dtype=bool)
    state_keys_all = jnp.ones((BLOCK, NSTATE), dtype=bool)

    def advance(carried, pieces):
        asking, own_keys, own_values, old_keys, old_values, opening = pieces
        current = jnp.where(opening, initial, carried)
        state_proj = bidirectional_pass(jnp.einsum('sd,djn->sjn', normed(current, state_gain), sqkv, precision=PRECISION_TOP))
        reach_prior, reach_current = window_masks(opening)
        allowed = jnp.concatenate([reach_prior, reach_current, state_keys_all], axis=1)
        token_mixture = attend(split_heads(asking), split_heads(jnp.concatenate([old_keys, own_keys, state_proj[:, 1]], axis=0)), split_heads(jnp.concatenate([old_values, own_values, state_proj[:, 2]], axis=0)), allowed)
        state_mixture = attend(split_heads(state_proj[:, 0]), split_heads(jnp.concatenate([own_keys, state_proj[:, 1]], axis=0)), split_heads(jnp.concatenate([own_values, state_proj[:, 2]], axis=0)), every_key)
        update = lower_backward(jnp.dot(bidirectional_pass(state_mixture.reshape(NSTATE, D)), sout, precision=PRECISION_TOP))
        fresh = retain * current + (1.0 - retain) * update
        return (fresh, (token_mixture.reshape(BLOCK, D), fresh))
    _, (mixture_output, state_vectors) = lax.scan(jax.checkpoint(advance), initial, (queries, key_rows, value_rows, prior_keys, prior_values, begins))
    return (residual_stream + lower_backward(jnp.einsum('urx,xt->urt', bidirectional_pass(mixture_output), output_weight, precision=PRECISION_TOP)), state_vectors)

def forward(inputs, weights, flags):
    gain_a, wqkv_a, wout_a, gain_b, up_b, down_b, gain_c, gain_s, wqkv_c, sqkv_c, wout_c, sout_c, gate_bias, init_states, gain_d, up_d, down_d = weights
    results = []
    closing = []
    for group_index in range(N_DP):
        begins, closes, lively, numbers = flags[group_index]
        residual_stream = plain_layer(inputs[group_index], gain_a, wqkv_a, wout_a, begins)
        residual_stream = feed_layer(residual_stream, gain_b, up_b, down_b)
        residual_stream, state_vectors = recurrent_layer(residual_stream, gain_c, gain_s, wqkv_c, sqkv_c, wout_c, sout_c, gate_bias, init_states, begins)
        residual_stream = feed_layer(residual_stream, gain_d, up_d, down_d)
        results.append(jnp.where(lively[:, None, None], residual_stream, 0.0))
        chosen = ((numbers[:, None] == jnp.arange(SLOTS, dtype=jnp.int32)[None, :]) & (closes & lively)[:, None]).astype(residual_stream.dtype)
        closing.append(jnp.einsum('cs,cnd->nsd', chosen, state_vectors, precision=PRECISION_TOP))
    return (jnp.stack(results), jnp.stack(closing))

def reference(layer_input, output_grad, seg_blocks, seg_group, gain_a, wqkv_a, wout_a, gain_b, up_b, down_b, gain_c, gain_s, wqkv_c, sqkv_c, wout_c, sout_c, gate_bias, init_states, gain_d, up_d, down_d):
    weights = tuple((weight.astype(jnp.float32) for weight in (gain_a, wqkv_a, wout_a, gain_b, up_b, down_b, gain_c, gain_s, wqkv_c, sqkv_c, wout_c, sout_c, gate_bias, init_states, gain_d, up_d, down_d)))
    flags = [layout(seg_blocks, seg_group, group_index, CAP_BLOCKS) for group_index in range(N_DP)]
    primal = layer_input.astype(jnp.float32)

    def run_layers(inputs, params):
        return forward(inputs, params, flags)
    (result, closing), pullback = jax.vjp(run_layers, primal, weights)
    input_grad, grads = pullback((output_grad.astype(jnp.float32), jnp.zeros_like(closing)))
    return (result.astype(jnp.bfloat16), closing, input_grad, grads[0], grads[1], grads[2], grads[3], grads[4], grads[5], grads[6], grads[7], grads[8], grads[9], grads[10], grads[11], grads[12], grads[13], grads[14], grads[15], grads[16])
```

```python
import functools
import math

import jax
import jax.numpy as jnp
from jax import lax
from jax.experimental import pallas as pl
from jax.experimental.pallas import tpu as pltpu
from jax.sharding import PartitionSpec as P

HEAD_DIM = 128
SLOTS = 3


EPSILON = 1e-06
NEGATIVE = -1e30


def shifted(value, axis, by):
    devices = lax.axis_size(axis)
    pairs = [(i, i + by) for i in range(devices) if 0 <= i + by < devices]
    return lax.ppermute(value, axis, pairs)


def for_sending(value):
    return jax.tree.map(lambda a: a.astype(jnp.bfloat16) if a.dtype == jnp.float32 else a, value)


def layout(seg_blocks, seg_group, group_index, block_count):
    mine = seg_group == group_index
    lengths = jnp.where(mine, seg_blocks, 0)
    offsets = jnp.cumsum(lengths) - lengths
    ranking = jnp.cumsum(mine.astype(jnp.int32)) - mine.astype(jnp.int32)
    blocks = jnp.arange(block_count, dtype=jnp.int32)[None, :]
    inside = mine[:, None] & (blocks >= offsets[:, None]) & (blocks < (offsets + lengths)[:, None])
    begins = jnp.any(inside & (blocks == offsets[:, None]), axis=0)
    closes = jnp.any(inside & (blocks == (offsets + lengths - 1)[:, None]), axis=0)
    lively = jnp.any(inside, axis=0)
    numbers = jnp.sum(jnp.where(inside, ranking[:, None], 0), axis=0)
    return (begins, closes, lively, numbers)


def inverse_rms(values):
    return lax.rsqrt(jnp.mean(values * values, axis=-1, keepdims=True) + EPSILON)


def norm_back(values, gain, grad_normed):
    factor = inverse_rms(values)
    scaled = values * factor
    grad_scaled = grad_normed * gain
    grad_values = factor * (
        grad_scaled - scaled * jnp.mean(grad_scaled * scaled, axis=-1, keepdims=True)
    )
    return (grad_values, jnp.sum(grad_normed * scaled, axis=0))


def smooth(values):
    return jax.nn.gelu(values, approximate=True)


def split_heads(rows_in):
    return rows_in.reshape(rows_in.shape[0], -1, HEAD_DIM)


def attend_forward(queries, key_rows, value_rows, allowed):
    score_scale = 1.0 / math.sqrt(HEAD_DIM)
    scores = (
        jnp.einsum("rhd,khd->hrk", queries, key_rows, preferred_element_type=jnp.float32)
        * score_scale
    )
    scores = jnp.where(allowed[None], scores, NEGATIVE)
    largest = jnp.max(scores, axis=-1, keepdims=True)
    totals = jnp.sum(jnp.exp(scores - largest), axis=-1, keepdims=True)
    log_total = largest + jnp.log(totals)
    weights = jnp.exp(scores - log_total).astype(jnp.bfloat16)
    mixture_output = jnp.einsum(
        "hrk,khd->rhd", weights, value_rows, preferred_element_type=jnp.float32
    )
    return (mixture_output, log_total[..., 0])


def attend_backward(queries, key_rows, value_rows, allowed, log_total, grad_mixture):
    score_scale = 1.0 / math.sqrt(HEAD_DIM)
    scores = (
        jnp.einsum("rhd,khd->hrk", queries, key_rows, preferred_element_type=jnp.float32)
        * score_scale
    )
    scores = jnp.where(allowed[None], scores, NEGATIVE)
    weights = jnp.exp(scores - log_total[..., None])
    rounded = weights.astype(jnp.bfloat16)
    grad_weights = jnp.einsum(
        "rhd,khd->hrk", grad_mixture, value_rows, preferred_element_type=jnp.float32
    )
    grad_values = jnp.einsum(
        "hrk,rhd->khd", rounded, grad_mixture, preferred_element_type=jnp.float32
    )
    inner_sum = jnp.sum(weights * grad_weights, axis=-1, keepdims=True)
    grad_scores = (weights * (grad_weights - inner_sum)).astype(jnp.bfloat16)
    grad_queries = (
        jnp.einsum("hrk,khd->rhd", grad_scores, key_rows, preferred_element_type=jnp.float32)
        * score_scale
    )
    grad_keys = (
        jnp.einsum("hrk,rhd->khd", grad_scores, queries, preferred_element_type=jnp.float32)
        * score_scale
    )
    return (grad_queries, grad_keys, grad_values)


def place_row(store, position, value, active_tick):
    previous = lax.dynamic_index_in_dim(store, position, 0, False)
    return lax.dynamic_update_index_in_dim(
        store, jnp.where(active_tick, value, previous), position, 0
    )


def renewed(grad_sums, active_tick, changes):
    return tuple(
        (
            total + jnp.where(active_tick, changes[position], 0.0) if position in changes else total
            for position, total in enumerate(grad_sums)
        )
    )


def relay_body(
    layer_input,
    output_grad,
    seg_blocks,
    seg_group,
    gain_a,
    wqkv_a,
    wout_a,
    gain_b,
    up_b,
    down_b,
    gain_c,
    gain_s,
    wqkv_c,
    sqkv_c,
    wout_c,
    sout_c,
    gate_bias,
    init_states,
    gain_d,
    up_d,
    down_d,
):
    block_count = layer_input.shape[1]
    shard_rows = layer_input.shape[2]
    model_width = layer_input.shape[3]
    tensor_count = lax.axis_size("tensor")
    token_rows = shard_rows * tensor_count
    state_shard = init_states.shape[0]
    state_count = state_shard * tensor_count
    local_width = wqkv_a.shape[2]
    local_heads = local_width // HEAD_DIM
    section_index = lax.axis_index("section")
    group_index = lax.axis_index("dp")
    on_cell_section = section_index == 2
    begins, closes, lively, numbers = layout(seg_blocks, seg_group, group_index, block_count)
    token_gains = jnp.stack([gain_a, gain_b, gain_c, gain_d]).astype(jnp.float32)
    state_gain = gain_s.astype(jnp.float32)
    retain = jax.nn.sigmoid(gate_bias.astype(jnp.float32))
    initial = init_states.astype(jnp.float32)
    empty_state = jnp.zeros((state_count, model_width), jnp.float32)
    empty_token_store = jnp.zeros((token_rows, 4, local_width), jnp.bfloat16)
    empty_state_store = jnp.zeros((state_count, 4, local_width), jnp.bfloat16)
    empty_token_lse = jnp.zeros((local_heads, token_rows), jnp.float32)
    empty_state_lse = jnp.zeros((local_heads, state_count), jnp.float32)
    empty_carry = jnp.zeros((token_rows, local_width), jnp.float32)
    every_key = jnp.ones((state_count, token_rows + state_count), bool)
    state_keys_all = jnp.ones((token_rows, state_count), bool)

    def token_masks(opening):
        later_keys = lax.broadcasted_iota(
            jnp.int32, (token_rows, token_rows), 1
        ) > lax.broadcasted_iota(jnp.int32, (token_rows, token_rows), 0)
        return (jnp.logical_and(later_keys, jnp.logical_not(opening)), jnp.logical_not(later_keys))

    def plain_forward(normed_tok, normed_st, prior_block, opening):
        projected = jnp.einsum(
            "rd,dcn->rcn", normed_tok, wqkv_a, preferred_element_type=jnp.float32
        ).astype(jnp.bfloat16)
        reach_prior, reach_current = token_masks(opening)
        allowed = jnp.concatenate([reach_prior, reach_current], axis=1)
        key_rows = jnp.concatenate([prior_block[:, 1], projected[:, 1]], axis=0)
        value_rows = jnp.concatenate([prior_block[:, 2], projected[:, 2]], axis=0)
        mixture_output, token_lse = attend_forward(
            split_heads(projected[:, 0]), split_heads(key_rows), split_heads(value_rows), allowed
        )
        mixture_output = mixture_output.reshape(token_rows, local_width).astype(jnp.bfloat16)
        branch = jnp.dot(mixture_output, wout_a, preferred_element_type=jnp.float32)
        stored = jnp.concatenate([projected, mixture_output[:, None]], axis=1)
        return (branch, empty_state, stored, empty_state_store, token_lse, empty_state_lse)

    def feed_forward(up_projection_weight, down_projection_weight):

        def forward_fn(normed_tok, normed_st, prior_block, opening):
            hidden_rows = jnp.dot(
                normed_tok, up_projection_weight, preferred_element_type=jnp.float32
            )
            active_flags = smooth(hidden_rows).astype(jnp.bfloat16)
            branch = jnp.dot(
                active_flags, down_projection_weight, preferred_element_type=jnp.float32
            )
            return (
                branch,
                empty_state,
                empty_token_store,
                empty_state_store,
                empty_token_lse,
                empty_state_lse,
            )

        return forward_fn

    def recurrent_forward(normed_tok, normed_st, prior_block, opening):
        projected = jnp.einsum(
            "rd,dcn->rcn", normed_tok, wqkv_c, preferred_element_type=jnp.float32
        ).astype(jnp.bfloat16)
        state_proj = jnp.einsum(
            "sd,dcn->scn", normed_st, sqkv_c, preferred_element_type=jnp.float32
        ).astype(jnp.bfloat16)
        reach_prior, reach_current = token_masks(opening)
        allowed = jnp.concatenate([reach_prior, reach_current, state_keys_all], axis=1)
        token_keys = jnp.concatenate([prior_block[:, 1], projected[:, 1], state_proj[:, 1]], axis=0)
        token_values = jnp.concatenate(
            [prior_block[:, 2], projected[:, 2], state_proj[:, 2]], axis=0
        )
        token_mixture, token_lse = attend_forward(
            split_heads(projected[:, 0]),
            split_heads(token_keys),
            split_heads(token_values),
            allowed,
        )
        state_keys = jnp.concatenate([projected[:, 1], state_proj[:, 1]], axis=0)
        state_values = jnp.concatenate([projected[:, 2], state_proj[:, 2]], axis=0)
        state_mixture, state_lse = attend_forward(
            split_heads(state_proj[:, 0]),
            split_heads(state_keys),
            split_heads(state_values),
            every_key,
        )
        token_mixture = token_mixture.reshape(token_rows, local_width).astype(jnp.bfloat16)
        state_mixture = state_mixture.reshape(state_count, local_width).astype(jnp.bfloat16)
        branch = jnp.dot(token_mixture, wout_c, preferred_element_type=jnp.float32)
        update_term = jnp.dot(state_mixture, sout_c, preferred_element_type=jnp.float32)
        stored = jnp.concatenate([projected, token_mixture[:, None]], axis=1)
        state_stored = jnp.concatenate([state_proj, state_mixture[:, None]], axis=1)
        return (branch, update_term, stored, state_stored, token_lse, state_lse)

    def plain_backward(
        grad_tok,
        grad_st,
        normed_tok,
        normed_st,
        tok_block,
        st_block,
        prior_block,
        token_lse,
        state_lse,
        opening,
        carry_keys,
        carry_values,
        grad_sums,
        active_tick,
    ):
        reach_prior, reach_current = token_masks(opening)
        allowed = jnp.concatenate([reach_prior, reach_current], axis=1)
        key_rows = jnp.concatenate([prior_block[:, 1], tok_block[:, 1]], axis=0)
        value_rows = jnp.concatenate([prior_block[:, 2], tok_block[:, 2]], axis=0)
        weight_out = jnp.einsum(
            "rn,rd->nd", tok_block[:, 3], grad_tok, preferred_element_type=jnp.float32
        )
        grad_mixture = jnp.einsum(
            "rd,nd->rn", grad_tok, wout_a, preferred_element_type=jnp.float32
        ).astype(jnp.bfloat16)
        grad_query, grad_keys, grad_values = attend_backward(
            split_heads(tok_block[:, 0]),
            split_heads(key_rows),
            split_heads(value_rows),
            allowed,
            token_lse,
            split_heads(grad_mixture),
        )
        grad_query = grad_query.reshape(token_rows, local_width)
        grad_keys = grad_keys.reshape(2 * token_rows, local_width)
        grad_values = grad_values.reshape(2 * token_rows, local_width)
        grad_proj = jnp.stack(
            [
                grad_query,
                grad_keys[token_rows:] + carry_keys,
                grad_values[token_rows:] + carry_values,
            ],
            axis=1,
        ).astype(jnp.bfloat16)
        weight_in = jnp.einsum(
            "rd,rcn->dcn", normed_tok, grad_proj, preferred_element_type=jnp.float32
        )
        grad_normed = jnp.einsum(
            "rcn,dcn->rd", grad_proj, wqkv_a, preferred_element_type=jnp.float32
        )
        return (
            grad_normed,
            empty_state,
            grad_keys[:token_rows],
            grad_values[:token_rows],
            renewed(grad_sums, active_tick, {0: weight_in, 1: weight_out}),
        )

    def feed_backward(up_projection_weight, down_projection_weight, up_slot, down_slot):

        def backward_fn(
            grad_tok,
            grad_st,
            normed_tok,
            normed_st,
            tok_block,
            st_block,
            prior_block,
            token_lse,
            state_lse,
            opening,
            carry_keys,
            carry_values,
            grad_sums,
            active_tick,
        ):
            hidden_rows = jnp.dot(
                normed_tok, up_projection_weight, preferred_element_type=jnp.float32
            )
            active_flags, gelu_back = jax.vjp(smooth, hidden_rows)
            weight_down = jnp.einsum(
                "rf,rd->fd",
                active_flags.astype(jnp.bfloat16),
                grad_tok,
                preferred_element_type=jnp.float32,
            )
            grad_active = jnp.einsum(
                "rd,fd->rf", grad_tok, down_projection_weight, preferred_element_type=jnp.float32
            )
            grad_hidden = gelu_back(grad_active)[0].astype(jnp.bfloat16)
            weight_up = jnp.einsum(
                "rd,rf->df", normed_tok, grad_hidden, preferred_element_type=jnp.float32
            )
            grad_normed = jnp.einsum(
                "rf,df->rd", grad_hidden, up_projection_weight, preferred_element_type=jnp.float32
            )
            return (
                grad_normed,
                empty_state,
                empty_carry,
                empty_carry,
                renewed(grad_sums, active_tick, {up_slot: weight_up, down_slot: weight_down}),
            )

        return backward_fn

    def recurrent_backward(
        grad_tok,
        grad_st,
        normed_tok,
        normed_st,
        tok_block,
        st_block,
        prior_block,
        token_lse,
        state_lse,
        opening,
        carry_keys,
        carry_values,
        grad_sums,
        active_tick,
    ):
        reach_prior, reach_current = token_masks(opening)
        allowed = jnp.concatenate([reach_prior, reach_current, state_keys_all], axis=1)
        token_keys = jnp.concatenate([prior_block[:, 1], tok_block[:, 1], st_block[:, 1]], axis=0)
        token_values = jnp.concatenate([prior_block[:, 2], tok_block[:, 2], st_block[:, 2]], axis=0)
        state_keys = jnp.concatenate([tok_block[:, 1], st_block[:, 1]], axis=0)
        state_values = jnp.concatenate([tok_block[:, 2], st_block[:, 2]], axis=0)
        weight_out = jnp.einsum(
            "rn,rd->nd", tok_block[:, 3], grad_tok, preferred_element_type=jnp.float32
        )
        weight_state_out = jnp.einsum(
            "sn,sd->nd", st_block[:, 3], grad_st, preferred_element_type=jnp.float32
        )
        grad_token_mixture = jnp.einsum(
            "rd,nd->rn", grad_tok, wout_c, preferred_element_type=jnp.float32
        ).astype(jnp.bfloat16)
        grad_state_mixture = jnp.einsum(
            "sd,nd->sn", grad_st, sout_c, preferred_element_type=jnp.float32
        ).astype(jnp.bfloat16)
        grad_query, grad_keys, grad_values = attend_backward(
            split_heads(tok_block[:, 0]),
            split_heads(token_keys),
            split_heads(token_values),
            allowed,
            token_lse,
            split_heads(grad_token_mixture),
        )
        state_query, state_grad_keys, state_grad_values = attend_backward(
            split_heads(st_block[:, 0]),
            split_heads(state_keys),
            split_heads(state_values),
            every_key,
            state_lse,
            split_heads(grad_state_mixture),
        )
        grad_query = grad_query.reshape(token_rows, local_width)
        grad_keys = grad_keys.reshape(2 * token_rows + state_count, local_width)
        grad_values = grad_values.reshape(2 * token_rows + state_count, local_width)
        state_query = state_query.reshape(state_count, local_width)
        state_grad_keys = state_grad_keys.reshape(token_rows + state_count, local_width)
        state_grad_values = state_grad_values.reshape(token_rows + state_count, local_width)
        own_keys = (
            grad_keys[token_rows : 2 * token_rows] + state_grad_keys[:token_rows] + carry_keys
        )
        own_values = (
            grad_values[token_rows : 2 * token_rows] + state_grad_values[:token_rows] + carry_values
        )
        cell_keys = grad_keys[2 * token_rows :] + state_grad_keys[token_rows:]
        cell_values = grad_values[2 * token_rows :] + state_grad_values[token_rows:]
        grad_proj = jnp.stack([grad_query, own_keys, own_values], axis=1).astype(jnp.bfloat16)
        grad_state_proj = jnp.stack([state_query, cell_keys, cell_values], axis=1).astype(
            jnp.bfloat16
        )
        weight_in = jnp.einsum(
            "rd,rcn->dcn", normed_tok, grad_proj, preferred_element_type=jnp.float32
        )
        weight_state_in = jnp.einsum(
            "sd,scn->dcn", normed_st, grad_state_proj, preferred_element_type=jnp.float32
        )
        grad_normed = jnp.einsum(
            "rcn,dcn->rd", grad_proj, wqkv_c, preferred_element_type=jnp.float32
        )
        grad_state_normed = jnp.einsum(
            "scn,dcn->sd", grad_state_proj, sqkv_c, preferred_element_type=jnp.float32
        )
        changes = {4: weight_in, 5: weight_state_in, 6: weight_out, 7: weight_state_out}
        return (
            grad_normed,
            grad_state_normed,
            grad_keys[:token_rows],
            grad_values[:token_rows],
            renewed(grad_sums, active_tick, changes),
        )

    forward_branches = [
        plain_forward,
        feed_forward(up_b, down_b),
        recurrent_forward,
        feed_forward(up_d, down_d),
    ]
    backward_branches = [
        plain_backward,
        feed_backward(up_b, down_b, 2, 3),
        recurrent_backward,
        feed_backward(up_d, down_d, 8, 9),
    ]

    def forward_tick(tick_number, carried):
        (
            received,
            state_carry,
            tok_normed,
            st_normed,
            tok_stored,
            st_stored,
            tok_lse_all,
            st_lse_all,
            entered,
            state_entered,
            updates,
            leaving_rows,
            finals,
        ) = carried
        block_number = tick_number - section_index
        active_tick = (block_number >= 0) & (block_number < block_count)
        block_index = jnp.clip(block_number, 0, block_count - 1)
        opening = begins[block_index]
        entering = jnp.where(
            section_index == 0, layer_input[0, block_index].astype(jnp.float32), received
        )
        state_in = jnp.where(opening, initial, state_carry)
        token_gain = token_gains[section_index]
        normed_shard = (entering * inverse_rms(entering) * token_gain).astype(jnp.bfloat16)
        state_normed_shard = (state_in * inverse_rms(state_in) * state_gain).astype(jnp.bfloat16)
        normed_tok, normed_st = (
            lax.all_gather(normed_shard, "tensor", axis=0, tiled=True),
            lax.all_gather(state_normed_shard, "tensor", axis=0, tiled=True),
        )
        prior_block = tok_stored[jnp.maximum(block_index - 1, 0)]
        branch, update_term, stored, state_stored, token_lse, state_lse = lax.switch(
            section_index, forward_branches, normed_tok, normed_st, prior_block, opening
        )
        branch_shard, update_shard = (
            lax.psum_scatter(
                branch.astype(jnp.bfloat16), "tensor", scatter_dimension=0, tiled=True
            ).astype(jnp.float32),
            lax.psum_scatter(
                update_term.astype(jnp.bfloat16), "tensor", scatter_dimension=0, tiled=True
            ).astype(jnp.float32),
        )
        leaving = entering + branch_shard
        state_new = retain * state_in + (1.0 - retain) * update_shard
        tok_normed = place_row(tok_normed, block_index, normed_tok, active_tick)
        st_normed = place_row(st_normed, block_index, normed_st, active_tick)
        tok_stored = place_row(tok_stored, block_index, stored, active_tick)
        st_stored = place_row(st_stored, block_index, state_stored, active_tick)
        tok_lse_all = place_row(tok_lse_all, block_index, token_lse, active_tick)
        st_lse_all = place_row(st_lse_all, block_index, state_lse, active_tick)
        entered = place_row(entered, block_index, entering, active_tick)
        state_entered = place_row(state_entered, block_index, state_in, active_tick)
        updates = place_row(updates, block_index, update_shard, active_tick)
        leaving_rows = place_row(leaving_rows, block_index, leaving, active_tick)
        on_cell = active_tick & on_cell_section
        state_carry = jnp.where(on_cell, state_new, state_carry)
        keep_final = on_cell & closes[block_index] & lively[block_index]
        slot_hit = (jnp.arange(SLOTS, dtype=jnp.int32) == numbers[block_index])[
            None, :, None
        ] & keep_final
        finals = jnp.where(slot_hit, state_new[:, None, :], finals)
        received = shifted(leaving.astype(jnp.bfloat16), "section", 1).astype(leaving.dtype)
        return (
            received,
            state_carry,
            tok_normed,
            st_normed,
            tok_stored,
            st_stored,
            tok_lse_all,
            st_lse_all,
            entered,
            state_entered,
            updates,
            leaving_rows,
            finals,
        )

    forward_start = (
        jnp.zeros((shard_rows, model_width), jnp.float32),
        jnp.zeros((state_shard, model_width), jnp.float32),
        jnp.zeros((block_count, token_rows, model_width), jnp.bfloat16),
        jnp.zeros((block_count, state_count, model_width), jnp.bfloat16),
        jnp.zeros((block_count, token_rows, 4, local_width), jnp.bfloat16),
        jnp.zeros((block_count, state_count, 4, local_width), jnp.bfloat16),
        jnp.zeros((block_count, local_heads, token_rows), jnp.float32),
        jnp.zeros((block_count, local_heads, state_count), jnp.float32),
        jnp.zeros((block_count, shard_rows, model_width), jnp.float32),
        jnp.zeros((block_count, state_shard, model_width), jnp.float32),
        jnp.zeros((block_count, state_shard, model_width), jnp.float32),
        jnp.zeros((block_count, shard_rows, model_width), jnp.float32),
        jnp.zeros((state_shard, SLOTS, model_width), jnp.float32),
    )
    (
        _,
        _,
        tok_normed,
        st_normed,
        tok_stored,
        st_stored,
        tok_lse_all,
        st_lse_all,
        entered,
        state_entered,
        updates,
        leaving_rows,
        finals,
    ) = lax.fori_loop(0, block_count + 3, forward_tick, forward_start)
    gain_rows_of_section = jnp.array([0, 1, 2, 4], dtype=jnp.int32)
    small_rows = jnp.arange(6, dtype=jnp.int32)[:, None]

    def backward_tick(tick_number, carried):
        (
            received,
            state_grad,
            carry_keys,
            carry_values,
            grad_sums,
            smalls,
            initial_grad,
            input_rows,
        ) = carried
        block_number = block_count - 1 - tick_number + 3 - section_index
        active_tick = (block_number >= 0) & (block_number < block_count)
        block_index = jnp.clip(block_number, 0, block_count - 1)
        opening = begins[block_index]
        arriving = jnp.where(
            section_index == 3,
            output_grad[0, block_index].astype(jnp.float32)
            * lively[block_index].astype(jnp.float32),
            received,
        )
        update_grad = (1.0 - retain) * state_grad
        grad_tok, grad_st = (
            lax.all_gather(arriving.astype(jnp.bfloat16), "tensor", axis=0, tiled=True),
            lax.all_gather(update_grad.astype(jnp.bfloat16), "tensor", axis=0, tiled=True),
        )
        grad_normed_tok, grad_normed_st, prior_keys, prior_values, grad_sums = lax.switch(
            section_index,
            backward_branches,
            grad_tok,
            grad_st,
            tok_normed[block_index],
            st_normed[block_index],
            tok_stored[block_index],
            st_stored[block_index],
            tok_stored[jnp.maximum(block_index - 1, 0)],
            tok_lse_all[block_index],
            st_lse_all[block_index],
            opening,
            carry_keys,
            carry_values,
            grad_sums,
            active_tick,
        )
        tok_shard, st_shard = (
            lax.psum_scatter(
                grad_normed_tok.astype(jnp.bfloat16), "tensor", scatter_dimension=0, tiled=True
            ).astype(jnp.float32),
            lax.psum_scatter(
                grad_normed_st.astype(jnp.bfloat16), "tensor", scatter_dimension=0, tiled=True
            ).astype(jnp.float32),
        )
        grad_entering, token_gain_term = norm_back(
            entered[block_index], token_gains[section_index], tok_shard
        )
        leaving_grad = arriving + grad_entering
        state_in = state_entered[block_index]
        grad_state_norm, state_gain_term = norm_back(state_in, state_gain, st_shard)
        grad_state_in = retain * state_grad + grad_state_norm
        bias_term = (
            jnp.sum(state_grad * (state_in - updates[block_index]), axis=0)
            * retain
            * (1.0 - retain)
        )
        on_cell = active_tick & on_cell_section
        gain_part = (small_rows == gain_rows_of_section[section_index]).astype(
            jnp.float32
        ) * token_gain_term[None, :]
        cell_part = (small_rows == 3).astype(jnp.float32) * state_gain_term[None, :] + (
            small_rows == 5
        ).astype(jnp.float32) * bias_term[None, :]
        smalls = (
            smalls + jnp.where(active_tick, gain_part, 0.0) + jnp.where(on_cell, cell_part, 0.0)
        )
        initial_grad = initial_grad + jnp.where(on_cell & opening, grad_state_in, 0.0)
        state_grad = jnp.where(on_cell, jnp.where(opening, 0.0, grad_state_in), state_grad)
        carry_keys = jnp.where(active_tick, prior_keys, carry_keys)
        carry_values = jnp.where(active_tick, prior_values, carry_values)
        input_rows = place_row(input_rows, block_index, leaving_grad, active_tick)
        received = shifted(for_sending(leaving_grad), "section", -1).astype(leaving_grad.dtype)
        return (
            received,
            state_grad,
            carry_keys,
            carry_values,
            grad_sums,
            smalls,
            initial_grad,
            input_rows,
        )

    zero_grads = (
        jnp.zeros(wqkv_a.shape, jnp.float32),
        jnp.zeros(wout_a.shape, jnp.float32),
        jnp.zeros(up_b.shape, jnp.float32),
        jnp.zeros(down_b.shape, jnp.float32),
        jnp.zeros(wqkv_c.shape, jnp.float32),
        jnp.zeros(sqkv_c.shape, jnp.float32),
        jnp.zeros(wout_c.shape, jnp.float32),
        jnp.zeros(sout_c.shape, jnp.float32),
        jnp.zeros(up_d.shape, jnp.float32),
        jnp.zeros(down_d.shape, jnp.float32),
    )
    backward_start = (
        jnp.zeros((shard_rows, model_width), jnp.float32),
        jnp.zeros((state_shard, model_width), jnp.float32),
        empty_carry,
        empty_carry,
        zero_grads,
        jnp.zeros((6, model_width), jnp.float32),
        jnp.zeros((state_shard, model_width), jnp.float32),
        jnp.zeros((block_count, shard_rows, model_width), jnp.float32),
    )
    _, _, _, _, grad_sums, smalls, initial_grad, input_rows = lax.fori_loop(
        0, block_count + 3, backward_tick, backward_start
    )
    out_term = jnp.where(
        section_index == 3, leaving_rows * lively[:, None, None].astype(jnp.float32), 0.0
    )[None]
    input_term = jnp.where(section_index == 0, input_rows, 0.0)[None]
    final_term = jnp.where(section_index == 2, finals, 0.0)[None]
    out_share, input_share, final_share = (
        lax.psum_scatter(
            out_term.astype(jnp.bfloat16), "section", scatter_dimension=3, tiled=True
        ).astype(jnp.float32),
        lax.psum_scatter(
            input_term.astype(jnp.bfloat16), "section", scatter_dimension=3, tiled=True
        ).astype(jnp.float32),
        lax.psum_scatter(
            final_term.astype(jnp.bfloat16), "section", scatter_dimension=3, tiled=True
        ).astype(jnp.float32),
    )
    (
        grad_qkv_a,
        grad_out_a,
        grad_upper_b,
        grad_lower_b,
        grad_qkv_c,
        grad_state_qkv,
        grad_out_c,
        grad_state_out,
        grad_upper_d,
        grad_lower_d,
    ) = grad_sums
    totals = (
        lax.psum(grad_qkv_a.astype(jnp.bfloat16), "dp").astype(jnp.float32),
        lax.psum(grad_out_a.astype(jnp.bfloat16), "dp").astype(jnp.float32),
        lax.psum(grad_upper_b.astype(jnp.bfloat16), "dp").astype(jnp.float32),
        lax.psum(grad_lower_b.astype(jnp.bfloat16), "dp").astype(jnp.float32),
        lax.psum(grad_qkv_c.astype(jnp.bfloat16), "dp").astype(jnp.float32),
        lax.psum(grad_state_qkv.astype(jnp.bfloat16), "dp").astype(jnp.float32),
        lax.psum(grad_out_c.astype(jnp.bfloat16), "dp").astype(jnp.float32),
        lax.psum(grad_state_out.astype(jnp.bfloat16), "dp").astype(jnp.float32),
        lax.psum(grad_upper_d.astype(jnp.bfloat16), "dp").astype(jnp.float32),
        lax.psum(grad_lower_d.astype(jnp.bfloat16), "dp").astype(jnp.float32),
        lax.psum(initial_grad.astype(jnp.bfloat16), "dp").astype(jnp.float32),
    )
    small_total = lax.psum(smalls, ("dp", "tensor"))
    shares = (
        lax.psum_scatter(
            totals[0].astype(jnp.bfloat16), "section", scatter_dimension=0, tiled=True
        ).astype(jnp.float32),
        lax.psum_scatter(
            totals[1].astype(jnp.bfloat16), "section", scatter_dimension=1, tiled=True
        ).astype(jnp.float32),
        lax.psum_scatter(
            totals[2].astype(jnp.bfloat16), "section", scatter_dimension=0, tiled=True
        ).astype(jnp.float32),
        lax.psum_scatter(
            totals[3].astype(jnp.bfloat16), "section", scatter_dimension=1, tiled=True
        ).astype(jnp.float32),
        lax.psum_scatter(
            totals[4].astype(jnp.bfloat16), "section", scatter_dimension=0, tiled=True
        ).astype(jnp.float32),
        lax.psum_scatter(
            totals[5].astype(jnp.bfloat16), "section", scatter_dimension=0, tiled=True
        ).astype(jnp.float32),
        lax.psum_scatter(
            totals[6].astype(jnp.bfloat16), "section", scatter_dimension=1, tiled=True
        ).astype(jnp.float32),
        lax.psum_scatter(
            totals[7].astype(jnp.bfloat16), "section", scatter_dimension=1, tiled=True
        ).astype(jnp.float32),
        lax.psum_scatter(
            totals[8].astype(jnp.bfloat16), "section", scatter_dimension=0, tiled=True
        ).astype(jnp.float32),
        lax.psum_scatter(
            totals[9].astype(jnp.bfloat16), "section", scatter_dimension=1, tiled=True
        ).astype(jnp.float32),
        lax.psum_scatter(
            totals[10].astype(jnp.bfloat16), "section", scatter_dimension=1, tiled=True
        ).astype(jnp.float32),
        lax.psum_scatter(
            small_total.astype(jnp.bfloat16), "section", scatter_dimension=1, tiled=True
        ).astype(jnp.float32),
    )
    small_share = shares[11]
    return (
        out_share.astype(jnp.bfloat16),
        final_share,
        input_share,
        small_share[0],
        shares[0],
        shares[1],
        small_share[1],
        shares[2],
        shares[3],
        small_share[2],
        small_share[3],
        shares[4],
        shares[5],
        shares[6],
        shares[7],
        small_share[5],
        shares[10],
        small_share[4],
        shares[8],
        shares[9],
    )


CHAIN = 4
SCALE = 1.0 / math.sqrt(HEAD_DIM)
ALL_AXES = ("section", "dp", "tensor")
GROUP = ("section", "tensor")
VMEM_BYTES = 56 * 1024 * 1024


def block_of(section, tensor):
    high = section // 2
    return 2 * (2 * high + (tensor ^ high)) + section % 2


DEVICE_OF_BLOCK = [0] * 8
for _section in range(4):
    for _tensor in range(2):
        DEVICE_OF_BLOCK[block_of(_section, _tensor)] = 2 * _section + _tensor
TO_NEXT = [(DEVICE_OF_BLOCK[b], DEVICE_OF_BLOCK[b + 1]) for b in range(7)]
TO_PRIOR = [(there, here) for here, there in TO_NEXT]
SWAP = [(0, 1), (1, 0)]


def params(**extra):
    return pltpu.CompilerParams(vmem_limit_bytes=VMEM_BYTES, **extra)


def nt(a, b):
    return lax.dot_general(a, b, (((1,), (1,)), ((), ())), preferred_element_type=jnp.float32)


def nn(a, b):
    return lax.dot_general(a, b, (((1,), (0,)), ((), ())), preferred_element_type=jnp.float32)


def tn(a, b):
    return lax.dot_general(a, b, (((0,), (0,)), ((), ())), preferred_element_type=jnp.float32)


def bf(a):
    return a.astype(jnp.bfloat16)


def later_mask(rows):
    return lax.broadcasted_iota(jnp.int32, (rows, rows), 1) > lax.broadcasted_iota(
        jnp.int32, (rows, rows), 0
    )


def attend_kernel(with_states, *refs):
    if with_states:
        open_ref, q, k, v, pk, pv, sk, sv, out, lse = refs
    else:
        open_ref, q, k, v, pk, pv, out, lse = refs
    later = later_mask(q.shape[0])
    query = q[...]
    prior = jnp.where(open_ref[0] > 0, NEGATIVE, nt(query, pk[...]))
    scores = jnp.where(later, prior, nt(query, k[...])) * SCALE
    top = jnp.max(scores, axis=-1, keepdims=True)
    if with_states:
        more = nt(query, sk[...]) * SCALE
        top = jnp.maximum(top, jnp.max(more, axis=-1, keepdims=True))
    weights = jnp.exp(scores - top)
    total = jnp.sum(weights, axis=-1, keepdims=True)
    if with_states:
        more_weights = jnp.exp(more - top)
        total = total + jnp.sum(more_weights, axis=-1, keepdims=True)
    share = 1.0 / total
    weights = weights * share
    mixed = nn(bf(jnp.where(later, weights, 0.0)), pv[...]) + nn(
        bf(jnp.where(later, 0.0, weights)), v[...]
    )
    if with_states:
        mixed = mixed + nn(bf(more_weights * share), sv[...])
    out[...] = bf(mixed)
    lse[0] = top + jnp.log(total)


def head_block(rows, offset):
    return pl.BlockSpec((rows, HEAD_DIM), lambda h: (0, offset + h))


def attend(opening, proj, prior, states=None):
    rows, width = proj.shape[0], proj.shape[1] // 3
    heads = width // HEAD_DIM
    specs = [pl.BlockSpec(memory_space=pltpu.SMEM)]
    specs += [head_block(rows, i * heads) for i in range(3)]
    specs += [head_block(rows, i * heads) for i in range(2)]
    args = [opening, proj, proj, proj, prior, prior]
    keys = 2 * rows
    if states is not None:
        specs += [head_block(states.shape[0], i * heads) for i in (1, 2)]
        args += [states, states]
        keys += states.shape[0]
    return pl.pallas_call(
        functools.partial(attend_kernel, states is not None),
        grid=(heads,),
        in_specs=specs,
        out_specs=[
            head_block(rows, 0),
            pl.BlockSpec((1, rows, 1), lambda h: (h, 0, 0)),
        ],
        out_shape=[
            jax.ShapeDtypeStruct((rows, width), jnp.bfloat16),
            jax.ShapeDtypeStruct((heads, rows, 1), jnp.float32),
        ],
        compiler_params=params(),
        cost_estimate=pl.CostEstimate(
            flops=4 * rows * keys * width,
            bytes_accessed=2 * rows * width * 8,
            transcendentals=rows * keys * heads // 2,
        ),
        name="attend",
    )(*args)


def attend_back_kernel(with_states, *refs):
    if with_states:
        (open_ref, q, k, v, pk, pv, sk, sv, gmix, lse) = refs[:10]
        (gq, gk, gv, gpk, gpv, gsk, gsv) = refs[10:]
    else:
        (open_ref, q, k, v, pk, pv, gmix, lse) = refs[:8]
        (gq, gk, gv, gpk, gpv) = refs[8:]
    later = later_mask(q.shape[0])
    query, grad, log_total = q[...], gmix[...], lse[0]
    prior = jnp.where(open_ref[0] > 0, NEGATIVE, nt(query, pk[...]))
    scores = jnp.where(later, prior, nt(query, k[...])) * SCALE
    weights = jnp.exp(scores - log_total)
    grad_weights = jnp.where(later, nt(grad, pv[...]), nt(grad, v[...]))
    inner = jnp.sum(weights * grad_weights, axis=-1, keepdims=True)
    if with_states:
        more_weights = jnp.exp(nt(query, sk[...]) * SCALE - log_total)
        more_grad = nt(grad, sv[...])
        inner = inner + jnp.sum(more_weights * more_grad, axis=-1, keepdims=True)
    gpv[...] = tn(bf(jnp.where(later, weights, 0.0)), grad).astype(gpv.dtype)
    gv[...] = tn(bf(jnp.where(later, 0.0, weights)), grad)
    grad_scores = weights * (grad_weights - inner)
    from_prior = bf(jnp.where(later, grad_scores, 0.0))
    from_own = bf(jnp.where(later, 0.0, grad_scores))
    grad_query = nn(from_prior, pk[...]) + nn(from_own, k[...])
    gpk[...] = (tn(from_prior, query) * SCALE).astype(gpk.dtype)
    gk[...] = tn(from_own, query) * SCALE
    if with_states:
        from_states = bf(more_weights * (more_grad - inner))
        gsv[...] = tn(bf(more_weights), grad)
        gsk[...] = tn(from_states, query) * SCALE
        grad_query = grad_query + nn(from_states, sk[...])
    gq[...] = bf(grad_query * SCALE)


def attend_back(opening, proj, prior, grad_mixed, lse, states=None):
    rows, width = proj.shape[0], proj.shape[1] // 3
    heads = width // HEAD_DIM
    specs = [pl.BlockSpec(memory_space=pltpu.SMEM)]
    specs += [head_block(rows, i * heads) for i in range(3)]
    specs += [head_block(rows, i * heads) for i in range(2)]
    args = [opening, proj, proj, proj, prior, prior]
    keys = 2 * rows
    if states is not None:
        specs += [head_block(states.shape[0], i * heads) for i in (1, 2)]
        args += [states, states]
        keys += states.shape[0]
    specs += [head_block(rows, 0), pl.BlockSpec((1, rows, 1), lambda h: (h, 0, 0))]
    args += [grad_mixed, lse]
    kinds = [jnp.bfloat16, jnp.float32, jnp.float32, jnp.bfloat16, jnp.bfloat16]
    if states is not None:
        kinds += [jnp.float32, jnp.float32]
    return pl.pallas_call(
        functools.partial(attend_back_kernel, states is not None),
        grid=(heads,),
        in_specs=specs,
        out_specs=[head_block(rows, 0) for _ in kinds],
        out_shape=[jax.ShapeDtypeStruct((rows, width), kind) for kind in kinds],
        compiler_params=params(),
        cost_estimate=pl.CostEstimate(
            flops=10 * rows * keys * width,
            bytes_accessed=2 * rows * width * 24,
            transcendentals=rows * keys * heads // 2,
        ),
        name="attend_back",
    )(*args)


def state_step_kernel(
    state, gain, keep, own, other, own_v, other_v, sqkv, sout,
    hs, proj, mixed, lse, update, fresh, hidden, mix_store,
):
    h = pl.program_id(0)
    heads = pl.num_programs(0)
    half = heads // 2

    @pl.when(h == 0)
    def _():
        value = state[...]
        hidden[...] = bf(value * inverse_rms(value) * gain[...])
        hs[...] = hidden[...]

    first = h < half
    key = jnp.where(first, own[...], other[...])
    val = jnp.where(first, own_v[...], other_v[...])
    qkv = bf(nn(hidden[...], sqkv[0]))
    sq, sk, sv = (qkv[:, i * HEAD_DIM : (i + 1) * HEAD_DIM] for i in range(3))
    proj[0, 0], proj[0, 1], proj[0, 2] = sq, sk, sv
    score_tok = nt(sq, key) * SCALE
    score_st = nt(sq, sk) * SCALE
    top = jnp.maximum(
        jnp.max(score_tok, axis=-1, keepdims=True), jnp.max(score_st, axis=-1, keepdims=True)
    )
    p_tok = jnp.exp(score_tok - top)
    p_st = jnp.exp(score_st - top)
    total = jnp.sum(p_tok, axis=-1, keepdims=True) + jnp.sum(p_st, axis=-1, keepdims=True)
    share = 1.0 / total
    mix = bf(nn(bf(p_tok * share), val) + nn(bf(p_st * share), sv))
    mixed[0] = mix
    mix_store[h] = mix
    lse[0] = top + jnp.log(total)

    @pl.when(h == heads - 1)
    def _():
        term = jnp.zeros(state.shape, jnp.float32)
        for i in range(mix_store.shape[0]):
            term = term + nn(mix_store[i], sout[i])
        update[...] = term
        fresh[...] = keep[...] * state[...] + (1.0 - keep[...]) * term


def half_block(rows, offset, half, second):
    if second:
        return pl.BlockSpec((rows, HEAD_DIM), lambda h: (0, offset + jnp.maximum(h - half, 0)))
    return pl.BlockSpec((rows, HEAD_DIM), lambda h: (0, offset + jnp.minimum(h, half - 1)))


def whole(shape):
    return pl.BlockSpec(shape, lambda h: (0,) * len(shape))


def per_head(half, rows):
    return pl.BlockSpec((1, 3, rows, HEAD_DIM), lambda h: (h // half, 0, 0, h % half))


def state_step(state, gain, keep, own, other, sqkv, sout):
    count, width = state.shape
    rows = own.shape[0]
    heads = sqkv.shape[0]
    half = heads // 2
    return pl.pallas_call(
        state_step_kernel,
        grid=(heads,),
        in_specs=[
            whole((count, width)),
            whole((1, width)),
            whole((1, width)),
            half_block(rows, half, half, False),
            half_block(rows, half, half, True),
            half_block(rows, 2 * half, half, False),
            half_block(rows, 2 * half, half, True),
            pl.BlockSpec((1, width, 3 * HEAD_DIM), lambda h: (h, 0, 0)),
            whole(sout.shape),
        ],
        out_specs=[
            whole((count, width)),
            per_head(half, count),
            pl.BlockSpec((1, count, HEAD_DIM), lambda h: (h // half, 0, h % half)),
            pl.BlockSpec((1, count, 1), lambda h: (h, 0, 0)),
            whole((count, width)),
            whole((count, width)),
        ],
        out_shape=[
            jax.ShapeDtypeStruct((count, width), jnp.bfloat16),
            jax.ShapeDtypeStruct((2, 3, count, width // 2), jnp.bfloat16),
            jax.ShapeDtypeStruct((2, count, width // 2), jnp.bfloat16),
            jax.ShapeDtypeStruct((heads, count, 1), jnp.float32),
            jax.ShapeDtypeStruct((count, width), jnp.float32),
            jax.ShapeDtypeStruct((count, width), jnp.float32),
        ],
        scratch_shapes=[
            pltpu.VMEM((count, width), jnp.bfloat16),
            pltpu.VMEM((heads, count, HEAD_DIM), jnp.bfloat16),
        ],
        compiler_params=params(),
        cost_estimate=pl.CostEstimate(
            flops=count * width * (8 * width + 8 * count),
            bytes_accessed=20 * 1024 * 1024,
            transcendentals=count * count * 2 * heads,
        ),
        name="state_step",
    )(state, gain, keep, own, other, own, other, sqkv, sout)


def state_back_kernel(
    grad_new, state, update, gain, keep, hs_unused, proj, lse, own, other, own_v, other_v,
    tok_k0, tok_k1, tok_v0, tok_v1, sqkv, sout,
    grad_in, gproj, gtok, gup, small, grad_hidden, gup_store,
):
    h = pl.program_id(0)
    heads = pl.num_programs(0)
    half = heads // 2

    @pl.when(h == 0)
    def _():
        gup_store[...] = bf((1.0 - keep[...]) * grad_new[...])
        gup[...] = gup_store[...]
        grad_hidden[...] = jnp.zeros_like(grad_hidden)

    first = h < half
    key = jnp.where(first, own[...], other[...])
    val = jnp.where(first, own_v[...], other_v[...])
    grad = bf(nt(gup_store[...], sout[h]))
    sq, sk, sv = proj[0, 0], proj[0, 1], proj[0, 2]
    log_total = lse[0]
    p_tok = jnp.exp(nt(sq, key) * SCALE - log_total)
    p_st = jnp.exp(nt(sq, sk) * SCALE - log_total)
    d_tok = nt(grad, val)
    d_st = nt(grad, sv)
    inner = jnp.sum(p_tok * d_tok, axis=-1, keepdims=True) + jnp.sum(
        p_st * d_st, axis=-1, keepdims=True
    )
    s_tok = bf(p_tok * (d_tok - inner))
    s_st = bf(p_st * (d_st - inner))
    gtok[0, 1] = tn(bf(p_tok), grad)
    gtok[0, 0] = tn(s_tok, sq) * SCALE
    gsv = tn(bf(p_st), grad) + jnp.where(first, tok_v0[...], tok_v1[...])
    gsk = tn(s_st, sq) * SCALE + jnp.where(first, tok_k0[...], tok_k1[...])
    gsq = (nn(s_tok, key) + nn(s_st, sk)) * SCALE
    gqkv = jnp.concatenate([bf(gsq), bf(gsk), bf(gsv)], axis=1)
    for i in range(3):
        gproj[0, i] = gqkv[:, i * HEAD_DIM : (i + 1) * HEAD_DIM]
    grad_hidden[...] += nt(gqkv, sqkv[0])

    @pl.when(h == heads - 1)
    def _():
        value, back, new = state[...], grad_hidden[...], grad_new[...]
        factor = inverse_rms(value)
        scaled = value * factor
        through = back * gain[...]
        grad_in[...] = keep[...] * new + factor * (
            through - scaled * jnp.mean(through * scaled, axis=-1, keepdims=True)
        )
        small[0:1, :] = jnp.sum(back * scaled, axis=0, keepdims=True)
        small[1:2, :] = jnp.sum(new * (value - update[...]), axis=0, keepdims=True) * (
            keep[...] * (1.0 - keep[...])
        )


def state_back(
    grad_new, state, update, gain, keep, hs, proj, lse, own, other,
    tok_k0, tok_v0, tok_k1, tok_v1, sqkv, sout,
):
    count, width = state.shape
    rows = own.shape[0]
    heads = sqkv.shape[0]
    half = heads // 2
    return pl.pallas_call(
        state_back_kernel,
        grid=(heads,),
        in_specs=[
            whole((count, width)),
            whole((count, width)),
            whole((count, width)),
            whole((1, width)),
            whole((1, width)),
            pl.BlockSpec(memory_space=pl.ANY),
            per_head(half, count),
            pl.BlockSpec((1, count, 1), lambda h: (h, 0, 0)),
            half_block(rows, half, half, False),
            half_block(rows, half, half, True),
            half_block(rows, 2 * half, half, False),
            half_block(rows, 2 * half, half, True),
            half_block(count, 0, half, False),
            half_block(count, 0, half, True),
            half_block(count, 0, half, False),
            half_block(count, 0, half, True),
            pl.BlockSpec((1, width, 3 * HEAD_DIM), lambda h: (h, 0, 0)),
            whole(sout.shape),
        ],
        out_specs=[
            whole((count, width)),
            per_head(half, count),
            pl.BlockSpec((1, 2, rows, HEAD_DIM), lambda h: (h // half, 0, 0, h % half)),
            whole((count, width)),
            whole((2, width)),
        ],
        out_shape=[
            jax.ShapeDtypeStruct((count, width), jnp.float32),
            jax.ShapeDtypeStruct((2, 3, count, width // 2), jnp.bfloat16),
            jax.ShapeDtypeStruct((2, 2, rows, width // 2), jnp.float32),
            jax.ShapeDtypeStruct((count, width), jnp.bfloat16),
            jax.ShapeDtypeStruct((2, width), jnp.float32),
        ],
        scratch_shapes=[
            pltpu.VMEM((count, width), jnp.float32),
            pltpu.VMEM((count, width), jnp.bfloat16),
        ],
        compiler_params=params(),
        cost_estimate=pl.CostEstimate(
            flops=count * width * (16 * width + 20 * count),
            bytes_accessed=34 * 1024 * 1024,
            transcendentals=count * count * 2 * heads,
        ),
        name="state_back",
    )(
        grad_new, state, update, gain, keep, hs, proj, lse, own, other, own, other,
        tok_k0, tok_k1, tok_v0, tok_v1, sqkv, sout,
    )


def by_rows_kernel(place, buffer, a, g, out):
    product = bf(tn(a[...], g[0]))
    for i in range(product.shape[1] // 256):
        out[0, 0, i] = product[:, i * 256 : (i + 1) * 256]


def by_columns_kernel(place, buffer, a, g, out):
    product = bf(tn(a[...], g[...]))
    for i in range(product.shape[0] // 256):
        out[0, 0, i] = product[i * 256 : (i + 1) * 256]


def weight_grad(buffer, place, a, g, tile, by_rows):
    rows = a.shape[0]
    sections = buffer.shape[0]
    if by_rows:
        parts, width = g.shape[0], g.shape[2]
        wide = min(width, 1024)
        steps = width // wide
        tiles = wide // 256
        grid = (sections, parts * steps)
        a_spec = pl.BlockSpec((rows, a.shape[1] // sections), lambda s, n, place: (0, s))
        g_spec = pl.BlockSpec((1, rows, wide), lambda s, n, place: (n // steps, 0, n % steps))
        kernel = by_rows_kernel
    else:
        wide = min(a.shape[1], 1024)
        tiles = wide // 256
        grid = (sections, a.shape[1] // wide)
        a_spec = pl.BlockSpec((rows, wide), lambda s, n, place: (0, n))
        g_spec = pl.BlockSpec((rows, g.shape[1] // sections), lambda s, n, place: (0, s))
        kernel = by_columns_kernel
    start = tile // tiles
    size = grid[0] * grid[1] * tiles * 256 * 256
    return pl.pallas_call(
        kernel,
        grid_spec=pltpu.PrefetchScalarGridSpec(
            num_scalar_prefetch=1,
            grid=grid,
            in_specs=[pl.BlockSpec(memory_space=pl.ANY), a_spec, g_spec],
            out_specs=pl.BlockSpec(
                (1, 1, tiles, 256, 256), lambda s, n, place: (s, place[0], start + n, 0, 0)
            ),
        ),
        out_shape=jax.ShapeDtypeStruct(buffer.shape, buffer.dtype),
        input_output_aliases={1: 0},
        compiler_params=params(),
        cost_estimate=pl.CostEstimate(
            flops=2 * rows * size, bytes_accessed=2 * size, transcendentals=0
        ),
        name="weight_grad",
    )(place, buffer, a, g)


def gelu_back(values, grad):
    return jax.vjp(smooth, values)[1](grad)[0]


def block_body(
    layer_input, output_grad, seg_blocks, seg_group, gain_a, wqkv_a, wout_a, gain_b, up_b, down_b,
    gain_c, gain_s, wqkv_c, sqkv_c, wout_c, sout_c, gate_bias, init_states, gain_d, up_d, down_d,
):
    sections, tensors = lax.axis_size("section"), lax.axis_size("tensor")
    block_count, shard_rows, width = layer_input.shape[1:]
    rows = shard_rows * tensors
    section, tensor = lax.axis_index("section"), lax.axis_index("tensor")
    block = block_of(section, tensor)
    begins, closes, lively, numbers = layout(
        seg_blocks, seg_group, lax.axis_index("dp"), block_count
    )
    alive = lively[block]
    starts = begins[block] | jnp.logical_not(alive)
    ends = closes[block] | jnp.logical_not(alive)
    opening = starts.astype(jnp.int32)[None]
    own_place = tensor[None]
    other_place = 1 - own_place
    f32 = jnp.float32
    gains = {k: v.astype(f32) for k, v in dict(a=gain_a, b=gain_b, c=gain_c, d=gain_d).items()}

    def in_order(own, other):
        low = jnp.where(tensor == 0, own, other)
        high = jnp.where(tensor == 0, other, own)
        return low, high

    partner = block_of(section, 1 - tensor)

    def whole_block(stack, mine, theirs):
        own = lax.dynamic_index_in_dim(stack[0], mine, 0, False)
        other = lax.ppermute(lax.dynamic_index_in_dim(stack[0], theirs, 0, False), "tensor", SWAP)
        return jnp.concatenate(in_order(own, other), axis=0)

    def other_half(weight):
        size = weight.shape[0] // sections
        piece = lax.dynamic_slice_in_dim(weight, section * size, size, 0)
        return lax.all_gather(lax.ppermute(piece, "tensor", SWAP), "section", axis=0, tiled=True)

    def flat(weight):
        return weight.reshape(weight.shape[0], -1)

    tokens = whole_block(layer_input, block, partner)
    before = whole_block(layer_input, jnp.maximum(block - 1, 0), jnp.maximum(partner - 1, 0))
    wqkv_a0 = flat(wqkv_a)
    wqkv_a1 = other_half(wqkv_a0)
    wout_a1 = other_half(wout_a)
    up_b1, down_b1 = other_half(up_b), other_half(down_b)
    wqkv_c0, sqkv_c0 = flat(wqkv_c), flat(sqkv_c)
    wqkv_c1, sqkv_c1 = other_half(wqkv_c0), other_half(sqkv_c0)
    sout_c1 = other_half(sout_c)
    wout_c1 = other_half(wout_c)
    up_d1, down_d1 = other_half(up_d), other_half(down_d)
    cotangent = whole_block(output_grad, block, partner)
    initial = jnp.concatenate(
        in_order(init_states, lax.ppermute(init_states, "tensor", SWAP)), axis=0
    ).astype(f32)

    def normed(values, gain):
        return bf(values * inverse_rms(values) * gain)

    def dot(a, b):
        return jnp.dot(a, b, preferred_element_type=f32)

    def dot_t(a, b):
        return lax.dot_general(a, b, (((1,), (1,)), ((), ())), preferred_element_type=f32)

    half = wout_a.shape[0]
    r0 = tokens.astype(f32)
    h0 = normed(r0, gains["a"])
    h_before = normed(before.astype(f32), gains["a"])
    pa0, pa1 = bf(dot(h0, wqkv_a0)), bf(dot(h0, wqkv_a1))
    prior_a0 = bf(dot(h_before, wqkv_a0[:, half:]))
    prior_a1 = bf(dot(h_before, wqkv_a1[:, half:]))
    oa0, lse_a0 = attend(opening, pa0, prior_a0)
    oa1, lse_a1 = attend(opening, pa1, prior_a1)
    r1 = r0 + (dot(oa0, wout_a) + dot(oa1, wout_a1))

    h1 = normed(r1, gains["b"])
    ub0, ub1 = dot(h1, up_b), dot(h1, up_b1)
    ab0, ab1 = bf(smooth(ub0)), bf(smooth(ub1))
    r2 = r1 + (dot(ab0, down_b) + dot(ab1, down_b1))

    h2 = normed(r2, gains["c"])
    pc0, pc1 = bf(dot(h2, wqkv_c0)), bf(dot(h2, wqkv_c1))
    halo = lax.ppermute(jnp.stack(in_order(pc0[:, half:], pc1[:, half:])), GROUP, TO_NEXT)
    prior_c0, prior_c1 = in_order(halo[0], halo[1])

    def by_head(own, other):
        pieces = []
        for weight in (own, other):
            w = weight.reshape(width, 3, half // HEAD_DIM, HEAD_DIM).transpose(2, 0, 1, 3)
            pieces.append(w.reshape(half // HEAD_DIM, width, 3 * HEAD_DIM))
        return jnp.concatenate(pieces, axis=0)

    sqkv_heads = by_head(sqkv_c0, sqkv_c1)
    sout_heads = jnp.concatenate([sout_c, sout_c1], axis=0).reshape(-1, HEAD_DIM, width)
    retain = jax.nn.sigmoid(gate_bias.astype(f32))[None, :]
    state_gain = gain_s.astype(f32)[None, :]
    state_in = initial
    for step in range(CHAIN):
        hs, ps, os, lse_s, update, state_new = state_step(
            state_in, state_gain, retain, pc0, pc1, sqkv_heads, sout_heads
        )
        if step < CHAIN - 1:
            carried = lax.ppermute(bf(state_new), GROUP, TO_NEXT).astype(f32)
            state_in = jnp.where(starts, initial, carried)

    def flat_states(i):
        return jnp.concatenate([ps[i, 0], ps[i, 1], ps[i, 2]], axis=1)

    ps0, ps1 = flat_states(0), flat_states(1)
    oc0, lse_c0 = attend(opening, pc0, prior_c0, ps0)
    oc1, lse_c1 = attend(opening, pc1, prior_c1, ps1)
    r3 = r2 + (dot(oc0, wout_c) + dot(oc1, wout_c1))

    h3 = normed(r3, gains["d"])
    ud0, ud1 = dot(h3, up_d), dot(h3, up_d1)
    ad0, ad1 = bf(smooth(ud0)), bf(smooth(ud1))
    r4 = r3 + (dot(ad0, down_d) + dot(ad1, down_d1))
    result = bf(jnp.where(alive, r4, 0.0))

    def scattered(value):
        tiles = value.reshape(tensors, shard_rows, sections, width // sections)
        tiles = tiles.transpose(2, 0, 1, 3).reshape(sections * tensors, shard_rows, -1)
        landed = lax.all_to_all(tiles, GROUP, 0, 0, tiled=True)
        return jnp.stack([landed[DEVICE_OF_BLOCK[b]] for b in range(block_count)])

    out_share = scattered(result)[None]
    state_tiles = scattered(bf(state_new))
    chosen = (
        (numbers[:, None] == jnp.arange(SLOTS, dtype=jnp.int32)[None, :])
        & (closes & lively)[:, None]
    )
    final_share = jnp.stack(
        [
            jnp.sum(jnp.where(chosen[:, i, None, None], state_tiles.astype(f32), 0.0), axis=0)
            for i in range(SLOTS)
        ],
        axis=1,
    )[None]

    def reduced(buffer):
        pieces = buffer.reshape((sections * tensors,) + buffer.shape[2:])
        share = lax.psum_scatter(pieces, GROUP, scatter_dimension=0, tiled=True)
        return lax.psum(share, "dp")[0].astype(f32)

    def empty(tiles):
        return jnp.zeros((sections, tensors, tiles, 256, 256), jnp.bfloat16)

    def feed_back(grad, values, h, gain, u0, u1, a0, a1, up0, up1, down0, down1):
        gy = bf(grad)
        tiles = up0.shape[1] // 256
        buffer = empty(2 * tiles)
        g0 = bf(gelu_back(u0, dot_t(gy, down0)))
        g1 = bf(gelu_back(u1, dot_t(gy, down1)))
        buffer = weight_grad(buffer, own_place, a0, gy, tiles, False)
        buffer = weight_grad(buffer, other_place, a1, gy, tiles, False)
        buffer = weight_grad(buffer, own_place, h, g0[None], 0, True)
        buffer = weight_grad(buffer, other_place, h, g1[None], 0, True)
        through = dot_t(g0, up0) + dot_t(g1, up1)
        back, gain_grad = norm_back(values, gain, through)
        return grad + back, gain_grad, buffer

    def up_share(share, tiles):
        return share[:tiles].transpose(1, 0, 2).reshape(256, -1)

    def down_share(share, tiles):
        return share[tiles : 2 * tiles].reshape(-1, 256)

    grad4 = jnp.where(alive, cotangent.astype(f32), 0.0)
    grad3, gain_d_grad, buffer_d = feed_back(
        grad4, r3, h3, gains["d"], ud0, ud1, ad0, ad1, up_d, up_d1, down_d, down_d1
    )
    share_d = reduced(buffer_d)

    gy3 = bf(grad3)
    tok0 = attend_back(opening, pc0, prior_c0, bf(dot_t(gy3, wout_c)), lse_c0, ps0)
    tok1 = attend_back(opening, pc1, prior_c1, bf(dot_t(gy3, wout_c1)), lse_c1, ps1)

    def halo_back(one, two):
        pair = in_order(
            jnp.concatenate([one[3], one[4]], axis=1), jnp.concatenate([two[3], two[4]], axis=1)
        )
        back = lax.ppermute(jnp.stack(pair), GROUP, TO_PRIOR).astype(f32)
        return in_order(back[0], back[1])

    halo_c0, halo_c1 = halo_back(tok0, tok1)
    grad_new = jnp.zeros_like(initial)
    for step in range(CHAIN):
        grad_state, gproj, gtok, gup, small = state_back(
            grad_new, state_in, update, state_gain, retain, hs, ps, lse_s, pc0, pc1,
            tok0[5], tok0[6], tok1[5], tok1[6], sqkv_heads, sout_heads,
        )
        if step < CHAIN - 1:
            carried = lax.ppermute(bf(grad_state), GROUP, TO_PRIOR).astype(f32)
            grad_new = jnp.where(ends, 0.0, carried)

    def projected_back(parts, halo_part, extra=None):
        gk, gv = parts[1], parts[2]
        if extra is not None:
            gk, gv = gk + extra[0], gv + extra[1]
        return jnp.stack([parts[0], bf(gk + halo_part[:, :half]), bf(gv + halo_part[:, half:])])

    gc0 = projected_back(tok0, halo_c0, gtok[0])
    gc1 = projected_back(tok1, halo_c1, gtok[1])
    buffer_c = empty(17)
    buffer_c = weight_grad(buffer_c, own_place, h2, gc0, 0, True)
    buffer_c = weight_grad(buffer_c, other_place, h2, gc1, 0, True)
    buffer_c = weight_grad(buffer_c, own_place, hs, gproj[0], 6, True)
    buffer_c = weight_grad(buffer_c, other_place, hs, gproj[1], 6, True)
    buffer_c = weight_grad(buffer_c, own_place, oc0, gy3, 12, False)
    buffer_c = weight_grad(buffer_c, other_place, oc1, gy3, 12, False)
    buffer_c = weight_grad(buffer_c, own_place, os[0], gup, 14, False)
    buffer_c = weight_grad(buffer_c, other_place, os[1], gup, 14, False)
    first_grad = bf(jnp.where(begins[block], grad_state, 0.0))
    first_tiles = first_grad.reshape(tensors, -1, sections, 256).transpose(2, 0, 1, 3)
    buffer_c = lax.dynamic_update_slice(buffer_c, first_tiles[:, :, None], (0, 0, 16, 0, 0))
    share_c = reduced(buffer_c)

    def through_qkv(g, w):
        return sum(dot_t(g[i], w[:, i * half : (i + 1) * half]) for i in range(3))

    back_c, gain_c_grad = norm_back(
        r2, gains["c"], through_qkv(gc0, wqkv_c0) + through_qkv(gc1, wqkv_c1)
    )
    grad2 = grad3 + back_c

    grad1, gain_b_grad, buffer_b = feed_back(
        grad2, r1, h1, gains["b"], ub0, ub1, ab0, ab1, up_b, up_b1, down_b, down_b1
    )
    share_b = reduced(buffer_b)

    gy1 = bf(grad1)
    att0 = attend_back(opening, pa0, prior_a0, bf(dot_t(gy1, wout_a)), lse_a0)
    att1 = attend_back(opening, pa1, prior_a1, bf(dot_t(gy1, wout_a1)), lse_a1)
    halo_a0, halo_a1 = halo_back(att0, att1)
    ga0, ga1 = projected_back(att0, halo_a0), projected_back(att1, halo_a1)
    buffer_a = empty(8)
    buffer_a = weight_grad(buffer_a, own_place, oa0, gy1, 6, False)
    buffer_a = weight_grad(buffer_a, other_place, oa1, gy1, 6, False)
    buffer_a = weight_grad(buffer_a, own_place, h0, ga0, 0, True)
    buffer_a = weight_grad(buffer_a, other_place, h0, ga1, 0, True)
    share_a = reduced(buffer_a)
    back_a, gain_a_grad = norm_back(
        r0, gains["a"], through_qkv(ga0, wqkv_a0) + through_qkv(ga1, wqkv_a1)
    )
    input_share = scattered(bf(grad1 + back_a)).astype(f32)[None]

    smalls = jnp.stack(
        [gain_a_grad, gain_b_grad, gain_c_grad, small[0], gain_d_grad, small[1]]
    )
    smalls = lax.psum(smalls, ALL_AXES)
    small_share = lax.dynamic_slice_in_dim(
        smalls, section * (width // sections), width // sections, 1
    )

    def qkv_share(share, tile):
        return (
            share[tile : tile + 6].reshape(3, 2, 256, 256).transpose(2, 0, 1, 3).reshape(256, 3, 512)
        )

    def out_rows(share, tile):
        return share[tile : tile + 2].reshape(-1, 256)

    return (
        out_share,
        final_share,
        input_share,
        small_share[0],
        qkv_share(share_a, 0),
        out_rows(share_a, 6),
        small_share[1],
        up_share(share_b, 8),
        down_share(share_b, 8),
        small_share[2],
        small_share[3],
        qkv_share(share_c, 0),
        qkv_share(share_c, 6),
        out_rows(share_c, 12),
        out_rows(share_c, 14),
        small_share[5],
        share_c[16],
        small_share[4],
        up_share(share_d, 8),
        down_share(share_d, 8),
    )


def chosen(*arrays):
    devices = (lax.axis_size("section"), lax.axis_size("tensor"))
    if devices == (4, 2) and arrays[0].shape[1] == 8:
        return block_body(*arrays)
    return relay_body(*arrays)


def solution(mesh):
    in_specs = (
        P("dp", None, "tensor", None),
        P("dp", None, "tensor", None),
        P(),
        P(),
        P(),
        P(None, None, "tensor"),
        P("tensor", None),
        P(),
        P(None, "tensor"),
        P("tensor", None),
        P(),
        P(),
        P(None, None, "tensor"),
        P(None, None, "tensor"),
        P("tensor", None),
        P("tensor", None),
        P(),
        P("tensor", None),
        P(),
        P(None, "tensor"),
        P("tensor", None),
    )
    out_specs = (
        P("dp", None, "tensor", "section"),
        P("dp", "tensor", None, "section"),
        P("dp", None, "tensor", "section"),
        P("section"),
        P("section", None, "tensor"),
        P("tensor", "section"),
        P("section"),
        P("section", "tensor"),
        P("tensor", "section"),
        P("section"),
        P("section"),
        P("section", None, "tensor"),
        P("section", None, "tensor"),
        P("tensor", "section"),
        P("tensor", "section"),
        P("section"),
        P("tensor", "section"),
        P("section"),
        P("section", "tensor"),
        P("tensor", "section"),
    )
    return jax.shard_map(chosen, mesh=mesh, in_specs=in_specs, out_specs=out_specs, check_vma=False)
```

```python
import functools
import math

import jax
import jax.numpy as jnp
from jax import lax
from jax.experimental import pallas as pl
from jax.experimental.pallas import tpu as pltpu
from jax.sharding import PartitionSpec as P

SECTION, DP, TENSOR = "section", "dp", "tensor"
HEAD_DIM = 128
SLOTS = 3


EPSILON = 1e-06
NEGATIVE = -1e30


def shifted(value, axis, by):
    devices = lax.axis_size(axis)
    pairs = [(i, i + by) for i in range(devices) if 0 <= i + by < devices]
    return lax.ppermute(value, axis, pairs)


def for_sending(value):
    return jax.tree.map(lambda a: a.astype(jnp.bfloat16) if a.dtype == jnp.float32 else a, value)


def layout(seg_blocks, seg_group, group_index, block_count):
    mine = seg_group == group_index
    lengths = jnp.where(mine, seg_blocks, 0)
    offsets = jnp.cumsum(lengths) - lengths
    ranking = jnp.cumsum(mine.astype(jnp.int32)) - mine.astype(jnp.int32)
    blocks = jnp.arange(block_count, dtype=jnp.int32)[None, :]
    inside = mine[:, None] & (blocks >= offsets[:, None]) & (blocks < (offsets + lengths)[:, None])
    begins = jnp.any(inside & (blocks == offsets[:, None]), axis=0)
    closes = jnp.any(inside & (blocks == (offsets + lengths - 1)[:, None]), axis=0)
    lively = jnp.any(inside, axis=0)
    numbers = jnp.sum(jnp.where(inside, ranking[:, None], 0), axis=0)
    return (begins, closes, lively, numbers)


def inverse_rms(values):
    return lax.rsqrt(jnp.mean(values * values, axis=-1, keepdims=True) + EPSILON)


def norm_back(values, gain, grad_normed):
    factor = inverse_rms(values)
    scaled = values * factor
    grad_scaled = grad_normed * gain
    grad_values = factor * (
        grad_scaled - scaled * jnp.mean(grad_scaled * scaled, axis=-1, keepdims=True)
    )
    return (grad_values, jnp.sum(grad_normed * scaled, axis=0))


def smooth(values):
    return jax.nn.gelu(values, approximate=True)


def split_heads(rows_in):
    return rows_in.reshape(rows_in.shape[0], -1, HEAD_DIM)


def attend_forward(queries, key_rows, value_rows, allowed):
    score_scale = 1.0 / math.sqrt(HEAD_DIM)
    scores = (
        jnp.einsum("rhd,khd->hrk", queries, key_rows, preferred_element_type=jnp.float32)
        * score_scale
    )
    scores = jnp.where(allowed[None], scores, NEGATIVE)
    largest = jnp.max(scores, axis=-1, keepdims=True)
    totals = jnp.sum(jnp.exp(scores - largest), axis=-1, keepdims=True)
    log_total = largest + jnp.log(totals)
    weights = jnp.exp(scores - log_total).astype(jnp.bfloat16)
    mixture_output = jnp.einsum(
        "hrk,khd->rhd", weights, value_rows, preferred_element_type=jnp.float32
    )
    return (mixture_output, log_total[..., 0])


def attend_backward(queries, key_rows, value_rows, allowed, log_total, grad_mixture):
    score_scale = 1.0 / math.sqrt(HEAD_DIM)
    scores = (
        jnp.einsum("rhd,khd->hrk", queries, key_rows, preferred_element_type=jnp.float32)
        * score_scale
    )
    scores = jnp.where(allowed[None], scores, NEGATIVE)
    weights = jnp.exp(scores - log_total[..., None])
    rounded = weights.astype(jnp.bfloat16)
    grad_weights = jnp.einsum(
        "rhd,khd->hrk", grad_mixture, value_rows, preferred_element_type=jnp.float32
    )
    grad_values = jnp.einsum(
        "hrk,rhd->khd", rounded, grad_mixture, preferred_element_type=jnp.float32
    )
    inner_sum = jnp.sum(weights * grad_weights, axis=-1, keepdims=True)
    grad_scores = (weights * (grad_weights - inner_sum)).astype(jnp.bfloat16)
    grad_queries = (
        jnp.einsum("hrk,khd->rhd", grad_scores, key_rows, preferred_element_type=jnp.float32)
        * score_scale
    )
    grad_keys = (
        jnp.einsum("hrk,rhd->khd", grad_scores, queries, preferred_element_type=jnp.float32)
        * score_scale
    )
    return (grad_queries, grad_keys, grad_values)


def place_row(store, position, value, active_tick):
    previous = lax.dynamic_index_in_dim(store, position, 0, False)
    return lax.dynamic_update_index_in_dim(
        store, jnp.where(active_tick, value, previous), position, 0
    )


def renewed(grad_sums, active_tick, changes):
    return tuple(
        (
            total + jnp.where(active_tick, changes[position], 0.0) if position in changes else total
            for position, total in enumerate(grad_sums)
        )
    )


def relay_body(
    layer_input,
    output_grad,
    seg_blocks,
    seg_group,
    gain_a,
    wqkv_a,
    wout_a,
    gain_b,
    up_b,
    down_b,
    gain_c,
    gain_s,
    wqkv_c,
    sqkv_c,
    wout_c,
    sout_c,
    gate_bias,
    init_states,
    gain_d,
    up_d,
    down_d,
):
    block_count = layer_input.shape[1]
    shard_rows = layer_input.shape[2]
    model_width = layer_input.shape[3]
    tensor_count = lax.axis_size(TENSOR)
    token_rows = shard_rows * tensor_count
    state_shard = init_states.shape[0]
    state_count = state_shard * tensor_count
    local_width = wqkv_a.shape[2]
    local_heads = local_width // HEAD_DIM
    section_index = lax.axis_index(SECTION)
    group_index = lax.axis_index(DP)
    on_cell_section = section_index == 2
    begins, closes, lively, numbers = layout(seg_blocks, seg_group, group_index, block_count)
    token_gains = jnp.stack([gain_a, gain_b, gain_c, gain_d]).astype(jnp.float32)
    state_gain = gain_s.astype(jnp.float32)
    retain = jax.nn.sigmoid(gate_bias.astype(jnp.float32))
    initial = init_states.astype(jnp.float32)
    empty_state = jnp.zeros((state_count, model_width), jnp.float32)
    empty_token_store = jnp.zeros((token_rows, 4, local_width), jnp.bfloat16)
    empty_state_store = jnp.zeros((state_count, 4, local_width), jnp.bfloat16)
    empty_token_lse = jnp.zeros((local_heads, token_rows), jnp.float32)
    empty_state_lse = jnp.zeros((local_heads, state_count), jnp.float32)
    empty_carry = jnp.zeros((token_rows, local_width), jnp.float32)
    every_key = jnp.ones((state_count, token_rows + state_count), bool)
    state_keys_all = jnp.ones((token_rows, state_count), bool)

    def token_masks(opening):
        later_keys = lax.broadcasted_iota(
            jnp.int32, (token_rows, token_rows), 1
        ) > lax.broadcasted_iota(jnp.int32, (token_rows, token_rows), 0)
        return (jnp.logical_and(later_keys, jnp.logical_not(opening)), jnp.logical_not(later_keys))

    def plain_forward(normed_tok, normed_st, prior_block, opening):
        projected = jnp.einsum(
            "rd,dcn->rcn", normed_tok, wqkv_a, preferred_element_type=jnp.float32
        ).astype(jnp.bfloat16)
        reach_prior, reach_current = token_masks(opening)
        allowed = jnp.concatenate([reach_prior, reach_current], axis=1)
        key_rows = jnp.concatenate([prior_block[:, 1], projected[:, 1]], axis=0)
        value_rows = jnp.concatenate([prior_block[:, 2], projected[:, 2]], axis=0)
        mixture_output, token_lse = attend_forward(
            split_heads(projected[:, 0]), split_heads(key_rows), split_heads(value_rows), allowed
        )
        mixture_output = mixture_output.reshape(token_rows, local_width).astype(jnp.bfloat16)
        branch = jnp.dot(mixture_output, wout_a, preferred_element_type=jnp.float32)
        stored = jnp.concatenate([projected, mixture_output[:, None]], axis=1)
        return (branch, empty_state, stored, empty_state_store, token_lse, empty_state_lse)

    def feed_forward(up_projection_weight, down_projection_weight):

        def forward_fn(normed_tok, normed_st, prior_block, opening):
            hidden_rows = jnp.dot(
                normed_tok, up_projection_weight, preferred_element_type=jnp.float32
            )
            active_flags = smooth(hidden_rows).astype(jnp.bfloat16)
            branch = jnp.dot(
                active_flags, down_projection_weight, preferred_element_type=jnp.float32
            )
            return (
                branch,
                empty_state,
                empty_token_store,
                empty_state_store,
                empty_token_lse,
                empty_state_lse,
            )

        return forward_fn

    def recurrent_forward(normed_tok, normed_st, prior_block, opening):
        projected = jnp.einsum(
            "rd,dcn->rcn", normed_tok, wqkv_c, preferred_element_type=jnp.float32
        ).astype(jnp.bfloat16)
        state_proj = jnp.einsum(
            "sd,dcn->scn", normed_st, sqkv_c, preferred_element_type=jnp.float32
        ).astype(jnp.bfloat16)
        reach_prior, reach_current = token_masks(opening)
        allowed = jnp.concatenate([reach_prior, reach_current, state_keys_all], axis=1)
        token_keys = jnp.concatenate([prior_block[:, 1], projected[:, 1], state_proj[:, 1]], axis=0)
        token_values = jnp.concatenate(
            [prior_block[:, 2], projected[:, 2], state_proj[:, 2]], axis=0
        )
        token_mixture, token_lse = attend_forward(
            split_heads(projected[:, 0]),
            split_heads(token_keys),
            split_heads(token_values),
            allowed,
        )
        state_keys = jnp.concatenate([projected[:, 1], state_proj[:, 1]], axis=0)
        state_values = jnp.concatenate([projected[:, 2], state_proj[:, 2]], axis=0)
        state_mixture, state_lse = attend_forward(
            split_heads(state_proj[:, 0]),
            split_heads(state_keys),
            split_heads(state_values),
            every_key,
        )
        token_mixture = token_mixture.reshape(token_rows, local_width).astype(jnp.bfloat16)
        state_mixture = state_mixture.reshape(state_count, local_width).astype(jnp.bfloat16)
        branch = jnp.dot(token_mixture, wout_c, preferred_element_type=jnp.float32)
        update_term = jnp.dot(state_mixture, sout_c, preferred_element_type=jnp.float32)
        stored = jnp.concatenate([projected, token_mixture[:, None]], axis=1)
        state_stored = jnp.concatenate([state_proj, state_mixture[:, None]], axis=1)
        return (branch, update_term, stored, state_stored, token_lse, state_lse)

    def plain_backward(
        grad_tok,
        grad_st,
        normed_tok,
        normed_st,
        tok_block,
        st_block,
        prior_block,
        token_lse,
        state_lse,
        opening,
        carry_keys,
        carry_values,
        grad_sums,
        active_tick,
    ):
        reach_prior, reach_current = token_masks(opening)
        allowed = jnp.concatenate([reach_prior, reach_current], axis=1)
        key_rows = jnp.concatenate([prior_block[:, 1], tok_block[:, 1]], axis=0)
        value_rows = jnp.concatenate([prior_block[:, 2], tok_block[:, 2]], axis=0)
        weight_out = jnp.einsum(
            "rn,rd->nd", tok_block[:, 3], grad_tok, preferred_element_type=jnp.float32
        )
        grad_mixture = jnp.einsum(
            "rd,nd->rn", grad_tok, wout_a, preferred_element_type=jnp.float32
        ).astype(jnp.bfloat16)
        grad_query, grad_keys, grad_values = attend_backward(
            split_heads(tok_block[:, 0]),
            split_heads(key_rows),
            split_heads(value_rows),
            allowed,
            token_lse,
            split_heads(grad_mixture),
        )
        grad_query = grad_query.reshape(token_rows, local_width)
        grad_keys = grad_keys.reshape(2 * token_rows, local_width)
        grad_values = grad_values.reshape(2 * token_rows, local_width)
        grad_proj = jnp.stack(
            [
                grad_query,
                grad_keys[token_rows:] + carry_keys,
                grad_values[token_rows:] + carry_values,
            ],
            axis=1,
        ).astype(jnp.bfloat16)
        weight_in = jnp.einsum(
            "rd,rcn->dcn", normed_tok, grad_proj, preferred_element_type=jnp.float32
        )
        grad_normed = jnp.einsum(
            "rcn,dcn->rd", grad_proj, wqkv_a, preferred_element_type=jnp.float32
        )
        return (
            grad_normed,
            empty_state,
            grad_keys[:token_rows],
            grad_values[:token_rows],
            renewed(grad_sums, active_tick, {0: weight_in, 1: weight_out}),
        )

    def feed_backward(up_projection_weight, down_projection_weight, up_slot, down_slot):

        def backward_fn(
            grad_tok,
            grad_st,
            normed_tok,
            normed_st,
            tok_block,
            st_block,
            prior_block,
            token_lse,
            state_lse,
            opening,
            carry_keys,
            carry_values,
            grad_sums,
            active_tick,
        ):
            hidden_rows = jnp.dot(
                normed_tok, up_projection_weight, preferred_element_type=jnp.float32
            )
            active_flags, gelu_back = jax.vjp(smooth, hidden_rows)
            weight_down = jnp.einsum(
                "rf,rd->fd",
                active_flags.astype(jnp.bfloat16),
                grad_tok,
                preferred_element_type=jnp.float32,
            )
            grad_active = jnp.einsum(
                "rd,fd->rf", grad_tok, down_projection_weight, preferred_element_type=jnp.float32
            )
            grad_hidden = gelu_back(grad_active)[0].astype(jnp.bfloat16)
            weight_up = jnp.einsum(
                "rd,rf->df", normed_tok, grad_hidden, preferred_element_type=jnp.float32
            )
            grad_normed = jnp.einsum(
                "rf,df->rd", grad_hidden, up_projection_weight, preferred_element_type=jnp.float32
            )
            return (
                grad_normed,
                empty_state,
                empty_carry,
                empty_carry,
                renewed(grad_sums, active_tick, {up_slot: weight_up, down_slot: weight_down}),
            )

        return backward_fn

    def recurrent_backward(
        grad_tok,
        grad_st,
        normed_tok,
        normed_st,
        tok_block,
        st_block,
        prior_block,
        token_lse,
        state_lse,
        opening,
        carry_keys,
        carry_values,
        grad_sums,
        active_tick,
    ):
        reach_prior, reach_current = token_masks(opening)
        allowed = jnp.concatenate([reach_prior, reach_current, state_keys_all], axis=1)
        token_keys = jnp.concatenate([prior_block[:, 1], tok_block[:, 1], st_block[:, 1]], axis=0)
        token_values = jnp.concatenate([prior_block[:, 2], tok_block[:, 2], st_block[:, 2]], axis=0)
        state_keys = jnp.concatenate([tok_block[:, 1], st_block[:, 1]], axis=0)
        state_values = jnp.concatenate([tok_block[:, 2], st_block[:, 2]], axis=0)
        weight_out = jnp.einsum(
            "rn,rd->nd", tok_block[:, 3], grad_tok, preferred_element_type=jnp.float32
        )
        weight_state_out = jnp.einsum(
            "sn,sd->nd", st_block[:, 3], grad_st, preferred_element_type=jnp.float32
        )
        grad_token_mixture = jnp.einsum(
            "rd,nd->rn", grad_tok, wout_c, preferred_element_type=jnp.float32
        ).astype(jnp.bfloat16)
        grad_state_mixture = jnp.einsum(
            "sd,nd->sn", grad_st, sout_c, preferred_element_type=jnp.float32
        ).astype(jnp.bfloat16)
        grad_query, grad_keys, grad_values = attend_backward(
            split_heads(tok_block[:, 0]),
            split_heads(token_keys),
            split_heads(token_values),
            allowed,
            token_lse,
            split_heads(grad_token_mixture),
        )
        state_query, state_grad_keys, state_grad_values = attend_backward(
            split_heads(st_block[:, 0]),
            split_heads(state_keys),
            split_heads(state_values),
            every_key,
            state_lse,
            split_heads(grad_state_mixture),
        )
        grad_query = grad_query.reshape(token_rows, local_width)
        grad_keys = grad_keys.reshape(2 * token_rows + state_count, local_width)
        grad_values = grad_values.reshape(2 * token_rows + state_count, local_width)
        state_query = state_query.reshape(state_count, local_width)
        state_grad_keys = state_grad_keys.reshape(token_rows + state_count, local_width)
        state_grad_values = state_grad_values.reshape(token_rows + state_count, local_width)
        own_keys = (
            grad_keys[token_rows : 2 * token_rows] + state_grad_keys[:token_rows] + carry_keys
        )
        own_values = (
            grad_values[token_rows : 2 * token_rows] + state_grad_values[:token_rows] + carry_values
        )
        cell_keys = grad_keys[2 * token_rows :] + state_grad_keys[token_rows:]
        cell_values = grad_values[2 * token_rows :] + state_grad_values[token_rows:]
        grad_proj = jnp.stack([grad_query, own_keys, own_values], axis=1).astype(jnp.bfloat16)
        grad_state_proj = jnp.stack([state_query, cell_keys, cell_values], axis=1).astype(
            jnp.bfloat16
        )
        weight_in = jnp.einsum(
            "rd,rcn->dcn", normed_tok, grad_proj, preferred_element_type=jnp.float32
        )
        weight_state_in = jnp.einsum(
            "sd,scn->dcn", normed_st, grad_state_proj, preferred_element_type=jnp.float32
        )
        grad_normed = jnp.einsum(
            "rcn,dcn->rd", grad_proj, wqkv_c, preferred_element_type=jnp.float32
        )
        grad_state_normed = jnp.einsum(
            "scn,dcn->sd", grad_state_proj, sqkv_c, preferred_element_type=jnp.float32
        )
        changes = {4: weight_in, 5: weight_state_in, 6: weight_out, 7: weight_state_out}
        return (
            grad_normed,
            grad_state_normed,
            grad_keys[:token_rows],
            grad_values[:token_rows],
            renewed(grad_sums, active_tick, changes),
        )

    forward_branches = [
        plain_forward,
        feed_forward(up_b, down_b),
        recurrent_forward,
        feed_forward(up_d, down_d),
    ]
    backward_branches = [
        plain_backward,
        feed_backward(up_b, down_b, 2, 3),
        recurrent_backward,
        feed_backward(up_d, down_d, 8, 9),
    ]

    def forward_tick(tick_number, carried):
        (
            received,
            state_carry,
            tok_normed,
            st_normed,
            tok_stored,
            st_stored,
            tok_lse_all,
            st_lse_all,
            entered,
            state_entered,
            updates,
            leaving_rows,
            finals,
        ) = carried
        block_number = tick_number - section_index
        active_tick = (block_number >= 0) & (block_number < block_count)
        block_index = jnp.clip(block_number, 0, block_count - 1)
        opening = begins[block_index]
        entering = jnp.where(
            section_index == 0, layer_input[0, block_index].astype(jnp.float32), received
        )
        state_in = jnp.where(opening, initial, state_carry)
        token_gain = token_gains[section_index]
        normed_shard = (entering * inverse_rms(entering) * token_gain).astype(jnp.bfloat16)
        state_normed_shard = (state_in * inverse_rms(state_in) * state_gain).astype(jnp.bfloat16)
        normed_tok, normed_st = (
            lax.all_gather(normed_shard, TENSOR, axis=0, tiled=True),
            lax.all_gather(state_normed_shard, TENSOR, axis=0, tiled=True),
        )
        prior_block = tok_stored[jnp.maximum(block_index - 1, 0)]
        branch, update_term, stored, state_stored, token_lse, state_lse = lax.switch(
            section_index, forward_branches, normed_tok, normed_st, prior_block, opening
        )
        branch_shard, update_shard = (
            lax.psum_scatter(
                branch.astype(jnp.bfloat16), TENSOR, scatter_dimension=0, tiled=True
            ).astype(jnp.float32),
            lax.psum_scatter(
                update_term.astype(jnp.bfloat16), TENSOR, scatter_dimension=0, tiled=True
            ).astype(jnp.float32),
        )
        leaving = entering + branch_shard
        state_new = retain * state_in + (1.0 - retain) * update_shard
        tok_normed = place_row(tok_normed, block_index, normed_tok, active_tick)
        st_normed = place_row(st_normed, block_index, normed_st, active_tick)
        tok_stored = place_row(tok_stored, block_index, stored, active_tick)
        st_stored = place_row(st_stored, block_index, state_stored, active_tick)
        tok_lse_all = place_row(tok_lse_all, block_index, token_lse, active_tick)
        st_lse_all = place_row(st_lse_all, block_index, state_lse, active_tick)
        entered = place_row(entered, block_index, entering, active_tick)
        state_entered = place_row(state_entered, block_index, state_in, active_tick)
        updates = place_row(updates, block_index, update_shard, active_tick)
        leaving_rows = place_row(leaving_rows, block_index, leaving, active_tick)
        on_cell = active_tick & on_cell_section
        state_carry = jnp.where(on_cell, state_new, state_carry)
        keep_final = on_cell & closes[block_index] & lively[block_index]
        slot_hit = (jnp.arange(SLOTS, dtype=jnp.int32) == numbers[block_index])[
            None, :, None
        ] & keep_final
        finals = jnp.where(slot_hit, state_new[:, None, :], finals)
        received = shifted(leaving.astype(jnp.bfloat16), SECTION, 1).astype(leaving.dtype)
        return (
            received,
            state_carry,
            tok_normed,
            st_normed,
            tok_stored,
            st_stored,
            tok_lse_all,
            st_lse_all,
            entered,
            state_entered,
            updates,
            leaving_rows,
            finals,
        )

    forward_start = (
        jnp.zeros((shard_rows, model_width), jnp.float32),
        jnp.zeros((state_shard, model_width), jnp.float32),
        jnp.zeros((block_count, token_rows, model_width), jnp.bfloat16),
        jnp.zeros((block_count, state_count, model_width), jnp.bfloat16),
        jnp.zeros((block_count, token_rows, 4, local_width), jnp.bfloat16),
        jnp.zeros((block_count, state_count, 4, local_width), jnp.bfloat16),
        jnp.zeros((block_count, local_heads, token_rows), jnp.float32),
        jnp.zeros((block_count, local_heads, state_count), jnp.float32),
        jnp.zeros((block_count, shard_rows, model_width), jnp.float32),
        jnp.zeros((block_count, state_shard, model_width), jnp.float32),
        jnp.zeros((block_count, state_shard, model_width), jnp.float32),
        jnp.zeros((block_count, shard_rows, model_width), jnp.float32),
        jnp.zeros((state_shard, SLOTS, model_width), jnp.float32),
    )
    (
        _,
        _,
        tok_normed,
        st_normed,
        tok_stored,
        st_stored,
        tok_lse_all,
        st_lse_all,
        entered,
        state_entered,
        updates,
        leaving_rows,
        finals,
    ) = lax.fori_loop(0, block_count + 3, forward_tick, forward_start)
    gain_rows_of_section = jnp.array([0, 1, 2, 4], dtype=jnp.int32)
    small_rows = jnp.arange(6, dtype=jnp.int32)[:, None]

    def backward_tick(tick_number, carried):
        (
            received,
            state_grad,
            carry_keys,
            carry_values,
            grad_sums,
            smalls,
            initial_grad,
            input_rows,
        ) = carried
        block_number = block_count - 1 - tick_number + 3 - section_index
        active_tick = (block_number >= 0) & (block_number < block_count)
        block_index = jnp.clip(block_number, 0, block_count - 1)
        opening = begins[block_index]
        arriving = jnp.where(
            section_index == 3,
            output_grad[0, block_index].astype(jnp.float32)
            * lively[block_index].astype(jnp.float32),
            received,
        )
        update_grad = (1.0 - retain) * state_grad
        grad_tok, grad_st = (
            lax.all_gather(arriving.astype(jnp.bfloat16), TENSOR, axis=0, tiled=True),
            lax.all_gather(update_grad.astype(jnp.bfloat16), TENSOR, axis=0, tiled=True),
        )
        grad_normed_tok, grad_normed_st, prior_keys, prior_values, grad_sums = lax.switch(
            section_index,
            backward_branches,
            grad_tok,
            grad_st,
            tok_normed[block_index],
            st_normed[block_index],
            tok_stored[block_index],
            st_stored[block_index],
            tok_stored[jnp.maximum(block_index - 1, 0)],
            tok_lse_all[block_index],
            st_lse_all[block_index],
            opening,
            carry_keys,
            carry_values,
            grad_sums,
            active_tick,
        )
        tok_shard, st_shard = (
            lax.psum_scatter(
                grad_normed_tok.astype(jnp.bfloat16), TENSOR, scatter_dimension=0, tiled=True
            ).astype(jnp.float32),
            lax.psum_scatter(
                grad_normed_st.astype(jnp.bfloat16), TENSOR, scatter_dimension=0, tiled=True
            ).astype(jnp.float32),
        )
        grad_entering, token_gain_term = norm_back(
            entered[block_index], token_gains[section_index], tok_shard
        )
        leaving_grad = arriving + grad_entering
        state_in = state_entered[block_index]
        grad_state_norm, state_gain_term = norm_back(state_in, state_gain, st_shard)
        grad_state_in = retain * state_grad + grad_state_norm
        bias_term = (
            jnp.sum(state_grad * (state_in - updates[block_index]), axis=0)
            * retain
            * (1.0 - retain)
        )
        on_cell = active_tick & on_cell_section
        gain_part = (small_rows == gain_rows_of_section[section_index]).astype(
            jnp.float32
        ) * token_gain_term[None, :]
        cell_part = (small_rows == 3).astype(jnp.float32) * state_gain_term[None, :] + (
            small_rows == 5
        ).astype(jnp.float32) * bias_term[None, :]
        smalls = (
            smalls + jnp.where(active_tick, gain_part, 0.0) + jnp.where(on_cell, cell_part, 0.0)
        )
        initial_grad = initial_grad + jnp.where(on_cell & opening, grad_state_in, 0.0)
        state_grad = jnp.where(on_cell, jnp.where(opening, 0.0, grad_state_in), state_grad)
        carry_keys = jnp.where(active_tick, prior_keys, carry_keys)
        carry_values = jnp.where(active_tick, prior_values, carry_values)
        input_rows = place_row(input_rows, block_index, leaving_grad, active_tick)
        received = shifted(for_sending(leaving_grad), SECTION, -1).astype(leaving_grad.dtype)
        return (
            received,
            state_grad,
            carry_keys,
            carry_values,
            grad_sums,
            smalls,
            initial_grad,
            input_rows,
        )

    zero_grads = (
        jnp.zeros(wqkv_a.shape, jnp.float32),
        jnp.zeros(wout_a.shape, jnp.float32),
        jnp.zeros(up_b.shape, jnp.float32),
        jnp.zeros(down_b.shape, jnp.float32),
        jnp.zeros(wqkv_c.shape, jnp.float32),
        jnp.zeros(sqkv_c.shape, jnp.float32),
        jnp.zeros(wout_c.shape, jnp.float32),
        jnp.zeros(sout_c.shape, jnp.float32),
        jnp.zeros(up_d.shape, jnp.float32),
        jnp.zeros(down_d.shape, jnp.float32),
    )
    backward_start = (
        jnp.zeros((shard_rows, model_width), jnp.float32),
        jnp.zeros((state_shard, model_width), jnp.float32),
        empty_carry,
        empty_carry,
        zero_grads,
        jnp.zeros((6, model_width), jnp.float32),
        jnp.zeros((state_shard, model_width), jnp.float32),
        jnp.zeros((block_count, shard_rows, model_width), jnp.float32),
    )
    _, _, _, _, grad_sums, smalls, initial_grad, input_rows = lax.fori_loop(
        0, block_count + 3, backward_tick, backward_start
    )
    out_term = jnp.where(
        section_index == 3, leaving_rows * lively[:, None, None].astype(jnp.float32), 0.0
    )[None]
    input_term = jnp.where(section_index == 0, input_rows, 0.0)[None]
    final_term = jnp.where(section_index == 2, finals, 0.0)[None]
    out_share, input_share, final_share = (
        lax.psum_scatter(
            out_term.astype(jnp.bfloat16), SECTION, scatter_dimension=3, tiled=True
        ).astype(jnp.float32),
        lax.psum_scatter(
            input_term.astype(jnp.bfloat16), SECTION, scatter_dimension=3, tiled=True
        ).astype(jnp.float32),
        lax.psum_scatter(
            final_term.astype(jnp.bfloat16), SECTION, scatter_dimension=3, tiled=True
        ).astype(jnp.float32),
    )
    (
        grad_qkv_a,
        grad_out_a,
        grad_upper_b,
        grad_lower_b,
        grad_qkv_c,
        grad_state_qkv,
        grad_out_c,
        grad_state_out,
        grad_upper_d,
        grad_lower_d,
    ) = grad_sums
    totals = (
        lax.psum(grad_qkv_a.astype(jnp.bfloat16), DP).astype(jnp.float32),
        lax.psum(grad_out_a.astype(jnp.bfloat16), DP).astype(jnp.float32),
        lax.psum(grad_upper_b.astype(jnp.bfloat16), DP).astype(jnp.float32),
        lax.psum(grad_lower_b.astype(jnp.bfloat16), DP).astype(jnp.float32),
        lax.psum(grad_qkv_c.astype(jnp.bfloat16), DP).astype(jnp.float32),
        lax.psum(grad_state_qkv.astype(jnp.bfloat16), DP).astype(jnp.float32),
        lax.psum(grad_out_c.astype(jnp.bfloat16), DP).astype(jnp.float32),
        lax.psum(grad_state_out.astype(jnp.bfloat16), DP).astype(jnp.float32),
        lax.psum(grad_upper_d.astype(jnp.bfloat16), DP).astype(jnp.float32),
        lax.psum(grad_lower_d.astype(jnp.bfloat16), DP).astype(jnp.float32),
        lax.psum(initial_grad.astype(jnp.bfloat16), DP).astype(jnp.float32),
    )
    small_total = lax.psum(smalls, (DP, TENSOR))
    shares = (
        lax.psum_scatter(
            totals[0].astype(jnp.bfloat16), SECTION, scatter_dimension=0, tiled=True
        ).astype(jnp.float32),
        lax.psum_scatter(
            totals[1].astype(jnp.bfloat16), SECTION, scatter_dimension=1, tiled=True
        ).astype(jnp.float32),
        lax.psum_scatter(
            totals[2].astype(jnp.bfloat16), SECTION, scatter_dimension=0, tiled=True
        ).astype(jnp.float32),
        lax.psum_scatter(
            totals[3].astype(jnp.bfloat16), SECTION, scatter_dimension=1, tiled=True
        ).astype(jnp.float32),
        lax.psum_scatter(
            totals[4].astype(jnp.bfloat16), SECTION, scatter_dimension=0, tiled=True
        ).astype(jnp.float32),
        lax.psum_scatter(
            totals[5].astype(jnp.bfloat16), SECTION, scatter_dimension=0, tiled=True
        ).astype(jnp.float32),
        lax.psum_scatter(
            totals[6].astype(jnp.bfloat16), SECTION, scatter_dimension=1, tiled=True
        ).astype(jnp.float32),
        lax.psum_scatter(
            totals[7].astype(jnp.bfloat16), SECTION, scatter_dimension=1, tiled=True
        ).astype(jnp.float32),
        lax.psum_scatter(
            totals[8].astype(jnp.bfloat16), SECTION, scatter_dimension=0, tiled=True
        ).astype(jnp.float32),
        lax.psum_scatter(
            totals[9].astype(jnp.bfloat16), SECTION, scatter_dimension=1, tiled=True
        ).astype(jnp.float32),
        lax.psum_scatter(
            totals[10].astype(jnp.bfloat16), SECTION, scatter_dimension=1, tiled=True
        ).astype(jnp.float32),
        lax.psum_scatter(
            small_total.astype(jnp.bfloat16), SECTION, scatter_dimension=1, tiled=True
        ).astype(jnp.float32),
    )
    small_share = shares[11]
    return (
        out_share.astype(jnp.bfloat16),
        final_share,
        input_share,
        small_share[0],
        shares[0],
        shares[1],
        small_share[1],
        shares[2],
        shares[3],
        small_share[2],
        small_share[3],
        shares[4],
        shares[5],
        shares[6],
        shares[7],
        small_share[5],
        shares[10],
        small_share[4],
        shares[8],
        shares[9],
    )


CHAIN = 4
MESH = pl.DeviceIdType.MESH
SCALE = 1.0 / math.sqrt(HEAD_DIM)
LOG2_SCALE = SCALE * math.log2(math.e)
ALL_AXES = (SECTION, DP, TENSOR)
GROUP = (SECTION, TENSOR)
VMEM_BYTES = 60 * 1024 * 1024
CHUNK = 256


def block_of(section, tensor):
    high = section // 2
    return 2 * (2 * high + (tensor + high) % 2) + section % 2


DEVICE_OF_BLOCK = [0] * 8
for _section in range(4):
    for _tensor in range(2):
        DEVICE_OF_BLOCK[block_of(_section, _tensor)] = 2 * _section + _tensor
TO_NEXT = [(DEVICE_OF_BLOCK[b], DEVICE_OF_BLOCK[b + 1]) for b in range(7)]
TO_PRIOR = [(there, here) for here, there in TO_NEXT]
SWAP = [(0, 1), (1, 0)]


def params(**extra):
    return pltpu.CompilerParams(vmem_limit_bytes=VMEM_BYTES, **extra)


def nt(a, b):
    return lax.dot_general(a, b, (((1,), (1,)), ((), ())), preferred_element_type=jnp.float32)


def nn(a, b):
    return lax.dot_general(a, b, (((1,), (0,)), ((), ())), preferred_element_type=jnp.float32)


def tn(a, b):
    return lax.dot_general(a, b, (((0,), (0,)), ((), ())), preferred_element_type=jnp.float32)


def bf(a):
    return a.astype(jnp.bfloat16)


def with_ones(values):
    return jnp.concatenate([values, jnp.ones_like(values)], axis=1)


def later_mask(rows):
    return lax.broadcasted_iota(jnp.int32, (rows, rows), 1) > lax.broadcasted_iota(
        jnp.int32, (rows, rows), 0
    )


def window_scores(query, k, pk, start, rows, bar):
    stop = start + query.shape[0]
    own = nt(query, k[:stop])
    prior = nt(query, pk[start:]) + bar
    later = later_mask(query.shape[0])
    pieces = [jnp.where(later, prior[:, : stop - start], own[:, start:])]
    if start:
        pieces = [own[:, :start]] + pieces
    if stop < rows:
        pieces = pieces + [prior[:, stop - start :]]
    return jnp.concatenate(pieces, axis=1) if len(pieces) > 1 else pieces[0]


def window_parts(values, start):
    size = values.shape[0]
    later = later_mask(size)
    middle = values[:, start : start + size]
    zero = jnp.zeros_like(middle)
    own, prior = jnp.where(later, zero, middle), jnp.where(later, middle, zero)
    if start:
        own = jnp.concatenate([values[:, :start], own], axis=1)
    if start + size < values.shape[1]:
        prior = jnp.concatenate([prior, values[:, start + size :]], axis=1)
    return own, prior


def attend_kernel(with_states, *refs):
    if with_states:
        open_ref, q, k, v, pk, pv, sk, sv, out, lse = refs
    else:
        open_ref, q, k, v, pk, pv, out, lse = refs
    rows = q.shape[0]
    bar = jnp.where(open_ref[0] > 0, NEGATIVE, 0.0)
    keys, prior_keys = k[...], pk[...]
    values, prior_values = with_ones(v[...]), with_ones(pv[...])
    if with_states:
        state_keys, state_values = sk[...], with_ones(sv[...])
    for start in range(0, rows, CHUNK):
        query = q[start : start + CHUNK]
        scores = window_scores(query, keys, prior_keys, start, rows, bar)
        top = jnp.max(scores, axis=-1, keepdims=True)
        if with_states:
            more = nt(query, state_keys)
            top = jnp.maximum(top, jnp.max(more, axis=-1, keepdims=True))
        own, prior = window_parts(bf(jnp.exp2((scores - top) * LOG2_SCALE)), start)
        mixed = nn(own, values[: start + CHUNK]) + nn(prior, prior_values[start:])
        if with_states:
            mixed = mixed + nn(bf(jnp.exp2((more - top) * LOG2_SCALE)), state_values)
        total = mixed[:, HEAD_DIM:]
        out[start : start + CHUNK] = bf(mixed[:, :HEAD_DIM] / total)
        lse[0, start : start + CHUNK] = top * LOG2_SCALE + jnp.log2(total[:, :1])


def head_block(rows, offset):
    return pl.BlockSpec((rows, HEAD_DIM), lambda h: (0, offset + h))


def attend(opening, proj, prior, states=None):
    rows, width = proj.shape[0], proj.shape[1] // 3
    heads = width // HEAD_DIM
    specs = [pl.BlockSpec(memory_space=pltpu.SMEM)]
    specs += [head_block(rows, i * heads) for i in range(3)]
    specs += [head_block(rows, i * heads) for i in range(2)]
    args = [opening, proj, proj, proj, prior, prior]
    keys = 2 * rows
    if states is not None:
        specs += [head_block(states.shape[0], i * heads) for i in (1, 2)]
        args += [states, states]
        keys += states.shape[0]
    return pl.pallas_call(
        functools.partial(attend_kernel, states is not None),
        grid=(heads,),
        in_specs=specs,
        out_specs=[
            head_block(rows, 0),
            pl.BlockSpec((1, rows, 1), lambda h: (h, 0, 0)),
        ],
        out_shape=[
            jax.ShapeDtypeStruct((rows, width), jnp.bfloat16),
            jax.ShapeDtypeStruct((heads, rows, 1), jnp.float32),
        ],
        compiler_params=params(),
        cost_estimate=pl.CostEstimate(
            flops=4 * rows * keys * width,
            bytes_accessed=2 * rows * width * 8,
            transcendentals=rows * keys * heads // 2,
        ),
    )(*args)


def attend_back_kernel(with_states, *refs):
    if with_states:
        (open_ref, q, k, v, pk, pv, sk, sv, gmix, mix, lse) = refs[:11]
        (gq, gk, gv, gpk, gpv, gsk, gsv) = refs[11:18]
    else:
        (open_ref, q, k, v, pk, pv, gmix, mix, lse) = refs[:9]
        (gq, gk, gv, gpk, gpv) = refs[9:14]
    gpk_sum, gpv_sum = refs[-2:]
    rows = q.shape[0]
    bar = jnp.where(open_ref[0] > 0, NEGATIVE, 0.0)
    keys, prior_keys, values, prior_values = k[...], pk[...], v[...], pv[...]
    if with_states:
        state_keys, state_values = sk[...], sv[...]
    for start in range(0, rows, CHUNK):
        stop = start + CHUNK
        query, grad, log_total = q[start:stop], gmix[start:stop], lse[0, start:stop]
        inner = jnp.sum(
            grad.astype(jnp.float32) * mix[start:stop].astype(jnp.float32), axis=-1, keepdims=True
        )
        scores = window_scores(query, keys, prior_keys, start, rows, bar)
        weights = jnp.exp2(scores * LOG2_SCALE - log_total)
        grad_weights = window_scores(grad, values, prior_values, start, rows, 0.0)
        own, prior = window_parts(bf(weights), start)
        own_scores, prior_scores = window_parts(bf(weights * (grad_weights - inner)), start)
        grad_query = nn(own_scores, keys[:stop]) + nn(prior_scores, prior_keys[start:])
        add_own_v, add_own_k = tn(own, grad), tn(own_scores, query)
        add_prior_v, add_prior_k = tn(prior, grad), tn(prior_scores, query)
        if with_states:
            more = jnp.exp2(nt(query, state_keys) * LOG2_SCALE - log_total)
            from_states = bf(more * (nt(grad, state_values) - inner))
            grad_query = grad_query + nn(from_states, state_keys)
            add_sv, add_sk = tn(bf(more), grad), tn(from_states, query)
        gq[start:stop] = bf(grad_query * SCALE)
        if start == 0:
            gv[:stop], gk[:stop] = add_own_v, add_own_k * SCALE
            gpv_sum[...], gpk_sum[...] = add_prior_v, add_prior_k
            if with_states:
                gsv[...], gsk[...] = add_sv, add_sk * SCALE
        else:
            gv[:start] += add_own_v[:start]
            gk[:start] += add_own_k[:start] * SCALE
            gv[start:stop], gk[start:stop] = add_own_v[start:], add_own_k[start:] * SCALE
            gpv_sum[start:] += add_prior_v
            gpk_sum[start:] += add_prior_k
            if with_states:
                gsv[...] += add_sv
                gsk[...] += add_sk * SCALE
    gpv[...] = bf(gpv_sum[...])
    gpk[...] = bf(gpk_sum[...] * SCALE)


def attend_back(opening, proj, prior, grad_mixed, mixed, lse, states=None):
    rows, width = proj.shape[0], proj.shape[1] // 3
    heads = width // HEAD_DIM
    specs = [pl.BlockSpec(memory_space=pltpu.SMEM)]
    specs += [head_block(rows, i * heads) for i in range(3)]
    specs += [head_block(rows, i * heads) for i in range(2)]
    args = [opening, proj, proj, proj, prior, prior]
    keys = 2 * rows
    if states is not None:
        specs += [head_block(states.shape[0], i * heads) for i in (1, 2)]
        args += [states, states]
        keys += states.shape[0]
    specs += [head_block(rows, 0), head_block(rows, 0)]
    specs += [pl.BlockSpec((1, rows, 1), lambda h: (h, 0, 0))]
    args += [grad_mixed, mixed, lse]
    kinds = [jnp.bfloat16, jnp.float32, jnp.float32, jnp.bfloat16, jnp.bfloat16]
    if states is not None:
        kinds += [jnp.float32, jnp.float32]
    return pl.pallas_call(
        functools.partial(attend_back_kernel, states is not None),
        grid=(heads,),
        in_specs=specs,
        out_specs=[head_block(rows, 0) for _ in kinds],
        out_shape=[jax.ShapeDtypeStruct((rows, width), kind) for kind in kinds],
        scratch_shapes=[pltpu.VMEM((rows, HEAD_DIM), jnp.float32)] * 2,
        compiler_params=params(),
        cost_estimate=pl.CostEstimate(
            flops=10 * rows * keys * width,
            bytes_accessed=2 * rows * width * 24,
            transcendentals=rows * keys * heads // 2,
        ),
    )(*args)


KINDS = 9


class Spread:
    def __init__(self, sources, targets, send, recv):
        section, tensor, group = (lax.axis_index(a) for a in (SECTION, TENSOR, DP))
        self.sources, self.targets, self.send, self.recv = sources, targets, send, recv
        self.core, self.high, self.near = section % 2, section // 2, group % 2
        self.across = {TENSOR: 1 - tensor}
        self.along = {SECTION: (section + 2) % 4}
        self.beside = {DP: group + 1 - 2 * self.near}
        self.other = {SECTION: section + 1 - 2 * self.core}

    def partners(self):
        return [self.across, self.along, self.beside, self.other]

    def copy(self, kind, w):
        size = self.targets[w].shape[0] // 8
        y, z = self.high, self.near
        high, near, first, rows, to = (
            (y, z, 0, size, self.across),
            (y, z, 0, size, self.along),
            (y, z, 0, size, self.beside),
            (y, 1 - z, 0, size // 2, self.along),
            (1 - y, z, size // 2, size // 2, self.beside),
            (y, z, 0, size, self.other),
            (1 - y, z, 0, size, self.other),
            (y, 1 - z, 0, size, self.other),
            (1 - y, 1 - z, 0, size, self.other),
        )[kind]
        part = (near * 2 + high) * 2 + self.core
        where = pl.ds(pl.multiple_of(part * size + first, rows), rows)
        source = self.sources[w] if kind == 0 else self.targets[w]
        return pltpu.make_async_remote_copy(
            src_ref=source.at[where], dst_ref=self.targets[w].at[where],
            send_sem=self.send.at[kind * len(self.targets) + w],
            recv_sem=self.recv.at[kind * len(self.targets) + w],
            device_id=to, device_id_type=MESH,
        )

    def begin(self, w):
        self.copy(0, w).start()

    def hop(self, w):
        self.copy(0, w).wait_recv()
        for kind in (1, 2, 5):
            self.copy(kind, w).start()

    def cross(self, w):
        for kind in (1, 2):
            self.copy(kind, w).wait_recv()
        for kind in (3, 4, 6, 7):
            self.copy(kind, w).start()

    def close(self, w):
        for kind in (3, 4):
            self.copy(kind, w).wait_recv()
        self.copy(8, w).start()

    def end(self, w):
        for kind in (5, 6, 7, 8):
            self.copy(kind, w).wait_recv()
        for kind in range(KINDS):
            self.copy(kind, w).wait_send()


class Join:
    def __init__(self, source, theirs, mine, target, local, send, recv, i):
        tensor = lax.axis_index(TENSOR)
        rows = source.shape[-2]
        where = pl.ds(pl.multiple_of(tensor * rows, rows), rows)

        def of(index):
            return source if index is None else source.at[0, index]

        self.own = pltpu.make_async_copy(of(mine), target.at[where], local.at[i])
        self.remote = pltpu.make_async_remote_copy(
            src_ref=of(theirs), dst_ref=target.at[where], send_sem=send.at[i], recv_sem=recv.at[i],
            device_id={TENSOR: 1 - tensor}, device_id_type=MESH,
        )

    def start(self):
        self.remote.start()
        self.own.start()

    def wait(self):
        self.remote.wait()
        self.own.wait()


def meet(partners):
    barrier = pltpu.get_barrier_semaphore()
    for partner in partners:
        pl.semaphore_signal(barrier, inc=1, device_id=partner, device_id_type=MESH)
    pl.semaphore_wait(barrier, len(partners))


def gather_kernel(count, layer_input, init_states, *refs):
    sources, refs = refs[:count], refs[count:]
    tokens, before, initial = refs[:3]
    targets = refs[3 : 3 + count]
    send, recv, local, join_send, join_recv = refs[3 + count :]
    spread = Spread(sources, targets, send, recv)
    section, tensor = lax.axis_index(SECTION), lax.axis_index(TENSOR)
    block, partner = block_of(section, tensor), block_of(section, 1 - tensor)
    joins = [
        Join(layer_input, partner, block, tokens, local, join_send, join_recv, 0),
        Join(
            layer_input, jnp.maximum(partner - 1, 0), jnp.maximum(block - 1, 0),
            before, local, join_send, join_recv, 1,
        ),
        Join(init_states, None, None, initial, local, join_send, join_recv, 2),
    ]
    meet(spread.partners())
    for w in range(2):
        spread.begin(w)
    for w in range(count + 3):
        if w < count:
            spread.hop(w)
        if w + 2 < count:
            spread.begin(w + 2)
        elif w + 2 < count + 3:
            joins[w + 2 - count].start()
        if 0 <= w - 2 < count:
            spread.cross(w - 2)
        if 0 <= w - 3 < count:
            spread.close(w - 3)
    for w in range(count):
        spread.end(w)
    for join in joins:
        join.wait()


def gather(layer_input, init_states, weights):
    count = len(weights)
    rows, width = 2 * layer_input.shape[2], layer_input.shape[3]
    dma = pltpu.SemaphoreType.DMA
    anywhere = pl.BlockSpec(memory_space=pl.ANY)
    shapes = [(rows, width)] * 2 + [(2 * init_states.shape[0], width)] + [w.shape for w in weights]
    results = pl.pallas_call(
        functools.partial(gather_kernel, count),
        in_specs=[anywhere] * (2 + count),
        out_specs=[anywhere] * (3 + count),
        out_shape=[jax.ShapeDtypeStruct(s, jnp.bfloat16) for s in shapes],
        scratch_shapes=[dma((KINDS * count,))] * 2 + [dma((3,))] * 3,
        compiler_params=params(collective_id=4, has_side_effects=True),
        cost_estimate=pl.CostEstimate(flops=0, bytes_accessed=200 * 1024 * 1024, transcendentals=0),
    )(layer_input, init_states, *weights)
    return results[:3], results[3:]


def neighbours():
    section, tensor = lax.axis_index(SECTION), lax.axis_index(TENSOR)
    block = block_of(section, tensor)

    return place_of((block + 7) % 8), place_of((block + 1) % 8)


def place_of(block):
    pair = block // 2
    high = pair // 2
    return {SECTION: 2 * high + block % 2, TENSOR: (pair + high) % 2}


class Scatter:
    def __init__(self, values, landed, send, recv, local):
        section, tensor = lax.axis_index(SECTION), lax.axis_index(TENSOR)
        block = block_of(section, tensor)
        self.members = [place_of((block + i) % 8) for i in range(1, 8)]
        rows, width = values[0].shape[0] // 2, values[0].shape[1] // 4

        def piece(value, to):
            high = pl.multiple_of(to[TENSOR] * rows, rows)
            left = pl.multiple_of(to[SECTION] * width, width)
            return value.at[pl.ds(high, rows), pl.ds(left, width)]

        self.copies = [
            pltpu.make_async_remote_copy(
                src_ref=piece(value, to), dst_ref=landed.at[j, block],
                send_sem=send.at[j * 7 + i], recv_sem=recv.at[j * 7 + i],
                device_id=to, device_id_type=MESH,
            )
            for j, value in enumerate(values)
            for i, to in enumerate(self.members)
        ]
        self.own = [
            pltpu.make_async_copy(
                piece(value, {SECTION: section, TENSOR: tensor}), landed.at[j, block], local.at[j]
            )
            for j, value in enumerate(values)
        ]

    def start(self):
        for copy in self.copies + self.own:
            copy.start()

    def wait(self):
        for copy in self.copies + self.own:
            copy.wait()


def pass_on(sent, landed, send_sem, recv_sem, slot, part, target):
    rows = pl.ds(part * CHUNK, CHUNK)
    return pltpu.make_async_remote_copy(
        src_ref=sent.at[slot, rows],
        dst_ref=landed.at[slot, rows],
        send_sem=send_sem.at[slot, part],
        recv_sem=recv_sem.at[slot, part],
        device_id=target,
        device_id_type=MESH,
    )


def chain_kernel(
    initial, starts, gain, keep, own, other, sqkv0, sqkv1, sout0, sout1, output_grad,
    state, hs, ps0, ps1, os0, os1, lse, update, fresh, cotangent,
    sent, landed, send_sem, recv_sem, local, join_send, join_recv,
):
    prior, following = neighbours()
    section, tensor = lax.axis_index(SECTION), lax.axis_index(TENSOR)
    join = Join(
        output_grad, block_of(section, 1 - tensor), block_of(section, tensor),
        cotangent, local, join_send, join_recv, 0,
    )
    meet([prior, following, {TENSOR: 1 - tensor}])
    join.start()
    count, width = initial.shape
    half = os0.shape[1]
    parts = count // CHUNK
    state[...] = initial[...]

    def copy(slot, part):
        return pass_on(sent, landed, send_sem, recv_sem, slot, part, following)

    def one_round(turn, nothing):
        for part in range(parts):
            rows = slice(part * CHUNK, (part + 1) * CHUNK)

            @pl.when(turn > 0)
            def _():
                slot = turn - 1
                copy(slot, part).wait_recv()
                state[rows] = jnp.where(
                    starts[...] > 0.0, initial[rows], landed[slot, rows].astype(jnp.float32)
                )

            value = state[rows]
            hidden = bf(value * inverse_rms(value) * gain[...])
            hs[rows] = hidden
            ps0[rows] = bf(nn(hidden, sqkv0[...]))
            ps1[rows] = bf(nn(hidden, sqkv1[...]))

        def one_head(h, carry):
            at = [pl.ds(pl.multiple_of(i * half + h * HEAD_DIM, HEAD_DIM), HEAD_DIM) for i in range(3)]
            for which, (tok, st, mixed) in enumerate(((own, ps0, os0), (other, ps1, os1))):
                tok_key, tok_value = tok[:, at[1]], with_ones(tok[:, at[2]])
                key, value = st[:, at[1]], with_ones(st[:, at[2]])
                for part in range(parts):
                    rows = slice(part * CHUNK, (part + 1) * CHUNK)
                    query = st[rows, at[0]]
                    score_tok, score = nt(query, tok_key), nt(query, key)
                    top = jnp.maximum(
                        jnp.max(score_tok, axis=-1, keepdims=True),
                        jnp.max(score, axis=-1, keepdims=True),
                    )
                    mix = nn(bf(jnp.exp2((score_tok - top) * LOG2_SCALE)), tok_value) + nn(
                        bf(jnp.exp2((score - top) * LOG2_SCALE)), value
                    )
                    total = mix[:, HEAD_DIM:]
                    mixed[rows, at[0]] = bf(mix[:, :HEAD_DIM] / total)
                    lse[which, h, rows] = top * LOG2_SCALE + jnp.log2(total[:, :1])
            return carry

        lax.fori_loop(0, half // HEAD_DIM, one_head, 0)
        for part in range(parts):
            rows = slice(part * CHUNK, (part + 1) * CHUNK)
            term = nn(os0[rows], sout0[...]) + nn(os1[rows], sout1[...])
            update[rows] = term
            renewed_state = keep[...] * state[rows] + (1.0 - keep[...]) * term
            fresh[rows] = renewed_state

            @pl.when(turn < CHAIN - 1)
            def _():
                sent[turn, rows] = bf(renewed_state)
                copy(turn, part).start()

        return nothing

    lax.fori_loop(0, CHAIN, one_round, 0)
    for slot in range(CHAIN - 1):
        for part in range(parts):
            copy(slot, part).wait_send()
    join.wait()


def chain(initial, starts, gain, keep, own, other, sqkv0, sqkv1, sout0, sout1, output_grad):
    count, width = initial.shape
    half = sout0.shape[0]
    heads = half // HEAD_DIM
    bf16, f32 = jnp.bfloat16, jnp.float32
    vmem, anywhere = pl.BlockSpec(memory_space=pltpu.VMEM), pl.BlockSpec(memory_space=pl.ANY)
    dma = pltpu.SemaphoreType.DMA
    parts = count // CHUNK
    return pl.pallas_call(
        chain_kernel,
        in_specs=[vmem] * 10 + [anywhere],
        out_specs=[vmem] * 9 + [anywhere],
        out_shape=[
            jax.ShapeDtypeStruct((count, width), f32),
            jax.ShapeDtypeStruct((count, width), bf16),
            jax.ShapeDtypeStruct((count, 3 * half), bf16),
            jax.ShapeDtypeStruct((count, 3 * half), bf16),
            jax.ShapeDtypeStruct((count, half), bf16),
            jax.ShapeDtypeStruct((count, half), bf16),
            jax.ShapeDtypeStruct((2, heads, count, 1), f32),
            jax.ShapeDtypeStruct((count, width), f32),
            jax.ShapeDtypeStruct((count, width), f32),
            jax.ShapeDtypeStruct((2 * output_grad.shape[2], width), bf16),
        ],
        scratch_shapes=[
            pltpu.VMEM((CHAIN - 1, count, width), bf16),
            pltpu.VMEM((CHAIN - 1, count, width), bf16),
            dma((CHAIN - 1, parts)), dma((CHAIN - 1, parts)),
            dma((1,)), dma((1,)), dma((1,)),
        ],
        compiler_params=params(collective_id=1, has_side_effects=True),
        cost_estimate=pl.CostEstimate(
            flops=CHAIN * count * width * (8 * width + 8 * count),
            bytes_accessed=25 * 1024 * 1024,
            transcendentals=CHAIN * count * count * 4 * heads,
        ),
    )(initial, starts, gain, keep, own, other, sqkv0, sqkv1, sout0, sout1, output_grad)


def chain_back_kernel(
    ends, state, update, gain, keep, own, other, ps0, ps1, os0, os1, lse,
    tok_k0, tok_v0, tok_k1, tok_v1, sqkv0, sqkv1, sout0, sout1, result, ending,
    grad_state, gproj0, gproj1, gtok0, gtok1, gup, small, scattered,
    weights, grad_os0, grad_os1, sent, landed, send_sem, recv_sem, piece_send, piece_recv, piece_sem,
):
    prior, following = neighbours()
    scatter = Scatter((result, ending), scattered, piece_send, piece_recv, piece_sem)
    meet([prior, following] + scatter.members)
    scatter.start()
    count, width = state.shape
    half = os0.shape[1]
    heads = half // HEAD_DIM
    parts = count // CHUNK
    sides = (
        (own, ps0, os0, tok_k0, tok_v0, gproj0, gtok0, grad_os0),
        (other, ps1, os1, tok_k1, tok_v1, gproj1, gtok1, grad_os1),
    )

    def lanes(h):
        return [pl.ds(pl.multiple_of(i * half + h * HEAD_DIM, HEAD_DIM), HEAD_DIM) for i in range(3)]

    def copy(slot, part):
        return pass_on(sent, landed, send_sem, recv_sem, slot, part, prior)

    def prepare(h, carry):
        at = lanes(h)
        for which, (tok, st, *_) in enumerate(sides):
            tok_key, key = tok[:, at[1]], st[:, at[1]]
            for part in range(parts):
                rows = slice(part * CHUNK, (part + 1) * CHUNK)
                query, log_total = st[rows, at[0]], lse[which, h, rows]
                weights[which, h, rows, :count] = bf(
                    jnp.exp2(nt(query, tok_key) * LOG2_SCALE - log_total)
                )
                weights[which, h, rows, count:] = bf(
                    jnp.exp2(nt(query, key) * LOG2_SCALE - log_total)
                )
        return carry

    lax.fori_loop(0, heads, prepare, 0)
    grad_state[...] = jnp.zeros_like(grad_state)

    def one_round(turn, nothing):
        for part in range(parts):
            rows = slice(part * CHUNK, (part + 1) * CHUNK)

            @pl.when(turn > 0)
            def _():
                slot = turn - 1
                copy(slot, part).wait_recv()
                grad_state[rows] = jnp.where(
                    ends[...] > 0.0, 0.0, landed[slot, rows].astype(jnp.float32)
                )

            out = bf((1.0 - keep[...]) * grad_state[rows])
            gup[rows] = out
            grad_os0[rows] = bf(nt(out, sout0[...]))
            grad_os1[rows] = bf(nt(out, sout1[...]))

        def one_head(h, carry):
            at = lanes(h)
            for which, (tok, st, mixed, given_k, given_v, gproj, gtok, grad_os) in enumerate(sides):
                tok_key, tok_value = tok[:, at[1]], tok[:, at[2]]
                key, value = st[:, at[1]], st[:, at[2]]
                for part in range(parts):
                    rows = slice(part * CHUNK, (part + 1) * CHUNK)
                    query, grad = st[rows, at[0]], grad_os[rows, at[0]]
                    inner = jnp.sum(
                        grad.astype(jnp.float32) * mixed[rows, at[0]].astype(jnp.float32),
                        axis=-1, keepdims=True,
                    )
                    p_tok, p = weights[which, h, rows, :count], weights[which, h, rows, count:]
                    s_tok = bf(p_tok.astype(jnp.float32) * (nt(grad, tok_value) - inner))
                    s = bf(p.astype(jnp.float32) * (nt(grad, value) - inner))
                    gproj[rows, at[0]] = bf((nn(s_tok, tok_key) + nn(s, key)) * SCALE)
                    gk, gv = tn(s, query) * SCALE, tn(p, grad)
                    if part == 0:
                        total_k, total_v = gk + given_k[:, at[0]], gv + given_v[:, at[0]]
                    else:
                        total_k, total_v = total_k + gk, total_v + gv

                    @pl.when(turn == CHAIN - 1)
                    def _():
                        gtk, gtv = tn(s_tok, query) * SCALE, tn(p_tok, grad)
                        if part == 0:
                            gtok[:, at[0]], gtok[:, at[1]] = gtk, gtv
                        else:
                            gtok[:, at[0]] += gtk
                            gtok[:, at[1]] += gtv

                gproj[:, at[1]], gproj[:, at[2]] = bf(total_k), bf(total_v)
            return carry

        lax.fori_loop(0, heads, one_head, 0)
        for part in range(parts):
            rows = slice(part * CHUNK, (part + 1) * CHUNK)
            back = nt(gproj0[rows], sqkv0[...]) + nt(gproj1[rows], sqkv1[...])
            value, new = state[rows], grad_state[rows]
            factor = inverse_rms(value)
            scaled = value * factor
            through = back * gain[...]
            leaving = keep[...] * new + factor * (
                through - scaled * jnp.mean(through * scaled, axis=-1, keepdims=True)
            )

            @pl.when(turn < CHAIN - 1)
            def _():
                sent[turn, rows] = bf(leaving)
                copy(turn, part).start()

            @pl.when(turn == CHAIN - 1)
            def _():
                gain_term = jnp.sum(back * scaled, axis=0, keepdims=True)
                bias_term = jnp.sum(new * (value - update[rows]), axis=0, keepdims=True) * (
                    keep[...] * (1.0 - keep[...])
                )
                if part == 0:
                    small[0:1, :], small[1:2, :] = gain_term, bias_term
                else:
                    small[0:1, :] += gain_term
                    small[1:2, :] += bias_term
                grad_state[rows] = leaving

        return nothing

    lax.fori_loop(0, CHAIN, one_round, 0)
    for slot in range(CHAIN - 1):
        for part in range(parts):
            copy(slot, part).wait_send()
    scatter.wait()


def chain_back(
    ends, state, update, gain, keep, own, other, ps0, ps1, os0, os1, lse,
    tok_k0, tok_v0, tok_k1, tok_v1, sqkv0, sqkv1, sout0, sout1, result, ending,
):
    count, width = state.shape
    half = sout0.shape[0]
    heads = half // HEAD_DIM
    bf16, f32 = jnp.bfloat16, jnp.float32
    vmem, anywhere = pl.BlockSpec(memory_space=pltpu.VMEM), pl.BlockSpec(memory_space=pl.ANY)
    dma = pltpu.SemaphoreType.DMA
    parts = count // CHUNK
    rows = own.shape[0]
    return pl.pallas_call(
        chain_back_kernel,
        in_specs=[vmem] * 20 + [anywhere] * 2,
        out_specs=[vmem] * 7 + [anywhere],
        out_shape=[
            jax.ShapeDtypeStruct((count, width), f32),
            jax.ShapeDtypeStruct((count, 3 * half), bf16),
            jax.ShapeDtypeStruct((count, 3 * half), bf16),
            jax.ShapeDtypeStruct((rows, 2 * half), f32),
            jax.ShapeDtypeStruct((rows, 2 * half), f32),
            jax.ShapeDtypeStruct((count, width), bf16),
            jax.ShapeDtypeStruct((2, width), f32),
            jax.ShapeDtypeStruct((2, 8, rows // 2, width // 4), bf16),
        ],
        scratch_shapes=[
            pltpu.VMEM((2, heads, count, rows + count), bf16),
            pltpu.VMEM((count, half), bf16),
            pltpu.VMEM((count, half), bf16),
            pltpu.VMEM((CHAIN - 1, count, width), bf16),
            pltpu.VMEM((CHAIN - 1, count, width), bf16),
            dma((CHAIN - 1, parts)), dma((CHAIN - 1, parts)), dma((14,)), dma((14,)), dma((2,)),
        ],
        compiler_params=params(collective_id=2, has_side_effects=True),
        cost_estimate=pl.CostEstimate(
            flops=CHAIN * count * width * (16 * width + 16 * count),
            bytes_accessed=45 * 1024 * 1024,
            transcendentals=count * count * 4 * heads,
        ),
    )(
        ends, state, update, gain, keep, own, other, ps0, ps1, os0, os1, lse,
        tok_k0, tok_v0, tok_k1, tok_v1, sqkv0, sqkv1, sout0, sout1, result, ending,
    )


RING = 8
SHORT_RING = 4
TILE = 256
LAGS = (0, 1, 2, 4, 6, 7, 8, 9, 10)
UP_D, DOWN_D, UP_B, DOWN_B, OUT_C, QKV_C, SOUT_C, SQKV_C, QKV_A, OUT_A = range(10)
WEIGHTS = (
    (UP_D, True, 8), (DOWN_D, False, 8), (UP_B, True, 8), (DOWN_B, False, 8), (OUT_C, False, 2),
    (QKV_C, True, 6), (SOUT_C, False, 2), (SQKV_C, True, 6), (QKV_A, True, 6), (OUT_A, False, 2),
)
STARTS = [sum(w[2] for w in WEIGHTS[:i]) for i in range(len(WEIGHTS))]
PLAIN = sum(w[2] for w in WEIGHTS)
TILES = PLAIN + 2


def grads_kernel(*refs):
    count = len(WEIGHTS)
    lefts, panels_own, panels_other = refs[:count], refs[count : 2 * count], refs[2 * count : 3 * count]
    first, small, rows_out = refs[3 * count : 3 * count + 3]
    refs = refs[3 * count + 3 :]
    outs, last_out, landed = refs[:count], refs[count], refs[count + 1]
    (
        left, panel, pair, core_in, kept1, first_in, kept2, second_in, kept3, third_in, kept4, fourth_in, result,
        left_sem, panel_sem, last_sem, core_send, core_recv, first_send, first_recv, second_send, second_recv,
        send_sem, recv_sem, piece_send, piece_recv, piece_sem,
    ) = refs[count + 2 :]
    section, tensor, group = (lax.axis_index(a) for a in (SECTION, TENSOR, DP))
    core, high = section % 2, section // 2
    near, far = group % 2, group // 2
    half, quarter = TILE // 2, TILE // 4
    other_core = {SECTION: section + 1 - 2 * core}
    near_group = {DP: group + 1 - 2 * near}
    far_group = {DP: (group + 2) % 4}
    scatter = Scatter((rows_out,), landed, piece_send, piece_recv, piece_sem)
    meet(scatter.members + [near_group, far_group])
    scatter.start()

    def remote(source, target, sems, recvs, where, partner):
        return pltpu.make_async_remote_copy(
            src_ref=source, dst_ref=target, send_sem=sems.at[where], recv_sem=recvs.at[where],
            device_id=partner, device_id_type=MESH,
        )

    def left_copy(w):
        return pltpu.make_async_copy(lefts[w], left.at[w % 3], left_sem.at[w % 3])

    left_copy(0).start()

    def panel_copies(w, k):
        slot = k % SHORT_RING
        columns = pl.ds(pl.multiple_of((k - STARTS[w]) * TILE, TILE), TILE)
        return [
            pltpu.make_async_copy(source[w].at[:, columns], panel.at[slot, j], panel_sem.at[2 * slot + j])
            for j, source in enumerate((panels_own, panels_other))
        ]

    def last_copies(which):
        slot = (PLAIN + which) % SHORT_RING
        for i in range(8):
            s, t = i // 2, i % 2
            columns = slice(s * TILE, (s + 1) * TILE)
            source = small.at[:, columns] if which else first.at[t * TILE : (t + 1) * TILE, columns]
            yield pltpu.make_async_copy(source, pair.at[slot, s % 2, s // 2, t], last_sem.at[i])

    def core_copy(k):
        slot = k % RING
        return remote(
            pair.at[k % SHORT_RING, 1 - core], core_in.at[slot], core_send, core_recv, slot, other_core
        )

    def order(k):
        turn = k % 2
        send = (
            (1 - turn) * (1 - tensor) + turn * (2 - 2 * high),
            (1 - turn) * (3 - tensor) + turn * (3 - 2 * high),
        )
        keep = (
            (1 - turn) * tensor + turn * 2 * high,
            (1 - turn) * (2 + tensor) + turn * (2 * high + 1),
        )
        return send, keep, (1 - turn) * high + turn * tensor

    def partner_of(turn):
        return {
            SECTION: section * (1 - turn) + ((section + 2) % 4) * turn,
            TENSOR: tensor + (1 - turn) * (1 - 2 * tensor),
        }

    def first_copy(k, i):
        slot = k % RING
        return remote(
            kept1.at[k % SHORT_RING, order(k)[0][i]], first_in.at[slot, i], first_send, first_recv,
            2 * slot + i, partner_of(k % 2),
        )

    def second_copy(k):
        slot = k % RING
        return remote(
            kept2.at[slot, 1 - order(k)[2]], second_in.at[slot], second_send, second_recv,
            slot, partner_of(1 - k % 2),
        )

    def third_copy(k):
        slot = k % RING
        return remote(
            kept3.at[slot, pl.ds((1 - near) * half, half)], third_in.at[slot], send_sem, recv_sem,
            slot, near_group,
        )

    def fourth_copy(k):
        slot = k % RING
        return remote(
            kept4.at[slot, pl.ds((1 - far) * quarter, quarter)], fourth_in.at[slot], send_sem, recv_sem,
            RING + slot, far_group,
        )

    def back_far(k):
        rows = pl.ds(near * half + far * quarter, quarter)
        return remote(
            result.at[k, rows], result.at[k, rows], send_sem, recv_sem, 2 * RING + k % RING, far_group
        )

    def back_near(k):
        rows = pl.ds(near * half, half)
        return remote(
            result.at[k, rows], result.at[k, rows], send_sem, recv_sem, 3 * RING + k % RING, near_group
        )

    def add(a, b):
        return bf(a.astype(jnp.float32) + b.astype(jnp.float32))

    def fetch(k):
        for w in range(count):

            @pl.when((k >= STARTS[w]) & (k < STARTS[w] + WEIGHTS[w][2]))
            def _():
                for copy in panel_copies(w, k):
                    copy.start()

            if w + 1 < count:

                @pl.when(k == STARTS[w])
                def _():
                    left_copy(w + 1).start()

    def multiply(k):
        slot = k % SHORT_RING

        @pl.when(k < PLAIN)
        def _():
            at = 0
            for w in range(count):
                if w:
                    at = at + jnp.where(k >= STARTS[w], 1, 0)

                @pl.when(k == STARTS[w])
                def _():
                    left_copy(w).wait()

            for j, place in enumerate((tensor, 1 - tensor)):
                pltpu.make_async_copy(
                    panels_own[0].at[:, :TILE], panel.at[slot, j], panel_sem.at[2 * slot + j]
                ).wait()
                product = bf(tn(panel[slot, j], left[at % 3]))
                for s in range(4):
                    pair[slot, s % 2, s // 2, place] = product[:, s * TILE : (s + 1) * TILE]

        for which in range(2):

            @pl.when(k == PLAIN + which)
            def _():
                for copy in last_copies(which):
                    copy.start()
                for copy in last_copies(which):
                    copy.wait()

        core_copy(k).start()

    def over_cores(k):
        core_copy(k).wait()
        for i in range(4):
            kept1[k % SHORT_RING, i] = add(
                pair[k % SHORT_RING, core, i // 2, i % 2], core_in[k % RING, i // 2, i % 2]
            )
        for i in range(2):
            first_copy(k, i).start()

    def over_first(k):
        slot = k % RING
        for i in range(2):
            first_copy(k, i).wait()
        for i in range(2):
            kept2[slot, i] = add(kept1[k % SHORT_RING, order(k)[1][i]], first_in[slot, i])
        second_copy(k).start()

    def over_second(k):
        slot = k % RING
        second_copy(k).wait()
        kept3[slot] = add(kept2[slot, order(k)[2]], second_in[slot])
        third_copy(k).start()

    def over_near(k):
        slot = k % RING
        third_copy(k).wait()
        kept4[slot] = add(kept3[slot, pl.ds(near * half, half)], third_in[slot])
        fourth_copy(k).start()

    def over_far(k):
        slot = k % RING
        fourth_copy(k).wait()
        result[k, pl.ds(near * half + far * quarter, quarter)] = add(
            kept4[slot, pl.ds(far * quarter, quarter)], fourth_in[slot]
        )
        back_far(k).start()

    def from_far(k):
        back_far(k).wait()
        back_near(k).start()

    def from_near(k):
        back_near(k).wait()
        for w in range(count):

            @pl.when((k >= STARTS[w]) & (k < STARTS[w] + WEIGHTS[w][2]))
            def _():
                at = pl.ds(pl.multiple_of((k - STARTS[w]) * TILE, TILE), TILE)
                if WEIGHTS[w][1]:
                    outs[w][:, at] = bf(result[k].astype(jnp.float32).T)
                else:
                    outs[w][at, :] = result[k]

        @pl.when(k >= PLAIN)
        def _():
            last_out[k - PLAIN] = result[k]

    stages = (
        fetch, multiply, over_cores, over_first, over_second, over_near, over_far, from_far, from_near
    )

    def step(i, nothing):
        for stage, lag in zip(stages, LAGS):
            k = i - lag

            @pl.when((k >= 0) & (k < TILES))
            def _():
                stage(k)

        return nothing

    lax.fori_loop(0, TILES + LAGS[-1], step, 0)
    scatter.wait()


def weight_grads(operands, first, small, rows_out):
    bf16 = jnp.bfloat16
    dma = pltpu.SemaphoreType.DMA
    anywhere, vmem = pl.BlockSpec(memory_space=pl.ANY), pl.BlockSpec(memory_space=pltpu.VMEM)
    count = len(WEIGHTS)
    rows, width = operands[WEIGHTS[0][0]][0].shape
    shapes = [(TILE, n * TILE) if by_rows else (n * TILE, TILE) for _, by_rows, n in WEIGHTS]
    shapes += [(2, TILE, TILE)]
    results = pl.pallas_call(
        grads_kernel,
        in_specs=[anywhere] * (3 * count + 3),
        out_specs=[vmem] * (count + 1) + [anywhere],
        out_shape=[jax.ShapeDtypeStruct(s, bf16) for s in shapes + [(1, 8, TILE, TILE)]],
        scratch_shapes=[
            pltpu.VMEM((3, rows, width), bf16),
            pltpu.VMEM((SHORT_RING, 2, rows, TILE), bf16),
            pltpu.VMEM((SHORT_RING, 2, 2, 2, TILE, TILE), bf16),
            pltpu.VMEM((RING, 2, 2, TILE, TILE), bf16),
            pltpu.VMEM((SHORT_RING, 4, TILE, TILE), bf16),
            pltpu.VMEM((RING, 2, TILE, TILE), bf16),
            pltpu.VMEM((RING, 2, TILE, TILE), bf16),
            pltpu.VMEM((RING, TILE, TILE), bf16),
            pltpu.VMEM((RING, TILE, TILE), bf16),
            pltpu.VMEM((RING, TILE // 2, TILE), bf16),
            pltpu.VMEM((RING, TILE // 2, TILE), bf16),
            pltpu.VMEM((RING, TILE // 4, TILE), bf16),
            pltpu.VMEM((TILES, TILE, TILE), bf16),
            dma((3,)), dma((2 * SHORT_RING,)), dma((8,)),
            dma((RING,)), dma((RING,)),
            dma((2 * RING,)), dma((2 * RING,)), dma((RING,)), dma((RING,)),
            dma((4 * RING,)), dma((4 * RING,)), dma((7,)), dma((7,)), dma((1,)),
        ],
        compiler_params=params(collective_id=3, has_side_effects=True),
        cost_estimate=pl.CostEstimate(
            flops=2 * 8 * TILES * TILE * TILE * rows,
            bytes_accessed=40 * TILES * TILE * TILE,
            transcendentals=0,
        ),
    )(*(operands[w[0]][i] for i in range(3) for w in WEIGHTS), first, small, rows_out)
    shares = {w[0]: r for w, r in zip(WEIGHTS, results)}
    return shares, results[count], results[count + 1]


def gelu_back(values, grad):
    return jax.vjp(smooth, values)[1](grad)[0]


def block_body(
    layer_input, output_grad, seg_blocks, seg_group, gain_a, wqkv_a, wout_a, gain_b, up_b, down_b,
    gain_c, gain_s, wqkv_c, sqkv_c, wout_c, sout_c, gate_bias, init_states, gain_d, up_d, down_d,
):
    sections, tensors = lax.axis_size(SECTION), lax.axis_size(TENSOR)
    block_count, shard_rows, width = layer_input.shape[1:]
    rows = shard_rows * tensors
    section, tensor = lax.axis_index(SECTION), lax.axis_index(TENSOR)
    block = block_of(section, tensor)
    begins, closes, lively, numbers = layout(
        seg_blocks, seg_group, lax.axis_index(DP), block_count
    )
    alive = lively[block]
    starts = begins[block] | jnp.logical_not(alive)
    ends = closes[block] | jnp.logical_not(alive)
    opening = starts.astype(jnp.int32)[None]
    f32 = jnp.float32
    ga, gb, gc, gd = (v.astype(f32) for v in (gain_a, gain_b, gain_c, gain_d))

    def in_order(own, other):
        low = jnp.where(tensor == 0, own, other)
        high = jnp.where(tensor == 0, other, own)
        return low, high

    def other_half(weight):
        size = weight.shape[0] // sections
        piece = lax.dynamic_slice_in_dim(weight, section * size, size, 0)
        landed = lax.ppermute(piece, TENSOR, SWAP)
        return lax.all_gather(landed, SECTION, axis=0, tiled=True)

    def flat(weight):
        return jnp.concatenate([weight[:, i] for i in range(3)], axis=1)

    wqkv_a0, wqkv_c0, sqkv_c0 = flat(wqkv_a), flat(wqkv_c), flat(sqkv_c)
    (tokens, before, initial), others = gather(
        layer_input, init_states,
        (wqkv_a0, wout_a, up_b, down_b, wqkv_c0, sqkv_c0, sout_c, wout_c),
    )
    wqkv_a1, wout_a1, up_b1, down_b1, wqkv_c1, sqkv_c1, sout_c1, wout_c1 = others
    tokens, late_up, late_down = lax.optimization_barrier((tokens, up_d, down_d))
    up_d1, down_d1 = other_half(late_up), other_half(late_down)
    initial = initial.astype(f32)

    def normed(values, gain):
        return bf(values * inverse_rms(values) * gain)

    def dot(a, b):
        return jnp.dot(a, b, preferred_element_type=f32)

    def dot_t(a, b):
        return lax.dot_general(a, b, (((1,), (1,)), ((), ())), preferred_element_type=f32)

    half = wout_a.shape[0]
    r0 = tokens.astype(f32)
    h0 = normed(r0, ga)
    h_before = normed(before.astype(f32), ga)
    pa0, pa1 = bf(dot(h0, wqkv_a0)), bf(dot(h0, wqkv_a1))
    prior_a0 = bf(dot(h_before, wqkv_a0[:, half:]))
    prior_a1 = bf(dot(h_before, wqkv_a1[:, half:]))
    oa0, lse_a0 = attend(opening, pa0, prior_a0)
    oa1, lse_a1 = attend(opening, pa1, prior_a1)
    r1 = r0 + (dot(oa0, wout_a) + dot(oa1, wout_a1))

    h1 = normed(r1, gb)
    ub0, ub1 = dot(h1, up_b), dot(h1, up_b1)
    ab0, ab1 = bf(smooth(ub0)), bf(smooth(ub1))
    r2 = r1 + (dot(ab0, down_b) + dot(ab1, down_b1))

    h2 = normed(r2, gc)
    pc0, pc1 = bf(dot(h2, wqkv_c0)), bf(dot(h2, wqkv_c1))
    halo = lax.ppermute(jnp.stack(in_order(pc0[:, half:], pc1[:, half:])), GROUP, TO_NEXT)
    prior_c0, prior_c1 = in_order(halo[0], halo[1])

    retain = jax.nn.sigmoid(gate_bias.astype(f32))[None, :]
    state_gain = gain_s.astype(f32)[None, :]

    def flag(value):
        return jnp.broadcast_to(value.astype(f32), (1, width))

    (
        state_in, hs, ps0, ps1, os0, os1, lse_s, update, state_new, cotangent
    ) = chain(
        initial, flag(starts), state_gain, retain, pc0, pc1,
        sqkv_c0, sqkv_c1, sout_c, sout_c1, output_grad,
    )
    oc0, lse_c0 = attend(opening, pc0, prior_c0, ps0)
    oc1, lse_c1 = attend(opening, pc1, prior_c1, ps1)
    r3 = r2 + (dot(oc0, wout_c) + dot(oc1, wout_c1))

    h3 = normed(r3, gd)
    ud0, ud1 = dot(h3, up_d), dot(h3, up_d1)
    ad0, ad1 = bf(smooth(ud0)), bf(smooth(ud1))
    r4 = r3 + (dot(ad0, down_d) + dot(ad1, down_d1))
    result = bf(jnp.where(alive, r4, 0.0))

    def feed_back(up_name, down_name, grad, values, h, gain, u0, u1, a0, a1, up0, up1, down0, down1):
        gy = bf(grad)
        g0 = bf(gelu_back(u0, dot_t(gy, down0)))
        g1 = bf(gelu_back(u1, dot_t(gy, down1)))
        operands[down_name] = (gy, a0, a1)
        operands[up_name] = (h, g0, g1)
        through = dot_t(g0, up0) + dot_t(g1, up1)
        back, gain_grad = norm_back(values, gain, through)
        return grad + back, gain_grad

    operands = {}
    grad4 = jnp.where(alive, cotangent.astype(f32), 0.0)
    grad3, gain_d_grad = feed_back(
        UP_D, DOWN_D, grad4, r3, h3, gd, ud0, ud1, ad0, ad1, up_d, up_d1, down_d, down_d1
    )
    gy3 = bf(grad3)
    tok0 = attend_back(opening, pc0, prior_c0, bf(dot_t(gy3, wout_c)), oc0, lse_c0, ps0)
    tok1 = attend_back(opening, pc1, prior_c1, bf(dot_t(gy3, wout_c1)), oc1, lse_c1, ps1)

    def halo_back(one, two):
        pair = in_order(
            jnp.concatenate([one[3], one[4]], axis=1), jnp.concatenate([two[3], two[4]], axis=1)
        )
        back = lax.ppermute(jnp.stack(pair), GROUP, TO_PRIOR).astype(f32)
        return in_order(back[0], back[1])

    halo_c0, halo_c1 = halo_back(tok0, tok1)
    grad_state, gs0, gs1, gtok0, gtok1, gup, small, landed = chain_back(
        flag(ends), state_in, update, state_gain, retain, pc0, pc1, ps0, ps1, os0, os1, lse_s,
        tok0[5], tok0[6], tok1[5], tok1[6], sqkv_c0, sqkv_c1, sout_c, sout_c1, result, bf(state_new),
    )

    def projected_back(parts, halo_part, extra=None):
        pair = jnp.concatenate([parts[1], parts[2]], axis=1) + halo_part
        if extra is not None:
            pair = pair + extra
        return jnp.concatenate([parts[0], bf(pair)], axis=1)

    gc0 = projected_back(tok0, halo_c0, gtok0)
    gc1 = projected_back(tok1, halo_c1, gtok1)
    operands[QKV_C] = (h2, gc0, gc1)
    operands[SQKV_C] = (hs, gs0, gs1)
    operands[OUT_C] = (gy3, oc0, oc1)
    operands[SOUT_C] = (gup, os0, os1)
    first_grad = bf(jnp.where(begins[block], grad_state, 0.0))
    def through_qkv(g, w):
        return dot_t(g, w)

    back_c, gain_c_grad = norm_back(
        r2, gc, through_qkv(gc0, wqkv_c0) + through_qkv(gc1, wqkv_c1)
    )
    grad2 = grad3 + back_c

    grad1, gain_b_grad = feed_back(
        UP_B, DOWN_B, grad2, r1, h1, gb, ub0, ub1, ab0, ab1, up_b, up_b1, down_b, down_b1
    )

    gy1 = bf(grad1)
    att0 = attend_back(opening, pa0, prior_a0, bf(dot_t(gy1, wout_a)), oa0, lse_a0)
    att1 = attend_back(opening, pa1, prior_a1, bf(dot_t(gy1, wout_a1)), oa1, lse_a1)
    halo_a0, halo_a1 = halo_back(att0, att1)
    ga0, ga1 = projected_back(att0, halo_a0), projected_back(att1, halo_a1)
    operands[QKV_A] = (h0, ga0, ga1)
    operands[OUT_A] = (gy1, oa0, oa1)
    back_a, gain_a_grad = norm_back(
        r0, ga, through_qkv(ga0, wqkv_a0) + through_qkv(ga1, wqkv_a1)
    )
    smalls = jnp.stack(
        [gain_a_grad, gain_b_grad, gain_c_grad, small[0], gain_d_grad, small[1]]
    )
    shares, last_share, landed_input = weight_grads(
        operands, first_grad, jnp.pad(bf(smalls), ((0, TILE - 6), (0, 0))), bf(grad1 + back_a)
    )
    small_share = last_share[1].astype(f32)
    chosen = (
        (numbers[:, None] == jnp.arange(SLOTS, dtype=jnp.int32)[None, :])
        & (closes & lively)[:, None]
    )
    state_tiles = landed[1].astype(f32)
    final_share = jnp.stack(
        [
            jnp.sum(jnp.where(chosen[:, i, None, None], state_tiles, 0.0), axis=0)
            for i in range(SLOTS)
        ],
        axis=1,
    )

    def share(name):
        value = shares[name].astype(f32)
        return value.reshape(value.shape[0], 3, -1) if name in (QKV_A, QKV_C, SQKV_C) else value

    return (
        landed[0][None],
        final_share[None],
        landed_input.astype(f32),
        small_share[0],
        share(QKV_A),
        share(OUT_A),
        small_share[1],
        share(UP_B),
        share(DOWN_B),
        small_share[2],
        small_share[3],
        share(QKV_C),
        share(SQKV_C),
        share(OUT_C),
        share(SOUT_C),
        small_share[5],
        last_share[0].astype(f32),
        small_share[4],
        share(UP_D),
        share(DOWN_D),
    )


def chosen(*arrays):
    devices = (lax.axis_size(SECTION), lax.axis_size(TENSOR), lax.axis_size(DP))
    if devices == (4, 2, 4) and arrays[0].shape[1] == 8:
        return block_body(*arrays)
    return relay_body(*arrays)


def solution(mesh):
    in_specs = (
        P(DP, None, TENSOR, None),
        P(DP, None, TENSOR, None),
        P(),
        P(),
        P(),
        P(None, None, TENSOR),
        P(TENSOR, None),
        P(),
        P(None, TENSOR),
        P(TENSOR, None),
        P(),
        P(),
        P(None, None, TENSOR),
        P(None, None, TENSOR),
        P(TENSOR, None),
        P(TENSOR, None),
        P(),
        P(TENSOR, None),
        P(),
        P(None, TENSOR),
        P(TENSOR, None),
    )
    out_specs = (
        P(DP, None, TENSOR, SECTION),
        P(DP, TENSOR, None, SECTION),
        P(DP, None, TENSOR, SECTION),
        P(SECTION),
        P(SECTION, None, TENSOR),
        P(TENSOR, SECTION),
        P(SECTION),
        P(SECTION, TENSOR),
        P(TENSOR, SECTION),
        P(SECTION),
        P(SECTION),
        P(SECTION, None, TENSOR),
        P(SECTION, None, TENSOR),
        P(TENSOR, SECTION),
        P(TENSOR, SECTION),
        P(SECTION),
        P(TENSOR, SECTION),
        P(SECTION),
        P(SECTION, TENSOR),
        P(TENSOR, SECTION),
    )
    return jax.shard_map(chosen, mesh=mesh, in_specs=in_specs, out_specs=out_specs, check_vma=False)
```

```python
import functools
import math

import jax
import jax.numpy as jnp
from jax import lax
from jax.experimental import pallas as pl
from jax.experimental.pallas import tpu as pltpu
from jax.sharding import PartitionSpec as P

SECTION, DP, TENSOR = "section", "dp", "tensor"
HEAD_DIM = 128
SLOTS = 3


EPSILON = 1e-06
NEGATIVE = -1e30


def shifted(value, axis, by):
    devices = lax.axis_size(axis)
    pairs = [(i, i + by) for i in range(devices) if 0 <= i + by < devices]
    return lax.ppermute(value, axis, pairs)


def for_sending(value):
    return jax.tree.map(lambda a: a.astype(jnp.bfloat16) if a.dtype == jnp.float32 else a, value)


def layout(seg_blocks, seg_group, group_index, block_count):
    mine = seg_group == group_index
    lengths = jnp.where(mine, seg_blocks, 0)
    offsets = jnp.cumsum(lengths) - lengths
    ranking = jnp.cumsum(mine.astype(jnp.int32)) - mine.astype(jnp.int32)
    blocks = jnp.arange(block_count, dtype=jnp.int32)[None, :]
    inside = mine[:, None] & (blocks >= offsets[:, None]) & (blocks < (offsets + lengths)[:, None])
    begins = jnp.any(inside & (blocks == offsets[:, None]), axis=0)
    closes = jnp.any(inside & (blocks == (offsets + lengths - 1)[:, None]), axis=0)
    lively = jnp.any(inside, axis=0)
    numbers = jnp.sum(jnp.where(inside, ranking[:, None], 0), axis=0)
    return (begins, closes, lively, numbers)


def inverse_rms(values):
    return lax.rsqrt(jnp.mean(values * values, axis=-1, keepdims=True) + EPSILON)


def norm_back(values, gain, grad_normed):
    factor = inverse_rms(values)
    scaled = values * factor
    grad_scaled = grad_normed * gain
    grad_values = factor * (
        grad_scaled - scaled * jnp.mean(grad_scaled * scaled, axis=-1, keepdims=True)
    )
    return (grad_values, jnp.sum(grad_normed * scaled, axis=0))


def smooth(values):
    return jax.nn.gelu(values, approximate=True)


def split_heads(rows_in):
    return rows_in.reshape(rows_in.shape[0], -1, HEAD_DIM)


def attend_forward(queries, key_rows, value_rows, allowed):
    score_scale = 1.0 / math.sqrt(HEAD_DIM)
    scores = (
        jnp.einsum("rhd,khd->hrk", queries, key_rows, preferred_element_type=jnp.float32)
        * score_scale
    )
    scores = jnp.where(allowed[None], scores, NEGATIVE)
    largest = jnp.max(scores, axis=-1, keepdims=True)
    totals = jnp.sum(jnp.exp(scores - largest), axis=-1, keepdims=True)
    log_total = largest + jnp.log(totals)
    weights = jnp.exp(scores - log_total).astype(jnp.bfloat16)
    mixture_output = jnp.einsum(
        "hrk,khd->rhd", weights, value_rows, preferred_element_type=jnp.float32
    )
    return (mixture_output, log_total[..., 0])


def attend_backward(queries, key_rows, value_rows, allowed, log_total, grad_mixture):
    score_scale = 1.0 / math.sqrt(HEAD_DIM)
    scores = (
        jnp.einsum("rhd,khd->hrk", queries, key_rows, preferred_element_type=jnp.float32)
        * score_scale
    )
    scores = jnp.where(allowed[None], scores, NEGATIVE)
    weights = jnp.exp(scores - log_total[..., None])
    rounded = weights.astype(jnp.bfloat16)
    grad_weights = jnp.einsum(
        "rhd,khd->hrk", grad_mixture, value_rows, preferred_element_type=jnp.float32
    )
    grad_values = jnp.einsum(
        "hrk,rhd->khd", rounded, grad_mixture, preferred_element_type=jnp.float32
    )
    inner_sum = jnp.sum(weights * grad_weights, axis=-1, keepdims=True)
    grad_scores = (weights * (grad_weights - inner_sum)).astype(jnp.bfloat16)
    grad_queries = (
        jnp.einsum("hrk,khd->rhd", grad_scores, key_rows, preferred_element_type=jnp.float32)
        * score_scale
    )
    grad_keys = (
        jnp.einsum("hrk,rhd->khd", grad_scores, queries, preferred_element_type=jnp.float32)
        * score_scale
    )
    return (grad_queries, grad_keys, grad_values)


def place_row(store, position, value, active_tick):
    previous = lax.dynamic_index_in_dim(store, position, 0, False)
    return lax.dynamic_update_index_in_dim(
        store, jnp.where(active_tick, value, previous), position, 0
    )


def renewed(grad_sums, active_tick, changes):
    return tuple(
        (
            total + jnp.where(active_tick, changes[position], 0.0) if position in changes else total
            for position, total in enumerate(grad_sums)
        )
    )


def relay_body(
    layer_input,
    output_grad,
    seg_blocks,
    seg_group,
    gain_a,
    wqkv_a,
    wout_a,
    gain_b,
    up_b,
    down_b,
    gain_c,
    gain_s,
    wqkv_c,
    sqkv_c,
    wout_c,
    sout_c,
    gate_bias,
    init_states,
    gain_d,
    up_d,
    down_d,
):
    block_count = layer_input.shape[1]
    shard_rows = layer_input.shape[2]
    model_width = layer_input.shape[3]
    tensor_count = lax.axis_size(TENSOR)
    token_rows = shard_rows * tensor_count
    state_shard = init_states.shape[0]
    state_count = state_shard * tensor_count
    local_width = wqkv_a.shape[2]
    local_heads = local_width // HEAD_DIM
    section_index = lax.axis_index(SECTION)
    group_index = lax.axis_index(DP)
    on_cell_section = section_index == 2
    begins, closes, lively, numbers = layout(seg_blocks, seg_group, group_index, block_count)
    token_gains = jnp.stack([gain_a, gain_b, gain_c, gain_d]).astype(jnp.float32)
    state_gain = gain_s.astype(jnp.float32)
    retain = jax.nn.sigmoid(gate_bias.astype(jnp.float32))
    initial = init_states.astype(jnp.float32)
    empty_state = jnp.zeros((state_count, model_width), jnp.float32)
    empty_token_store = jnp.zeros((token_rows, 4, local_width), jnp.bfloat16)
    empty_state_store = jnp.zeros((state_count, 4, local_width), jnp.bfloat16)
    empty_token_lse = jnp.zeros((local_heads, token_rows), jnp.float32)
    empty_state_lse = jnp.zeros((local_heads, state_count), jnp.float32)
    empty_carry = jnp.zeros((token_rows, local_width), jnp.float32)
    every_key = jnp.ones((state_count, token_rows + state_count), bool)
    state_keys_all = jnp.ones((token_rows, state_count), bool)

    def token_masks(opening):
        later_keys = lax.broadcasted_iota(
            jnp.int32, (token_rows, token_rows), 1
        ) > lax.broadcasted_iota(jnp.int32, (token_rows, token_rows), 0)
        return (jnp.logical_and(later_keys, jnp.logical_not(opening)), jnp.logical_not(later_keys))

    def plain_forward(normed_tok, normed_st, prior_block, opening):
        projected = jnp.einsum(
            "rd,dcn->rcn", normed_tok, wqkv_a, preferred_element_type=jnp.float32
        ).astype(jnp.bfloat16)
        reach_prior, reach_current = token_masks(opening)
        allowed = jnp.concatenate([reach_prior, reach_current], axis=1)
        key_rows = jnp.concatenate([prior_block[:, 1], projected[:, 1]], axis=0)
        value_rows = jnp.concatenate([prior_block[:, 2], projected[:, 2]], axis=0)
        mixture_output, token_lse = attend_forward(
            split_heads(projected[:, 0]), split_heads(key_rows), split_heads(value_rows), allowed
        )
        mixture_output = mixture_output.reshape(token_rows, local_width).astype(jnp.bfloat16)
        branch = jnp.dot(mixture_output, wout_a, preferred_element_type=jnp.float32)
        stored = jnp.concatenate([projected, mixture_output[:, None]], axis=1)
        return (branch, empty_state, stored, empty_state_store, token_lse, empty_state_lse)

    def feed_forward(up_projection_weight, down_projection_weight):

        def forward_fn(normed_tok, normed_st, prior_block, opening):
            hidden_rows = jnp.dot(
                normed_tok, up_projection_weight, preferred_element_type=jnp.float32
            )
            active_flags = smooth(hidden_rows).astype(jnp.bfloat16)
            branch = jnp.dot(
                active_flags, down_projection_weight, preferred_element_type=jnp.float32
            )
            return (
                branch,
                empty_state,
                empty_token_store,
                empty_state_store,
                empty_token_lse,
                empty_state_lse,
            )

        return forward_fn

    def recurrent_forward(normed_tok, normed_st, prior_block, opening):
        projected = jnp.einsum(
            "rd,dcn->rcn", normed_tok, wqkv_c, preferred_element_type=jnp.float32
        ).astype(jnp.bfloat16)
        state_proj = jnp.einsum(
            "sd,dcn->scn", normed_st, sqkv_c, preferred_element_type=jnp.float32
        ).astype(jnp.bfloat16)
        reach_prior, reach_current = token_masks(opening)
        allowed = jnp.concatenate([reach_prior, reach_current, state_keys_all], axis=1)
        token_keys = jnp.concatenate([prior_block[:, 1], projected[:, 1], state_proj[:, 1]], axis=0)
        token_values = jnp.concatenate(
            [prior_block[:, 2], projected[:, 2], state_proj[:, 2]], axis=0
        )
        token_mixture, token_lse = attend_forward(
            split_heads(projected[:, 0]),
            split_heads(token_keys),
            split_heads(token_values),
            allowed,
        )
        state_keys = jnp.concatenate([projected[:, 1], state_proj[:, 1]], axis=0)
        state_values = jnp.concatenate([projected[:, 2], state_proj[:, 2]], axis=0)
        state_mixture, state_lse = attend_forward(
            split_heads(state_proj[:, 0]),
            split_heads(state_keys),
            split_heads(state_values),
            every_key,
        )
        token_mixture = token_mixture.reshape(token_rows, local_width).astype(jnp.bfloat16)
        state_mixture = state_mixture.reshape(state_count, local_width).astype(jnp.bfloat16)
        branch = jnp.dot(token_mixture, wout_c, preferred_element_type=jnp.float32)
        update_term = jnp.dot(state_mixture, sout_c, preferred_element_type=jnp.float32)
        stored = jnp.concatenate([projected, token_mixture[:, None]], axis=1)
        state_stored = jnp.concatenate([state_proj, state_mixture[:, None]], axis=1)
        return (branch, update_term, stored, state_stored, token_lse, state_lse)

    def plain_backward(
        grad_tok,
        grad_st,
        normed_tok,
        normed_st,
        tok_block,
        st_block,
        prior_block,
        token_lse,
        state_lse,
        opening,
        carry_keys,
        carry_values,
        grad_sums,
        active_tick,
    ):
        reach_prior, reach_current = token_masks(opening)
        allowed = jnp.concatenate([reach_prior, reach_current], axis=1)
        key_rows = jnp.concatenate([prior_block[:, 1], tok_block[:, 1]], axis=0)
        value_rows = jnp.concatenate([prior_block[:, 2], tok_block[:, 2]], axis=0)
        weight_out = jnp.einsum(
            "rn,rd->nd", tok_block[:, 3], grad_tok, preferred_element_type=jnp.float32
        )
        grad_mixture = jnp.einsum(
            "rd,nd->rn", grad_tok, wout_a, preferred_element_type=jnp.float32
        ).astype(jnp.bfloat16)
        grad_query, grad_keys, grad_values = attend_backward(
            split_heads(tok_block[:, 0]),
            split_heads(key_rows),
            split_heads(value_rows),
            allowed,
            token_lse,
            split_heads(grad_mixture),
        )
        grad_query = grad_query.reshape(token_rows, local_width)
        grad_keys = grad_keys.reshape(2 * token_rows, local_width)
        grad_values = grad_values.reshape(2 * token_rows, local_width)
        grad_proj = jnp.stack(
            [
                grad_query,
                grad_keys[token_rows:] + carry_keys,
                grad_values[token_rows:] + carry_values,
            ],
            axis=1,
        ).astype(jnp.bfloat16)
        weight_in = jnp.einsum(
            "rd,rcn->dcn", normed_tok, grad_proj, preferred_element_type=jnp.float32
        )
        grad_normed = jnp.einsum(
            "rcn,dcn->rd", grad_proj, wqkv_a, preferred_element_type=jnp.float32
        )
        return (
            grad_normed,
            empty_state,
            grad_keys[:token_rows],
            grad_values[:token_rows],
            renewed(grad_sums, active_tick, {0: weight_in, 1: weight_out}),
        )

    def feed_backward(up_projection_weight, down_projection_weight, up_slot, down_slot):

        def backward_fn(
            grad_tok,
            grad_st,
            normed_tok,
            normed_st,
            tok_block,
            st_block,
            prior_block,
            token_lse,
            state_lse,
            opening,
            carry_keys,
            carry_values,
            grad_sums,
            active_tick,
        ):
            hidden_rows = jnp.dot(
                normed_tok, up_projection_weight, preferred_element_type=jnp.float32
            )
            active_flags, gelu_back = jax.vjp(smooth, hidden_rows)
            weight_down = jnp.einsum(
                "rf,rd->fd",
                active_flags.astype(jnp.bfloat16),
                grad_tok,
                preferred_element_type=jnp.float32,
            )
            grad_active = jnp.einsum(
                "rd,fd->rf", grad_tok, down_projection_weight, preferred_element_type=jnp.float32
            )
            grad_hidden = gelu_back(grad_active)[0].astype(jnp.bfloat16)
            weight_up = jnp.einsum(
                "rd,rf->df", normed_tok, grad_hidden, preferred_element_type=jnp.float32
            )
            grad_normed = jnp.einsum(
                "rf,df->rd", grad_hidden, up_projection_weight, preferred_element_type=jnp.float32
            )
            return (
                grad_normed,
                empty_state,
                empty_carry,
                empty_carry,
                renewed(grad_sums, active_tick, {up_slot: weight_up, down_slot: weight_down}),
            )

        return backward_fn

    def recurrent_backward(
        grad_tok,
        grad_st,
        normed_tok,
        normed_st,
        tok_block,
        st_block,
        prior_block,
        token_lse,
        state_lse,
        opening,
        carry_keys,
        carry_values,
        grad_sums,
        active_tick,
    ):
        reach_prior, reach_current = token_masks(opening)
        allowed = jnp.concatenate([reach_prior, reach_current, state_keys_all], axis=1)
        token_keys = jnp.concatenate([prior_block[:, 1], tok_block[:, 1], st_block[:, 1]], axis=0)
        token_values = jnp.concatenate([prior_block[:, 2], tok_block[:, 2], st_block[:, 2]], axis=0)
        state_keys = jnp.concatenate([tok_block[:, 1], st_block[:, 1]], axis=0)
        state_values = jnp.concatenate([tok_block[:, 2], st_block[:, 2]], axis=0)
        weight_out = jnp.einsum(
            "rn,rd->nd", tok_block[:, 3], grad_tok, preferred_element_type=jnp.float32
        )
        weight_state_out = jnp.einsum(
            "sn,sd->nd", st_block[:, 3], grad_st, preferred_element_type=jnp.float32
        )
        grad_token_mixture = jnp.einsum(
            "rd,nd->rn", grad_tok, wout_c, preferred_element_type=jnp.float32
        ).astype(jnp.bfloat16)
        grad_state_mixture = jnp.einsum(
            "sd,nd->sn", grad_st, sout_c, preferred_element_type=jnp.float32
        ).astype(jnp.bfloat16)
        grad_query, grad_keys, grad_values = attend_backward(
            split_heads(tok_block[:, 0]),
            split_heads(token_keys),
            split_heads(token_values),
            allowed,
            token_lse,
            split_heads(grad_token_mixture),
        )
        state_query, state_grad_keys, state_grad_values = attend_backward(
            split_heads(st_block[:, 0]),
            split_heads(state_keys),
            split_heads(state_values),
            every_key,
            state_lse,
            split_heads(grad_state_mixture),
        )
        grad_query = grad_query.reshape(token_rows, local_width)
        grad_keys = grad_keys.reshape(2 * token_rows + state_count, local_width)
        grad_values = grad_values.reshape(2 * token_rows + state_count, local_width)
        state_query = state_query.reshape(state_count, local_width)
        state_grad_keys = state_grad_keys.reshape(token_rows + state_count, local_width)
        state_grad_values = state_grad_values.reshape(token_rows + state_count, local_width)
        own_keys = (
            grad_keys[token_rows : 2 * token_rows] + state_grad_keys[:token_rows] + carry_keys
        )
        own_values = (
            grad_values[token_rows : 2 * token_rows] + state_grad_values[:token_rows] + carry_values
        )
        cell_keys = grad_keys[2 * token_rows :] + state_grad_keys[token_rows:]
        cell_values = grad_values[2 * token_rows :] + state_grad_values[token_rows:]
        grad_proj = jnp.stack([grad_query, own_keys, own_values], axis=1).astype(jnp.bfloat16)
        grad_state_proj = jnp.stack([state_query, cell_keys, cell_values], axis=1).astype(
            jnp.bfloat16
        )
        weight_in = jnp.einsum(
            "rd,rcn->dcn", normed_tok, grad_proj, preferred_element_type=jnp.float32
        )
        weight_state_in = jnp.einsum(
            "sd,scn->dcn", normed_st, grad_state_proj, preferred_element_type=jnp.float32
        )
        grad_normed = jnp.einsum(
            "rcn,dcn->rd", grad_proj, wqkv_c, preferred_element_type=jnp.float32
        )
        grad_state_normed = jnp.einsum(
            "scn,dcn->sd", grad_state_proj, sqkv_c, preferred_element_type=jnp.float32
        )
        changes = {4: weight_in, 5: weight_state_in, 6: weight_out, 7: weight_state_out}
        return (
            grad_normed,
            grad_state_normed,
            grad_keys[:token_rows],
            grad_values[:token_rows],
            renewed(grad_sums, active_tick, changes),
        )

    forward_branches = [
        plain_forward,
        feed_forward(up_b, down_b),
        recurrent_forward,
        feed_forward(up_d, down_d),
    ]
    backward_branches = [
        plain_backward,
        feed_backward(up_b, down_b, 2, 3),
        recurrent_backward,
        feed_backward(up_d, down_d, 8, 9),
    ]

    def forward_tick(tick_number, carried):
        (
            received,
            state_carry,
            tok_normed,
            st_normed,
            tok_stored,
            st_stored,
            tok_lse_all,
            st_lse_all,
            entered,
            state_entered,
            updates,
            leaving_rows,
            finals,
        ) = carried
        block_number = tick_number - section_index
        active_tick = (block_number >= 0) & (block_number < block_count)
        block_index = jnp.clip(block_number, 0, block_count - 1)
        opening = begins[block_index]
        entering = jnp.where(
            section_index == 0, layer_input[0, block_index].astype(jnp.float32), received
        )
        state_in = jnp.where(opening, initial, state_carry)
        token_gain = token_gains[section_index]
        normed_shard = (entering * inverse_rms(entering) * token_gain).astype(jnp.bfloat16)
        state_normed_shard = (state_in * inverse_rms(state_in) * state_gain).astype(jnp.bfloat16)
        normed_tok, normed_st = (
            lax.all_gather(normed_shard, TENSOR, axis=0, tiled=True),
            lax.all_gather(state_normed_shard, TENSOR, axis=0, tiled=True),
        )
        prior_block = tok_stored[jnp.maximum(block_index - 1, 0)]
        branch, update_term, stored, state_stored, token_lse, state_lse = lax.switch(
            section_index, forward_branches, normed_tok, normed_st, prior_block, opening
        )
        branch_shard, update_shard = (
            lax.psum_scatter(
                branch.astype(jnp.bfloat16), TENSOR, scatter_dimension=0, tiled=True
            ).astype(jnp.float32),
            lax.psum_scatter(
                update_term.astype(jnp.bfloat16), TENSOR, scatter_dimension=0, tiled=True
            ).astype(jnp.float32),
        )
        leaving = entering + branch_shard
        state_new = retain * state_in + (1.0 - retain) * update_shard
        tok_normed = place_row(tok_normed, block_index, normed_tok, active_tick)
        st_normed = place_row(st_normed, block_index, normed_st, active_tick)
        tok_stored = place_row(tok_stored, block_index, stored, active_tick)
        st_stored = place_row(st_stored, block_index, state_stored, active_tick)
        tok_lse_all = place_row(tok_lse_all, block_index, token_lse, active_tick)
        st_lse_all = place_row(st_lse_all, block_index, state_lse, active_tick)
        entered = place_row(entered, block_index, entering, active_tick)
        state_entered = place_row(state_entered, block_index, state_in, active_tick)
        updates = place_row(updates, block_index, update_shard, active_tick)
        leaving_rows = place_row(leaving_rows, block_index, leaving, active_tick)
        on_cell = active_tick & on_cell_section
        state_carry = jnp.where(on_cell, state_new, state_carry)
        keep_final = on_cell & closes[block_index] & lively[block_index]
        slot_hit = (jnp.arange(SLOTS, dtype=jnp.int32) == numbers[block_index])[
            None, :, None
        ] & keep_final
        finals = jnp.where(slot_hit, state_new[:, None, :], finals)
        received = shifted(leaving.astype(jnp.bfloat16), SECTION, 1).astype(leaving.dtype)
        return (
            received,
            state_carry,
            tok_normed,
            st_normed,
            tok_stored,
            st_stored,
            tok_lse_all,
            st_lse_all,
            entered,
            state_entered,
            updates,
            leaving_rows,
            finals,
        )

    forward_start = (
        jnp.zeros((shard_rows, model_width), jnp.float32),
        jnp.zeros((state_shard, model_width), jnp.float32),
        jnp.zeros((block_count, token_rows, model_width), jnp.bfloat16),
        jnp.zeros((block_count, state_count, model_width), jnp.bfloat16),
        jnp.zeros((block_count, token_rows, 4, local_width), jnp.bfloat16),
        jnp.zeros((block_count, state_count, 4, local_width), jnp.bfloat16),
        jnp.zeros((block_count, local_heads, token_rows), jnp.float32),
        jnp.zeros((block_count, local_heads, state_count), jnp.float32),
        jnp.zeros((block_count, shard_rows, model_width), jnp.float32),
        jnp.zeros((block_count, state_shard, model_width), jnp.float32),
        jnp.zeros((block_count, state_shard, model_width), jnp.float32),
        jnp.zeros((block_count, shard_rows, model_width), jnp.float32),
        jnp.zeros((state_shard, SLOTS, model_width), jnp.float32),
    )
    (
        _,
        _,
        tok_normed,
        st_normed,
        tok_stored,
        st_stored,
        tok_lse_all,
        st_lse_all,
        entered,
        state_entered,
        updates,
        leaving_rows,
        finals,
    ) = lax.fori_loop(0, block_count + 3, forward_tick, forward_start)
    gain_rows_of_section = jnp.array([0, 1, 2, 4], dtype=jnp.int32)
    small_rows = jnp.arange(6, dtype=jnp.int32)[:, None]

    def backward_tick(tick_number, carried):
        (
            received,
            state_grad,
            carry_keys,
            carry_values,
            grad_sums,
            smalls,
            initial_grad,
            input_rows,
        ) = carried
        block_number = block_count - 1 - tick_number + 3 - section_index
        active_tick = (block_number >= 0) & (block_number < block_count)
        block_index = jnp.clip(block_number, 0, block_count - 1)
        opening = begins[block_index]
        arriving = jnp.where(
            section_index == 3,
            output_grad[0, block_index].astype(jnp.float32)
            * lively[block_index].astype(jnp.float32),
            received,
        )
        update_grad = (1.0 - retain) * state_grad
        grad_tok, grad_st = (
            lax.all_gather(arriving.astype(jnp.bfloat16), TENSOR, axis=0, tiled=True),
            lax.all_gather(update_grad.astype(jnp.bfloat16), TENSOR, axis=0, tiled=True),
        )
        grad_normed_tok, grad_normed_st, prior_keys, prior_values, grad_sums = lax.switch(
            section_index,
            backward_branches,
            grad_tok,
            grad_st,
            tok_normed[block_index],
            st_normed[block_index],
            tok_stored[block_index],
            st_stored[block_index],
            tok_stored[jnp.maximum(block_index - 1, 0)],
            tok_lse_all[block_index],
            st_lse_all[block_index],
            opening,
            carry_keys,
            carry_values,
            grad_sums,
            active_tick,
        )
        tok_shard, st_shard = (
            lax.psum_scatter(
                grad_normed_tok.astype(jnp.bfloat16), TENSOR, scatter_dimension=0, tiled=True
            ).astype(jnp.float32),
            lax.psum_scatter(
                grad_normed_st.astype(jnp.bfloat16), TENSOR, scatter_dimension=0, tiled=True
            ).astype(jnp.float32),
        )
        grad_entering, token_gain_term = norm_back(
            entered[block_index], token_gains[section_index], tok_shard
        )
        leaving_grad = arriving + grad_entering
        state_in = state_entered[block_index]
        grad_state_norm, state_gain_term = norm_back(state_in, state_gain, st_shard)
        grad_state_in = retain * state_grad + grad_state_norm
        bias_term = (
            jnp.sum(state_grad * (state_in - updates[block_index]), axis=0)
            * retain
            * (1.0 - retain)
        )
        on_cell = active_tick & on_cell_section
        gain_part = (small_rows == gain_rows_of_section[section_index]).astype(
            jnp.float32
        ) * token_gain_term[None, :]
        cell_part = (small_rows == 3).astype(jnp.float32) * state_gain_term[None, :] + (
            small_rows == 5
        ).astype(jnp.float32) * bias_term[None, :]
        smalls = (
            smalls + jnp.where(active_tick, gain_part, 0.0) + jnp.where(on_cell, cell_part, 0.0)
        )
        initial_grad = initial_grad + jnp.where(on_cell & opening, grad_state_in, 0.0)
        state_grad = jnp.where(on_cell, jnp.where(opening, 0.0, grad_state_in), state_grad)
        carry_keys = jnp.where(active_tick, prior_keys, carry_keys)
        carry_values = jnp.where(active_tick, prior_values, carry_values)
        input_rows = place_row(input_rows, block_index, leaving_grad, active_tick)
        received = shifted(for_sending(leaving_grad), SECTION, -1).astype(leaving_grad.dtype)
        return (
            received,
            state_grad,
            carry_keys,
            carry_values,
            grad_sums,
            smalls,
            initial_grad,
            input_rows,
        )

    zero_grads = (
        jnp.zeros(wqkv_a.shape, jnp.float32),
        jnp.zeros(wout_a.shape, jnp.float32),
        jnp.zeros(up_b.shape, jnp.float32),
        jnp.zeros(down_b.shape, jnp.float32),
        jnp.zeros(wqkv_c.shape, jnp.float32),
        jnp.zeros(sqkv_c.shape, jnp.float32),
        jnp.zeros(wout_c.shape, jnp.float32),
        jnp.zeros(sout_c.shape, jnp.float32),
        jnp.zeros(up_d.shape, jnp.float32),
        jnp.zeros(down_d.shape, jnp.float32),
    )
    backward_start = (
        jnp.zeros((shard_rows, model_width), jnp.float32),
        jnp.zeros((state_shard, model_width), jnp.float32),
        empty_carry,
        empty_carry,
        zero_grads,
        jnp.zeros((6, model_width), jnp.float32),
        jnp.zeros((state_shard, model_width), jnp.float32),
        jnp.zeros((block_count, shard_rows, model_width), jnp.float32),
    )
    _, _, _, _, grad_sums, smalls, initial_grad, input_rows = lax.fori_loop(
        0, block_count + 3, backward_tick, backward_start
    )
    out_term = jnp.where(
        section_index == 3, leaving_rows * lively[:, None, None].astype(jnp.float32), 0.0
    )[None]
    input_term = jnp.where(section_index == 0, input_rows, 0.0)[None]
    final_term = jnp.where(section_index == 2, finals, 0.0)[None]
    out_share, input_share, final_share = (
        lax.psum_scatter(
            out_term.astype(jnp.bfloat16), SECTION, scatter_dimension=3, tiled=True
        ).astype(jnp.float32),
        lax.psum_scatter(
            input_term.astype(jnp.bfloat16), SECTION, scatter_dimension=3, tiled=True
        ).astype(jnp.float32),
        lax.psum_scatter(
            final_term.astype(jnp.bfloat16), SECTION, scatter_dimension=3, tiled=True
        ).astype(jnp.float32),
    )
    (
        grad_qkv_a,
        grad_out_a,
        grad_upper_b,
        grad_lower_b,
        grad_qkv_c,
        grad_state_qkv,
        grad_out_c,
        grad_state_out,
        grad_upper_d,
        grad_lower_d,
    ) = grad_sums
    totals = (
        lax.psum(grad_qkv_a.astype(jnp.bfloat16), DP).astype(jnp.float32),
        lax.psum(grad_out_a.astype(jnp.bfloat16), DP).astype(jnp.float32),
        lax.psum(grad_upper_b.astype(jnp.bfloat16), DP).astype(jnp.float32),
        lax.psum(grad_lower_b.astype(jnp.bfloat16), DP).astype(jnp.float32),
        lax.psum(grad_qkv_c.astype(jnp.bfloat16), DP).astype(jnp.float32),
        lax.psum(grad_state_qkv.astype(jnp.bfloat16), DP).astype(jnp.float32),
        lax.psum(grad_out_c.astype(jnp.bfloat16), DP).astype(jnp.float32),
        lax.psum(grad_state_out.astype(jnp.bfloat16), DP).astype(jnp.float32),
        lax.psum(grad_upper_d.astype(jnp.bfloat16), DP).astype(jnp.float32),
        lax.psum(grad_lower_d.astype(jnp.bfloat16), DP).astype(jnp.float32),
        lax.psum(initial_grad.astype(jnp.bfloat16), DP).astype(jnp.float32),
    )
    small_total = lax.psum(smalls, (DP, TENSOR))
    shares = (
        lax.psum_scatter(
            totals[0].astype(jnp.bfloat16), SECTION, scatter_dimension=0, tiled=True
        ).astype(jnp.float32),
        lax.psum_scatter(
            totals[1].astype(jnp.bfloat16), SECTION, scatter_dimension=1, tiled=True
        ).astype(jnp.float32),
        lax.psum_scatter(
            totals[2].astype(jnp.bfloat16), SECTION, scatter_dimension=0, tiled=True
        ).astype(jnp.float32),
        lax.psum_scatter(
            totals[3].astype(jnp.bfloat16), SECTION, scatter_dimension=1, tiled=True
        ).astype(jnp.float32),
        lax.psum_scatter(
            totals[4].astype(jnp.bfloat16), SECTION, scatter_dimension=0, tiled=True
        ).astype(jnp.float32),
        lax.psum_scatter(
            totals[5].astype(jnp.bfloat16), SECTION, scatter_dimension=0, tiled=True
        ).astype(jnp.float32),
        lax.psum_scatter(
            totals[6].astype(jnp.bfloat16), SECTION, scatter_dimension=1, tiled=True
        ).astype(jnp.float32),
        lax.psum_scatter(
            totals[7].astype(jnp.bfloat16), SECTION, scatter_dimension=1, tiled=True
        ).astype(jnp.float32),
        lax.psum_scatter(
            totals[8].astype(jnp.bfloat16), SECTION, scatter_dimension=0, tiled=True
        ).astype(jnp.float32),
        lax.psum_scatter(
            totals[9].astype(jnp.bfloat16), SECTION, scatter_dimension=1, tiled=True
        ).astype(jnp.float32),
        lax.psum_scatter(
            totals[10].astype(jnp.bfloat16), SECTION, scatter_dimension=1, tiled=True
        ).astype(jnp.float32),
        lax.psum_scatter(
            small_total.astype(jnp.bfloat16), SECTION, scatter_dimension=1, tiled=True
        ).astype(jnp.float32),
    )
    small_share = shares[11]
    return (
        out_share.astype(jnp.bfloat16),
        final_share,
        input_share,
        small_share[0],
        shares[0],
        shares[1],
        small_share[1],
        shares[2],
        shares[3],
        small_share[2],
        small_share[3],
        shares[4],
        shares[5],
        shares[6],
        shares[7],
        small_share[5],
        shares[10],
        small_share[4],
        shares[8],
        shares[9],
    )


CHAIN = 4
MESH = pl.DeviceIdType.MESH
SCALE = 1.0 / math.sqrt(HEAD_DIM)
LOG2_SCALE = SCALE * math.log2(math.e)
ALL_AXES = (SECTION, DP, TENSOR)
GROUP = (SECTION, TENSOR)
VMEM_BYTES = 60 * 1024 * 1024
CHUNK = 256


def block_of(section, tensor):
    high = section // 2
    return 2 * (2 * high + (tensor + high) % 2) + section % 2


DEVICE_OF_BLOCK = [0] * 8
for _section in range(4):
    for _tensor in range(2):
        DEVICE_OF_BLOCK[block_of(_section, _tensor)] = 2 * _section + _tensor
TO_NEXT = [(DEVICE_OF_BLOCK[b], DEVICE_OF_BLOCK[b + 1]) for b in range(7)]
TO_PRIOR = [(there, here) for here, there in TO_NEXT]
SWAP = [(0, 1), (1, 0)]


def params(**extra):
    return pltpu.CompilerParams(vmem_limit_bytes=VMEM_BYTES, **extra)


def nt(a, b):
    return lax.dot_general(a, b, (((1,), (1,)), ((), ())), preferred_element_type=jnp.float32)


def nn(a, b):
    return lax.dot_general(a, b, (((1,), (0,)), ((), ())), preferred_element_type=jnp.float32)


def tn(a, b):
    return lax.dot_general(a, b, (((0,), (0,)), ((), ())), preferred_element_type=jnp.float32)


def bf(a):
    return a.astype(jnp.bfloat16)


def with_ones(values):
    return jnp.concatenate([values, jnp.ones_like(values)], axis=1)


def later_mask(rows):
    return lax.broadcasted_iota(jnp.int32, (rows, rows), 1) > lax.broadcasted_iota(
        jnp.int32, (rows, rows), 0
    )


def window_scores(query, k, pk, start, rows, bar):
    stop = start + query.shape[0]
    own = nt(query, k[:stop])
    prior = nt(query, pk[start:]) + bar
    later = later_mask(query.shape[0])
    pieces = [jnp.where(later, prior[:, : stop - start], own[:, start:])]
    if start:
        pieces = [own[:, :start]] + pieces
    if stop < rows:
        pieces = pieces + [prior[:, stop - start :]]
    return jnp.concatenate(pieces, axis=1) if len(pieces) > 1 else pieces[0]


def window_parts(values, start):
    size = values.shape[0]
    later = later_mask(size)
    middle = values[:, start : start + size]
    zero = jnp.zeros_like(middle)
    own, prior = jnp.where(later, zero, middle), jnp.where(later, middle, zero)
    if start:
        own = jnp.concatenate([values[:, :start], own], axis=1)
    if start + size < values.shape[1]:
        prior = jnp.concatenate([prior, values[:, start + size :]], axis=1)
    return own, prior


def attend_kernel(with_states, *refs):
    if with_states:
        open_ref, q, k, v, pk, pv, sk, sv, out, lse = refs
    else:
        open_ref, q, k, v, pk, pv, out, lse = refs
    rows = q.shape[0]
    bar = jnp.where(open_ref[0] > 0, NEGATIVE, 0.0)
    keys, prior_keys = k[...], pk[...]
    values, prior_values = with_ones(v[...]), with_ones(pv[...])
    if with_states:
        state_keys, state_values = sk[...], with_ones(sv[...])
    for start in range(0, rows, CHUNK):
        query = q[start : start + CHUNK]
        scores = window_scores(query, keys, prior_keys, start, rows, bar)
        top = jnp.max(scores, axis=-1, keepdims=True)
        if with_states:
            more = nt(query, state_keys)
            top = jnp.maximum(top, jnp.max(more, axis=-1, keepdims=True))
        own, prior = window_parts(bf(jnp.exp2((scores - top) * LOG2_SCALE)), start)
        mixed = nn(own, values[: start + CHUNK]) + nn(prior, prior_values[start:])
        if with_states:
            mixed = mixed + nn(bf(jnp.exp2((more - top) * LOG2_SCALE)), state_values)
        total = mixed[:, HEAD_DIM:]
        out[start : start + CHUNK] = bf(mixed[:, :HEAD_DIM] / total)
        lse[0, start : start + CHUNK] = top * LOG2_SCALE + jnp.log2(total[:, :1])


def head_block(rows, offset):
    return pl.BlockSpec((rows, HEAD_DIM), lambda h: (0, offset + h))


def attend(opening, proj, prior, states=None):
    rows, width = proj.shape[0], proj.shape[1] // 3
    heads = width // HEAD_DIM
    specs = [pl.BlockSpec(memory_space=pltpu.SMEM)]
    specs += [head_block(rows, i * heads) for i in range(3)]
    specs += [head_block(rows, i * heads) for i in range(2)]
    args = [opening, proj, proj, proj, prior, prior]
    keys = 2 * rows
    if states is not None:
        specs += [head_block(states.shape[0], i * heads) for i in (1, 2)]
        args += [states, states]
        keys += states.shape[0]
    return pl.pallas_call(
        functools.partial(attend_kernel, states is not None),
        grid=(heads,),
        in_specs=specs,
        out_specs=[
            head_block(rows, 0),
            pl.BlockSpec((1, rows, 1), lambda h: (h, 0, 0)),
        ],
        out_shape=[
            jax.ShapeDtypeStruct((rows, width), jnp.bfloat16),
            jax.ShapeDtypeStruct((heads, rows, 1), jnp.float32),
        ],
        compiler_params=params(),
        cost_estimate=pl.CostEstimate(
            flops=4 * rows * keys * width,
            bytes_accessed=2 * rows * width * 8,
            transcendentals=rows * keys * heads // 2,
        ),
    )(*args)


def attend_back_kernel(with_states, *refs):
    if with_states:
        (open_ref, q, k, v, pk, pv, sk, sv, gmix, mix, lse) = refs[:11]
        (gq, gk, gv, gpk, gpv, gsk, gsv) = refs[11:18]
    else:
        (open_ref, q, k, v, pk, pv, gmix, mix, lse) = refs[:9]
        (gq, gk, gv, gpk, gpv) = refs[9:14]
    gpk_sum, gpv_sum = refs[-2:]
    rows = q.shape[0]
    bar = jnp.where(open_ref[0] > 0, NEGATIVE, 0.0)
    keys, prior_keys, values, prior_values = k[...], pk[...], v[...], pv[...]
    if with_states:
        state_keys, state_values = sk[...], sv[...]
    for start in range(0, rows, CHUNK):
        stop = start + CHUNK
        query, grad, log_total = q[start:stop], gmix[start:stop], lse[0, start:stop]
        inner = jnp.sum(
            grad.astype(jnp.float32) * mix[start:stop].astype(jnp.float32), axis=-1, keepdims=True
        )
        scores = window_scores(query, keys, prior_keys, start, rows, bar)
        weights = jnp.exp2(scores * LOG2_SCALE - log_total)
        grad_weights = window_scores(grad, values, prior_values, start, rows, 0.0)
        own, prior = window_parts(bf(weights), start)
        own_scores, prior_scores = window_parts(bf(weights * (grad_weights - inner)), start)
        grad_query = nn(own_scores, keys[:stop]) + nn(prior_scores, prior_keys[start:])
        add_own_v, add_own_k = tn(own, grad), tn(own_scores, query)
        add_prior_v, add_prior_k = tn(prior, grad), tn(prior_scores, query)
        if with_states:
            more = jnp.exp2(nt(query, state_keys) * LOG2_SCALE - log_total)
            from_states = bf(more * (nt(grad, state_values) - inner))
            grad_query = grad_query + nn(from_states, state_keys)
            add_sv, add_sk = tn(bf(more), grad), tn(from_states, query)
        gq[start:stop] = bf(grad_query * SCALE)
        if start == 0:
            gv[:stop], gk[:stop] = add_own_v, add_own_k * SCALE
            gpv_sum[...], gpk_sum[...] = add_prior_v, add_prior_k
            if with_states:
                gsv[...], gsk[...] = add_sv, add_sk * SCALE
        else:
            gv[:start] += add_own_v[:start]
            gk[:start] += add_own_k[:start] * SCALE
            gv[start:stop], gk[start:stop] = add_own_v[start:], add_own_k[start:] * SCALE
            gpv_sum[start:] += add_prior_v
            gpk_sum[start:] += add_prior_k
            if with_states:
                gsv[...] += add_sv
                gsk[...] += add_sk * SCALE
    gpv[...] = bf(gpv_sum[...])
    gpk[...] = bf(gpk_sum[...] * SCALE)


def attend_back(opening, proj, prior, grad_mixed, mixed, lse, states=None):
    rows, width = proj.shape[0], proj.shape[1] // 3
    heads = width // HEAD_DIM
    specs = [pl.BlockSpec(memory_space=pltpu.SMEM)]
    specs += [head_block(rows, i * heads) for i in range(3)]
    specs += [head_block(rows, i * heads) for i in range(2)]
    args = [opening, proj, proj, proj, prior, prior]
    keys = 2 * rows
    if states is not None:
        specs += [head_block(states.shape[0], i * heads) for i in (1, 2)]
        args += [states, states]
        keys += states.shape[0]
    specs += [head_block(rows, 0), head_block(rows, 0)]
    specs += [pl.BlockSpec((1, rows, 1), lambda h: (h, 0, 0))]
    args += [grad_mixed, mixed, lse]
    kinds = [jnp.bfloat16, jnp.float32, jnp.float32, jnp.bfloat16, jnp.bfloat16]
    if states is not None:
        kinds += [jnp.float32, jnp.float32]
    return pl.pallas_call(
        functools.partial(attend_back_kernel, states is not None),
        grid=(heads,),
        in_specs=specs,
        out_specs=[head_block(rows, 0) for _ in kinds],
        out_shape=[jax.ShapeDtypeStruct((rows, width), kind) for kind in kinds],
        scratch_shapes=[pltpu.VMEM((rows, HEAD_DIM), jnp.float32)] * 2,
        compiler_params=params(),
        cost_estimate=pl.CostEstimate(
            flops=10 * rows * keys * width,
            bytes_accessed=2 * rows * width * 24,
            transcendentals=rows * keys * heads // 2,
        ),
    )(*args)


KINDS = 9
FLIGHT = 4


class Spread:
    def __init__(self, sources, targets, send, recv):
        section, tensor, group = (lax.axis_index(a) for a in (SECTION, TENSOR, DP))
        self.sources, self.targets, self.send, self.recv = sources, targets, send, recv
        self.core, self.high, self.near = section % 2, section // 2, group % 2
        self.across = {TENSOR: 1 - tensor}
        self.along = {SECTION: (section + 2) % 4}
        self.beside = {DP: group + 1 - 2 * self.near}
        self.other = {SECTION: section + 1 - 2 * self.core}

    def partners(self):
        return [self.across, self.along, self.beside, self.other]

    def copy(self, kind, w):
        size = self.targets[w].shape[0] // 8
        y, z = self.high, self.near
        high, near, first, rows, to = (
            (y, z, 0, size, self.across),
            (y, z, 0, size, self.along),
            (y, z, 0, size, self.beside),
            (y, 1 - z, 0, size // 2, self.along),
            (1 - y, z, size // 2, size // 2, self.beside),
            (y, z, 0, size, self.other),
            (1 - y, z, 0, size, self.other),
            (y, 1 - z, 0, size, self.other),
            (1 - y, 1 - z, 0, size, self.other),
        )[kind]
        part = (near * 2 + high) * 2 + self.core
        where = pl.ds(pl.multiple_of(part * size + first, rows), rows)
        source = self.sources[w] if kind == 0 else self.targets[w]
        return pltpu.make_async_remote_copy(
            src_ref=source.at[where], dst_ref=self.targets[w].at[where],
            send_sem=self.send.at[kind * len(self.targets) + w],
            recv_sem=self.recv.at[kind * len(self.targets) + w],
            device_id=to, device_id_type=MESH,
        )

    def begin(self, w):
        self.copy(0, w).start()

    def hop(self, w):
        self.copy(0, w).wait_recv()
        for kind in (1, 2, 5):
            self.copy(kind, w).start()

    def cross(self, w):
        for kind in (1, 2):
            self.copy(kind, w).wait_recv()
        for kind in (3, 4, 6, 7):
            self.copy(kind, w).start()

    def close(self, w):
        for kind in (3, 4):
            self.copy(kind, w).wait_recv()
        self.copy(8, w).start()

    def end(self, w):
        for kind in (5, 6, 7, 8):
            self.copy(kind, w).wait_recv()
        for kind in range(KINDS):
            self.copy(kind, w).wait_send()


class Join:
    def __init__(self, source, theirs, mine, target, local, send, recv, i):
        tensor = lax.axis_index(TENSOR)
        rows = source.shape[-2]
        where = pl.ds(pl.multiple_of(tensor * rows, rows), rows)

        def of(index):
            return source if index is None else source.at[0, index]

        self.own = pltpu.make_async_copy(of(mine), target.at[where], local.at[i])
        self.remote = pltpu.make_async_remote_copy(
            src_ref=of(theirs), dst_ref=target.at[where], send_sem=send.at[i], recv_sem=recv.at[i],
            device_id={TENSOR: 1 - tensor}, device_id_type=MESH,
        )

    def start(self):
        self.remote.start()
        self.own.start()

    def wait(self):
        self.remote.wait()
        self.own.wait()


def meet(partners):
    barrier = pltpu.get_barrier_semaphore()
    for partner in partners:
        pl.semaphore_signal(barrier, inc=1, device_id=partner, device_id_type=MESH)
    pl.semaphore_wait(barrier, len(partners))


def gather_kernel(count, layer_input, init_states, *refs):
    sources, refs = refs[:count], refs[count:]
    tokens, before, initial = refs[:3]
    targets = refs[3 : 3 + count]
    send, recv, local, join_send, join_recv = refs[3 + count :]
    spread = Spread(sources, targets, send, recv)
    section, tensor = lax.axis_index(SECTION), lax.axis_index(TENSOR)
    block, partner = block_of(section, tensor), block_of(section, 1 - tensor)
    joins = [
        Join(layer_input, partner, block, tokens, local, join_send, join_recv, 0),
        Join(
            layer_input, jnp.maximum(partner - 1, 0), jnp.maximum(block - 1, 0),
            before, local, join_send, join_recv, 1,
        ),
        Join(init_states, None, None, initial, local, join_send, join_recv, 2),
    ]
    meet(spread.partners())
    def begin(i):
        if i < count:
            spread.begin(i)
        elif i < count + len(joins):
            joins[i - count].start()

    for i in range(FLIGHT):
        begin(i)
    for w in range(count + 3):
        if w < count:
            spread.hop(w)
        begin(w + FLIGHT)
        if 0 <= w - 2 < count:
            spread.cross(w - 2)
        if 0 <= w - 3 < count:
            spread.close(w - 3)
    for w in range(count):
        spread.end(w)
    for join in joins:
        join.wait()


def gather(layer_input, init_states, weights):
    count = len(weights)
    rows, width = 2 * layer_input.shape[2], layer_input.shape[3]
    dma = pltpu.SemaphoreType.DMA
    anywhere = pl.BlockSpec(memory_space=pl.ANY)
    shapes = [(rows, width)] * 2 + [(2 * init_states.shape[0], width)] + [w.shape for w in weights]
    results = pl.pallas_call(
        functools.partial(gather_kernel, count),
        in_specs=[anywhere] * (2 + count),
        out_specs=[anywhere] * (3 + count),
        out_shape=[jax.ShapeDtypeStruct(s, jnp.bfloat16) for s in shapes],
        scratch_shapes=[dma((KINDS * count,))] * 2 + [dma((3,))] * 3,
        compiler_params=params(collective_id=4, has_side_effects=True),
        cost_estimate=pl.CostEstimate(flops=0, bytes_accessed=200 * 1024 * 1024, transcendentals=0),
    )(layer_input, init_states, *weights)
    return results[:3], results[3:]


def neighbours():
    section, tensor = lax.axis_index(SECTION), lax.axis_index(TENSOR)
    block = block_of(section, tensor)

    return place_of((block + 7) % 8), place_of((block + 1) % 8)


def place_of(block):
    pair = block // 2
    high = pair // 2
    return {SECTION: 2 * high + block % 2, TENSOR: (pair + high) % 2}


class Scatter:
    def __init__(self, values, landed, send, recv, local):
        section, tensor = lax.axis_index(SECTION), lax.axis_index(TENSOR)
        block = block_of(section, tensor)
        self.members = [place_of((block + i) % 8) for i in range(1, 8)]
        rows, width = values[0].shape[0] // 2, values[0].shape[1] // 4

        def piece(value, to):
            high = pl.multiple_of(to[TENSOR] * rows, rows)
            left = pl.multiple_of(to[SECTION] * width, width)
            return value.at[pl.ds(high, rows), pl.ds(left, width)]

        self.copies = [
            pltpu.make_async_remote_copy(
                src_ref=piece(value, to), dst_ref=landed.at[j, block],
                send_sem=send.at[j * 7 + i], recv_sem=recv.at[j * 7 + i],
                device_id=to, device_id_type=MESH,
            )
            for j, value in enumerate(values)
            for i, to in enumerate(self.members)
        ]
        self.own = [
            pltpu.make_async_copy(
                piece(value, {SECTION: section, TENSOR: tensor}), landed.at[j, block], local.at[j]
            )
            for j, value in enumerate(values)
        ]

    def start(self):
        for copy in self.copies + self.own:
            copy.start()

    def wait(self):
        for copy in self.copies + self.own:
            copy.wait()


def pass_on(sent, landed, send_sem, recv_sem, slot, part, target):
    rows = pl.ds(part * CHUNK, CHUNK)
    return pltpu.make_async_remote_copy(
        src_ref=sent.at[slot, rows],
        dst_ref=landed.at[slot, rows],
        send_sem=send_sem.at[slot, part],
        recv_sem=recv_sem.at[slot, part],
        device_id=target,
        device_id_type=MESH,
    )


def chain_kernel(
    initial, starts, gain, keep, own, other, sqkv0, sqkv1, sout0, sout1, output_grad,
    state, hs, ps0, ps1, os0, os1, lse, update, fresh, cotangent,
    sent, landed, send_sem, recv_sem, local, join_send, join_recv,
):
    prior, following = neighbours()
    section, tensor = lax.axis_index(SECTION), lax.axis_index(TENSOR)
    join = Join(
        output_grad, block_of(section, 1 - tensor), block_of(section, tensor),
        cotangent, local, join_send, join_recv, 0,
    )
    meet([prior, following, {TENSOR: 1 - tensor}])
    join.start()
    count, width = initial.shape
    half = os0.shape[1]
    parts = count // CHUNK
    state[...] = initial[...]

    def copy(slot, part):
        return pass_on(sent, landed, send_sem, recv_sem, slot, part, following)

    def work(turn):
        for part in range(parts):
            rows = slice(part * CHUNK, (part + 1) * CHUNK)

            @pl.when(turn > 0)
            def _():
                slot = turn - 1
                copy(slot, part).wait_recv()
                state[rows] = jnp.where(
                    starts[...] > 0.0, initial[rows], landed[slot, rows].astype(jnp.float32)
                )

            value = state[rows]
            hidden = bf(value * inverse_rms(value) * gain[...])
            hs[rows] = hidden
            ps0[rows] = bf(nn(hidden, sqkv0[...]))
            ps1[rows] = bf(nn(hidden, sqkv1[...]))

        def one_head(h, carry):
            at = [pl.ds(pl.multiple_of(i * half + h * HEAD_DIM, HEAD_DIM), HEAD_DIM) for i in range(3)]
            for which, (tok, st, mixed) in enumerate(((own, ps0, os0), (other, ps1, os1))):
                tok_key, tok_value = tok[:, at[1]], with_ones(tok[:, at[2]])
                key, value = st[:, at[1]], with_ones(st[:, at[2]])
                for part in range(parts):
                    rows = slice(part * CHUNK, (part + 1) * CHUNK)
                    query = st[rows, at[0]]
                    score_tok, score = nt(query, tok_key), nt(query, key)
                    top = jnp.maximum(
                        jnp.max(score_tok, axis=-1, keepdims=True),
                        jnp.max(score, axis=-1, keepdims=True),
                    )
                    mix = nn(bf(jnp.exp2((score_tok - top) * LOG2_SCALE)), tok_value) + nn(
                        bf(jnp.exp2((score - top) * LOG2_SCALE)), value
                    )
                    total = mix[:, HEAD_DIM:]
                    mixed[rows, at[0]] = bf(mix[:, :HEAD_DIM] / total)
                    lse[which, h, rows] = top * LOG2_SCALE + jnp.log2(total[:, :1])
            return carry

        lax.fori_loop(0, half // HEAD_DIM, one_head, 0, unroll=True)
        for part in range(parts):
            rows = slice(part * CHUNK, (part + 1) * CHUNK)
            term = nn(os0[rows], sout0[...]) + nn(os1[rows], sout1[...])
            update[rows] = term
            renewed_state = keep[...] * state[rows] + (1.0 - keep[...]) * term
            fresh[rows] = renewed_state

            @pl.when(turn < CHAIN - 1)
            def _():
                sent[turn, rows] = bf(renewed_state)
                copy(turn, part).start()

    parity = block_of(section, tensor) % 2

    def one_round(turn, nothing):
        pl.when(parity == turn % 2)(lambda: work(turn))
        return nothing

    lax.fori_loop(0, CHAIN, one_round, 0)
    for slot in range(CHAIN - 1):

        @pl.when(parity == slot % 2)
        def _():
            for part in range(parts):
                copy(slot, part).wait_send()

    join.wait()


def chain(initial, starts, gain, keep, own, other, sqkv0, sqkv1, sout0, sout1, output_grad):
    count, width = initial.shape
    half = sout0.shape[0]
    heads = half // HEAD_DIM
    bf16, f32 = jnp.bfloat16, jnp.float32
    vmem, anywhere = pl.BlockSpec(memory_space=pltpu.VMEM), pl.BlockSpec(memory_space=pl.ANY)
    dma = pltpu.SemaphoreType.DMA
    parts = count // CHUNK
    return pl.pallas_call(
        chain_kernel,
        in_specs=[vmem] * 10 + [anywhere],
        out_specs=[vmem] * 9 + [anywhere],
        out_shape=[
            jax.ShapeDtypeStruct((count, width), f32),
            jax.ShapeDtypeStruct((count, width), bf16),
            jax.ShapeDtypeStruct((count, 3 * half), bf16),
            jax.ShapeDtypeStruct((count, 3 * half), bf16),
            jax.ShapeDtypeStruct((count, half), bf16),
            jax.ShapeDtypeStruct((count, half), bf16),
            jax.ShapeDtypeStruct((2, heads, count, 1), f32),
            jax.ShapeDtypeStruct((count, width), f32),
            jax.ShapeDtypeStruct((count, width), f32),
            jax.ShapeDtypeStruct((2 * output_grad.shape[2], width), bf16),
        ],
        scratch_shapes=[
            pltpu.VMEM((CHAIN - 1, count, width), bf16),
            pltpu.VMEM((CHAIN - 1, count, width), bf16),
            dma((CHAIN - 1, parts)), dma((CHAIN - 1, parts)),
            dma((1,)), dma((1,)), dma((1,)),
        ],
        compiler_params=params(collective_id=1, has_side_effects=True),
        cost_estimate=pl.CostEstimate(
            flops=CHAIN * count * width * (8 * width + 8 * count),
            bytes_accessed=25 * 1024 * 1024,
            transcendentals=CHAIN * count * count * 4 * heads,
        ),
    )(initial, starts, gain, keep, own, other, sqkv0, sqkv1, sout0, sout1, output_grad)


LATE = 10


def chain_back_kernel(
    ends, gain, keep, own, other, ps0, ps1, os0, os1, lse, *refs,
):
    distant, refs = refs[:LATE], refs[LATE:]
    result, ending, grad_state, gproj0, gproj1, gtok0, gtok1, gup, small, scattered = refs[:10]
    fetched, refs = refs[10 : 10 + LATE], refs[10 + LATE :]
    state, update, tok_k0, tok_v0, tok_k1, tok_v1, sqkv0, sqkv1, sout0, sout1 = fetched
    (
        weights, grad_os0, grad_os1, sent, landed, send_sem, recv_sem, piece_send, piece_recv, piece_sem, late_sem
    ) = refs
    fetches = [
        pltpu.make_async_copy(source, target, late_sem.at[i])
        for i, (source, target) in enumerate(zip(distant, fetched))
    ]
    for fetch in fetches:
        fetch.start()
    prior, following = neighbours()
    scatter = Scatter((result, ending), scattered, piece_send, piece_recv, piece_sem)
    meet([prior, following] + scatter.members)
    scatter.start()
    count, width = state.shape
    half = os0.shape[1]
    heads = half // HEAD_DIM
    parts = count // CHUNK
    sides = (
        (own, ps0, os0, tok_k0, tok_v0, gproj0, gtok0, grad_os0),
        (other, ps1, os1, tok_k1, tok_v1, gproj1, gtok1, grad_os1),
    )

    def lanes(h):
        return [pl.ds(pl.multiple_of(i * half + h * HEAD_DIM, HEAD_DIM), HEAD_DIM) for i in range(3)]

    def copy(slot, part):
        return pass_on(sent, landed, send_sem, recv_sem, slot, part, prior)

    def prepare(h, carry):
        at = lanes(h)
        for which, (tok, st, *_) in enumerate(sides):
            tok_key, key = tok[:, at[1]], st[:, at[1]]
            for part in range(parts):
                rows = slice(part * CHUNK, (part + 1) * CHUNK)
                query, log_total = st[rows, at[0]], lse[which, h, rows]
                weights[which, h, rows, :count] = bf(
                    jnp.exp2(nt(query, tok_key) * LOG2_SCALE - log_total)
                )
                weights[which, h, rows, count:] = bf(
                    jnp.exp2(nt(query, key) * LOG2_SCALE - log_total)
                )
        return carry

    lax.fori_loop(0, heads, prepare, 0)
    for fetch in fetches:
        fetch.wait()
    grad_state[...] = jnp.zeros_like(grad_state)

    def work(turn):
        for part in range(parts):
            rows = slice(part * CHUNK, (part + 1) * CHUNK)

            @pl.when(turn > 0)
            def _():
                slot = turn - 1
                copy(slot, part).wait_recv()
                grad_state[rows] = jnp.where(
                    ends[...] > 0.0, 0.0, landed[slot, rows].astype(jnp.float32)
                )

            out = bf((1.0 - keep[...]) * grad_state[rows])
            gup[rows] = out
            grad_os0[rows] = bf(nt(out, sout0[...]))
            grad_os1[rows] = bf(nt(out, sout1[...]))

        def one_head(h, carry):
            at = lanes(h)
            for which, (tok, st, mixed, given_k, given_v, gproj, gtok, grad_os) in enumerate(sides):
                tok_key, tok_value = tok[:, at[1]], tok[:, at[2]]
                key, value = st[:, at[1]], st[:, at[2]]
                for part in range(parts):
                    rows = slice(part * CHUNK, (part + 1) * CHUNK)
                    query, grad = st[rows, at[0]], grad_os[rows, at[0]]
                    inner = jnp.sum(
                        grad.astype(jnp.float32) * mixed[rows, at[0]].astype(jnp.float32),
                        axis=-1, keepdims=True,
                    )
                    p_tok, p = weights[which, h, rows, :count], weights[which, h, rows, count:]
                    s_tok = bf(p_tok.astype(jnp.float32) * (nt(grad, tok_value) - inner))
                    s = bf(p.astype(jnp.float32) * (nt(grad, value) - inner))
                    gproj[rows, at[0]] = bf((nn(s_tok, tok_key) + nn(s, key)) * SCALE)
                    gk, gv = tn(s, query) * SCALE, tn(p, grad)
                    if part == 0:
                        total_k, total_v = gk + given_k[:, at[0]], gv + given_v[:, at[0]]
                    else:
                        total_k, total_v = total_k + gk, total_v + gv

                    @pl.when(turn >= CHAIN - 2)
                    def _():
                        gtk, gtv = tn(s_tok, query) * SCALE, tn(p_tok, grad)
                        if part == 0:
                            gtok[:, at[0]], gtok[:, at[1]] = gtk, gtv
                        else:
                            gtok[:, at[0]] += gtk
                            gtok[:, at[1]] += gtv

                gproj[:, at[1]], gproj[:, at[2]] = bf(total_k), bf(total_v)
            return carry

        lax.fori_loop(0, heads, one_head, 0, unroll=True)
        for part in range(parts):
            rows = slice(part * CHUNK, (part + 1) * CHUNK)
            back = nt(gproj0[rows], sqkv0[...]) + nt(gproj1[rows], sqkv1[...])
            value, new = state[rows], grad_state[rows]
            factor = inverse_rms(value)
            scaled = value * factor
            through = back * gain[...]
            leaving = keep[...] * new + factor * (
                through - scaled * jnp.mean(through * scaled, axis=-1, keepdims=True)
            )

            @pl.when(turn < CHAIN - 1)
            def _():
                sent[turn, rows] = bf(leaving)
                copy(turn, part).start()

            @pl.when(turn >= CHAIN - 2)
            def _():
                gain_term = jnp.sum(back * scaled, axis=0, keepdims=True)
                bias_term = jnp.sum(new * (value - update[rows]), axis=0, keepdims=True) * (
                    keep[...] * (1.0 - keep[...])
                )
                if part == 0:
                    small[0:1, :], small[1:2, :] = gain_term, bias_term
                else:
                    small[0:1, :] += gain_term
                    small[1:2, :] += bias_term
                grad_state[rows] = leaving

    parity = 1 - block_of(lax.axis_index(SECTION), lax.axis_index(TENSOR)) % 2

    def one_round(turn, nothing):
        pl.when(parity == turn % 2)(lambda: work(turn))
        return nothing

    lax.fori_loop(0, CHAIN, one_round, 0)
    for slot in range(CHAIN - 1):

        @pl.when(parity == slot % 2)
        def _():
            for part in range(parts):
                copy(slot, part).wait_send()

    scatter.wait()


def chain_back(
    ends, state, update, gain, keep, own, other, ps0, ps1, os0, os1, lse,
    tok_k0, tok_v0, tok_k1, tok_v1, sqkv0, sqkv1, sout0, sout1, result, ending,
):
    count, width = state.shape
    half = sout0.shape[0]
    heads = half // HEAD_DIM
    bf16, f32 = jnp.bfloat16, jnp.float32
    vmem, anywhere = pl.BlockSpec(memory_space=pltpu.VMEM), pl.BlockSpec(memory_space=pl.ANY)
    dma = pltpu.SemaphoreType.DMA
    parts = count // CHUNK
    rows = own.shape[0]
    distant = (state, update, tok_k0, tok_v0, tok_k1, tok_v1, sqkv0, sqkv1, sout0, sout1)
    return pl.pallas_call(
        chain_back_kernel,
        in_specs=[vmem] * 10 + [anywhere] * (LATE + 2),
        out_specs=[vmem] * 7 + [anywhere],
        out_shape=[
            jax.ShapeDtypeStruct((count, width), f32),
            jax.ShapeDtypeStruct((count, 3 * half), bf16),
            jax.ShapeDtypeStruct((count, 3 * half), bf16),
            jax.ShapeDtypeStruct((rows, 2 * half), f32),
            jax.ShapeDtypeStruct((rows, 2 * half), f32),
            jax.ShapeDtypeStruct((count, width), bf16),
            jax.ShapeDtypeStruct((2, width), f32),
            jax.ShapeDtypeStruct((2, 8, rows // 2, width // 4), bf16),
        ],
        scratch_shapes=[pltpu.VMEM(late.shape, late.dtype) for late in distant]
        + [
            pltpu.VMEM((2, heads, count, rows + count), bf16),
            pltpu.VMEM((count, half), bf16),
            pltpu.VMEM((count, half), bf16),
            pltpu.VMEM((CHAIN - 1, count, width), bf16),
            pltpu.VMEM((CHAIN - 1, count, width), bf16),
            dma((CHAIN - 1, parts)), dma((CHAIN - 1, parts)), dma((14,)), dma((14,)), dma((2,)), dma((LATE,)),
        ],
        compiler_params=params(collective_id=2, has_side_effects=True),
        cost_estimate=pl.CostEstimate(
            flops=CHAIN * count * width * (16 * width + 16 * count),
            bytes_accessed=45 * 1024 * 1024,
            transcendentals=count * count * 4 * heads,
        ),
    )(ends, gain, keep, own, other, ps0, ps1, os0, os1, lse, *distant, result, ending)


RING = 8
SHORT_RING = 4
TILE = 256
LAGS = (0, 1, 2, 4, 6, 7, 8, 9, 10)
UP_D, DOWN_D, UP_B, DOWN_B, OUT_C, QKV_C, SOUT_C, SQKV_C, QKV_A, OUT_A = range(10)
WEIGHTS = (
    (UP_D, True, 8), (DOWN_D, False, 8), (UP_B, True, 8), (DOWN_B, False, 8), (OUT_C, False, 2),
    (QKV_C, True, 6), (SOUT_C, False, 2), (SQKV_C, True, 6), (QKV_A, True, 6), (OUT_A, False, 2),
)
STARTS = [sum(w[2] for w in WEIGHTS[:i]) for i in range(len(WEIGHTS))]
PLAIN = sum(w[2] for w in WEIGHTS)
TILES = PLAIN + 2


def grads_kernel(*refs):
    count = len(WEIGHTS)
    lefts, panels_own, panels_other = refs[:count], refs[count : 2 * count], refs[2 * count : 3 * count]
    first, small, rows_out = refs[3 * count : 3 * count + 3]
    refs = refs[3 * count + 3 :]
    outs, last_out, landed = refs[:count], refs[count], refs[count + 1]
    (
        left, panel, pair, core_in, kept1, first_in, kept2, second_in, kept3, third_in, kept4, fourth_in, result,
        left_sem, panel_sem, last_sem, core_send, core_recv, first_send, first_recv, second_send, second_recv,
        send_sem, recv_sem, piece_send, piece_recv, piece_sem,
    ) = refs[count + 2 :]
    section, tensor, group = (lax.axis_index(a) for a in (SECTION, TENSOR, DP))
    core, high = section % 2, section // 2
    near, far = group % 2, group // 2
    half, quarter = TILE // 2, TILE // 4
    other_core = {SECTION: section + 1 - 2 * core}
    near_group = {DP: group + 1 - 2 * near}
    far_group = {DP: (group + 2) % 4}
    scatter = Scatter((rows_out,), landed, piece_send, piece_recv, piece_sem)
    meet(scatter.members + [near_group, far_group])
    scatter.start()

    def remote(source, target, sems, recvs, where, partner):
        return pltpu.make_async_remote_copy(
            src_ref=source, dst_ref=target, send_sem=sems.at[where], recv_sem=recvs.at[where],
            device_id=partner, device_id_type=MESH,
        )

    def left_copy(w):
        return pltpu.make_async_copy(lefts[w], left.at[w % 3], left_sem.at[w % 3])

    left_copy(0).start()

    def panel_copies(w, k):
        slot = k % SHORT_RING
        columns = pl.ds(pl.multiple_of((k - STARTS[w]) * TILE, TILE), TILE)
        return [
            pltpu.make_async_copy(source[w].at[:, columns], panel.at[slot, j], panel_sem.at[2 * slot + j])
            for j, source in enumerate((panels_own, panels_other))
        ]

    def last_copies(which):
        slot = (PLAIN + which) % SHORT_RING
        for i in range(8):
            s, t = i // 2, i % 2
            columns = slice(s * TILE, (s + 1) * TILE)
            source = small.at[:, columns] if which else first.at[t * TILE : (t + 1) * TILE, columns]
            yield pltpu.make_async_copy(source, pair.at[slot, s % 2, s // 2, t], last_sem.at[i])

    def core_copy(k):
        slot = k % RING
        return remote(
            pair.at[k % SHORT_RING, 1 - core], core_in.at[slot], core_send, core_recv, slot, other_core
        )

    def order(k):
        turn = k % 2
        send = (
            (1 - turn) * (1 - tensor) + turn * (2 - 2 * high),
            (1 - turn) * (3 - tensor) + turn * (3 - 2 * high),
        )
        keep = (
            (1 - turn) * tensor + turn * 2 * high,
            (1 - turn) * (2 + tensor) + turn * (2 * high + 1),
        )
        return send, keep, (1 - turn) * high + turn * tensor

    def partner_of(turn):
        return {
            SECTION: section * (1 - turn) + ((section + 2) % 4) * turn,
            TENSOR: tensor + (1 - turn) * (1 - 2 * tensor),
        }

    def first_copy(k, i):
        slot = k % RING
        return remote(
            kept1.at[k % SHORT_RING, order(k)[0][i]], first_in.at[slot, i], first_send, first_recv,
            2 * slot + i, partner_of(k % 2),
        )

    def second_copy(k):
        slot = k % RING
        return remote(
            kept2.at[slot, 1 - order(k)[2]], second_in.at[slot], second_send, second_recv,
            slot, partner_of(1 - k % 2),
        )

    def third_copy(k):
        slot = k % RING
        return remote(
            kept3.at[slot, pl.ds((1 - near) * half, half)], third_in.at[slot], send_sem, recv_sem,
            slot, near_group,
        )

    def fourth_copy(k):
        slot = k % RING
        return remote(
            kept4.at[slot, pl.ds((1 - far) * quarter, quarter)], fourth_in.at[slot], send_sem, recv_sem,
            RING + slot, far_group,
        )

    def back_far(k):
        rows = pl.ds(near * half + far * quarter, quarter)
        return remote(
            result.at[k, rows], result.at[k, rows], send_sem, recv_sem, 2 * RING + k % RING, far_group
        )

    def back_near(k):
        rows = pl.ds(near * half, half)
        return remote(
            result.at[k, rows], result.at[k, rows], send_sem, recv_sem, 3 * RING + k % RING, near_group
        )

    def add(a, b):
        return bf(a.astype(jnp.float32) + b.astype(jnp.float32))

    def fetch(k):
        for w in range(count):

            @pl.when((k >= STARTS[w]) & (k < STARTS[w] + WEIGHTS[w][2]))
            def _():
                for copy in panel_copies(w, k):
                    copy.start()

            if w + 1 < count:

                @pl.when(k == STARTS[w])
                def _():
                    left_copy(w + 1).start()

    def multiply(k):
        slot = k % SHORT_RING

        @pl.when(k < PLAIN)
        def _():
            at = 0
            for w in range(count):
                if w:
                    at = at + jnp.where(k >= STARTS[w], 1, 0)

                @pl.when(k == STARTS[w])
                def _():
                    left_copy(w).wait()

            for j, place in enumerate((tensor, 1 - tensor)):
                pltpu.make_async_copy(
                    panels_own[0].at[:, :TILE], panel.at[slot, j], panel_sem.at[2 * slot + j]
                ).wait()
                product = bf(tn(panel[slot, j], left[at % 3]))
                for s in range(4):
                    pair[slot, s % 2, s // 2, place] = product[:, s * TILE : (s + 1) * TILE]

        for which in range(2):

            @pl.when(k == PLAIN + which)
            def _():
                for copy in last_copies(which):
                    copy.start()
                for copy in last_copies(which):
                    copy.wait()

        core_copy(k).start()

    def over_cores(k):
        core_copy(k).wait()
        for i in range(4):
            kept1[k % SHORT_RING, i] = add(
                pair[k % SHORT_RING, core, i // 2, i % 2], core_in[k % RING, i // 2, i % 2]
            )
        for i in range(2):
            first_copy(k, i).start()

    def over_first(k):
        slot = k % RING
        for i in range(2):
            first_copy(k, i).wait()
        for i in range(2):
            kept2[slot, i] = add(kept1[k % SHORT_RING, order(k)[1][i]], first_in[slot, i])
        second_copy(k).start()

    def over_second(k):
        slot = k % RING
        second_copy(k).wait()
        kept3[slot] = add(kept2[slot, order(k)[2]], second_in[slot])
        third_copy(k).start()

    def over_near(k):
        slot = k % RING
        third_copy(k).wait()
        kept4[slot] = add(kept3[slot, pl.ds(near * half, half)], third_in[slot])
        fourth_copy(k).start()

    def over_far(k):
        slot = k % RING
        fourth_copy(k).wait()
        result[k, pl.ds(near * half + far * quarter, quarter)] = add(
            kept4[slot, pl.ds(far * quarter, quarter)], fourth_in[slot]
        )
        back_far(k).start()

    def from_far(k):
        back_far(k).wait()
        back_near(k).start()

    def from_near(k):
        back_near(k).wait()
        for w in range(count):

            @pl.when((k >= STARTS[w]) & (k < STARTS[w] + WEIGHTS[w][2]))
            def _():
                at = pl.ds(pl.multiple_of((k - STARTS[w]) * TILE, TILE), TILE)
                if WEIGHTS[w][1]:
                    outs[w][:, at] = bf(result[k].astype(jnp.float32).T)
                else:
                    outs[w][at, :] = result[k]

        @pl.when(k >= PLAIN)
        def _():
            last_out[k - PLAIN] = result[k]

    stages = (
        fetch, multiply, over_cores, over_first, over_second, over_near, over_far, from_far, from_near
    )

    def step(i, nothing):
        for stage, lag in zip(stages, LAGS):
            k = i - lag

            @pl.when((k >= 0) & (k < TILES))
            def _():
                stage(k)

        return nothing

    lax.fori_loop(0, TILES + LAGS[-1], step, 0)
    scatter.wait()


def weight_grads(operands, first, small, rows_out):
    bf16 = jnp.bfloat16
    dma = pltpu.SemaphoreType.DMA
    anywhere, vmem = pl.BlockSpec(memory_space=pl.ANY), pl.BlockSpec(memory_space=pltpu.VMEM)
    count = len(WEIGHTS)
    rows, width = operands[WEIGHTS[0][0]][0].shape
    shapes = [(TILE, n * TILE) if by_rows else (n * TILE, TILE) for _, by_rows, n in WEIGHTS]
    shapes += [(2, TILE, TILE)]
    results = pl.pallas_call(
        grads_kernel,
        in_specs=[anywhere] * (3 * count + 3),
        out_specs=[vmem] * (count + 1) + [anywhere],
        out_shape=[jax.ShapeDtypeStruct(s, bf16) for s in shapes + [(1, 8, TILE, TILE)]],
        scratch_shapes=[
            pltpu.VMEM((3, rows, width), bf16),
            pltpu.VMEM((SHORT_RING, 2, rows, TILE), bf16),
            pltpu.VMEM((SHORT_RING, 2, 2, 2, TILE, TILE), bf16),
            pltpu.VMEM((RING, 2, 2, TILE, TILE), bf16),
            pltpu.VMEM((SHORT_RING, 4, TILE, TILE), bf16),
            pltpu.VMEM((RING, 2, TILE, TILE), bf16),
            pltpu.VMEM((RING, 2, TILE, TILE), bf16),
            pltpu.VMEM((RING, TILE, TILE), bf16),
            pltpu.VMEM((RING, TILE, TILE), bf16),
            pltpu.VMEM((RING, TILE // 2, TILE), bf16),
            pltpu.VMEM((RING, TILE // 2, TILE), bf16),
            pltpu.VMEM((RING, TILE // 4, TILE), bf16),
            pltpu.VMEM((TILES, TILE, TILE), bf16),
            dma((3,)), dma((2 * SHORT_RING,)), dma((8,)),
            dma((RING,)), dma((RING,)),
            dma((2 * RING,)), dma((2 * RING,)), dma((RING,)), dma((RING,)),
            dma((4 * RING,)), dma((4 * RING,)), dma((7,)), dma((7,)), dma((1,)),
        ],
        compiler_params=params(collective_id=3, has_side_effects=True),
        cost_estimate=pl.CostEstimate(
            flops=2 * 8 * TILES * TILE * TILE * rows,
            bytes_accessed=40 * TILES * TILE * TILE,
            transcendentals=0,
        ),
    )(*(operands[w[0]][i] for i in range(3) for w in WEIGHTS), first, small, rows_out)
    shares = {w[0]: r for w, r in zip(WEIGHTS, results)}
    return shares, results[count], results[count + 1]


def gelu_back(values, grad):
    return jax.vjp(smooth, values)[1](grad)[0]


def block_body(
    layer_input, output_grad, seg_blocks, seg_group, gain_a, wqkv_a, wout_a, gain_b, up_b, down_b,
    gain_c, gain_s, wqkv_c, sqkv_c, wout_c, sout_c, gate_bias, init_states, gain_d, up_d, down_d,
):
    sections, tensors = lax.axis_size(SECTION), lax.axis_size(TENSOR)
    block_count, shard_rows, width = layer_input.shape[1:]
    rows = shard_rows * tensors
    section, tensor = lax.axis_index(SECTION), lax.axis_index(TENSOR)
    block = block_of(section, tensor)
    begins, closes, lively, numbers = layout(
        seg_blocks, seg_group, lax.axis_index(DP), block_count
    )
    alive = lively[block]
    starts = begins[block] | jnp.logical_not(alive)
    ends = closes[block] | jnp.logical_not(alive)
    opening = starts.astype(jnp.int32)[None]
    f32 = jnp.float32
    ga, gb, gc, gd = (v.astype(f32) for v in (gain_a, gain_b, gain_c, gain_d))

    def in_order(own, other):
        low = jnp.where(tensor == 0, own, other)
        high = jnp.where(tensor == 0, other, own)
        return low, high

    def other_half(weight):
        size = weight.shape[0] // sections
        piece = lax.dynamic_slice_in_dim(weight, section * size, size, 0)
        landed = lax.ppermute(piece, TENSOR, SWAP)
        return lax.all_gather(landed, SECTION, axis=0, tiled=True)

    def flat(weight):
        return jnp.concatenate([weight[:, i] for i in range(3)], axis=1)

    wqkv_a0, wqkv_c0, sqkv_c0 = flat(wqkv_a), flat(wqkv_c), flat(sqkv_c)
    (tokens, before, initial), others = gather(
        layer_input, init_states,
        (wqkv_a0, wout_a, up_b, down_b, wqkv_c0, sqkv_c0, sout_c, wout_c),
    )
    wqkv_a1, wout_a1, up_b1, down_b1, wqkv_c1, sqkv_c1, sout_c1, wout_c1 = others
    tokens, late_up, late_down = lax.optimization_barrier((tokens, up_d, down_d))
    up_d1, down_d1 = other_half(late_up), other_half(late_down)
    initial = initial.astype(f32)

    def normed(values, gain):
        return bf(values * inverse_rms(values) * gain)

    def dot(a, b):
        return jnp.dot(a, b, preferred_element_type=f32)

    def dot_t(a, b):
        return lax.dot_general(a, b, (((1,), (1,)), ((), ())), preferred_element_type=f32)

    half = wout_a.shape[0]
    r0 = tokens.astype(f32)
    h0 = normed(r0, ga)
    h_before = normed(before.astype(f32), ga)
    pa0, pa1 = bf(dot(h0, wqkv_a0)), bf(dot(h0, wqkv_a1))
    prior_a0 = bf(dot(h_before, wqkv_a0[:, half:]))
    prior_a1 = bf(dot(h_before, wqkv_a1[:, half:]))
    oa0, lse_a0 = attend(opening, pa0, prior_a0)
    oa1, lse_a1 = attend(opening, pa1, prior_a1)
    r1 = r0 + (dot(oa0, wout_a) + dot(oa1, wout_a1))

    h1 = normed(r1, gb)
    ub0, ub1 = dot(h1, up_b), dot(h1, up_b1)
    ab0, ab1 = bf(smooth(ub0)), bf(smooth(ub1))
    r2 = r1 + (dot(ab0, down_b) + dot(ab1, down_b1))

    h2 = normed(r2, gc)
    pc0, pc1 = bf(dot(h2, wqkv_c0)), bf(dot(h2, wqkv_c1))
    halo = lax.ppermute(jnp.stack(in_order(pc0[:, half:], pc1[:, half:])), GROUP, TO_NEXT)
    prior_c0, prior_c1 = in_order(halo[0], halo[1])

    retain = jax.nn.sigmoid(gate_bias.astype(f32))[None, :]
    state_gain = gain_s.astype(f32)[None, :]

    def flag(value):
        return jnp.broadcast_to(value.astype(f32), (1, width))

    (
        state_in, hs, ps0, ps1, os0, os1, lse_s, update, state_new, cotangent
    ) = chain(
        initial, flag(starts), state_gain, retain, pc0, pc1,
        sqkv_c0, sqkv_c1, sout_c, sout_c1, output_grad,
    )
    oc0, lse_c0 = attend(opening, pc0, prior_c0, ps0)
    oc1, lse_c1 = attend(opening, pc1, prior_c1, ps1)
    r3 = r2 + (dot(oc0, wout_c) + dot(oc1, wout_c1))

    h3 = normed(r3, gd)
    ud0, ud1 = dot(h3, up_d), dot(h3, up_d1)
    ad0, ad1 = bf(smooth(ud0)), bf(smooth(ud1))
    r4 = r3 + (dot(ad0, down_d) + dot(ad1, down_d1))
    result = bf(jnp.where(alive, r4, 0.0))

    def feed_back(up_name, down_name, grad, values, h, gain, u0, u1, a0, a1, up0, up1, down0, down1):
        gy = bf(grad)
        g0 = bf(gelu_back(u0, dot_t(gy, down0)))
        g1 = bf(gelu_back(u1, dot_t(gy, down1)))
        operands[down_name] = (gy, a0, a1)
        operands[up_name] = (h, g0, g1)
        through = dot_t(g0, up0) + dot_t(g1, up1)
        back, gain_grad = norm_back(values, gain, through)
        return grad + back, gain_grad

    operands = {}
    grad4 = jnp.where(alive, cotangent.astype(f32), 0.0)
    grad3, gain_d_grad = feed_back(
        UP_D, DOWN_D, grad4, r3, h3, gd, ud0, ud1, ad0, ad1, up_d, up_d1, down_d, down_d1
    )
    gy3 = bf(grad3)
    tok0 = attend_back(opening, pc0, prior_c0, bf(dot_t(gy3, wout_c)), oc0, lse_c0, ps0)
    tok1 = attend_back(opening, pc1, prior_c1, bf(dot_t(gy3, wout_c1)), oc1, lse_c1, ps1)

    def halo_back(one, two):
        pair = in_order(
            jnp.concatenate([one[3], one[4]], axis=1), jnp.concatenate([two[3], two[4]], axis=1)
        )
        back = lax.ppermute(jnp.stack(pair), GROUP, TO_PRIOR).astype(f32)
        return in_order(back[0], back[1])

    halo_c0, halo_c1 = halo_back(tok0, tok1)
    grad_state, gs0, gs1, gtok0, gtok1, gup, small, landed = chain_back(
        flag(ends), state_in, update, state_gain, retain, pc0, pc1, ps0, ps1, os0, os1, lse_s,
        tok0[5], tok0[6], tok1[5], tok1[6], sqkv_c0, sqkv_c1, sout_c, sout_c1, result, bf(state_new),
    )

    def projected_back(parts, halo_part, extra=None):
        pair = jnp.concatenate([parts[1], parts[2]], axis=1) + halo_part
        if extra is not None:
            pair = pair + extra
        return jnp.concatenate([parts[0], bf(pair)], axis=1)

    gc0 = projected_back(tok0, halo_c0, gtok0)
    gc1 = projected_back(tok1, halo_c1, gtok1)
    operands[QKV_C] = (h2, gc0, gc1)
    operands[SQKV_C] = (hs, gs0, gs1)
    operands[OUT_C] = (gy3, oc0, oc1)
    operands[SOUT_C] = (gup, os0, os1)
    first_grad = bf(jnp.where(begins[block], grad_state, 0.0))
    def through_qkv(g, w):
        return dot_t(g, w)

    back_c, gain_c_grad = norm_back(
        r2, gc, through_qkv(gc0, wqkv_c0) + through_qkv(gc1, wqkv_c1)
    )
    grad2 = grad3 + back_c

    grad1, gain_b_grad = feed_back(
        UP_B, DOWN_B, grad2, r1, h1, gb, ub0, ub1, ab0, ab1, up_b, up_b1, down_b, down_b1
    )

    gy1 = bf(grad1)
    att0 = attend_back(opening, pa0, prior_a0, bf(dot_t(gy1, wout_a)), oa0, lse_a0)
    att1 = attend_back(opening, pa1, prior_a1, bf(dot_t(gy1, wout_a1)), oa1, lse_a1)
    halo_a0, halo_a1 = halo_back(att0, att1)
    ga0, ga1 = projected_back(att0, halo_a0), projected_back(att1, halo_a1)
    operands[QKV_A] = (h0, ga0, ga1)
    operands[OUT_A] = (gy1, oa0, oa1)
    back_a, gain_a_grad = norm_back(
        r0, ga, through_qkv(ga0, wqkv_a0) + through_qkv(ga1, wqkv_a1)
    )
    smalls = jnp.stack(
        [gain_a_grad, gain_b_grad, gain_c_grad, small[0], gain_d_grad, small[1]]
    )
    shares, last_share, landed_input = weight_grads(
        operands, first_grad, jnp.pad(bf(smalls), ((0, TILE - 6), (0, 0))), bf(grad1 + back_a)
    )
    small_share = last_share[1].astype(f32)
    chosen = (
        (numbers[:, None] == jnp.arange(SLOTS, dtype=jnp.int32)[None, :])
        & (closes & lively)[:, None]
    )
    state_tiles = landed[1].astype(f32)
    final_share = jnp.stack(
        [
            jnp.sum(jnp.where(chosen[:, i, None, None], state_tiles, 0.0), axis=0)
            for i in range(SLOTS)
        ],
        axis=1,
    )

    def share(name):
        value = shares[name].astype(f32)
        return value.reshape(value.shape[0], 3, -1) if name in (QKV_A, QKV_C, SQKV_C) else value

    return (
        landed[0][None],
        final_share[None],
        landed_input.astype(f32),
        small_share[0],
        share(QKV_A),
        share(OUT_A),
        small_share[1],
        share(UP_B),
        share(DOWN_B),
        small_share[2],
        small_share[3],
        share(QKV_C),
        share(SQKV_C),
        share(OUT_C),
        share(SOUT_C),
        small_share[5],
        last_share[0].astype(f32),
        small_share[4],
        share(UP_D),
        share(DOWN_D),
    )


def chosen(*arrays):
    devices = (lax.axis_size(SECTION), lax.axis_size(TENSOR), lax.axis_size(DP))
    if devices == (4, 2, 4) and arrays[0].shape[1] == 8:
        return block_body(*arrays)
    return relay_body(*arrays)


def solution(mesh):
    in_specs = (
        P(DP, None, TENSOR, None),
        P(DP, None, TENSOR, None),
        P(),
        P(),
        P(),
        P(None, None, TENSOR),
        P(TENSOR, None),
        P(),
        P(None, TENSOR),
        P(TENSOR, None),
        P(),
        P(),
        P(None, None, TENSOR),
        P(None, None, TENSOR),
        P(TENSOR, None),
        P(TENSOR, None),
        P(),
        P(TENSOR, None),
        P(),
        P(None, TENSOR),
        P(TENSOR, None),
    )
    out_specs = (
        P(DP, None, TENSOR, SECTION),
        P(DP, TENSOR, None, SECTION),
        P(DP, None, TENSOR, SECTION),
        P(SECTION),
        P(SECTION, None, TENSOR),
        P(TENSOR, SECTION),
        P(SECTION),
        P(SECTION, TENSOR),
        P(TENSOR, SECTION),
        P(SECTION),
        P(SECTION),
        P(SECTION, None, TENSOR),
        P(SECTION, None, TENSOR),
        P(TENSOR, SECTION),
        P(TENSOR, SECTION),
        P(SECTION),
        P(TENSOR, SECTION),
        P(SECTION),
        P(SECTION, TENSOR),
        P(TENSOR, SECTION),
    )
    return jax.shard_map(chosen, mesh=mesh, in_specs=in_specs, out_specs=out_specs, check_vma=False)
```

```python
import functools
import math

import jax
import jax.numpy as jnp
from jax import lax
from jax.experimental import pallas as pl
from jax.experimental.pallas import tpu as pltpu
from jax.sharding import PartitionSpec as P

SECTION, DP, TENSOR = "section", "dp", "tensor"
HEAD_DIM = 128
SLOTS = 3


EPSILON = 1e-06
NEGATIVE = -1e30


def shifted(value, axis, by):
    devices = lax.axis_size(axis)
    pairs = [(i, i + by) for i in range(devices) if 0 <= i + by < devices]
    return lax.ppermute(value, axis, pairs)


def for_sending(value):
    return jax.tree.map(lambda a: a.astype(jnp.bfloat16) if a.dtype == jnp.float32 else a, value)


def layout(seg_blocks, seg_group, group_index, block_count):
    mine = seg_group == group_index
    lengths = jnp.where(mine, seg_blocks, 0)
    offsets = jnp.cumsum(lengths) - lengths
    ranking = jnp.cumsum(mine.astype(jnp.int32)) - mine.astype(jnp.int32)
    blocks = jnp.arange(block_count, dtype=jnp.int32)[None, :]
    inside = mine[:, None] & (blocks >= offsets[:, None]) & (blocks < (offsets + lengths)[:, None])
    begins = jnp.any(inside & (blocks == offsets[:, None]), axis=0)
    closes = jnp.any(inside & (blocks == (offsets + lengths - 1)[:, None]), axis=0)
    lively = jnp.any(inside, axis=0)
    numbers = jnp.sum(jnp.where(inside, ranking[:, None], 0), axis=0)
    return (begins, closes, lively, numbers)


def inverse_rms(values):
    return lax.rsqrt(jnp.mean(values * values, axis=-1, keepdims=True) + EPSILON)


def norm_back(values, gain, grad_normed):
    factor = inverse_rms(values)
    scaled = values * factor
    grad_scaled = grad_normed * gain
    grad_values = factor * (
        grad_scaled - scaled * jnp.mean(grad_scaled * scaled, axis=-1, keepdims=True)
    )
    return (grad_values, jnp.sum(grad_normed * scaled, axis=0))


def smooth(values):
    return jax.nn.gelu(values, approximate=True)


def split_heads(rows_in):
    return rows_in.reshape(rows_in.shape[0], -1, HEAD_DIM)


def attend_forward(queries, key_rows, value_rows, allowed):
    score_scale = 1.0 / math.sqrt(HEAD_DIM)
    scores = (
        jnp.einsum("rhd,khd->hrk", queries, key_rows, preferred_element_type=jnp.float32)
        * score_scale
    )
    scores = jnp.where(allowed[None], scores, NEGATIVE)
    largest = jnp.max(scores, axis=-1, keepdims=True)
    totals = jnp.sum(jnp.exp(scores - largest), axis=-1, keepdims=True)
    log_total = largest + jnp.log(totals)
    weights = jnp.exp(scores - log_total).astype(jnp.bfloat16)
    mixture_output = jnp.einsum(
        "hrk,khd->rhd", weights, value_rows, preferred_element_type=jnp.float32
    )
    return (mixture_output, log_total[..., 0])


def attend_backward(queries, key_rows, value_rows, allowed, log_total, grad_mixture):
    score_scale = 1.0 / math.sqrt(HEAD_DIM)
    scores = (
        jnp.einsum("rhd,khd->hrk", queries, key_rows, preferred_element_type=jnp.float32)
        * score_scale
    )
    scores = jnp.where(allowed[None], scores, NEGATIVE)
    weights = jnp.exp(scores - log_total[..., None])
    rounded = weights.astype(jnp.bfloat16)
    grad_weights = jnp.einsum(
        "rhd,khd->hrk", grad_mixture, value_rows, preferred_element_type=jnp.float32
    )
    grad_values = jnp.einsum(
        "hrk,rhd->khd", rounded, grad_mixture, preferred_element_type=jnp.float32
    )
    inner_sum = jnp.sum(weights * grad_weights, axis=-1, keepdims=True)
    grad_scores = (weights * (grad_weights - inner_sum)).astype(jnp.bfloat16)
    grad_queries = (
        jnp.einsum("hrk,khd->rhd", grad_scores, key_rows, preferred_element_type=jnp.float32)
        * score_scale
    )
    grad_keys = (
        jnp.einsum("hrk,rhd->khd", grad_scores, queries, preferred_element_type=jnp.float32)
        * score_scale
    )
    return (grad_queries, grad_keys, grad_values)


def place_row(store, position, value, active_tick):
    previous = lax.dynamic_index_in_dim(store, position, 0, False)
    return lax.dynamic_update_index_in_dim(
        store, jnp.where(active_tick, value, previous), position, 0
    )


def renewed(grad_sums, active_tick, changes):
    return tuple(
        (
            total + jnp.where(active_tick, changes[position], 0.0) if position in changes else total
            for position, total in enumerate(grad_sums)
        )
    )


def relay_body(
    layer_input,
    output_grad,
    seg_blocks,
    seg_group,
    gain_a,
    wqkv_a,
    wout_a,
    gain_b,
    up_b,
    down_b,
    gain_c,
    gain_s,
    wqkv_c,
    sqkv_c,
    wout_c,
    sout_c,
    gate_bias,
    init_states,
    gain_d,
    up_d,
    down_d,
):
    block_count = layer_input.shape[1]
    shard_rows = layer_input.shape[2]
    model_width = layer_input.shape[3]
    tensor_count = lax.axis_size(TENSOR)
    token_rows = shard_rows * tensor_count
    state_shard = init_states.shape[0]
    state_count = state_shard * tensor_count
    local_width = wqkv_a.shape[2]
    local_heads = local_width // HEAD_DIM
    section_index = lax.axis_index(SECTION)
    group_index = lax.axis_index(DP)
    on_cell_section = section_index == 2
    begins, closes, lively, numbers = layout(seg_blocks, seg_group, group_index, block_count)
    token_gains = jnp.stack([gain_a, gain_b, gain_c, gain_d]).astype(jnp.float32)
    state_gain = gain_s.astype(jnp.float32)
    retain = jax.nn.sigmoid(gate_bias.astype(jnp.float32))
    initial = init_states.astype(jnp.float32)
    empty_state = jnp.zeros((state_count, model_width), jnp.float32)
    empty_token_store = jnp.zeros((token_rows, 4, local_width), jnp.bfloat16)
    empty_state_store = jnp.zeros((state_count, 4, local_width), jnp.bfloat16)
    empty_token_lse = jnp.zeros((local_heads, token_rows), jnp.float32)
    empty_state_lse = jnp.zeros((local_heads, state_count), jnp.float32)
    empty_carry = jnp.zeros((token_rows, local_width), jnp.float32)
    every_key = jnp.ones((state_count, token_rows + state_count), bool)
    state_keys_all = jnp.ones((token_rows, state_count), bool)

    def token_masks(opening):
        later_keys = lax.broadcasted_iota(
            jnp.int32, (token_rows, token_rows), 1
        ) > lax.broadcasted_iota(jnp.int32, (token_rows, token_rows), 0)
        return (jnp.logical_and(later_keys, jnp.logical_not(opening)), jnp.logical_not(later_keys))

    def plain_forward(normed_tok, normed_st, prior_block, opening):
        projected = jnp.einsum(
            "rd,dcn->rcn", normed_tok, wqkv_a, preferred_element_type=jnp.float32
        ).astype(jnp.bfloat16)
        reach_prior, reach_current = token_masks(opening)
        allowed = jnp.concatenate([reach_prior, reach_current], axis=1)
        key_rows = jnp.concatenate([prior_block[:, 1], projected[:, 1]], axis=0)
        value_rows = jnp.concatenate([prior_block[:, 2], projected[:, 2]], axis=0)
        mixture_output, token_lse = attend_forward(
            split_heads(projected[:, 0]), split_heads(key_rows), split_heads(value_rows), allowed
        )
        mixture_output = mixture_output.reshape(token_rows, local_width).astype(jnp.bfloat16)
        branch = jnp.dot(mixture_output, wout_a, preferred_element_type=jnp.float32)
        stored = jnp.concatenate([projected, mixture_output[:, None]], axis=1)
        return (branch, empty_state, stored, empty_state_store, token_lse, empty_state_lse)

    def feed_forward(up_projection_weight, down_projection_weight):

        def forward_fn(normed_tok, normed_st, prior_block, opening):
            hidden_rows = jnp.dot(
                normed_tok, up_projection_weight, preferred_element_type=jnp.float32
            )
            active_flags = smooth(hidden_rows).astype(jnp.bfloat16)
            branch = jnp.dot(
                active_flags, down_projection_weight, preferred_element_type=jnp.float32
            )
            return (
                branch,
                empty_state,
                empty_token_store,
                empty_state_store,
                empty_token_lse,
                empty_state_lse,
            )

        return forward_fn

    def recurrent_forward(normed_tok, normed_st, prior_block, opening):
        projected = jnp.einsum(
            "rd,dcn->rcn", normed_tok, wqkv_c, preferred_element_type=jnp.float32
        ).astype(jnp.bfloat16)
        state_proj = jnp.einsum(
            "sd,dcn->scn", normed_st, sqkv_c, preferred_element_type=jnp.float32
        ).astype(jnp.bfloat16)
        reach_prior, reach_current = token_masks(opening)
        allowed = jnp.concatenate([reach_prior, reach_current, state_keys_all], axis=1)
        token_keys = jnp.concatenate([prior_block[:, 1], projected[:, 1], state_proj[:, 1]], axis=0)
        token_values = jnp.concatenate(
            [prior_block[:, 2], projected[:, 2], state_proj[:, 2]], axis=0
        )
        token_mixture, token_lse = attend_forward(
            split_heads(projected[:, 0]),
            split_heads(token_keys),
            split_heads(token_values),
            allowed,
        )
        state_keys = jnp.concatenate([projected[:, 1], state_proj[:, 1]], axis=0)
        state_values = jnp.concatenate([projected[:, 2], state_proj[:, 2]], axis=0)
        state_mixture, state_lse = attend_forward(
            split_heads(state_proj[:, 0]),
            split_heads(state_keys),
            split_heads(state_values),
            every_key,
        )
        token_mixture = token_mixture.reshape(token_rows, local_width).astype(jnp.bfloat16)
        state_mixture = state_mixture.reshape(state_count, local_width).astype(jnp.bfloat16)
        branch = jnp.dot(token_mixture, wout_c, preferred_element_type=jnp.float32)
        update_term = jnp.dot(state_mixture, sout_c, preferred_element_type=jnp.float32)
        stored = jnp.concatenate([projected, token_mixture[:, None]], axis=1)
        state_stored = jnp.concatenate([state_proj, state_mixture[:, None]], axis=1)
        return (branch, update_term, stored, state_stored, token_lse, state_lse)

    def plain_backward(
        grad_tok,
        grad_st,
        normed_tok,
        normed_st,
        tok_block,
        st_block,
        prior_block,
        token_lse,
        state_lse,
        opening,
        carry_keys,
        carry_values,
        grad_sums,
        active_tick,
    ):
        reach_prior, reach_current = token_masks(opening)
        allowed = jnp.concatenate([reach_prior, reach_current], axis=1)
        key_rows = jnp.concatenate([prior_block[:, 1], tok_block[:, 1]], axis=0)
        value_rows = jnp.concatenate([prior_block[:, 2], tok_block[:, 2]], axis=0)
        weight_out = jnp.einsum(
            "rn,rd->nd", tok_block[:, 3], grad_tok, preferred_element_type=jnp.float32
        )
        grad_mixture = jnp.einsum(
            "rd,nd->rn", grad_tok, wout_a, preferred_element_type=jnp.float32
        ).astype(jnp.bfloat16)
        grad_query, grad_keys, grad_values = attend_backward(
            split_heads(tok_block[:, 0]),
            split_heads(key_rows),
            split_heads(value_rows),
            allowed,
            token_lse,
            split_heads(grad_mixture),
        )
        grad_query = grad_query.reshape(token_rows, local_width)
        grad_keys = grad_keys.reshape(2 * token_rows, local_width)
        grad_values = grad_values.reshape(2 * token_rows, local_width)
        grad_proj = jnp.stack(
            [
                grad_query,
                grad_keys[token_rows:] + carry_keys,
                grad_values[token_rows:] + carry_values,
            ],
            axis=1,
        ).astype(jnp.bfloat16)
        weight_in = jnp.einsum(
            "rd,rcn->dcn", normed_tok, grad_proj, preferred_element_type=jnp.float32
        )
        grad_normed = jnp.einsum(
            "rcn,dcn->rd", grad_proj, wqkv_a, preferred_element_type=jnp.float32
        )
        return (
            grad_normed,
            empty_state,
            grad_keys[:token_rows],
            grad_values[:token_rows],
            renewed(grad_sums, active_tick, {0: weight_in, 1: weight_out}),
        )

    def feed_backward(up_projection_weight, down_projection_weight, up_slot, down_slot):

        def backward_fn(
            grad_tok,
            grad_st,
            normed_tok,
            normed_st,
            tok_block,
            st_block,
            prior_block,
            token_lse,
            state_lse,
            opening,
            carry_keys,
            carry_values,
            grad_sums,
            active_tick,
        ):
            hidden_rows = jnp.dot(
                normed_tok, up_projection_weight, preferred_element_type=jnp.float32
            )
            active_flags, gelu_back = jax.vjp(smooth, hidden_rows)
            weight_down = jnp.einsum(
                "rf,rd->fd",
                active_flags.astype(jnp.bfloat16),
                grad_tok,
                preferred_element_type=jnp.float32,
            )
            grad_active = jnp.einsum(
                "rd,fd->rf", grad_tok, down_projection_weight, preferred_element_type=jnp.float32
            )
            grad_hidden = gelu_back(grad_active)[0].astype(jnp.bfloat16)
            weight_up = jnp.einsum(
                "rd,rf->df", normed_tok, grad_hidden, preferred_element_type=jnp.float32
            )
            grad_normed = jnp.einsum(
                "rf,df->rd", grad_hidden, up_projection_weight, preferred_element_type=jnp.float32
            )
            return (
                grad_normed,
                empty_state,
                empty_carry,
                empty_carry,
                renewed(grad_sums, active_tick, {up_slot: weight_up, down_slot: weight_down}),
            )

        return backward_fn

    def recurrent_backward(
        grad_tok,
        grad_st,
        normed_tok,
        normed_st,
        tok_block,
        st_block,
        prior_block,
        token_lse,
        state_lse,
        opening,
        carry_keys,
        carry_values,
        grad_sums,
        active_tick,
    ):
        reach_prior, reach_current = token_masks(opening)
        allowed = jnp.concatenate([reach_prior, reach_current, state_keys_all], axis=1)
        token_keys = jnp.concatenate([prior_block[:, 1], tok_block[:, 1], st_block[:, 1]], axis=0)
        token_values = jnp.concatenate([prior_block[:, 2], tok_block[:, 2], st_block[:, 2]], axis=0)
        state_keys = jnp.concatenate([tok_block[:, 1], st_block[:, 1]], axis=0)
        state_values = jnp.concatenate([tok_block[:, 2], st_block[:, 2]], axis=0)
        weight_out = jnp.einsum(
            "rn,rd->nd", tok_block[:, 3], grad_tok, preferred_element_type=jnp.float32
        )
        weight_state_out = jnp.einsum(
            "sn,sd->nd", st_block[:, 3], grad_st, preferred_element_type=jnp.float32
        )
        grad_token_mixture = jnp.einsum(
            "rd,nd->rn", grad_tok, wout_c, preferred_element_type=jnp.float32
        ).astype(jnp.bfloat16)
        grad_state_mixture = jnp.einsum(
            "sd,nd->sn", grad_st, sout_c, preferred_element_type=jnp.float32
        ).astype(jnp.bfloat16)
        grad_query, grad_keys, grad_values = attend_backward(
            split_heads(tok_block[:, 0]),
            split_heads(token_keys),
            split_heads(token_values),
            allowed,
            token_lse,
            split_heads(grad_token_mixture),
        )
        state_query, state_grad_keys, state_grad_values = attend_backward(
            split_heads(st_block[:, 0]),
            split_heads(state_keys),
            split_heads(state_values),
            every_key,
            state_lse,
            split_heads(grad_state_mixture),
        )
        grad_query = grad_query.reshape(token_rows, local_width)
        grad_keys = grad_keys.reshape(2 * token_rows + state_count, local_width)
        grad_values = grad_values.reshape(2 * token_rows + state_count, local_width)
        state_query = state_query.reshape(state_count, local_width)
        state_grad_keys = state_grad_keys.reshape(token_rows + state_count, local_width)
        state_grad_values = state_grad_values.reshape(token_rows + state_count, local_width)
        own_keys = (
            grad_keys[token_rows : 2 * token_rows] + state_grad_keys[:token_rows] + carry_keys
        )
        own_values = (
            grad_values[token_rows : 2 * token_rows] + state_grad_values[:token_rows] + carry_values
        )
        cell_keys = grad_keys[2 * token_rows :] + state_grad_keys[token_rows:]
        cell_values = grad_values[2 * token_rows :] + state_grad_values[token_rows:]
        grad_proj = jnp.stack([grad_query, own_keys, own_values], axis=1).astype(jnp.bfloat16)
        grad_state_proj = jnp.stack([state_query, cell_keys, cell_values], axis=1).astype(
            jnp.bfloat16
        )
        weight_in = jnp.einsum(
            "rd,rcn->dcn", normed_tok, grad_proj, preferred_element_type=jnp.float32
        )
        weight_state_in = jnp.einsum(
            "sd,scn->dcn", normed_st, grad_state_proj, preferred_element_type=jnp.float32
        )
        grad_normed = jnp.einsum(
            "rcn,dcn->rd", grad_proj, wqkv_c, preferred_element_type=jnp.float32
        )
        grad_state_normed = jnp.einsum(
            "scn,dcn->sd", grad_state_proj, sqkv_c, preferred_element_type=jnp.float32
        )
        changes = {4: weight_in, 5: weight_state_in, 6: weight_out, 7: weight_state_out}
        return (
            grad_normed,
            grad_state_normed,
            grad_keys[:token_rows],
            grad_values[:token_rows],
            renewed(grad_sums, active_tick, changes),
        )

    forward_branches = [
        plain_forward,
        feed_forward(up_b, down_b),
        recurrent_forward,
        feed_forward(up_d, down_d),
    ]
    backward_branches = [
        plain_backward,
        feed_backward(up_b, down_b, 2, 3),
        recurrent_backward,
        feed_backward(up_d, down_d, 8, 9),
    ]

    def forward_tick(tick_number, carried):
        (
            received,
            state_carry,
            tok_normed,
            st_normed,
            tok_stored,
            st_stored,
            tok_lse_all,
            st_lse_all,
            entered,
            state_entered,
            updates,
            leaving_rows,
            finals,
        ) = carried
        block_number = tick_number - section_index
        active_tick = (block_number >= 0) & (block_number < block_count)
        block_index = jnp.clip(block_number, 0, block_count - 1)
        opening = begins[block_index]
        entering = jnp.where(
            section_index == 0, layer_input[0, block_index].astype(jnp.float32), received
        )
        state_in = jnp.where(opening, initial, state_carry)
        token_gain = token_gains[section_index]
        normed_shard = (entering * inverse_rms(entering) * token_gain).astype(jnp.bfloat16)
        state_normed_shard = (state_in * inverse_rms(state_in) * state_gain).astype(jnp.bfloat16)
        normed_tok, normed_st = (
            lax.all_gather(normed_shard, TENSOR, axis=0, tiled=True),
            lax.all_gather(state_normed_shard, TENSOR, axis=0, tiled=True),
        )
        prior_block = tok_stored[jnp.maximum(block_index - 1, 0)]
        branch, update_term, stored, state_stored, token_lse, state_lse = lax.switch(
            section_index, forward_branches, normed_tok, normed_st, prior_block, opening
        )
        branch_shard, update_shard = (
            lax.psum_scatter(
                branch.astype(jnp.bfloat16), TENSOR, scatter_dimension=0, tiled=True
            ).astype(jnp.float32),
            lax.psum_scatter(
                update_term.astype(jnp.bfloat16), TENSOR, scatter_dimension=0, tiled=True
            ).astype(jnp.float32),
        )
        leaving = entering + branch_shard
        state_new = retain * state_in + (1.0 - retain) * update_shard
        tok_normed = place_row(tok_normed, block_index, normed_tok, active_tick)
        st_normed = place_row(st_normed, block_index, normed_st, active_tick)
        tok_stored = place_row(tok_stored, block_index, stored, active_tick)
        st_stored = place_row(st_stored, block_index, state_stored, active_tick)
        tok_lse_all = place_row(tok_lse_all, block_index, token_lse, active_tick)
        st_lse_all = place_row(st_lse_all, block_index, state_lse, active_tick)
        entered = place_row(entered, block_index, entering, active_tick)
        state_entered = place_row(state_entered, block_index, state_in, active_tick)
        updates = place_row(updates, block_index, update_shard, active_tick)
        leaving_rows = place_row(leaving_rows, block_index, leaving, active_tick)
        on_cell = active_tick & on_cell_section
        state_carry = jnp.where(on_cell, state_new, state_carry)
        keep_final = on_cell & closes[block_index] & lively[block_index]
        slot_hit = (jnp.arange(SLOTS, dtype=jnp.int32) == numbers[block_index])[
            None, :, None
        ] & keep_final
        finals = jnp.where(slot_hit, state_new[:, None, :], finals)
        received = shifted(leaving.astype(jnp.bfloat16), SECTION, 1).astype(leaving.dtype)
        return (
            received,
            state_carry,
            tok_normed,
            st_normed,
            tok_stored,
            st_stored,
            tok_lse_all,
            st_lse_all,
            entered,
            state_entered,
            updates,
            leaving_rows,
            finals,
        )

    forward_start = (
        jnp.zeros((shard_rows, model_width), jnp.float32),
        jnp.zeros((state_shard, model_width), jnp.float32),
        jnp.zeros((block_count, token_rows, model_width), jnp.bfloat16),
        jnp.zeros((block_count, state_count, model_width), jnp.bfloat16),
        jnp.zeros((block_count, token_rows, 4, local_width), jnp.bfloat16),
        jnp.zeros((block_count, state_count, 4, local_width), jnp.bfloat16),
        jnp.zeros((block_count, local_heads, token_rows), jnp.float32),
        jnp.zeros((block_count, local_heads, state_count), jnp.float32),
        jnp.zeros((block_count, shard_rows, model_width), jnp.float32),
        jnp.zeros((block_count, state_shard, model_width), jnp.float32),
        jnp.zeros((block_count, state_shard, model_width), jnp.float32),
        jnp.zeros((block_count, shard_rows, model_width), jnp.float32),
        jnp.zeros((state_shard, SLOTS, model_width), jnp.float32),
    )
    (
        _,
        _,
        tok_normed,
        st_normed,
        tok_stored,
        st_stored,
        tok_lse_all,
        st_lse_all,
        entered,
        state_entered,
        updates,
        leaving_rows,
        finals,
    ) = lax.fori_loop(0, block_count + 3, forward_tick, forward_start)
    gain_rows_of_section = jnp.array([0, 1, 2, 4], dtype=jnp.int32)
    small_rows = jnp.arange(6, dtype=jnp.int32)[:, None]

    def backward_tick(tick_number, carried):
        (
            received,
            state_grad,
            carry_keys,
            carry_values,
            grad_sums,
            smalls,
            initial_grad,
            input_rows,
        ) = carried
        block_number = block_count - 1 - tick_number + 3 - section_index
        active_tick = (block_number >= 0) & (block_number < block_count)
        block_index = jnp.clip(block_number, 0, block_count - 1)
        opening = begins[block_index]
        arriving = jnp.where(
            section_index == 3,
            output_grad[0, block_index].astype(jnp.float32)
            * lively[block_index].astype(jnp.float32),
            received,
        )
        update_grad = (1.0 - retain) * state_grad
        grad_tok, grad_st = (
            lax.all_gather(arriving.astype(jnp.bfloat16), TENSOR, axis=0, tiled=True),
            lax.all_gather(update_grad.astype(jnp.bfloat16), TENSOR, axis=0, tiled=True),
        )
        grad_normed_tok, grad_normed_st, prior_keys, prior_values, grad_sums = lax.switch(
            section_index,
            backward_branches,
            grad_tok,
            grad_st,
            tok_normed[block_index],
            st_normed[block_index],
            tok_stored[block_index],
            st_stored[block_index],
            tok_stored[jnp.maximum(block_index - 1, 0)],
            tok_lse_all[block_index],
            st_lse_all[block_index],
            opening,
            carry_keys,
            carry_values,
            grad_sums,
            active_tick,
        )
        tok_shard, st_shard = (
            lax.psum_scatter(
                grad_normed_tok.astype(jnp.bfloat16), TENSOR, scatter_dimension=0, tiled=True
            ).astype(jnp.float32),
            lax.psum_scatter(
                grad_normed_st.astype(jnp.bfloat16), TENSOR, scatter_dimension=0, tiled=True
            ).astype(jnp.float32),
        )
        grad_entering, token_gain_term = norm_back(
            entered[block_index], token_gains[section_index], tok_shard
        )
        leaving_grad = arriving + grad_entering
        state_in = state_entered[block_index]
        grad_state_norm, state_gain_term = norm_back(state_in, state_gain, st_shard)
        grad_state_in = retain * state_grad + grad_state_norm
        bias_term = (
            jnp.sum(state_grad * (state_in - updates[block_index]), axis=0)
            * retain
            * (1.0 - retain)
        )
        on_cell = active_tick & on_cell_section
        gain_part = (small_rows == gain_rows_of_section[section_index]).astype(
            jnp.float32
        ) * token_gain_term[None, :]
        cell_part = (small_rows == 3).astype(jnp.float32) * state_gain_term[None, :] + (
            small_rows == 5
        ).astype(jnp.float32) * bias_term[None, :]
        smalls = (
            smalls + jnp.where(active_tick, gain_part, 0.0) + jnp.where(on_cell, cell_part, 0.0)
        )
        initial_grad = initial_grad + jnp.where(on_cell & opening, grad_state_in, 0.0)
        state_grad = jnp.where(on_cell, jnp.where(opening, 0.0, grad_state_in), state_grad)
        carry_keys = jnp.where(active_tick, prior_keys, carry_keys)
        carry_values = jnp.where(active_tick, prior_values, carry_values)
        input_rows = place_row(input_rows, block_index, leaving_grad, active_tick)
        received = shifted(for_sending(leaving_grad), SECTION, -1).astype(leaving_grad.dtype)
        return (
            received,
            state_grad,
            carry_keys,
            carry_values,
            grad_sums,
            smalls,
            initial_grad,
            input_rows,
        )

    zero_grads = (
        jnp.zeros(wqkv_a.shape, jnp.float32),
        jnp.zeros(wout_a.shape, jnp.float32),
        jnp.zeros(up_b.shape, jnp.float32),
        jnp.zeros(down_b.shape, jnp.float32),
        jnp.zeros(wqkv_c.shape, jnp.float32),
        jnp.zeros(sqkv_c.shape, jnp.float32),
        jnp.zeros(wout_c.shape, jnp.float32),
        jnp.zeros(sout_c.shape, jnp.float32),
        jnp.zeros(up_d.shape, jnp.float32),
        jnp.zeros(down_d.shape, jnp.float32),
    )
    backward_start = (
        jnp.zeros((shard_rows, model_width), jnp.float32),
        jnp.zeros((state_shard, model_width), jnp.float32),
        empty_carry,
        empty_carry,
        zero_grads,
        jnp.zeros((6, model_width), jnp.float32),
        jnp.zeros((state_shard, model_width), jnp.float32),
        jnp.zeros((block_count, shard_rows, model_width), jnp.float32),
    )
    _, _, _, _, grad_sums, smalls, initial_grad, input_rows = lax.fori_loop(
        0, block_count + 3, backward_tick, backward_start
    )
    out_term = jnp.where(
        section_index == 3, leaving_rows * lively[:, None, None].astype(jnp.float32), 0.0
    )[None]
    input_term = jnp.where(section_index == 0, input_rows, 0.0)[None]
    final_term = jnp.where(section_index == 2, finals, 0.0)[None]
    out_share, input_share, final_share = (
        lax.psum_scatter(
            out_term.astype(jnp.bfloat16), SECTION, scatter_dimension=3, tiled=True
        ).astype(jnp.float32),
        lax.psum_scatter(
            input_term.astype(jnp.bfloat16), SECTION, scatter_dimension=3, tiled=True
        ).astype(jnp.float32),
        lax.psum_scatter(
            final_term.astype(jnp.bfloat16), SECTION, scatter_dimension=3, tiled=True
        ).astype(jnp.float32),
    )
    (
        grad_qkv_a,
        grad_out_a,
        grad_upper_b,
        grad_lower_b,
        grad_qkv_c,
        grad_state_qkv,
        grad_out_c,
        grad_state_out,
        grad_upper_d,
        grad_lower_d,
    ) = grad_sums
    totals = (
        lax.psum(grad_qkv_a.astype(jnp.bfloat16), DP).astype(jnp.float32),
        lax.psum(grad_out_a.astype(jnp.bfloat16), DP).astype(jnp.float32),
        lax.psum(grad_upper_b.astype(jnp.bfloat16), DP).astype(jnp.float32),
        lax.psum(grad_lower_b.astype(jnp.bfloat16), DP).astype(jnp.float32),
        lax.psum(grad_qkv_c.astype(jnp.bfloat16), DP).astype(jnp.float32),
        lax.psum(grad_state_qkv.astype(jnp.bfloat16), DP).astype(jnp.float32),
        lax.psum(grad_out_c.astype(jnp.bfloat16), DP).astype(jnp.float32),
        lax.psum(grad_state_out.astype(jnp.bfloat16), DP).astype(jnp.float32),
        lax.psum(grad_upper_d.astype(jnp.bfloat16), DP).astype(jnp.float32),
        lax.psum(grad_lower_d.astype(jnp.bfloat16), DP).astype(jnp.float32),
        lax.psum(initial_grad.astype(jnp.bfloat16), DP).astype(jnp.float32),
    )
    small_total = lax.psum(smalls, (DP, TENSOR))
    shares = (
        lax.psum_scatter(
            totals[0].astype(jnp.bfloat16), SECTION, scatter_dimension=0, tiled=True
        ).astype(jnp.float32),
        lax.psum_scatter(
            totals[1].astype(jnp.bfloat16), SECTION, scatter_dimension=1, tiled=True
        ).astype(jnp.float32),
        lax.psum_scatter(
            totals[2].astype(jnp.bfloat16), SECTION, scatter_dimension=0, tiled=True
        ).astype(jnp.float32),
        lax.psum_scatter(
            totals[3].astype(jnp.bfloat16), SECTION, scatter_dimension=1, tiled=True
        ).astype(jnp.float32),
        lax.psum_scatter(
            totals[4].astype(jnp.bfloat16), SECTION, scatter_dimension=0, tiled=True
        ).astype(jnp.float32),
        lax.psum_scatter(
            totals[5].astype(jnp.bfloat16), SECTION, scatter_dimension=0, tiled=True
        ).astype(jnp.float32),
        lax.psum_scatter(
            totals[6].astype(jnp.bfloat16), SECTION, scatter_dimension=1, tiled=True
        ).astype(jnp.float32),
        lax.psum_scatter(
            totals[7].astype(jnp.bfloat16), SECTION, scatter_dimension=1, tiled=True
        ).astype(jnp.float32),
        lax.psum_scatter(
            totals[8].astype(jnp.bfloat16), SECTION, scatter_dimension=0, tiled=True
        ).astype(jnp.float32),
        lax.psum_scatter(
            totals[9].astype(jnp.bfloat16), SECTION, scatter_dimension=1, tiled=True
        ).astype(jnp.float32),
        lax.psum_scatter(
            totals[10].astype(jnp.bfloat16), SECTION, scatter_dimension=1, tiled=True
        ).astype(jnp.float32),
        lax.psum_scatter(
            small_total.astype(jnp.bfloat16), SECTION, scatter_dimension=1, tiled=True
        ).astype(jnp.float32),
    )
    small_share = shares[11]
    return (
        out_share.astype(jnp.bfloat16),
        final_share,
        input_share,
        small_share[0],
        shares[0],
        shares[1],
        small_share[1],
        shares[2],
        shares[3],
        small_share[2],
        small_share[3],
        shares[4],
        shares[5],
        shares[6],
        shares[7],
        small_share[5],
        shares[10],
        small_share[4],
        shares[8],
        shares[9],
    )


CHAIN = 4
MESH = pl.DeviceIdType.MESH
SCALE = 1.0 / math.sqrt(HEAD_DIM)
LOG2_SCALE = SCALE * math.log2(math.e)
ALL_AXES = (SECTION, DP, TENSOR)
GROUP = (SECTION, TENSOR)
VMEM_BYTES = 60 * 1024 * 1024
CHUNK = 256


def block_of(section, tensor):
    high = section // 2
    return 2 * (2 * high + (tensor + high) % 2) + section % 2


DEVICE_OF_BLOCK = [0] * 8
for _section in range(4):
    for _tensor in range(2):
        DEVICE_OF_BLOCK[block_of(_section, _tensor)] = 2 * _section + _tensor
TO_NEXT = [(DEVICE_OF_BLOCK[b], DEVICE_OF_BLOCK[b + 1]) for b in range(7)]
TO_PRIOR = [(there, here) for here, there in TO_NEXT]
SWAP = [(0, 1), (1, 0)]


def params(**extra):
    return pltpu.CompilerParams(vmem_limit_bytes=VMEM_BYTES, **extra)


def nt(a, b):
    return lax.dot_general(a, b, (((1,), (1,)), ((), ())), preferred_element_type=jnp.float32)


def nn(a, b):
    return lax.dot_general(a, b, (((1,), (0,)), ((), ())), preferred_element_type=jnp.float32)


def tn(a, b):
    return lax.dot_general(a, b, (((0,), (0,)), ((), ())), preferred_element_type=jnp.float32)


def bf(a):
    return a.astype(jnp.bfloat16)


def with_ones(values):
    return jnp.concatenate([values, jnp.ones_like(values)], axis=1)


def later_mask(rows):
    return lax.broadcasted_iota(jnp.int32, (rows, rows), 1) > lax.broadcasted_iota(
        jnp.int32, (rows, rows), 0
    )


def window_scores(query, k, pk, start, rows, bar):
    stop = start + query.shape[0]
    own = nt(query, k[:stop])
    prior = nt(query, pk[start:]) + bar
    later = later_mask(query.shape[0])
    pieces = [jnp.where(later, prior[:, : stop - start], own[:, start:])]
    if start:
        pieces = [own[:, :start]] + pieces
    if stop < rows:
        pieces = pieces + [prior[:, stop - start :]]
    return jnp.concatenate(pieces, axis=1) if len(pieces) > 1 else pieces[0]


def window_parts(values, start):
    size = values.shape[0]
    later = later_mask(size)
    middle = values[:, start : start + size]
    zero = jnp.zeros_like(middle)
    own, prior = jnp.where(later, zero, middle), jnp.where(later, middle, zero)
    if start:
        own = jnp.concatenate([values[:, :start], own], axis=1)
    if start + size < values.shape[1]:
        prior = jnp.concatenate([prior, values[:, start + size :]], axis=1)
    return own, prior


def attend_kernel(with_states, *refs):
    if with_states:
        open_ref, q, k, v, pk, pv, sk, sv, out, lse = refs
    else:
        open_ref, q, k, v, pk, pv, out, lse = refs
    rows = q.shape[0]
    bar = jnp.where(open_ref[0] > 0, NEGATIVE, 0.0)
    keys, prior_keys = k[...], pk[...]
    values, prior_values = with_ones(v[...]), with_ones(pv[...])
    if with_states:
        state_keys, state_values = sk[...], with_ones(sv[...])
    for start in range(0, rows, CHUNK):
        query = q[start : start + CHUNK]
        scores = window_scores(query, keys, prior_keys, start, rows, bar)
        top = jnp.max(scores, axis=-1, keepdims=True)
        if with_states:
            more = nt(query, state_keys)
            top = jnp.maximum(top, jnp.max(more, axis=-1, keepdims=True))
        own, prior = window_parts(bf(jnp.exp2((scores - top) * LOG2_SCALE)), start)
        mixed = nn(own, values[: start + CHUNK]) + nn(prior, prior_values[start:])
        if with_states:
            mixed = mixed + nn(bf(jnp.exp2((more - top) * LOG2_SCALE)), state_values)
        total = mixed[:, HEAD_DIM:]
        out[start : start + CHUNK] = bf(mixed[:, :HEAD_DIM] / total)
        lse[0, start : start + CHUNK] = top * LOG2_SCALE + jnp.log2(total[:, :1])


def side_blocks(rows, offset, heads):
    return (
        pl.BlockSpec((rows, HEAD_DIM), lambda h: (0, offset + jnp.minimum(h, heads - 1))),
        pl.BlockSpec((rows, HEAD_DIM), lambda h: (0, offset + jnp.maximum(h - heads, 0))),
    )


def lse_blocks(rows, heads):
    return (
        pl.BlockSpec((1, rows, 1), lambda h: (jnp.minimum(h, heads - 1), 0, 0)),
        pl.BlockSpec((1, rows, 1), lambda h: (jnp.maximum(h - heads, 0), 0, 0)),
    )


def both_sides(kernel, inputs, outputs, open_ref, *refs):
    ins, outs, scratch = refs[: 2 * inputs], refs[2 * inputs : 2 * (inputs + outputs)], refs[2 * (inputs + outputs) :]
    own = pl.program_id(0) < pl.num_programs(0) // 2
    pl.when(own)(lambda: kernel(open_ref, *ins[:inputs], *outs[:outputs], *scratch))
    pl.when(jnp.logical_not(own))(lambda: kernel(open_ref, *ins[inputs:], *outs[outputs:], *scratch))


def attend(opening, projs, priors, states=None):
    rows, width = projs[0].shape[0], projs[0].shape[1] // 3
    heads = width // HEAD_DIM
    columns = [side_blocks(rows, i * heads, heads) for i in (0, 1, 2, 0, 1)]
    arrays = [projs, projs, projs, priors, priors]
    keys = 2 * rows
    if states is not None:
        columns += [side_blocks(states[0].shape[0], i * heads, heads) for i in (1, 2)]
        arrays += [states, states]
        keys += states[0].shape[0]
    outs = [side_blocks(rows, 0, heads), lse_blocks(rows, heads)]
    mixed0, lse0, mixed1, lse1 = pl.pallas_call(
        functools.partial(
            both_sides, functools.partial(attend_kernel, states is not None), len(arrays), 2
        ),
        grid=(2 * heads,),
        in_specs=[pl.BlockSpec(memory_space=pltpu.SMEM)]
        + [pair[side] for side in range(2) for pair in columns],
        out_specs=[pair[side] for side in range(2) for pair in outs],
        out_shape=[
            jax.ShapeDtypeStruct((rows, width), jnp.bfloat16),
            jax.ShapeDtypeStruct((heads, rows, 1), jnp.float32),
        ]
        * 2,
        compiler_params=params(),
        cost_estimate=pl.CostEstimate(
            flops=8 * rows * keys * width,
            bytes_accessed=4 * rows * width * 8,
            transcendentals=rows * keys * heads,
        ),
    )(opening, *(pair[side] for side in range(2) for pair in arrays))
    return mixed0, lse0, mixed1, lse1


def attend_back_kernel(with_states, *refs):
    if with_states:
        (open_ref, q, k, v, pk, pv, sk, sv, gmix, mix, lse) = refs[:11]
        (gq, gk, gv, gpk, gpv, gsk, gsv) = refs[11:18]
    else:
        (open_ref, q, k, v, pk, pv, gmix, mix, lse) = refs[:9]
        (gq, gk, gv, gpk, gpv) = refs[9:14]
    gpk_sum, gpv_sum = refs[-2:]
    rows = q.shape[0]
    bar = jnp.where(open_ref[0] > 0, NEGATIVE, 0.0)
    keys, prior_keys, values, prior_values = k[...], pk[...], v[...], pv[...]
    if with_states:
        state_keys, state_values = sk[...], sv[...]
    for start in range(0, rows, CHUNK):
        stop = start + CHUNK
        query, grad, log_total = q[start:stop], gmix[start:stop], lse[0, start:stop]
        inner = jnp.sum(
            grad.astype(jnp.float32) * mix[start:stop].astype(jnp.float32), axis=-1, keepdims=True
        )
        scores = window_scores(query, keys, prior_keys, start, rows, bar)
        weights = jnp.exp2(scores * LOG2_SCALE - log_total)
        grad_weights = window_scores(grad, values, prior_values, start, rows, 0.0)
        own, prior = window_parts(bf(weights), start)
        own_scores, prior_scores = window_parts(bf(weights * (grad_weights - inner)), start)
        grad_query = nn(own_scores, keys[:stop]) + nn(prior_scores, prior_keys[start:])
        add_own_v, add_own_k = tn(own, grad), tn(own_scores, query)
        add_prior_v, add_prior_k = tn(prior, grad), tn(prior_scores, query)
        if with_states:
            more = jnp.exp2(nt(query, state_keys) * LOG2_SCALE - log_total)
            from_states = bf(more * (nt(grad, state_values) - inner))
            grad_query = grad_query + nn(from_states, state_keys)
            add_sv, add_sk = tn(bf(more), grad), tn(from_states, query)
        gq[start:stop] = bf(grad_query * SCALE)
        if start == 0:
            gv[:stop], gk[:stop] = add_own_v, add_own_k * SCALE
            gpv_sum[...], gpk_sum[...] = add_prior_v, add_prior_k
            if with_states:
                gsv[...], gsk[...] = add_sv, add_sk * SCALE
        else:
            gv[:start] += add_own_v[:start]
            gk[:start] += add_own_k[:start] * SCALE
            gv[start:stop], gk[start:stop] = add_own_v[start:], add_own_k[start:] * SCALE
            gpv_sum[start:] += add_prior_v
            gpk_sum[start:] += add_prior_k
            if with_states:
                gsv[...] += add_sv
                gsk[...] += add_sk * SCALE
    gpv[...] = bf(gpv_sum[...])
    gpk[...] = bf(gpk_sum[...] * SCALE)


def attend_back(opening, projs, priors, grads, mixed, lse, states=None):
    rows, width = projs[0].shape[0], projs[0].shape[1] // 3
    heads = width // HEAD_DIM
    columns = [side_blocks(rows, i * heads, heads) for i in (0, 1, 2, 0, 1)]
    arrays = [projs, projs, projs, priors, priors]
    kinds = [jnp.bfloat16, jnp.float32, jnp.float32, jnp.bfloat16, jnp.bfloat16]
    keys = 2 * rows
    if states is not None:
        columns += [side_blocks(states[0].shape[0], i * heads, heads) for i in (1, 2)]
        arrays += [states, states]
        kinds += [jnp.float32, jnp.float32]
        keys += states[0].shape[0]
    columns += [side_blocks(rows, 0, heads)] * 2 + [lse_blocks(rows, heads)]
    arrays += [grads, mixed, lse]
    results = pl.pallas_call(
        functools.partial(
            both_sides, functools.partial(attend_back_kernel, states is not None), len(arrays), len(kinds)
        ),
        grid=(2 * heads,),
        in_specs=[pl.BlockSpec(memory_space=pltpu.SMEM)]
        + [pair[side] for side in range(2) for pair in columns],
        out_specs=[side_blocks(rows, 0, heads)[side] for side in range(2) for _ in kinds],
        out_shape=[jax.ShapeDtypeStruct((rows, width), kind) for kind in kinds] * 2,
        scratch_shapes=[pltpu.VMEM((rows, HEAD_DIM), jnp.float32)] * 2,
        compiler_params=params(),
        cost_estimate=pl.CostEstimate(
            flops=20 * rows * keys * width,
            bytes_accessed=4 * rows * width * 24,
            transcendentals=rows * keys * heads,
        ),
    )(opening, *(pair[side] for side in range(2) for pair in arrays))
    return results[: len(kinds)], results[len(kinds) :]


KINDS = 9
FLIGHT = 4


class Spread:
    def __init__(self, sources, targets, send, recv):
        section, tensor, group = (lax.axis_index(a) for a in (SECTION, TENSOR, DP))
        self.sources, self.targets, self.send, self.recv = sources, targets, send, recv
        self.core, self.high, self.near = section % 2, section // 2, group % 2
        self.across = {TENSOR: 1 - tensor}
        self.along = {SECTION: (section + 2) % 4}
        self.beside = {DP: group + 1 - 2 * self.near}
        self.other = {SECTION: section + 1 - 2 * self.core}

    def partners(self):
        return [self.across, self.along, self.beside, self.other]

    def copy(self, kind, w):
        size = self.targets[w].shape[0] // 8
        y, z = self.high, self.near
        high, near, first, rows, to = (
            (y, z, 0, size, self.across),
            (y, z, 0, size, self.along),
            (y, z, 0, size, self.beside),
            (y, 1 - z, 0, size // 2, self.along),
            (1 - y, z, size // 2, size // 2, self.beside),
            (y, z, 0, size, self.other),
            (1 - y, z, 0, size, self.other),
            (y, 1 - z, 0, size, self.other),
            (1 - y, 1 - z, 0, size, self.other),
        )[kind]
        part = (near * 2 + high) * 2 + self.core
        where = pl.ds(pl.multiple_of(part * size + first, rows), rows)
        source = self.sources[w] if kind == 0 else self.targets[w]
        return pltpu.make_async_remote_copy(
            src_ref=source.at[where], dst_ref=self.targets[w].at[where],
            send_sem=self.send.at[kind * len(self.targets) + w],
            recv_sem=self.recv.at[kind * len(self.targets) + w],
            device_id=to, device_id_type=MESH,
        )

    def begin(self, w):
        self.copy(0, w).start()

    def hop(self, w):
        self.copy(0, w).wait_recv()
        for kind in (1, 2, 5):
            self.copy(kind, w).start()

    def cross(self, w):
        for kind in (1, 2):
            self.copy(kind, w).wait_recv()
        for kind in (3, 4, 6, 7):
            self.copy(kind, w).start()

    def close(self, w):
        for kind in (3, 4):
            self.copy(kind, w).wait_recv()
        self.copy(8, w).start()

    def end(self, w):
        for kind in (5, 6, 7, 8):
            self.copy(kind, w).wait_recv()
        for kind in range(KINDS):
            self.copy(kind, w).wait_send()


class Join:
    def __init__(self, source, theirs, mine, target, local, send, recv, i):
        tensor = lax.axis_index(TENSOR)
        rows = source.shape[-2]
        where = pl.ds(pl.multiple_of(tensor * rows, rows), rows)

        def of(index):
            return source if index is None else source.at[0, index]

        self.own = pltpu.make_async_copy(of(mine), target.at[where], local.at[i])
        self.remote = pltpu.make_async_remote_copy(
            src_ref=of(theirs), dst_ref=target.at[where], send_sem=send.at[i], recv_sem=recv.at[i],
            device_id={TENSOR: 1 - tensor}, device_id_type=MESH,
        )

    def start(self):
        self.remote.start()
        self.own.start()

    def wait(self):
        self.remote.wait()
        self.own.wait()


def meet(partners):
    barrier = pltpu.get_barrier_semaphore()
    for partner in partners:
        pl.semaphore_signal(barrier, inc=1, device_id=partner, device_id_type=MESH)
    pl.semaphore_wait(barrier, len(partners))


def gather_kernel(count, layer_input, init_states, *refs):
    sources, refs = refs[:count], refs[count:]
    tokens, before, initial = refs[:3]
    targets = refs[3 : 3 + count]
    send, recv, local, join_send, join_recv = refs[3 + count :]
    spread = Spread(sources, targets, send, recv)
    section, tensor = lax.axis_index(SECTION), lax.axis_index(TENSOR)
    block, partner = block_of(section, tensor), block_of(section, 1 - tensor)
    joins = [
        Join(layer_input, partner, block, tokens, local, join_send, join_recv, 0),
        Join(
            layer_input, jnp.maximum(partner - 1, 0), jnp.maximum(block - 1, 0),
            before, local, join_send, join_recv, 1,
        ),
        Join(init_states, None, None, initial, local, join_send, join_recv, 2),
    ]
    meet(spread.partners())
    def begin(i):
        if i < count:
            spread.begin(i)
        elif i < count + len(joins):
            joins[i - count].start()

    for i in range(FLIGHT):
        begin(i)
    for w in range(count + 2):
        if w < count:
            spread.hop(w)
        begin(w + FLIGHT)
        if 0 <= w - 1 < count:
            spread.cross(w - 1)
        if 0 <= w - 2 < count:
            spread.close(w - 2)
    for w in range(count):
        spread.end(w)
    for join in joins:
        join.wait()


def gather(layer_input, init_states, weights):
    count = len(weights)
    rows, width = 2 * layer_input.shape[2], layer_input.shape[3]
    dma = pltpu.SemaphoreType.DMA
    anywhere = pl.BlockSpec(memory_space=pl.ANY)
    shapes = [(rows, width)] * 2 + [(2 * init_states.shape[0], width)] + [w.shape for w in weights]
    results = pl.pallas_call(
        functools.partial(gather_kernel, count),
        in_specs=[anywhere] * (2 + count),
        out_specs=[anywhere] * (3 + count),
        out_shape=[jax.ShapeDtypeStruct(s, jnp.bfloat16) for s in shapes],
        scratch_shapes=[dma((KINDS * count,))] * 2 + [dma((3,))] * 3,
        compiler_params=params(collective_id=4, has_side_effects=True),
        cost_estimate=pl.CostEstimate(flops=0, bytes_accessed=200 * 1024 * 1024, transcendentals=0),
    )(layer_input, init_states, *weights)
    return results[:3], results[3:]


def neighbours():
    section, tensor = lax.axis_index(SECTION), lax.axis_index(TENSOR)
    block = block_of(section, tensor)

    return place_of((block + 7) % 8), place_of((block + 1) % 8)


def place_of(block):
    pair = block // 2
    high = pair // 2
    return {SECTION: 2 * high + block % 2, TENSOR: (pair + high) % 2}


class Scatter:
    def __init__(self, values, landed, send, recv, local):
        section, tensor = lax.axis_index(SECTION), lax.axis_index(TENSOR)
        block = block_of(section, tensor)
        self.members = [place_of((block + i) % 8) for i in range(1, 8)]
        rows, width = values[0].shape[0] // 2, values[0].shape[1] // 4

        def piece(value, to):
            high = pl.multiple_of(to[TENSOR] * rows, rows)
            left = pl.multiple_of(to[SECTION] * width, width)
            return value.at[pl.ds(high, rows), pl.ds(left, width)]

        self.copies = [
            pltpu.make_async_remote_copy(
                src_ref=piece(value, to), dst_ref=landed.at[j, block],
                send_sem=send.at[j * 7 + i], recv_sem=recv.at[j * 7 + i],
                device_id=to, device_id_type=MESH,
            )
            for j, value in enumerate(values)
            for i, to in enumerate(self.members)
        ]
        self.own = [
            pltpu.make_async_copy(
                piece(value, {SECTION: section, TENSOR: tensor}), landed.at[j, block], local.at[j]
            )
            for j, value in enumerate(values)
        ]

    def start(self):
        for copy in self.copies + self.own:
            copy.start()

    def wait(self):
        for copy in self.copies + self.own:
            copy.wait()


def pass_on(sent, landed, send_sem, recv_sem, slot, part, target):
    rows = pl.ds(part * CHUNK, CHUNK)
    return pltpu.make_async_remote_copy(
        src_ref=sent.at[slot, rows],
        dst_ref=landed.at[slot, rows],
        send_sem=send_sem.at[slot, part],
        recv_sem=recv_sem.at[slot, part],
        device_id=target,
        device_id_type=MESH,
    )


def chain_kernel(
    initial, starts, gain, keep, own, other, sqkv0, sqkv1, sout0, sout1, output_grad,
    state, hs, ps0, ps1, os0, os1, lse, update, fresh, cotangent,
    sent, landed, send_sem, recv_sem, local, join_send, join_recv,
):
    prior, following = neighbours()
    section, tensor = lax.axis_index(SECTION), lax.axis_index(TENSOR)
    join = Join(
        output_grad, block_of(section, 1 - tensor), block_of(section, tensor),
        cotangent, local, join_send, join_recv, 0,
    )
    meet([prior, following, {TENSOR: 1 - tensor}])
    join.start()
    count, width = initial.shape
    half = os0.shape[1]
    parts = count // CHUNK
    state[...] = initial[...]

    def copy(slot, part):
        return pass_on(sent, landed, send_sem, recv_sem, slot, part, following)

    def work(turn):
        for part in range(parts):
            rows = slice(part * CHUNK, (part + 1) * CHUNK)

            @pl.when(turn > 0)
            def _():
                slot = turn - 1
                copy(slot, part).wait_recv()
                state[rows] = jnp.where(
                    starts[...] > 0.0, initial[rows], landed[slot, rows].astype(jnp.float32)
                )

            value = state[rows]
            hidden = bf(value * inverse_rms(value) * gain[...])
            hs[rows] = hidden
            ps0[rows] = bf(nn(hidden, sqkv0[...]))
            ps1[rows] = bf(nn(hidden, sqkv1[...]))

        def one_head(h, carry):
            at = [pl.ds(pl.multiple_of(i * half + h * HEAD_DIM, HEAD_DIM), HEAD_DIM) for i in range(3)]
            for which, (tok, st, mixed) in enumerate(((own, ps0, os0), (other, ps1, os1))):
                tok_key, tok_value = tok[:, at[1]], with_ones(tok[:, at[2]])
                key, value = st[:, at[1]], with_ones(st[:, at[2]])
                for part in range(parts):
                    rows = slice(part * CHUNK, (part + 1) * CHUNK)
                    query = st[rows, at[0]]
                    score_tok, score = nt(query, tok_key), nt(query, key)
                    top = jnp.maximum(
                        jnp.max(score_tok, axis=-1, keepdims=True),
                        jnp.max(score, axis=-1, keepdims=True),
                    )
                    mix = nn(bf(jnp.exp2((score_tok - top) * LOG2_SCALE)), tok_value) + nn(
                        bf(jnp.exp2((score - top) * LOG2_SCALE)), value
                    )
                    total = mix[:, HEAD_DIM:]
                    mixed[rows, at[0]] = bf(mix[:, :HEAD_DIM] / total)
                    lse[which, h, rows] = top * LOG2_SCALE + jnp.log2(total[:, :1])
            return carry

        lax.fori_loop(0, half // HEAD_DIM, one_head, 0, unroll=True)
        for part in range(parts):
            rows = slice(part * CHUNK, (part + 1) * CHUNK)
            term = nn(os0[rows], sout0[...]) + nn(os1[rows], sout1[...])
            update[rows] = term
            renewed_state = bf(keep[...] * state[rows] + (1.0 - keep[...]) * term)
            fresh[rows] = renewed_state

            @pl.when(turn < CHAIN - 1)
            def _():
                sent[turn, rows] = renewed_state
                copy(turn, part).start()

    parity = block_of(section, tensor) % 2

    def one_round(turn, nothing):
        pl.when(parity == turn % 2)(lambda: work(turn))
        return nothing

    lax.fori_loop(0, CHAIN, one_round, 0)
    for slot in range(CHAIN - 1):

        @pl.when(parity == slot % 2)
        def _():
            for part in range(parts):
                copy(slot, part).wait_send()

    join.wait()


def chain(initial, starts, gain, keep, own, other, sqkv0, sqkv1, sout0, sout1, output_grad):
    count, width = initial.shape
    half = sout0.shape[0]
    heads = half // HEAD_DIM
    bf16, f32 = jnp.bfloat16, jnp.float32
    vmem, anywhere = pl.BlockSpec(memory_space=pltpu.VMEM), pl.BlockSpec(memory_space=pl.ANY)
    dma = pltpu.SemaphoreType.DMA
    parts = count // CHUNK
    return pl.pallas_call(
        chain_kernel,
        in_specs=[vmem] * 10 + [anywhere],
        out_specs=[vmem] * 9 + [anywhere],
        out_shape=[
            jax.ShapeDtypeStruct((count, width), f32),
            jax.ShapeDtypeStruct((count, width), bf16),
            jax.ShapeDtypeStruct((count, 3 * half), bf16),
            jax.ShapeDtypeStruct((count, 3 * half), bf16),
            jax.ShapeDtypeStruct((count, half), bf16),
            jax.ShapeDtypeStruct((count, half), bf16),
            jax.ShapeDtypeStruct((2, heads, count, 1), f32),
            jax.ShapeDtypeStruct((count, width), f32),
            jax.ShapeDtypeStruct((count, width), bf16),
            jax.ShapeDtypeStruct((2 * output_grad.shape[2], width), bf16),
        ],
        scratch_shapes=[
            pltpu.VMEM((CHAIN - 1, count, width), bf16),
            pltpu.VMEM((CHAIN - 1, count, width), bf16),
            dma((CHAIN - 1, parts)), dma((CHAIN - 1, parts)),
            dma((1,)), dma((1,)), dma((1,)),
        ],
        compiler_params=params(collective_id=1, has_side_effects=True),
        cost_estimate=pl.CostEstimate(
            flops=CHAIN * count * width * (8 * width + 8 * count),
            bytes_accessed=25 * 1024 * 1024,
            transcendentals=CHAIN * count * count * 4 * heads,
        ),
    )(initial, starts, gain, keep, own, other, sqkv0, sqkv1, sout0, sout1, output_grad)


LATE = 10


def chain_back_kernel(
    starts, ends, gain, keep, own, other, ps0, ps1, os0, os1, lse, *refs,
):
    distant, refs = refs[:LATE], refs[LATE:]
    result, ending, first_grad, gproj0, gproj1, gtok0, gtok1, gup, small, scattered = refs[:10]
    fetched, refs = refs[10 : 10 + LATE], refs[10 + LATE :]
    state, update, tok_k0, tok_v0, tok_k1, tok_v1, sqkv0, sqkv1, sout0, sout1 = fetched
    (
        grad_state, weights, grad_os0, grad_os1, sent, landed, send_sem, recv_sem, piece_send, piece_recv, piece_sem, late_sem
    ) = refs
    fetches = [
        pltpu.make_async_copy(source, target, late_sem.at[i])
        for i, (source, target) in enumerate(zip(distant, fetched))
    ]
    for fetch in fetches:
        fetch.start()
    prior, following = neighbours()
    scatter = Scatter((result, ending), scattered, piece_send, piece_recv, piece_sem)
    meet([prior, following] + scatter.members)
    scatter.start()
    count, width = state.shape
    half = os0.shape[1]
    heads = half // HEAD_DIM
    parts = count // CHUNK
    sides = (
        (own, ps0, os0, tok_k0, tok_v0, gproj0, gtok0, grad_os0),
        (other, ps1, os1, tok_k1, tok_v1, gproj1, gtok1, grad_os1),
    )

    def lanes(h):
        return [pl.ds(pl.multiple_of(i * half + h * HEAD_DIM, HEAD_DIM), HEAD_DIM) for i in range(3)]

    def copy(slot, part):
        return pass_on(sent, landed, send_sem, recv_sem, slot, part, prior)

    def prepare(h, carry):
        at = lanes(h)
        for which, (tok, st, *_) in enumerate(sides):
            tok_key, key = tok[:, at[1]], st[:, at[1]]
            for part in range(parts):
                rows = slice(part * CHUNK, (part + 1) * CHUNK)
                query, log_total = st[rows, at[0]], lse[which, h, rows]
                weights[which, h, rows, :count] = bf(
                    jnp.exp2(nt(query, tok_key) * LOG2_SCALE - log_total)
                )
                weights[which, h, rows, count:] = bf(
                    jnp.exp2(nt(query, key) * LOG2_SCALE - log_total)
                )
        return carry

    lax.fori_loop(0, heads, prepare, 0)
    for fetch in fetches:
        fetch.wait()
    grad_state[...] = jnp.zeros_like(grad_state)

    def work(turn):
        for part in range(parts):
            rows = slice(part * CHUNK, (part + 1) * CHUNK)

            @pl.when(turn > 0)
            def _():
                slot = turn - 1
                copy(slot, part).wait_recv()
                grad_state[rows] = jnp.where(
                    ends[...] > 0.0, 0.0, landed[slot, rows].astype(jnp.float32)
                )

            out = bf((1.0 - keep[...]) * grad_state[rows])
            gup[rows] = out
            grad_os0[rows] = bf(nt(out, sout0[...]))
            grad_os1[rows] = bf(nt(out, sout1[...]))

        def one_head(h, carry):
            at = lanes(h)
            for which, (tok, st, mixed, given_k, given_v, gproj, gtok, grad_os) in enumerate(sides):
                tok_key, tok_value = tok[:, at[1]], tok[:, at[2]]
                key, value = st[:, at[1]], st[:, at[2]]
                for part in range(parts):
                    rows = slice(part * CHUNK, (part + 1) * CHUNK)
                    query, grad = st[rows, at[0]], grad_os[rows, at[0]]
                    inner = jnp.sum(
                        grad.astype(jnp.float32) * mixed[rows, at[0]].astype(jnp.float32),
                        axis=-1, keepdims=True,
                    )
                    p_tok, p = weights[which, h, rows, :count], weights[which, h, rows, count:]
                    s_tok = bf(p_tok.astype(jnp.float32) * (nt(grad, tok_value) - inner))
                    s = bf(p.astype(jnp.float32) * (nt(grad, value) - inner))
                    gproj[rows, at[0]] = bf((nn(s_tok, tok_key) + nn(s, key)) * SCALE)
                    gk, gv = tn(s, query) * SCALE, tn(p, grad)
                    if part == 0:
                        total_k, total_v = gk + given_k[:, at[0]], gv + given_v[:, at[0]]
                    else:
                        total_k, total_v = total_k + gk, total_v + gv

                    @pl.when(turn >= CHAIN - 2)
                    def _():
                        gtk, gtv = tn(s_tok, query) * SCALE, tn(p_tok, grad)
                        if part == 0:
                            gtok[:, at[0]], gtok[:, at[1]] = gtk, gtv
                        else:
                            gtok[:, at[0]] += gtk
                            gtok[:, at[1]] += gtv

                gproj[:, at[1]], gproj[:, at[2]] = bf(total_k), bf(total_v)
            return carry

        lax.fori_loop(0, heads, one_head, 0, unroll=True)
        for part in range(parts):
            rows = slice(part * CHUNK, (part + 1) * CHUNK)
            back = nt(gproj0[rows], sqkv0[...]) + nt(gproj1[rows], sqkv1[...])
            value, new = state[rows], grad_state[rows]
            factor = inverse_rms(value)
            scaled = value * factor
            through = back * gain[...]
            leaving = keep[...] * new + factor * (
                through - scaled * jnp.mean(through * scaled, axis=-1, keepdims=True)
            )

            @pl.when(turn < CHAIN - 1)
            def _():
                sent[turn, rows] = bf(leaving)
                copy(turn, part).start()

            @pl.when(turn >= CHAIN - 2)
            def _():
                gain_term = jnp.sum(back * scaled, axis=0, keepdims=True)
                bias_term = jnp.sum(new * (value - update[rows]), axis=0, keepdims=True) * (
                    keep[...] * (1.0 - keep[...])
                )
                if part == 0:
                    small[0:1, :], small[1:2, :] = gain_term, bias_term
                else:
                    small[0:1, :] += gain_term
                    small[1:2, :] += bias_term
                first_grad[rows] = bf(jnp.where(starts[...] > 0.0, leaving, 0.0))

    parity = 1 - block_of(lax.axis_index(SECTION), lax.axis_index(TENSOR)) % 2

    def one_round(turn, nothing):
        pl.when(parity == turn % 2)(lambda: work(turn))
        return nothing

    lax.fori_loop(0, CHAIN, one_round, 0)
    for slot in range(CHAIN - 1):

        @pl.when(parity == slot % 2)
        def _():
            for part in range(parts):
                copy(slot, part).wait_send()

    scatter.wait()


def chain_back(
    starts, ends, state, update, gain, keep, own, other, ps0, ps1, os0, os1, lse,
    tok_k0, tok_v0, tok_k1, tok_v1, sqkv0, sqkv1, sout0, sout1, result, ending,
):
    count, width = state.shape
    half = sout0.shape[0]
    heads = half // HEAD_DIM
    bf16, f32 = jnp.bfloat16, jnp.float32
    vmem, anywhere = pl.BlockSpec(memory_space=pltpu.VMEM), pl.BlockSpec(memory_space=pl.ANY)
    dma = pltpu.SemaphoreType.DMA
    parts = count // CHUNK
    rows = own.shape[0]
    distant = (state, update, tok_k0, tok_v0, tok_k1, tok_v1, sqkv0, sqkv1, sout0, sout1)
    return pl.pallas_call(
        chain_back_kernel,
        in_specs=[vmem] * 11 + [anywhere] * (LATE + 2),
        out_specs=[vmem] * 7 + [anywhere],
        out_shape=[
            jax.ShapeDtypeStruct((count, width), bf16),
            jax.ShapeDtypeStruct((count, 3 * half), bf16),
            jax.ShapeDtypeStruct((count, 3 * half), bf16),
            jax.ShapeDtypeStruct((rows, 2 * half), f32),
            jax.ShapeDtypeStruct((rows, 2 * half), f32),
            jax.ShapeDtypeStruct((count, width), bf16),
            jax.ShapeDtypeStruct((2, width), f32),
            jax.ShapeDtypeStruct((2, 8, rows // 2, width // 4), bf16),
        ],
        scratch_shapes=[pltpu.VMEM(late.shape, late.dtype) for late in distant]
        + [
            pltpu.VMEM((count, width), f32),
            pltpu.VMEM((2, heads, count, rows + count), bf16),
            pltpu.VMEM((count, half), bf16),
            pltpu.VMEM((count, half), bf16),
            pltpu.VMEM((CHAIN - 1, count, width), bf16),
            pltpu.VMEM((CHAIN - 1, count, width), bf16),
            dma((CHAIN - 1, parts)), dma((CHAIN - 1, parts)), dma((14,)), dma((14,)), dma((2,)), dma((LATE,)),
        ],
        compiler_params=params(collective_id=2, has_side_effects=True),
        cost_estimate=pl.CostEstimate(
            flops=CHAIN * count * width * (16 * width + 16 * count),
            bytes_accessed=45 * 1024 * 1024,
            transcendentals=count * count * 4 * heads,
        ),
    )(starts, ends, gain, keep, own, other, ps0, ps1, os0, os1, lse, *distant, result, ending)


RING = 8
SHORT_RING = 4
TILE = 256
TAIL = 12
LAGS = (0, 1, 2, 4, 6, 7, 8, 9, 10)
UP_D, DOWN_D, UP_B, DOWN_B, OUT_C, QKV_C, SOUT_C, SQKV_C, QKV_A, OUT_A = range(10)
WEIGHTS = (
    (UP_D, True, 8), (DOWN_D, False, 8), (UP_B, True, 8), (DOWN_B, False, 8), (OUT_C, False, 2),
    (QKV_C, True, 6), (SOUT_C, False, 2), (SQKV_C, True, 6), (QKV_A, True, 6), (OUT_A, False, 2),
)
STARTS = [sum(w[2] for w in WEIGHTS[:i]) for i in range(len(WEIGHTS))]
PLAIN = sum(w[2] for w in WEIGHTS)
TAIL_WEIGHT = [w[0] for w in WEIGHTS].index(QKV_A)
TAIL_INPUTS = 10
TILES = PLAIN + 2


def grads_kernel(*refs):
    count = len(WEIGHTS)
    lefts, refs = refs[:count], refs[count:]
    panels_own, panels_other, refs = list(refs[: count - 1]), list(refs[count - 1 : 2 * count - 2]), refs[2 * count - 2 :]
    first, small, leaving_keys, refs = refs[0], refs[1], refs[2:6], refs[6:]
    distant, gain, refs = refs[:TAIL_INPUTS], refs[TAIL_INPUTS], refs[TAIL_INPUTS + 1 :]
    outs, last_out, landed = refs[:count], refs[count], refs[count + 1]
    refs = refs[count + 2 :]
    (
        left, panel, pair, core_in, kept1, first_in, kept2, second_in, kept3, third_in, kept4, fourth_in, result,
        left_sem, panel_sem, last_sem, core_send, core_recv, first_send, first_recv, second_send, second_recv,
        send_sem, recv_sem, piece_send, piece_recv, piece_sem,
        halo, ga0, ga1, rows_out, small_rows, gain_sum, tail_sem, halo_send, halo_recv,
    ) = refs[:-TAIL_INPUTS]
    fetched = refs[-TAIL_INPUTS:]
    panels_own.insert(TAIL_WEIGHT, ga0)
    panels_other.insert(TAIL_WEIGHT, ga1)
    section, tensor, group = (lax.axis_index(a) for a in (SECTION, TENSOR, DP))
    core, high = section % 2, section // 2
    near, far = group % 2, group // 2
    half, quarter = TILE // 2, TILE // 4
    other_core = {SECTION: section + 1 - 2 * core}
    near_group = {DP: group + 1 - 2 * near}
    far_group = {DP: (group + 2) % 4}
    scatter = Scatter((rows_out,), landed, piece_send, piece_recv, piece_sem)
    tail_fetches = [
        pltpu.make_async_copy(source, target, tail_sem.at[i])
        for i, (source, target) in enumerate(zip(distant + (small,), fetched + (small_rows,)))
    ]
    for fetch in tail_fetches:
        fetch.start()
    prior, _ = neighbours()
    meet(scatter.members + [near_group, far_group])

    def halo_copy(i):
        to = 2 * ((tensor + prior[TENSOR] + i // 2) % 2) + i % 2
        return pltpu.make_async_remote_copy(
            src_ref=leaving_keys[i], dst_ref=halo.at[to], send_sem=halo_send.at[i],
            recv_sem=halo_recv.at[to], device_id=prior, device_id_type=MESH,
        )

    for i in range(4):
        halo_copy(i).start()

    def remote(source, target, sems, recvs, where, partner):
        return pltpu.make_async_remote_copy(
            src_ref=source, dst_ref=target, send_sem=sems.at[where], recv_sem=recvs.at[where],
            device_id=partner, device_id_type=MESH,
        )

    def left_copy(w):
        return pltpu.make_async_copy(lefts[w], left.at[w % 3], left_sem.at[w % 3])

    left_copy(0).start()

    def panel_copies(w, k):
        slot = k % SHORT_RING
        columns = pl.ds(pl.multiple_of((k - STARTS[w]) * TILE, TILE), TILE)
        return [
            pltpu.make_async_copy(source[w].at[:, columns], panel.at[slot, j], panel_sem.at[2 * slot + j])
            for j, source in enumerate((panels_own, panels_other))
        ]

    def last_copies(which):
        slot = (PLAIN + which) % SHORT_RING
        for i in range(8):
            s, t = i // 2, i % 2
            columns = slice(s * TILE, (s + 1) * TILE)
            source = small_rows.at[:, columns] if which else first.at[t * TILE : (t + 1) * TILE, columns]
            yield pltpu.make_async_copy(source, pair.at[slot, s % 2, s // 2, t], last_sem.at[i])

    def core_copy(k):
        slot = k % SHORT_RING
        return remote(
            pair.at[slot, 1 - core], core_in.at[slot], core_send, core_recv, slot, other_core
        )

    def order(k):
        turn = k % 2
        send = (
            (1 - turn) * (1 - tensor) + turn * (2 - 2 * high),
            (1 - turn) * (3 - tensor) + turn * (3 - 2 * high),
        )
        keep = (
            (1 - turn) * tensor + turn * 2 * high,
            (1 - turn) * (2 + tensor) + turn * (2 * high + 1),
        )
        return send, keep, (1 - turn) * high + turn * tensor

    def partner_of(turn):
        return {
            SECTION: section * (1 - turn) + ((section + 2) % 4) * turn,
            TENSOR: tensor + (1 - turn) * (1 - 2 * tensor),
        }

    def first_copy(k, i):
        slot = k % RING
        return remote(
            kept1.at[k % SHORT_RING, order(k)[0][i]], first_in.at[slot, i], first_send, first_recv,
            2 * slot + i, partner_of(k % 2),
        )

    def second_copy(k):
        slot = k % RING
        return remote(
            kept2.at[slot, 1 - order(k)[2]], second_in.at[slot], second_send, second_recv,
            slot, partner_of(1 - k % 2),
        )

    def third_copy(k):
        slot = k % RING
        return remote(
            kept3.at[slot, pl.ds((1 - near) * half, half)], third_in.at[slot], send_sem, recv_sem,
            slot, near_group,
        )

    def fourth_copy(k):
        slot = k % RING
        return remote(
            kept4.at[slot, pl.ds((1 - far) * quarter, quarter)], fourth_in.at[slot], send_sem, recv_sem,
            RING + slot, far_group,
        )

    def back_far(k):
        rows = pl.ds(near * half + far * quarter, quarter)
        return remote(
            result.at[k, rows], result.at[k, rows], send_sem, recv_sem, 2 * RING + k % RING, far_group
        )

    def back_near(k):
        rows = pl.ds(near * half, half)
        return remote(
            result.at[k, rows], result.at[k, rows], send_sem, recv_sem, 3 * RING + k % RING, near_group
        )

    def add(a, b):
        return bf(a.astype(jnp.float32) + b.astype(jnp.float32))

    def fetch(k):
        for w in range(count):

            @pl.when((k >= STARTS[w]) & (k < STARTS[w] + WEIGHTS[w][2]))
            def _():
                for copy in panel_copies(w, k):
                    copy.start()

            if w + 1 < count:

                @pl.when(k == STARTS[w])
                def _():
                    left_copy(w + 1).start()

    def multiply(k):
        slot = k % SHORT_RING

        @pl.when(k < PLAIN)
        def _():
            at = 0
            for w in range(count):
                if w:
                    at = at + jnp.where(k >= STARTS[w], 1, 0)

                @pl.when(k == STARTS[w])
                def _():
                    left_copy(w).wait()

            for j, place in enumerate((tensor, 1 - tensor)):
                pltpu.make_async_copy(
                    panels_own[0].at[:, :TILE], panel.at[slot, j], panel_sem.at[2 * slot + j]
                ).wait()
                product = bf(tn(panel[slot, j], left[at % 3]))
                for s in range(4):
                    pair[slot, s % 2, s // 2, place] = product[:, s * TILE : (s + 1) * TILE]

        for which in range(2):

            @pl.when(k == PLAIN + which)
            def _():
                for copy in last_copies(which):
                    copy.start()
                for copy in last_copies(which):
                    copy.wait()

        core_copy(k).start()

    def over_cores(k):
        core_copy(k).wait()
        for i in range(4):
            kept1[k % SHORT_RING, i] = add(
                pair[k % SHORT_RING, core, i // 2, i % 2], core_in[k % SHORT_RING, i // 2, i % 2]
            )
        for i in range(2):
            first_copy(k, i).start()

    def over_first(k):
        slot = k % RING
        for i in range(2):
            first_copy(k, i).wait()
        for i in range(2):
            kept2[slot, i] = add(kept1[k % SHORT_RING, order(k)[1][i]], first_in[slot, i])
        second_copy(k).start()

    def over_second(k):
        slot = k % RING
        second_copy(k).wait()
        kept3[slot] = add(kept2[slot, order(k)[2]], second_in[slot])
        third_copy(k).start()

    def over_near(k):
        slot = k % RING
        third_copy(k).wait()
        kept4[slot] = add(kept3[slot, pl.ds(near * half, half)], third_in[slot])
        fourth_copy(k).start()

    def over_far(k):
        slot = k % RING
        fourth_copy(k).wait()
        result[k, pl.ds(near * half + far * quarter, quarter)] = add(
            kept4[slot, pl.ds(far * quarter, quarter)], fourth_in[slot]
        )
        back_far(k).start()

    def from_far(k):
        back_far(k).wait()
        back_near(k).start()

    def from_near(k):
        back_near(k).wait()
        for w in range(count):

            @pl.when((k >= STARTS[w]) & (k < STARTS[w] + WEIGHTS[w][2]))
            def _():
                at = pl.ds(pl.multiple_of((k - STARTS[w]) * TILE, TILE), TILE)
                if WEIGHTS[w][1]:
                    outs[w][:, at] = bf(result[k].astype(jnp.float32).T)
                else:
                    outs[w][at, :] = result[k]

        @pl.when(k >= PLAIN)
        def _():
            last_out[k - PLAIN] = result[k]

    gq0, gk0, gv0, gq1, gk1, gv1, w0, w1, tokens, grad = fetched
    wide = gq0.shape[1]

    def tail_begin():
        for copy in tail_fetches:
            copy.wait()
        for i in range(4):
            halo_copy(i).wait_send()
            pltpu.make_async_remote_copy(
                src_ref=leaving_keys[i], dst_ref=halo.at[i], send_sem=halo_send.at[i],
                recv_sem=halo_recv.at[i], device_id=prior, device_id_type=MESH,
            ).wait_recv()
        gain_sum[...] = jnp.zeros_like(gain_sum)

    def tail_rows(start):
        rows = slice(start, start + CHUNK)
        for side, (to, q, k, v) in enumerate(((ga0, gq0, gk0, gv0), (ga1, gq1, gk1, gv1))):
            to[rows, :wide] = q[rows]
            to[rows, wide : 2 * wide] = bf(k[rows] + halo[2 * side, rows].astype(jnp.float32))
            to[rows, 2 * wide :] = bf(v[rows] + halo[2 * side + 1, rows].astype(jnp.float32))
        back = nt(ga0[rows], w0[...]) + nt(ga1[rows], w1[...])
        value = tokens[rows].astype(jnp.float32)
        factor = inverse_rms(value)
        scaled = value * factor
        through = back * gain[...]
        rows_out[rows] = bf(
            grad[rows]
            + factor * (through - scaled * jnp.mean(through * scaled, axis=-1, keepdims=True))
        )
        gain_sum[0:1] += jnp.sum(back * scaled, axis=0, keepdims=True)

    def tail_end():
        top = small_rows[:16].astype(jnp.float32)
        row = lax.broadcasted_iota(jnp.int32, top.shape, 0)
        small_rows[:16] = bf(jnp.where(row == 0, gain_sum[0:1], top))
        scatter.start()

    stages = (
        fetch, multiply, over_cores, over_first, over_second, over_near, over_far, from_far, from_near
    )

    def step(i, nothing):
        pl.when(i == TAIL)(tail_begin)
        for part in range(grad.shape[0] // CHUNK):
            pl.when(i == TAIL + 2 + 2 * part)(functools.partial(tail_rows, part * CHUNK))
        pl.when(i == TAIL + 3 + 2 * (grad.shape[0] // CHUNK))(tail_end)
        for stage, lag in zip(stages, LAGS):
            k = i - lag

            @pl.when((k >= 0) & (k < TILES))
            def _():
                stage(k)

        return nothing

    lax.fori_loop(0, TILES + LAGS[-1], step, 0)
    scatter.wait()


def weight_grads(operands, first, small, leaving_keys, tail, gain):
    bf16 = jnp.bfloat16
    dma = pltpu.SemaphoreType.DMA
    anywhere, vmem = pl.BlockSpec(memory_space=pl.ANY), pl.BlockSpec(memory_space=pltpu.VMEM)
    count = len(WEIGHTS)
    rows, width = operands[WEIGHTS[0][0]][0].shape
    shapes = [(TILE, n * TILE) if by_rows else (n * TILE, TILE) for _, by_rows, n in WEIGHTS]
    shapes += [(2, TILE, TILE)]
    results = pl.pallas_call(
        grads_kernel,
        in_specs=[anywhere] * (3 * count + 4 + TAIL_INPUTS) + [vmem],
        out_specs=[vmem] * (count + 1) + [anywhere],
        out_shape=[jax.ShapeDtypeStruct(s, bf16) for s in shapes + [(1, 8, TILE, TILE)]],
        scratch_shapes=[
            pltpu.VMEM((3, rows, width), bf16),
            pltpu.VMEM((SHORT_RING, 2, rows, TILE), bf16),
            pltpu.VMEM((SHORT_RING, 2, 2, 2, TILE, TILE), bf16),
            pltpu.VMEM((SHORT_RING, 2, 2, TILE, TILE), bf16),
            pltpu.VMEM((SHORT_RING, 4, TILE, TILE), bf16),
            pltpu.VMEM((RING, 2, TILE, TILE), bf16),
            pltpu.VMEM((RING, 2, TILE, TILE), bf16),
            pltpu.VMEM((RING, TILE, TILE), bf16),
            pltpu.VMEM((RING, TILE, TILE), bf16),
            pltpu.VMEM((RING, TILE // 2, TILE), bf16),
            pltpu.VMEM((RING, TILE // 2, TILE), bf16),
            pltpu.VMEM((RING, TILE // 4, TILE), bf16),
            pltpu.VMEM((TILES, TILE, TILE), bf16),
            dma((3,)), dma((2 * SHORT_RING,)), dma((8,)),
            dma((SHORT_RING,)), dma((SHORT_RING,)),
            dma((2 * RING,)), dma((2 * RING,)), dma((RING,)), dma((RING,)),
            dma((4 * RING,)), dma((4 * RING,)), dma((7,)), dma((7,)), dma((1,)),
            pltpu.VMEM((4, rows, width // 2), bf16),
            pltpu.VMEM((rows, 3 * width // 2), bf16),
            pltpu.VMEM((rows, 3 * width // 2), bf16),
            pltpu.VMEM((rows, width), bf16),
            pltpu.VMEM((TILE, width), bf16),
            pltpu.VMEM((8, width), jnp.float32),
            dma((TAIL_INPUTS + 1,)), dma((4,)), dma((4,)),
        ]
        + [pltpu.VMEM(value.shape, value.dtype) for value in tail],
        compiler_params=params(collective_id=3, has_side_effects=True),
        cost_estimate=pl.CostEstimate(
            flops=2 * 8 * TILES * TILE * TILE * rows,
            bytes_accessed=40 * TILES * TILE * TILE,
            transcendentals=0,
        ),
    )(
        *(operands[w[0]][0] for w in WEIGHTS),
        *(operands[w[0]][i] for i in (1, 2) for w in WEIGHTS if w[0] != QKV_A),
        first, small, *leaving_keys, *tail, gain,
    )
    shares = {w[0]: r for w, r in zip(WEIGHTS, results)}
    return shares, results[count], results[count + 1]


def last_layer_kernel(
    alive, h, gy, r, up0, up1, down0, down1, a0, a1, g0, g1, result, through, total, back
):
    step, steps = pl.program_id(0), pl.num_programs(0)

    @pl.when(step == 0)
    def _():
        total[...] = jnp.zeros_like(total)
        back[...] = jnp.zeros_like(back)

    def chunk(up, down, a_out, g_out):
        u = nn(h[...], up[...])
        square = u * u
        slope = math.sqrt(2.0 / math.pi)
        t = jnp.tanh(slope * (u + 0.044715 * (square * u)))
        a = bf(0.5 * u * (1.0 + t))
        a_out[...] = a
        total[...] += nn(a, down[...])
        rise = 0.5 * (1.0 + t) + 0.5 * u * (1.0 - t * t) * (slope + (3.0 * 0.044715 * slope) * square)
        g = bf(nt(gy[...], down[...]) * rise)
        g_out[...] = g
        back[...] += nt(g, up[...])

    pl.when(step < steps // 2)(lambda: chunk(up0, down0, a0, g0))
    pl.when(step >= steps // 2)(lambda: chunk(up1, down1, a1, g1))

    @pl.when(step == steps - 1)
    def _():
        result[...] = bf(jnp.where(alive[0] > 0, r[...] + total[...], 0.0))
        through[...] = back[...]


def last_layer(alive, h, gy, r, up0, up1, down0, down1):
    rows, width = h.shape
    hidden = up0.shape[1]
    wide = 512
    half = hidden // wide

    def first(i):
        return jnp.minimum(i, half - 1)

    def second(i):
        return jnp.maximum(i - half, 0)

    ups = [pl.BlockSpec((width, wide), lambda i, of=of: (0, of(i))) for of in (first, second)]
    downs = [pl.BlockSpec((wide, width), lambda i, of=of: (of(i), 0)) for of in (first, second)]
    hiddens = [pl.BlockSpec((rows, wide), lambda i, of=of: (0, of(i))) for of in (first, second)]
    kept = pl.BlockSpec((rows, width), lambda i: (0, 0))
    return pl.pallas_call(
        last_layer_kernel,
        grid=(2 * half,),
        in_specs=[pl.BlockSpec(memory_space=pltpu.SMEM), kept, kept, kept] + ups + downs,
        out_specs=hiddens + hiddens + [kept, kept],
        out_shape=[jax.ShapeDtypeStruct((rows, hidden), jnp.bfloat16)] * 4
        + [
            jax.ShapeDtypeStruct((rows, width), jnp.bfloat16),
            jax.ShapeDtypeStruct((rows, width), jnp.float32),
        ],
        scratch_shapes=[pltpu.VMEM((rows, width), jnp.float32)] * 2,
        compiler_params=params(),
        cost_estimate=pl.CostEstimate(
            flops=16 * rows * width * hidden,
            bytes_accessed=8 * width * hidden + 16 * rows * hidden,
            transcendentals=2 * rows * hidden,
        ),
    )(alive, h, gy, r, up0, up1, down0, down1)


def gelu_back(values, grad):
    return jax.vjp(smooth, values)[1](grad)[0]


def block_body(
    layer_input, output_grad, seg_blocks, seg_group, gain_a, wqkv_a, wout_a, gain_b, up_b, down_b,
    gain_c, gain_s, wqkv_c, sqkv_c, wout_c, sout_c, gate_bias, init_states, gain_d, up_d, down_d,
):
    sections, tensors = lax.axis_size(SECTION), lax.axis_size(TENSOR)
    block_count, shard_rows, width = layer_input.shape[1:]
    rows = shard_rows * tensors
    section, tensor = lax.axis_index(SECTION), lax.axis_index(TENSOR)
    block = block_of(section, tensor)
    begins, closes, lively, numbers = layout(
        seg_blocks, seg_group, lax.axis_index(DP), block_count
    )
    alive = lively[block]
    starts = begins[block] | jnp.logical_not(alive)
    ends = closes[block] | jnp.logical_not(alive)
    opening = starts.astype(jnp.int32)[None]
    f32 = jnp.float32
    ga, gb, gc, gd = (v.astype(f32) for v in (gain_a, gain_b, gain_c, gain_d))

    def in_order(own, other):
        low = jnp.where(tensor == 0, own, other)
        high = jnp.where(tensor == 0, other, own)
        return low, high

    def crossed(weight):
        size = weight.shape[0] // sections
        piece = lax.dynamic_slice_in_dim(weight, section * size, size, 0)
        return lax.ppermute(piece, TENSOR, SWAP)

    def flat(weight):
        return jnp.concatenate([weight[:, i] for i in range(3)], axis=1)

    wqkv_a0, wqkv_c0, sqkv_c0 = flat(wqkv_a), flat(wqkv_c), flat(sqkv_c)
    (tokens, before, initial), others = gather(
        layer_input, init_states,
        (wout_a, sout_c, wout_c, wqkv_a0, wqkv_c0, sqkv_c0, up_b, down_b),
    )
    wout_a1, sout_c1, wout_c1, wqkv_a1, wqkv_c1, sqkv_c1, up_b1, down_b1 = others
    tokens, late_up, late_down = lax.optimization_barrier((tokens, up_d, down_d))
    pieces = crossed(late_up), crossed(late_down)
    initial = initial.astype(f32)

    def normed(values, gain):
        return bf(values * inverse_rms(values) * gain)

    def dot(a, b):
        return jnp.dot(a, b, preferred_element_type=f32)

    def dot_t(a, b):
        return lax.dot_general(a, b, (((1,), (1,)), ((), ())), preferred_element_type=f32)

    half = wout_a.shape[0]
    r0 = tokens.astype(f32)
    h0 = normed(r0, ga)
    h_before = normed(before.astype(f32), ga)
    pa0, pa1 = bf(dot(h0, wqkv_a0)), bf(dot(h0, wqkv_a1))
    prior_a0 = bf(dot(h_before, wqkv_a0[:, half:]))
    prior_a1 = bf(dot(h_before, wqkv_a1[:, half:]))
    oa0, lse_a0, oa1, lse_a1 = attend(opening, (pa0, pa1), (prior_a0, prior_a1))
    r1 = r0 + (dot(oa0, wout_a) + dot(oa1, wout_a1))

    h1 = normed(r1, gb)
    ub0, ub1 = dot(h1, up_b), dot(h1, up_b1)
    ab0, ab1 = bf(smooth(ub0)), bf(smooth(ub1))
    ab0, *pieces = lax.optimization_barrier((ab0, *pieces))
    up_d1, down_d1 = (lax.all_gather(piece, SECTION, axis=0, tiled=True) for piece in pieces)
    r2 = r1 + (dot(ab0, down_b) + dot(ab1, down_b1))

    h2 = normed(r2, gc)
    pc0, pc1 = bf(dot(h2, wqkv_c0)), bf(dot(h2, wqkv_c1))
    halo = lax.ppermute(jnp.stack(in_order(pc0[:, half:], pc1[:, half:])), GROUP, TO_NEXT)
    prior_c0, prior_c1 = in_order(halo[0], halo[1])

    retain = jax.nn.sigmoid(gate_bias.astype(f32))[None, :]
    state_gain = gain_s.astype(f32)[None, :]

    def flag(value):
        return jnp.broadcast_to(value.astype(f32), (1, width))

    (
        state_in, hs, ps0, ps1, os0, os1, lse_s, update, state_new, cotangent
    ) = chain(
        initial, flag(starts), state_gain, retain, pc0, pc1,
        sqkv_c0, sqkv_c1, sout_c, sout_c1, output_grad,
    )
    oc0, lse_c0, oc1, lse_c1 = attend(opening, (pc0, pc1), (prior_c0, prior_c1), (ps0, ps1))
    r3 = r2 + (dot(oc0, wout_c) + dot(oc1, wout_c1))

    h3 = normed(r3, gd)
    def feed_back(up_name, down_name, grad, values, h, gain, u0, u1, a0, a1, up0, up1, down0, down1):
        gy = bf(grad)
        g0 = bf(gelu_back(u0, dot_t(gy, down0)))
        g1 = bf(gelu_back(u1, dot_t(gy, down1)))
        operands[down_name] = (gy, a0, a1)
        operands[up_name] = (h, g0, g1)
        through = dot_t(g0, up0) + dot_t(g1, up1)
        back, gain_grad = norm_back(values, gain, through)
        return grad + back, gain_grad

    operands = {}
    grad4 = jnp.where(alive, cotangent.astype(f32), 0.0)
    gy4 = bf(grad4)
    ad0, ad1, gd0, gd1, result, through_d = last_layer(
        alive.astype(jnp.int32)[None], h3, gy4, r3, up_d, up_d1, down_d, down_d1
    )
    operands[DOWN_D] = (gy4, ad0, ad1)
    operands[UP_D] = (h3, gd0, gd1)
    back_d, gain_d_grad = norm_back(r3, gd, through_d)
    grad3 = grad4 + back_d

    gy3 = bf(grad3)
    tok0, tok1 = attend_back(
        opening, (pc0, pc1), (prior_c0, prior_c1), (bf(dot_t(gy3, wout_c)), bf(dot_t(gy3, wout_c1))),
        (oc0, oc1), (lse_c0, lse_c1), (ps0, ps1),
    )

    def halo_back(one, two):
        pair = in_order(
            jnp.concatenate([one[3], one[4]], axis=1), jnp.concatenate([two[3], two[4]], axis=1)
        )
        back = lax.ppermute(jnp.stack(pair), GROUP, TO_PRIOR).astype(f32)
        return in_order(back[0], back[1])

    halo_c0, halo_c1 = halo_back(tok0, tok1)
    first_grad, gs0, gs1, gtok0, gtok1, gup, small, landed = chain_back(
        flag(starts), flag(ends), state_in, update, state_gain, retain, pc0, pc1, ps0, ps1, os0, os1, lse_s,
        tok0[5], tok0[6], tok1[5], tok1[6], sqkv_c0, sqkv_c1, sout_c, sout_c1, result, state_new,
    )

    def projected_back(parts, halo_part, extra=None):
        pair = jnp.concatenate([parts[1], parts[2]], axis=1) + halo_part
        if extra is not None:
            pair = pair + extra
        return jnp.concatenate([parts[0], bf(pair)], axis=1)

    gc0 = projected_back(tok0, halo_c0, gtok0)
    gc1 = projected_back(tok1, halo_c1, gtok1)
    operands[QKV_C] = (h2, gc0, gc1)
    operands[SQKV_C] = (hs, gs0, gs1)
    operands[OUT_C] = (gy3, oc0, oc1)
    operands[SOUT_C] = (gup, os0, os1)
    def through_qkv(g, w):
        return dot_t(g, w)

    back_c, gain_c_grad = norm_back(
        r2, gc, through_qkv(gc0, wqkv_c0) + through_qkv(gc1, wqkv_c1)
    )
    grad2 = grad3 + back_c

    grad1, gain_b_grad = feed_back(
        UP_B, DOWN_B, grad2, r1, h1, gb, ub0, ub1, ab0, ab1, up_b, up_b1, down_b, down_b1
    )

    gy1 = bf(grad1)
    att0, att1 = attend_back(
        opening, (pa0, pa1), (prior_a0, prior_a1), (bf(dot_t(gy1, wout_a)), bf(dot_t(gy1, wout_a1))),
        (oa0, oa1), (lse_a0, lse_a1),
    )
    operands[QKV_A] = (h0,)
    operands[OUT_A] = (gy1, oa0, oa1)
    smalls = jnp.stack(
        [jnp.zeros_like(gain_b_grad), gain_b_grad, gain_c_grad, small[0], gain_d_grad, small[1]]
    )
    shares, last_share, landed_input = weight_grads(
        operands, first_grad, jnp.pad(bf(smalls), ((0, TILE - 6), (0, 0))), (*att0[3:5], *att1[3:5]),
        (*att0[:3], *att1[:3], wqkv_a0, wqkv_a1, tokens, grad1), ga[None, :],
    )
    small_share = last_share[1].astype(f32)
    chosen = (
        (numbers[:, None] == jnp.arange(SLOTS, dtype=jnp.int32)[None, :])
        & (closes & lively)[:, None]
    )
    state_tiles = landed[1].astype(f32)
    final_share = jnp.stack(
        [
            jnp.sum(jnp.where(chosen[:, i, None, None], state_tiles, 0.0), axis=0)
            for i in range(SLOTS)
        ],
        axis=1,
    )

    def share(name):
        value = shares[name].astype(f32)
        return value.reshape(value.shape[0], 3, -1) if name in (QKV_A, QKV_C, SQKV_C) else value

    return (
        landed[0][None],
        final_share[None],
        landed_input.astype(f32),
        small_share[0],
        share(QKV_A),
        share(OUT_A),
        small_share[1],
        share(UP_B),
        share(DOWN_B),
        small_share[2],
        small_share[3],
        share(QKV_C),
        share(SQKV_C),
        share(OUT_C),
        share(SOUT_C),
        small_share[5],
        last_share[0].astype(f32),
        small_share[4],
        share(UP_D),
        share(DOWN_D),
    )


def chosen(*arrays):
    devices = (lax.axis_size(SECTION), lax.axis_size(TENSOR), lax.axis_size(DP))
    if devices == (4, 2, 4) and arrays[0].shape[1] == 8:
        return block_body(*arrays)
    return relay_body(*arrays)


def solution(mesh):
    in_specs = (
        P(DP, None, TENSOR, None),
        P(DP, None, TENSOR, None),
        P(),
        P(),
        P(),
        P(None, None, TENSOR),
        P(TENSOR, None),
        P(),
        P(None, TENSOR),
        P(TENSOR, None),
        P(),
        P(),
        P(None, None, TENSOR),
        P(None, None, TENSOR),
        P(TENSOR, None),
        P(TENSOR, None),
        P(),
        P(TENSOR, None),
        P(),
        P(None, TENSOR),
        P(TENSOR, None),
    )
    out_specs = (
        P(DP, None, TENSOR, SECTION),
        P(DP, TENSOR, None, SECTION),
        P(DP, None, TENSOR, SECTION),
        P(SECTION),
        P(SECTION, None, TENSOR),
        P(TENSOR, SECTION),
        P(SECTION),
        P(SECTION, TENSOR),
        P(TENSOR, SECTION),
        P(SECTION),
        P(SECTION),
        P(SECTION, None, TENSOR),
        P(SECTION, None, TENSOR),
        P(TENSOR, SECTION),
        P(TENSOR, SECTION),
        P(SECTION),
        P(TENSOR, SECTION),
        P(SECTION),
        P(SECTION, TENSOR),
        P(TENSOR, SECTION),
    )
    return jax.shard_map(chosen, mesh=mesh, in_specs=in_specs, out_specs=out_specs, check_vma=False)
```

```python
import functools
import math

import jax
import jax.numpy as jnp
from jax import lax
from jax.experimental import pallas as pl
from jax.experimental.pallas import tpu as pltpu
from jax.sharding import PartitionSpec as P

SECTION, DP, TENSOR = "section", "dp", "tensor"
HEAD_DIM = 128
SLOTS = 3


EPSILON = 1e-06
NEGATIVE = -1e30


def shifted(value, axis, by):
    devices = lax.axis_size(axis)
    pairs = [(i, i + by) for i in range(devices) if 0 <= i + by < devices]
    return lax.ppermute(value, axis, pairs)


def for_sending(value):
    return jax.tree.map(lambda a: a.astype(jnp.bfloat16) if a.dtype == jnp.float32 else a, value)


def layout(seg_blocks, seg_group, group_index, block_count):
    mine = seg_group == group_index
    lengths = jnp.where(mine, seg_blocks, 0)
    offsets = jnp.cumsum(lengths) - lengths
    ranking = jnp.cumsum(mine.astype(jnp.int32)) - mine.astype(jnp.int32)
    blocks = jnp.arange(block_count, dtype=jnp.int32)[None, :]
    inside = mine[:, None] & (blocks >= offsets[:, None]) & (blocks < (offsets + lengths)[:, None])
    begins = jnp.any(inside & (blocks == offsets[:, None]), axis=0)
    closes = jnp.any(inside & (blocks == (offsets + lengths - 1)[:, None]), axis=0)
    lively = jnp.any(inside, axis=0)
    numbers = jnp.sum(jnp.where(inside, ranking[:, None], 0), axis=0)
    return (begins, closes, lively, numbers)


def inverse_rms(values):
    return lax.rsqrt(jnp.mean(values * values, axis=-1, keepdims=True) + EPSILON)


def norm_back(values, gain, grad_normed):
    factor = inverse_rms(values)
    scaled = values * factor
    grad_scaled = grad_normed * gain
    grad_values = factor * (
        grad_scaled - scaled * jnp.mean(grad_scaled * scaled, axis=-1, keepdims=True)
    )
    return (grad_values, jnp.sum(grad_normed * scaled, axis=0))


def smooth(values):
    return jax.nn.gelu(values, approximate=True)


def split_heads(rows_in):
    return rows_in.reshape(rows_in.shape[0], -1, HEAD_DIM)


def attend_forward(queries, key_rows, value_rows, allowed):
    score_scale = 1.0 / math.sqrt(HEAD_DIM)
    scores = (
        jnp.einsum("rhd,khd->hrk", queries, key_rows, preferred_element_type=jnp.float32)
        * score_scale
    )
    scores = jnp.where(allowed[None], scores, NEGATIVE)
    largest = jnp.max(scores, axis=-1, keepdims=True)
    totals = jnp.sum(jnp.exp(scores - largest), axis=-1, keepdims=True)
    log_total = largest + jnp.log(totals)
    weights = jnp.exp(scores - log_total).astype(jnp.bfloat16)
    mixture_output = jnp.einsum(
        "hrk,khd->rhd", weights, value_rows, preferred_element_type=jnp.float32
    )
    return (mixture_output, log_total[..., 0])


def attend_backward(queries, key_rows, value_rows, allowed, log_total, grad_mixture):
    score_scale = 1.0 / math.sqrt(HEAD_DIM)
    scores = (
        jnp.einsum("rhd,khd->hrk", queries, key_rows, preferred_element_type=jnp.float32)
        * score_scale
    )
    scores = jnp.where(allowed[None], scores, NEGATIVE)
    weights = jnp.exp(scores - log_total[..., None])
    rounded = weights.astype(jnp.bfloat16)
    grad_weights = jnp.einsum(
        "rhd,khd->hrk", grad_mixture, value_rows, preferred_element_type=jnp.float32
    )
    grad_values = jnp.einsum(
        "hrk,rhd->khd", rounded, grad_mixture, preferred_element_type=jnp.float32
    )
    inner_sum = jnp.sum(weights * grad_weights, axis=-1, keepdims=True)
    grad_scores = (weights * (grad_weights - inner_sum)).astype(jnp.bfloat16)
    grad_queries = (
        jnp.einsum("hrk,khd->rhd", grad_scores, key_rows, preferred_element_type=jnp.float32)
        * score_scale
    )
    grad_keys = (
        jnp.einsum("hrk,rhd->khd", grad_scores, queries, preferred_element_type=jnp.float32)
        * score_scale
    )
    return (grad_queries, grad_keys, grad_values)


def place_row(store, position, value, active_tick):
    previous = lax.dynamic_index_in_dim(store, position, 0, False)
    return lax.dynamic_update_index_in_dim(
        store, jnp.where(active_tick, value, previous), position, 0
    )


def renewed(grad_sums, active_tick, changes):
    return tuple(
        (
            total + jnp.where(active_tick, changes[position], 0.0) if position in changes else total
            for position, total in enumerate(grad_sums)
        )
    )


def relay_body(
    layer_input,
    output_grad,
    seg_blocks,
    seg_group,
    gain_a,
    wqkv_a,
    wout_a,
    gain_b,
    up_b,
    down_b,
    gain_c,
    gain_s,
    wqkv_c,
    sqkv_c,
    wout_c,
    sout_c,
    gate_bias,
    init_states,
    gain_d,
    up_d,
    down_d,
):
    block_count = layer_input.shape[1]
    shard_rows = layer_input.shape[2]
    model_width = layer_input.shape[3]
    tensor_count = lax.axis_size(TENSOR)
    token_rows = shard_rows * tensor_count
    state_shard = init_states.shape[0]
    state_count = state_shard * tensor_count
    local_width = wqkv_a.shape[2]
    local_heads = local_width // HEAD_DIM
    section_index = lax.axis_index(SECTION)
    group_index = lax.axis_index(DP)
    on_cell_section = section_index == 2
    begins, closes, lively, numbers = layout(seg_blocks, seg_group, group_index, block_count)
    token_gains = jnp.stack([gain_a, gain_b, gain_c, gain_d]).astype(jnp.float32)
    state_gain = gain_s.astype(jnp.float32)
    retain = jax.nn.sigmoid(gate_bias.astype(jnp.float32))
    initial = init_states.astype(jnp.float32)
    empty_state = jnp.zeros((state_count, model_width), jnp.float32)
    empty_token_store = jnp.zeros((token_rows, 4, local_width), jnp.bfloat16)
    empty_state_store = jnp.zeros((state_count, 4, local_width), jnp.bfloat16)
    empty_token_lse = jnp.zeros((local_heads, token_rows), jnp.float32)
    empty_state_lse = jnp.zeros((local_heads, state_count), jnp.float32)
    empty_carry = jnp.zeros((token_rows, local_width), jnp.float32)
    every_key = jnp.ones((state_count, token_rows + state_count), bool)
    state_keys_all = jnp.ones((token_rows, state_count), bool)

    def token_masks(opening):
        later_keys = lax.broadcasted_iota(
            jnp.int32, (token_rows, token_rows), 1
        ) > lax.broadcasted_iota(jnp.int32, (token_rows, token_rows), 0)
        return (jnp.logical_and(later_keys, jnp.logical_not(opening)), jnp.logical_not(later_keys))

    def plain_forward(normed_tok, normed_st, prior_block, opening):
        projected = jnp.einsum(
            "rd,dcn->rcn", normed_tok, wqkv_a, preferred_element_type=jnp.float32
        ).astype(jnp.bfloat16)
        reach_prior, reach_current = token_masks(opening)
        allowed = jnp.concatenate([reach_prior, reach_current], axis=1)
        key_rows = jnp.concatenate([prior_block[:, 1], projected[:, 1]], axis=0)
        value_rows = jnp.concatenate([prior_block[:, 2], projected[:, 2]], axis=0)
        mixture_output, token_lse = attend_forward(
            split_heads(projected[:, 0]), split_heads(key_rows), split_heads(value_rows), allowed
        )
        mixture_output = mixture_output.reshape(token_rows, local_width).astype(jnp.bfloat16)
        branch = jnp.dot(mixture_output, wout_a, preferred_element_type=jnp.float32)
        stored = jnp.concatenate([projected, mixture_output[:, None]], axis=1)
        return (branch, empty_state, stored, empty_state_store, token_lse, empty_state_lse)

    def feed_forward(up_projection_weight, down_projection_weight):

        def forward_fn(normed_tok, normed_st, prior_block, opening):
            hidden_rows = jnp.dot(
                normed_tok, up_projection_weight, preferred_element_type=jnp.float32
            )
            active_flags = smooth(hidden_rows).astype(jnp.bfloat16)
            branch = jnp.dot(
                active_flags, down_projection_weight, preferred_element_type=jnp.float32
            )
            return (
                branch,
                empty_state,
                empty_token_store,
                empty_state_store,
                empty_token_lse,
                empty_state_lse,
            )

        return forward_fn

    def recurrent_forward(normed_tok, normed_st, prior_block, opening):
        projected = jnp.einsum(
            "rd,dcn->rcn", normed_tok, wqkv_c, preferred_element_type=jnp.float32
        ).astype(jnp.bfloat16)
        state_proj = jnp.einsum(
            "sd,dcn->scn", normed_st, sqkv_c, preferred_element_type=jnp.float32
        ).astype(jnp.bfloat16)
        reach_prior, reach_current = token_masks(opening)
        allowed = jnp.concatenate([reach_prior, reach_current, state_keys_all], axis=1)
        token_keys = jnp.concatenate([prior_block[:, 1], projected[:, 1], state_proj[:, 1]], axis=0)
        token_values = jnp.concatenate(
            [prior_block[:, 2], projected[:, 2], state_proj[:, 2]], axis=0
        )
        token_mixture, token_lse = attend_forward(
            split_heads(projected[:, 0]),
            split_heads(token_keys),
            split_heads(token_values),
            allowed,
        )
        state_keys = jnp.concatenate([projected[:, 1], state_proj[:, 1]], axis=0)
        state_values = jnp.concatenate([projected[:, 2], state_proj[:, 2]], axis=0)
        state_mixture, state_lse = attend_forward(
            split_heads(state_proj[:, 0]),
            split_heads(state_keys),
            split_heads(state_values),
            every_key,
        )
        token_mixture = token_mixture.reshape(token_rows, local_width).astype(jnp.bfloat16)
        state_mixture = state_mixture.reshape(state_count, local_width).astype(jnp.bfloat16)
        branch = jnp.dot(token_mixture, wout_c, preferred_element_type=jnp.float32)
        update_term = jnp.dot(state_mixture, sout_c, preferred_element_type=jnp.float32)
        stored = jnp.concatenate([projected, token_mixture[:, None]], axis=1)
        state_stored = jnp.concatenate([state_proj, state_mixture[:, None]], axis=1)
        return (branch, update_term, stored, state_stored, token_lse, state_lse)

    def plain_backward(
        grad_tok,
        grad_st,
        normed_tok,
        normed_st,
        tok_block,
        st_block,
        prior_block,
        token_lse,
        state_lse,
        opening,
        carry_keys,
        carry_values,
        grad_sums,
        active_tick,
    ):
        reach_prior, reach_current = token_masks(opening)
        allowed = jnp.concatenate([reach_prior, reach_current], axis=1)
        key_rows = jnp.concatenate([prior_block[:, 1], tok_block[:, 1]], axis=0)
        value_rows = jnp.concatenate([prior_block[:, 2], tok_block[:, 2]], axis=0)
        weight_out = jnp.einsum(
            "rn,rd->nd", tok_block[:, 3], grad_tok, preferred_element_type=jnp.float32
        )
        grad_mixture = jnp.einsum(
            "rd,nd->rn", grad_tok, wout_a, preferred_element_type=jnp.float32
        ).astype(jnp.bfloat16)
        grad_query, grad_keys, grad_values = attend_backward(
            split_heads(tok_block[:, 0]),
            split_heads(key_rows),
            split_heads(value_rows),
            allowed,
            token_lse,
            split_heads(grad_mixture),
        )
        grad_query = grad_query.reshape(token_rows, local_width)
        grad_keys = grad_keys.reshape(2 * token_rows, local_width)
        grad_values = grad_values.reshape(2 * token_rows, local_width)
        grad_proj = jnp.stack(
            [
                grad_query,
                grad_keys[token_rows:] + carry_keys,
                grad_values[token_rows:] + carry_values,
            ],
            axis=1,
        ).astype(jnp.bfloat16)
        weight_in = jnp.einsum(
            "rd,rcn->dcn", normed_tok, grad_proj, preferred_element_type=jnp.float32
        )
        grad_normed = jnp.einsum(
            "rcn,dcn->rd", grad_proj, wqkv_a, preferred_element_type=jnp.float32
        )
        return (
            grad_normed,
            empty_state,
            grad_keys[:token_rows],
            grad_values[:token_rows],
            renewed(grad_sums, active_tick, {0: weight_in, 1: weight_out}),
        )

    def feed_backward(up_projection_weight, down_projection_weight, up_slot, down_slot):

        def backward_fn(
            grad_tok,
            grad_st,
            normed_tok,
            normed_st,
            tok_block,
            st_block,
            prior_block,
            token_lse,
            state_lse,
            opening,
            carry_keys,
            carry_values,
            grad_sums,
            active_tick,
        ):
            hidden_rows = jnp.dot(
                normed_tok, up_projection_weight, preferred_element_type=jnp.float32
            )
            active_flags, gelu_back = jax.vjp(smooth, hidden_rows)
            weight_down = jnp.einsum(
                "rf,rd->fd",
                active_flags.astype(jnp.bfloat16),
                grad_tok,
                preferred_element_type=jnp.float32,
            )
            grad_active = jnp.einsum(
                "rd,fd->rf", grad_tok, down_projection_weight, preferred_element_type=jnp.float32
            )
            grad_hidden = gelu_back(grad_active)[0].astype(jnp.bfloat16)
            weight_up = jnp.einsum(
                "rd,rf->df", normed_tok, grad_hidden, preferred_element_type=jnp.float32
            )
            grad_normed = jnp.einsum(
                "rf,df->rd", grad_hidden, up_projection_weight, preferred_element_type=jnp.float32
            )
            return (
                grad_normed,
                empty_state,
                empty_carry,
                empty_carry,
                renewed(grad_sums, active_tick, {up_slot: weight_up, down_slot: weight_down}),
            )

        return backward_fn

    def recurrent_backward(
        grad_tok,
        grad_st,
        normed_tok,
        normed_st,
        tok_block,
        st_block,
        prior_block,
        token_lse,
        state_lse,
        opening,
        carry_keys,
        carry_values,
        grad_sums,
        active_tick,
    ):
        reach_prior, reach_current = token_masks(opening)
        allowed = jnp.concatenate([reach_prior, reach_current, state_keys_all], axis=1)
        token_keys = jnp.concatenate([prior_block[:, 1], tok_block[:, 1], st_block[:, 1]], axis=0)
        token_values = jnp.concatenate([prior_block[:, 2], tok_block[:, 2], st_block[:, 2]], axis=0)
        state_keys = jnp.concatenate([tok_block[:, 1], st_block[:, 1]], axis=0)
        state_values = jnp.concatenate([tok_block[:, 2], st_block[:, 2]], axis=0)
        weight_out = jnp.einsum(
            "rn,rd->nd", tok_block[:, 3], grad_tok, preferred_element_type=jnp.float32
        )
        weight_state_out = jnp.einsum(
            "sn,sd->nd", st_block[:, 3], grad_st, preferred_element_type=jnp.float32
        )
        grad_token_mixture = jnp.einsum(
            "rd,nd->rn", grad_tok, wout_c, preferred_element_type=jnp.float32
        ).astype(jnp.bfloat16)
        grad_state_mixture = jnp.einsum(
            "sd,nd->sn", grad_st, sout_c, preferred_element_type=jnp.float32
        ).astype(jnp.bfloat16)
        grad_query, grad_keys, grad_values = attend_backward(
            split_heads(tok_block[:, 0]),
            split_heads(token_keys),
            split_heads(token_values),
            allowed,
            token_lse,
            split_heads(grad_token_mixture),
        )
        state_query, state_grad_keys, state_grad_values = attend_backward(
            split_heads(st_block[:, 0]),
            split_heads(state_keys),
            split_heads(state_values),
            every_key,
            state_lse,
            split_heads(grad_state_mixture),
        )
        grad_query = grad_query.reshape(token_rows, local_width)
        grad_keys = grad_keys.reshape(2 * token_rows + state_count, local_width)
        grad_values = grad_values.reshape(2 * token_rows + state_count, local_width)
        state_query = state_query.reshape(state_count, local_width)
        state_grad_keys = state_grad_keys.reshape(token_rows + state_count, local_width)
        state_grad_values = state_grad_values.reshape(token_rows + state_count, local_width)
        own_keys = (
            grad_keys[token_rows : 2 * token_rows] + state_grad_keys[:token_rows] + carry_keys
        )
        own_values = (
            grad_values[token_rows : 2 * token_rows] + state_grad_values[:token_rows] + carry_values
        )
        cell_keys = grad_keys[2 * token_rows :] + state_grad_keys[token_rows:]
        cell_values = grad_values[2 * token_rows :] + state_grad_values[token_rows:]
        grad_proj = jnp.stack([grad_query, own_keys, own_values], axis=1).astype(jnp.bfloat16)
        grad_state_proj = jnp.stack([state_query, cell_keys, cell_values], axis=1).astype(
            jnp.bfloat16
        )
        weight_in = jnp.einsum(
            "rd,rcn->dcn", normed_tok, grad_proj, preferred_element_type=jnp.float32
        )
        weight_state_in = jnp.einsum(
            "sd,scn->dcn", normed_st, grad_state_proj, preferred_element_type=jnp.float32
        )
        grad_normed = jnp.einsum(
            "rcn,dcn->rd", grad_proj, wqkv_c, preferred_element_type=jnp.float32
        )
        grad_state_normed = jnp.einsum(
            "scn,dcn->sd", grad_state_proj, sqkv_c, preferred_element_type=jnp.float32
        )
        changes = {4: weight_in, 5: weight_state_in, 6: weight_out, 7: weight_state_out}
        return (
            grad_normed,
            grad_state_normed,
            grad_keys[:token_rows],
            grad_values[:token_rows],
            renewed(grad_sums, active_tick, changes),
        )

    forward_branches = [
        plain_forward,
        feed_forward(up_b, down_b),
        recurrent_forward,
        feed_forward(up_d, down_d),
    ]
    backward_branches = [
        plain_backward,
        feed_backward(up_b, down_b, 2, 3),
        recurrent_backward,
        feed_backward(up_d, down_d, 8, 9),
    ]

    def forward_tick(tick_number, carried):
        (
            received,
            state_carry,
            tok_normed,
            st_normed,
            tok_stored,
            st_stored,
            tok_lse_all,
            st_lse_all,
            entered,
            state_entered,
            updates,
            leaving_rows,
            finals,
        ) = carried
        block_number = tick_number - section_index
        active_tick = (block_number >= 0) & (block_number < block_count)
        block_index = jnp.clip(block_number, 0, block_count - 1)
        opening = begins[block_index]
        entering = jnp.where(
            section_index == 0, layer_input[0, block_index].astype(jnp.float32), received
        )
        state_in = jnp.where(opening, initial, state_carry)
        token_gain = token_gains[section_index]
        normed_shard = (entering * inverse_rms(entering) * token_gain).astype(jnp.bfloat16)
        state_normed_shard = (state_in * inverse_rms(state_in) * state_gain).astype(jnp.bfloat16)
        normed_tok, normed_st = (
            lax.all_gather(normed_shard, TENSOR, axis=0, tiled=True),
            lax.all_gather(state_normed_shard, TENSOR, axis=0, tiled=True),
        )
        prior_block = tok_stored[jnp.maximum(block_index - 1, 0)]
        branch, update_term, stored, state_stored, token_lse, state_lse = lax.switch(
            section_index, forward_branches, normed_tok, normed_st, prior_block, opening
        )
        branch_shard, update_shard = (
            lax.psum_scatter(
                branch.astype(jnp.bfloat16), TENSOR, scatter_dimension=0, tiled=True
            ).astype(jnp.float32),
            lax.psum_scatter(
                update_term.astype(jnp.bfloat16), TENSOR, scatter_dimension=0, tiled=True
            ).astype(jnp.float32),
        )
        leaving = entering + branch_shard
        state_new = retain * state_in + (1.0 - retain) * update_shard
        tok_normed = place_row(tok_normed, block_index, normed_tok, active_tick)
        st_normed = place_row(st_normed, block_index, normed_st, active_tick)
        tok_stored = place_row(tok_stored, block_index, stored, active_tick)
        st_stored = place_row(st_stored, block_index, state_stored, active_tick)
        tok_lse_all = place_row(tok_lse_all, block_index, token_lse, active_tick)
        st_lse_all = place_row(st_lse_all, block_index, state_lse, active_tick)
        entered = place_row(entered, block_index, entering, active_tick)
        state_entered = place_row(state_entered, block_index, state_in, active_tick)
        updates = place_row(updates, block_index, update_shard, active_tick)
        leaving_rows = place_row(leaving_rows, block_index, leaving, active_tick)
        on_cell = active_tick & on_cell_section
        state_carry = jnp.where(on_cell, state_new, state_carry)
        keep_final = on_cell & closes[block_index] & lively[block_index]
        slot_hit = (jnp.arange(SLOTS, dtype=jnp.int32) == numbers[block_index])[
            None, :, None
        ] & keep_final
        finals = jnp.where(slot_hit, state_new[:, None, :], finals)
        received = shifted(leaving.astype(jnp.bfloat16), SECTION, 1).astype(leaving.dtype)
        return (
            received,
            state_carry,
            tok_normed,
            st_normed,
            tok_stored,
            st_stored,
            tok_lse_all,
            st_lse_all,
            entered,
            state_entered,
            updates,
            leaving_rows,
            finals,
        )

    forward_start = (
        jnp.zeros((shard_rows, model_width), jnp.float32),
        jnp.zeros((state_shard, model_width), jnp.float32),
        jnp.zeros((block_count, token_rows, model_width), jnp.bfloat16),
        jnp.zeros((block_count, state_count, model_width), jnp.bfloat16),
        jnp.zeros((block_count, token_rows, 4, local_width), jnp.bfloat16),
        jnp.zeros((block_count, state_count, 4, local_width), jnp.bfloat16),
        jnp.zeros((block_count, local_heads, token_rows), jnp.float32),
        jnp.zeros((block_count, local_heads, state_count), jnp.float32),
        jnp.zeros((block_count, shard_rows, model_width), jnp.float32),
        jnp.zeros((block_count, state_shard, model_width), jnp.float32),
        jnp.zeros((block_count, state_shard, model_width), jnp.float32),
        jnp.zeros((block_count, shard_rows, model_width), jnp.float32),
        jnp.zeros((state_shard, SLOTS, model_width), jnp.float32),
    )
    (
        _,
        _,
        tok_normed,
        st_normed,
        tok_stored,
        st_stored,
        tok_lse_all,
        st_lse_all,
        entered,
        state_entered,
        updates,
        leaving_rows,
        finals,
    ) = lax.fori_loop(0, block_count + 3, forward_tick, forward_start)
    gain_rows_of_section = jnp.array([0, 1, 2, 4], dtype=jnp.int32)
    small_rows = jnp.arange(6, dtype=jnp.int32)[:, None]

    def backward_tick(tick_number, carried):
        (
            received,
            state_grad,
            carry_keys,
            carry_values,
            grad_sums,
            smalls,
            initial_grad,
            input_rows,
        ) = carried
        block_number = block_count - 1 - tick_number + 3 - section_index
        active_tick = (block_number >= 0) & (block_number < block_count)
        block_index = jnp.clip(block_number, 0, block_count - 1)
        opening = begins[block_index]
        arriving = jnp.where(
            section_index == 3,
            output_grad[0, block_index].astype(jnp.float32)
            * lively[block_index].astype(jnp.float32),
            received,
        )
        update_grad = (1.0 - retain) * state_grad
        grad_tok, grad_st = (
            lax.all_gather(arriving.astype(jnp.bfloat16), TENSOR, axis=0, tiled=True),
            lax.all_gather(update_grad.astype(jnp.bfloat16), TENSOR, axis=0, tiled=True),
        )
        grad_normed_tok, grad_normed_st, prior_keys, prior_values, grad_sums = lax.switch(
            section_index,
            backward_branches,
            grad_tok,
            grad_st,
            tok_normed[block_index],
            st_normed[block_index],
            tok_stored[block_index],
            st_stored[block_index],
            tok_stored[jnp.maximum(block_index - 1, 0)],
            tok_lse_all[block_index],
            st_lse_all[block_index],
            opening,
            carry_keys,
            carry_values,
            grad_sums,
            active_tick,
        )
        tok_shard, st_shard = (
            lax.psum_scatter(
                grad_normed_tok.astype(jnp.bfloat16), TENSOR, scatter_dimension=0, tiled=True
            ).astype(jnp.float32),
            lax.psum_scatter(
                grad_normed_st.astype(jnp.bfloat16), TENSOR, scatter_dimension=0, tiled=True
            ).astype(jnp.float32),
        )
        grad_entering, token_gain_term = norm_back(
            entered[block_index], token_gains[section_index], tok_shard
        )
        leaving_grad = arriving + grad_entering
        state_in = state_entered[block_index]
        grad_state_norm, state_gain_term = norm_back(state_in, state_gain, st_shard)
        grad_state_in = retain * state_grad + grad_state_norm
        bias_term = (
            jnp.sum(state_grad * (state_in - updates[block_index]), axis=0)
            * retain
            * (1.0 - retain)
        )
        on_cell = active_tick & on_cell_section
        gain_part = (small_rows == gain_rows_of_section[section_index]).astype(
            jnp.float32
        ) * token_gain_term[None, :]
        cell_part = (small_rows == 3).astype(jnp.float32) * state_gain_term[None, :] + (
            small_rows == 5
        ).astype(jnp.float32) * bias_term[None, :]
        smalls = (
            smalls + jnp.where(active_tick, gain_part, 0.0) + jnp.where(on_cell, cell_part, 0.0)
        )
        initial_grad = initial_grad + jnp.where(on_cell & opening, grad_state_in, 0.0)
        state_grad = jnp.where(on_cell, jnp.where(opening, 0.0, grad_state_in), state_grad)
        carry_keys = jnp.where(active_tick, prior_keys, carry_keys)
        carry_values = jnp.where(active_tick, prior_values, carry_values)
        input_rows = place_row(input_rows, block_index, leaving_grad, active_tick)
        received = shifted(for_sending(leaving_grad), SECTION, -1).astype(leaving_grad.dtype)
        return (
            received,
            state_grad,
            carry_keys,
            carry_values,
            grad_sums,
            smalls,
            initial_grad,
            input_rows,
        )

    zero_grads = (
        jnp.zeros(wqkv_a.shape, jnp.float32),
        jnp.zeros(wout_a.shape, jnp.float32),
        jnp.zeros(up_b.shape, jnp.float32),
        jnp.zeros(down_b.shape, jnp.float32),
        jnp.zeros(wqkv_c.shape, jnp.float32),
        jnp.zeros(sqkv_c.shape, jnp.float32),
        jnp.zeros(wout_c.shape, jnp.float32),
        jnp.zeros(sout_c.shape, jnp.float32),
        jnp.zeros(up_d.shape, jnp.float32),
        jnp.zeros(down_d.shape, jnp.float32),
    )
    backward_start = (
        jnp.zeros((shard_rows, model_width), jnp.float32),
        jnp.zeros((state_shard, model_width), jnp.float32),
        empty_carry,
        empty_carry,
        zero_grads,
        jnp.zeros((6, model_width), jnp.float32),
        jnp.zeros((state_shard, model_width), jnp.float32),
        jnp.zeros((block_count, shard_rows, model_width), jnp.float32),
    )
    _, _, _, _, grad_sums, smalls, initial_grad, input_rows = lax.fori_loop(
        0, block_count + 3, backward_tick, backward_start
    )
    out_term = jnp.where(
        section_index == 3, leaving_rows * lively[:, None, None].astype(jnp.float32), 0.0
    )[None]
    input_term = jnp.where(section_index == 0, input_rows, 0.0)[None]
    final_term = jnp.where(section_index == 2, finals, 0.0)[None]
    out_share, input_share, final_share = (
        lax.psum_scatter(
            out_term.astype(jnp.bfloat16), SECTION, scatter_dimension=3, tiled=True
        ).astype(jnp.float32),
        lax.psum_scatter(
            input_term.astype(jnp.bfloat16), SECTION, scatter_dimension=3, tiled=True
        ).astype(jnp.float32),
        lax.psum_scatter(
            final_term.astype(jnp.bfloat16), SECTION, scatter_dimension=3, tiled=True
        ).astype(jnp.float32),
    )
    (
        grad_qkv_a,
        grad_out_a,
        grad_upper_b,
        grad_lower_b,
        grad_qkv_c,
        grad_state_qkv,
        grad_out_c,
        grad_state_out,
        grad_upper_d,
        grad_lower_d,
    ) = grad_sums
    totals = (
        lax.psum(grad_qkv_a.astype(jnp.bfloat16), DP).astype(jnp.float32),
        lax.psum(grad_out_a.astype(jnp.bfloat16), DP).astype(jnp.float32),
        lax.psum(grad_upper_b.astype(jnp.bfloat16), DP).astype(jnp.float32),
        lax.psum(grad_lower_b.astype(jnp.bfloat16), DP).astype(jnp.float32),
        lax.psum(grad_qkv_c.astype(jnp.bfloat16), DP).astype(jnp.float32),
        lax.psum(grad_state_qkv.astype(jnp.bfloat16), DP).astype(jnp.float32),
        lax.psum(grad_out_c.astype(jnp.bfloat16), DP).astype(jnp.float32),
        lax.psum(grad_state_out.astype(jnp.bfloat16), DP).astype(jnp.float32),
        lax.psum(grad_upper_d.astype(jnp.bfloat16), DP).astype(jnp.float32),
        lax.psum(grad_lower_d.astype(jnp.bfloat16), DP).astype(jnp.float32),
        lax.psum(initial_grad.astype(jnp.bfloat16), DP).astype(jnp.float32),
    )
    small_total = lax.psum(smalls, (DP, TENSOR))
    shares = (
        lax.psum_scatter(
            totals[0].astype(jnp.bfloat16), SECTION, scatter_dimension=0, tiled=True
        ).astype(jnp.float32),
        lax.psum_scatter(
            totals[1].astype(jnp.bfloat16), SECTION, scatter_dimension=1, tiled=True
        ).astype(jnp.float32),
        lax.psum_scatter(
            totals[2].astype(jnp.bfloat16), SECTION, scatter_dimension=0, tiled=True
        ).astype(jnp.float32),
        lax.psum_scatter(
            totals[3].astype(jnp.bfloat16), SECTION, scatter_dimension=1, tiled=True
        ).astype(jnp.float32),
        lax.psum_scatter(
            totals[4].astype(jnp.bfloat16), SECTION, scatter_dimension=0, tiled=True
        ).astype(jnp.float32),
        lax.psum_scatter(
            totals[5].astype(jnp.bfloat16), SECTION, scatter_dimension=0, tiled=True
        ).astype(jnp.float32),
        lax.psum_scatter(
            totals[6].astype(jnp.bfloat16), SECTION, scatter_dimension=1, tiled=True
        ).astype(jnp.float32),
        lax.psum_scatter(
            totals[7].astype(jnp.bfloat16), SECTION, scatter_dimension=1, tiled=True
        ).astype(jnp.float32),
        lax.psum_scatter(
            totals[8].astype(jnp.bfloat16), SECTION, scatter_dimension=0, tiled=True
        ).astype(jnp.float32),
        lax.psum_scatter(
            totals[9].astype(jnp.bfloat16), SECTION, scatter_dimension=1, tiled=True
        ).astype(jnp.float32),
        lax.psum_scatter(
            totals[10].astype(jnp.bfloat16), SECTION, scatter_dimension=1, tiled=True
        ).astype(jnp.float32),
        lax.psum_scatter(
            small_total.astype(jnp.bfloat16), SECTION, scatter_dimension=1, tiled=True
        ).astype(jnp.float32),
    )
    small_share = shares[11]
    return (
        out_share.astype(jnp.bfloat16),
        final_share,
        input_share,
        small_share[0],
        shares[0],
        shares[1],
        small_share[1],
        shares[2],
        shares[3],
        small_share[2],
        small_share[3],
        shares[4],
        shares[5],
        shares[6],
        shares[7],
        small_share[5],
        shares[10],
        small_share[4],
        shares[8],
        shares[9],
    )


CHAIN = 4
MESH = pl.DeviceIdType.MESH
SCALE = 1.0 / math.sqrt(HEAD_DIM)
LOG2_SCALE = SCALE * math.log2(math.e)
ALL_AXES = (SECTION, DP, TENSOR)
GROUP = (SECTION, TENSOR)
VMEM_BYTES = 60 * 1024 * 1024
CHUNK = 256


def block_of(section, tensor):
    high = section // 2
    return 2 * (2 * high + (tensor + high) % 2) + section % 2


DEVICE_OF_BLOCK = [0] * 8
for _section in range(4):
    for _tensor in range(2):
        DEVICE_OF_BLOCK[block_of(_section, _tensor)] = 2 * _section + _tensor
TO_NEXT = [(DEVICE_OF_BLOCK[b], DEVICE_OF_BLOCK[b + 1]) for b in range(7)]
TO_PRIOR = [(there, here) for here, there in TO_NEXT]
SWAP = [(0, 1), (1, 0)]


def params(**extra):
    return pltpu.CompilerParams(vmem_limit_bytes=VMEM_BYTES, **extra)


def nt(a, b):
    return lax.dot_general(a, b, (((1,), (1,)), ((), ())), preferred_element_type=jnp.float32)


def nn(a, b):
    return lax.dot_general(a, b, (((1,), (0,)), ((), ())), preferred_element_type=jnp.float32)


def tn(a, b):
    return lax.dot_general(a, b, (((0,), (0,)), ((), ())), preferred_element_type=jnp.float32)


def bf(a):
    return a.astype(jnp.bfloat16)


def with_ones(values):
    return jnp.concatenate([values, jnp.ones_like(values)], axis=1)


def later_mask(rows):
    return lax.broadcasted_iota(jnp.int32, (rows, rows), 1) > lax.broadcasted_iota(
        jnp.int32, (rows, rows), 0
    )


def window_scores(query, k, pk, start, rows, bar):
    stop = start + query.shape[0]
    own = nt(query, k[:stop])
    prior = nt(query, pk[start:]) + bar
    later = later_mask(query.shape[0])
    pieces = [jnp.where(later, prior[:, : stop - start], own[:, start:])]
    if start:
        pieces = [own[:, :start]] + pieces
    if stop < rows:
        pieces = pieces + [prior[:, stop - start :]]
    return jnp.concatenate(pieces, axis=1) if len(pieces) > 1 else pieces[0]


def window_parts(values, start):
    size = values.shape[0]
    later = later_mask(size)
    middle = values[:, start : start + size]
    zero = jnp.zeros_like(middle)
    own, prior = jnp.where(later, zero, middle), jnp.where(later, middle, zero)
    if start:
        own = jnp.concatenate([values[:, :start], own], axis=1)
    if start + size < values.shape[1]:
        prior = jnp.concatenate([prior, values[:, start + size :]], axis=1)
    return own, prior


def attend_kernel(with_states, *refs):
    if with_states:
        open_ref, q, k, v, pk, pv, sk, sv, out, lse = refs
    else:
        open_ref, q, k, v, pk, pv, out, lse = refs
    rows = q.shape[0]
    bar = jnp.where(open_ref[0] > 0, NEGATIVE, 0.0)
    keys, prior_keys = k[...], pk[...]
    values, prior_values = with_ones(v[...]), with_ones(pv[...])
    if with_states:
        state_keys, state_values = sk[...], with_ones(sv[...])
    for start in range(0, rows, CHUNK):
        query = q[start : start + CHUNK]
        scores = window_scores(query, keys, prior_keys, start, rows, bar)
        top = jnp.max(scores, axis=-1, keepdims=True)
        if with_states:
            more = nt(query, state_keys)
            top = jnp.maximum(top, jnp.max(more, axis=-1, keepdims=True))
        own, prior = window_parts(bf(jnp.exp2((scores - top) * LOG2_SCALE)), start)
        mixed = nn(own, values[: start + CHUNK]) + nn(prior, prior_values[start:])
        if with_states:
            mixed = mixed + nn(bf(jnp.exp2((more - top) * LOG2_SCALE)), state_values)
        total = mixed[:, HEAD_DIM:]
        out[start : start + CHUNK] = bf(mixed[:, :HEAD_DIM] / total)
        lse[0, start : start + CHUNK] = top * LOG2_SCALE + jnp.log2(total[:, :1])


def side_blocks(rows, offset, heads):
    return (
        pl.BlockSpec((rows, HEAD_DIM), lambda h: (0, offset + jnp.minimum(h, heads - 1))),
        pl.BlockSpec((rows, HEAD_DIM), lambda h: (0, offset + jnp.maximum(h - heads, 0))),
    )


def lse_blocks(rows, heads):
    return (
        pl.BlockSpec((1, rows, 1), lambda h: (jnp.minimum(h, heads - 1), 0, 0)),
        pl.BlockSpec((1, rows, 1), lambda h: (jnp.maximum(h - heads, 0), 0, 0)),
    )


def both_sides(kernel, inputs, outputs, open_ref, *refs):
    ins, outs, scratch = refs[: 2 * inputs], refs[2 * inputs : 2 * (inputs + outputs)], refs[2 * (inputs + outputs) :]
    own = pl.program_id(0) < pl.num_programs(0) // 2
    pl.when(own)(lambda: kernel(open_ref, *ins[:inputs], *outs[:outputs], *scratch))
    pl.when(jnp.logical_not(own))(lambda: kernel(open_ref, *ins[inputs:], *outs[outputs:], *scratch))


def attend(opening, projs, priors, states=None):
    rows, width = projs[0].shape[0], projs[0].shape[1] // 3
    heads = width // HEAD_DIM
    columns = [side_blocks(rows, i * heads, heads) for i in (0, 1, 2, 0, 1)]
    arrays = [projs, projs, projs, priors, priors]
    keys = 2 * rows
    if states is not None:
        columns += [side_blocks(states[0].shape[0], i * heads, heads) for i in (1, 2)]
        arrays += [states, states]
        keys += states[0].shape[0]
    outs = [side_blocks(rows, 0, heads), lse_blocks(rows, heads)]
    mixed0, lse0, mixed1, lse1 = pl.pallas_call(
        functools.partial(
            both_sides, functools.partial(attend_kernel, states is not None), len(arrays), 2
        ),
        grid=(2 * heads,),
        in_specs=[pl.BlockSpec(memory_space=pltpu.SMEM)]
        + [pair[side] for side in range(2) for pair in columns],
        out_specs=[pair[side] for side in range(2) for pair in outs],
        out_shape=[
            jax.ShapeDtypeStruct((rows, width), jnp.bfloat16),
            jax.ShapeDtypeStruct((heads, rows, 1), jnp.float32),
        ]
        * 2,
        compiler_params=params(),
        cost_estimate=pl.CostEstimate(
            flops=8 * rows * keys * width,
            bytes_accessed=4 * rows * width * 8,
            transcendentals=rows * keys * heads,
        ),
    )(opening, *(pair[side] for side in range(2) for pair in arrays))
    return mixed0, lse0, mixed1, lse1


def attend_back_kernel(with_states, *refs):
    if with_states:
        (open_ref, q, k, v, pk, pv, sk, sv, gmix, mix, lse) = refs[:11]
        (gq, gk, gv, gpk, gpv, gsk, gsv) = refs[11:18]
    else:
        (open_ref, q, k, v, pk, pv, gmix, mix, lse) = refs[:9]
        (gq, gk, gv, gpk, gpv) = refs[9:14]
    gpk_sum, gpv_sum = refs[-2:]
    rows = q.shape[0]
    bar = jnp.where(open_ref[0] > 0, NEGATIVE, 0.0)
    keys, prior_keys, values, prior_values = k[...], pk[...], v[...], pv[...]
    if with_states:
        state_keys, state_values = sk[...], sv[...]
    for start in range(0, rows, CHUNK):
        stop = start + CHUNK
        query, grad, log_total = q[start:stop], gmix[start:stop], lse[0, start:stop]
        inner = jnp.sum(
            grad.astype(jnp.float32) * mix[start:stop].astype(jnp.float32), axis=-1, keepdims=True
        )
        scores = window_scores(query, keys, prior_keys, start, rows, bar)
        weights = jnp.exp2(scores * LOG2_SCALE - log_total)
        grad_weights = window_scores(grad, values, prior_values, start, rows, 0.0)
        own, prior = window_parts(bf(weights), start)
        own_scores, prior_scores = window_parts(bf(weights * (grad_weights - inner)), start)
        grad_query = nn(own_scores, keys[:stop]) + nn(prior_scores, prior_keys[start:])
        add_own_v, add_own_k = tn(own, grad), tn(own_scores, query)
        add_prior_v, add_prior_k = tn(prior, grad), tn(prior_scores, query)
        if with_states:
            more = jnp.exp2(nt(query, state_keys) * LOG2_SCALE - log_total)
            from_states = bf(more * (nt(grad, state_values) - inner))
            grad_query = grad_query + nn(from_states, state_keys)
            add_sv, add_sk = tn(bf(more), grad), tn(from_states, query)
        gq[start:stop] = bf(grad_query * SCALE)
        if start == 0:
            gv[:stop], gk[:stop] = add_own_v, add_own_k * SCALE
            gpv_sum[...], gpk_sum[...] = add_prior_v, add_prior_k
            if with_states:
                gsv[...], gsk[...] = add_sv, add_sk * SCALE
        else:
            gv[:start] += add_own_v[:start]
            gk[:start] += add_own_k[:start] * SCALE
            gv[start:stop], gk[start:stop] = add_own_v[start:], add_own_k[start:] * SCALE
            gpv_sum[start:] += add_prior_v
            gpk_sum[start:] += add_prior_k
            if with_states:
                gsv[...] += add_sv
                gsk[...] += add_sk * SCALE
    gpv[...] = bf(gpv_sum[...])
    gpk[...] = bf(gpk_sum[...] * SCALE)


def attend_back(opening, projs, priors, grads, mixed, lse, states=None):
    rows, width = projs[0].shape[0], projs[0].shape[1] // 3
    heads = width // HEAD_DIM
    columns = [side_blocks(rows, i * heads, heads) for i in (0, 1, 2, 0, 1)]
    arrays = [projs, projs, projs, priors, priors]
    kinds = [jnp.bfloat16, jnp.float32, jnp.float32, jnp.bfloat16, jnp.bfloat16]
    keys = 2 * rows
    if states is not None:
        columns += [side_blocks(states[0].shape[0], i * heads, heads) for i in (1, 2)]
        arrays += [states, states]
        kinds += [jnp.float32, jnp.float32]
        keys += states[0].shape[0]
    columns += [side_blocks(rows, 0, heads)] * 2 + [lse_blocks(rows, heads)]
    arrays += [grads, mixed, lse]
    results = pl.pallas_call(
        functools.partial(
            both_sides, functools.partial(attend_back_kernel, states is not None), len(arrays), len(kinds)
        ),
        grid=(2 * heads,),
        in_specs=[pl.BlockSpec(memory_space=pltpu.SMEM)]
        + [pair[side] for side in range(2) for pair in columns],
        out_specs=[side_blocks(rows, 0, heads)[side] for side in range(2) for _ in kinds],
        out_shape=[jax.ShapeDtypeStruct((rows, width), kind) for kind in kinds] * 2,
        scratch_shapes=[pltpu.VMEM((rows, HEAD_DIM), jnp.float32)] * 2,
        compiler_params=params(),
        cost_estimate=pl.CostEstimate(
            flops=20 * rows * keys * width,
            bytes_accessed=4 * rows * width * 24,
            transcendentals=rows * keys * heads,
        ),
    )(opening, *(pair[side] for side in range(2) for pair in arrays))
    return results[: len(kinds)], results[len(kinds) :]


KINDS = 9
FLIGHT = 4


class Spread:
    def __init__(self, sources, targets, send, recv):
        section, tensor, group = (lax.axis_index(a) for a in (SECTION, TENSOR, DP))
        self.sources, self.targets, self.send, self.recv = sources, targets, send, recv
        self.core, self.high, self.near = section % 2, section // 2, group % 2
        self.across = {TENSOR: 1 - tensor}
        self.along = {SECTION: (section + 2) % 4}
        self.beside = {DP: group + 1 - 2 * self.near}
        self.other = {SECTION: section + 1 - 2 * self.core}

    def partners(self):
        return [self.across, self.along, self.beside, self.other]

    def copy(self, kind, w):
        size = self.targets[w].shape[0] // 8
        y, z = self.high, self.near
        high, near, first, rows, to = (
            (y, z, 0, size, self.across),
            (y, z, 0, size, self.along),
            (y, z, 0, size, self.beside),
            (y, 1 - z, 0, size // 2, self.along),
            (1 - y, z, size // 2, size // 2, self.beside),
            (y, z, 0, size, self.other),
            (1 - y, z, 0, size, self.other),
            (y, 1 - z, 0, size, self.other),
            (1 - y, 1 - z, 0, size, self.other),
        )[kind]
        part = (near * 2 + high) * 2 + self.core
        where = pl.ds(pl.multiple_of(part * size + first, rows), rows)
        source = self.sources[w] if kind == 0 else self.targets[w]
        return pltpu.make_async_remote_copy(
            src_ref=source.at[where], dst_ref=self.targets[w].at[where],
            send_sem=self.send.at[kind * len(self.targets) + w],
            recv_sem=self.recv.at[kind * len(self.targets) + w],
            device_id=to, device_id_type=MESH,
        )

    def begin(self, w):
        self.copy(0, w).start()

    def hop(self, w):
        self.copy(0, w).wait_recv()
        for kind in (1, 2, 5):
            self.copy(kind, w).start()

    def cross(self, w):
        for kind in (1, 2):
            self.copy(kind, w).wait_recv()
        for kind in (3, 4, 6, 7):
            self.copy(kind, w).start()

    def close(self, w):
        for kind in (3, 4):
            self.copy(kind, w).wait_recv()
        self.copy(8, w).start()

    def end(self, w):
        for kind in (5, 6, 7, 8):
            self.copy(kind, w).wait_recv()
        for kind in range(KINDS):
            self.copy(kind, w).wait_send()


class Join:
    def __init__(self, source, theirs, mine, target, local, send, recv, i):
        tensor = lax.axis_index(TENSOR)
        rows = source.shape[-2]
        where = pl.ds(pl.multiple_of(tensor * rows, rows), rows)

        def of(index):
            return source if index is None else source.at[0, index]

        self.own = pltpu.make_async_copy(of(mine), target.at[where], local.at[i])
        self.remote = pltpu.make_async_remote_copy(
            src_ref=of(theirs), dst_ref=target.at[where], send_sem=send.at[i], recv_sem=recv.at[i],
            device_id={TENSOR: 1 - tensor}, device_id_type=MESH,
        )

    def start(self):
        self.remote.start()
        self.own.start()

    def wait(self):
        self.remote.wait()
        self.own.wait()


def meet(partners):
    barrier = pltpu.get_barrier_semaphore()
    for partner in partners:
        pl.semaphore_signal(barrier, inc=1, device_id=partner, device_id_type=MESH)
    pl.semaphore_wait(barrier, len(partners))


def gather_kernel(count, layer_input, init_states, *refs):
    sources, refs = refs[:count], refs[count:]
    tokens, before, initial = refs[:3]
    targets = refs[3 : 3 + count]
    send, recv, local, join_send, join_recv = refs[3 + count :]
    spread = Spread(sources, targets, send, recv)
    section, tensor = lax.axis_index(SECTION), lax.axis_index(TENSOR)
    block, partner = block_of(section, tensor), block_of(section, 1 - tensor)
    joins = [
        Join(layer_input, partner, block, tokens, local, join_send, join_recv, 0),
        Join(
            layer_input, jnp.maximum(partner - 1, 0), jnp.maximum(block - 1, 0),
            before, local, join_send, join_recv, 1,
        ),
        Join(init_states, None, None, initial, local, join_send, join_recv, 2),
    ]
    meet(spread.partners())
    def begin(i):
        if i < count:
            spread.begin(i)
        elif i < count + len(joins):
            joins[i - count].start()

    for i in range(FLIGHT):
        begin(i)
    for w in range(count + 2):
        if w < count:
            spread.hop(w)
        begin(w + FLIGHT)
        if 0 <= w - 1 < count:
            spread.cross(w - 1)
        if 0 <= w - 2 < count:
            spread.close(w - 2)
    for w in range(count):
        spread.end(w)
    for join in joins:
        join.wait()


def gather(layer_input, init_states, weights):
    count = len(weights)
    rows, width = 2 * layer_input.shape[2], layer_input.shape[3]
    dma = pltpu.SemaphoreType.DMA
    anywhere = pl.BlockSpec(memory_space=pl.ANY)
    shapes = [(rows, width)] * 2 + [(2 * init_states.shape[0], width)] + [w.shape for w in weights]
    results = pl.pallas_call(
        functools.partial(gather_kernel, count),
        in_specs=[anywhere] * (2 + count),
        out_specs=[anywhere] * (3 + count),
        out_shape=[jax.ShapeDtypeStruct(s, jnp.bfloat16) for s in shapes],
        scratch_shapes=[dma((KINDS * count,))] * 2 + [dma((3,))] * 3,
        compiler_params=params(collective_id=4, has_side_effects=True),
        cost_estimate=pl.CostEstimate(flops=0, bytes_accessed=200 * 1024 * 1024, transcendentals=0),
    )(layer_input, init_states, *weights)
    return results[:3], results[3:]


def neighbours():
    section, tensor = lax.axis_index(SECTION), lax.axis_index(TENSOR)
    block = block_of(section, tensor)

    return place_of((block + 7) % 8), place_of((block + 1) % 8)


def place_of(block):
    pair = block // 2
    high = pair // 2
    return {SECTION: 2 * high + block % 2, TENSOR: (pair + high) % 2}


class Scatter:
    def __init__(self, values, landed, send, recv, local):
        section, tensor = lax.axis_index(SECTION), lax.axis_index(TENSOR)
        block = block_of(section, tensor)
        self.members = [place_of((block + i) % 8) for i in range(1, 8)]
        rows, width = values[0].shape[0] // 2, values[0].shape[1] // 4

        def piece(value, to):
            high = pl.multiple_of(to[TENSOR] * rows, rows)
            left = pl.multiple_of(to[SECTION] * width, width)
            return value.at[pl.ds(high, rows), pl.ds(left, width)]

        self.copies = [
            pltpu.make_async_remote_copy(
                src_ref=piece(value, to), dst_ref=landed.at[j, block],
                send_sem=send.at[j * 7 + i], recv_sem=recv.at[j * 7 + i],
                device_id=to, device_id_type=MESH,
            )
            for j, value in enumerate(values)
            for i, to in enumerate(self.members)
        ]
        self.own = [
            pltpu.make_async_copy(
                piece(value, {SECTION: section, TENSOR: tensor}), landed.at[j, block], local.at[j]
            )
            for j, value in enumerate(values)
        ]

    def start(self):
        for copy in self.copies + self.own:
            copy.start()

    def wait(self):
        for copy in self.copies + self.own:
            copy.wait()


def pass_on(sent, landed, send_sem, recv_sem, slot, part, target):
    rows = pl.ds(part * CHUNK, CHUNK)
    return pltpu.make_async_remote_copy(
        src_ref=sent.at[slot, rows],
        dst_ref=landed.at[slot, rows],
        send_sem=send_sem.at[slot, part],
        recv_sem=recv_sem.at[slot, part],
        device_id=target,
        device_id_type=MESH,
    )


def chain_kernel(
    initial, starts, gain, keep, own, other, sqkv0, sqkv1, sout0, sout1, output_grad,
    state, hs, ps0, ps1, os0, os1, lse, update, fresh, cotangent,
    sent, landed, send_sem, recv_sem, local, join_send, join_recv,
):
    prior, following = neighbours()
    section, tensor = lax.axis_index(SECTION), lax.axis_index(TENSOR)
    join = Join(
        output_grad, block_of(section, 1 - tensor), block_of(section, tensor),
        cotangent, local, join_send, join_recv, 0,
    )
    meet([prior, following, {TENSOR: 1 - tensor}])
    join.start()
    count, width = initial.shape
    half = os0.shape[1]
    parts = count // CHUNK
    state[...] = initial[...].astype(jnp.float32)

    def copy(slot, part):
        return pass_on(sent, landed, send_sem, recv_sem, slot, part, following)

    def work(turn):
        for part in range(parts):
            rows = slice(part * CHUNK, (part + 1) * CHUNK)

            @pl.when(turn > 0)
            def _():
                slot = turn - 1
                copy(slot, part).wait_recv()
                state[rows] = jnp.where(
                    starts[...] > 0.0, initial[rows].astype(jnp.float32), landed[slot, rows].astype(jnp.float32)
                )

            value = state[rows]
            hidden = bf(value * inverse_rms(value) * gain[...])
            hs[rows] = hidden
            ps0[rows] = bf(nn(hidden, sqkv0[...]))
            ps1[rows] = bf(nn(hidden, sqkv1[...]))

        def one_head(h, carry):
            at = [pl.ds(pl.multiple_of(i * half + h * HEAD_DIM, HEAD_DIM), HEAD_DIM) for i in range(3)]
            for which, (tok, st, mixed) in enumerate(((own, ps0, os0), (other, ps1, os1))):
                tok_key, tok_value = tok[:, at[1]], with_ones(tok[:, at[2]])
                key, value = st[:, at[1]], with_ones(st[:, at[2]])
                for part in range(parts):
                    rows = slice(part * CHUNK, (part + 1) * CHUNK)
                    query = st[rows, at[0]]
                    score_tok, score = nt(query, tok_key), nt(query, key)
                    top = jnp.maximum(
                        jnp.max(score_tok, axis=-1, keepdims=True),
                        jnp.max(score, axis=-1, keepdims=True),
                    )
                    mix = nn(bf(jnp.exp2((score_tok - top) * LOG2_SCALE)), tok_value) + nn(
                        bf(jnp.exp2((score - top) * LOG2_SCALE)), value
                    )
                    total = mix[:, HEAD_DIM:]
                    mixed[rows, at[0]] = bf(mix[:, :HEAD_DIM] / total)
                    lse[which, h, rows] = top * LOG2_SCALE + jnp.log2(total[:, :1])
            return carry

        lax.fori_loop(0, half // HEAD_DIM, one_head, 0, unroll=True)
        for part in range(parts):
            rows = slice(part * CHUNK, (part + 1) * CHUNK)
            term = nn(os0[rows], sout0[...]) + nn(os1[rows], sout1[...])
            update[rows] = term
            renewed_state = bf(keep[...] * state[rows] + (1.0 - keep[...]) * term)
            fresh[rows] = renewed_state

            @pl.when(turn < CHAIN - 1)
            def _():
                sent[turn, rows] = renewed_state
                copy(turn, part).start()

    parity = block_of(section, tensor) % 2

    def one_round(turn, nothing):
        pl.when(parity == turn % 2)(lambda: work(turn))
        return nothing

    lax.fori_loop(0, CHAIN, one_round, 0)
    for slot in range(CHAIN - 1):

        @pl.when(parity == slot % 2)
        def _():
            for part in range(parts):
                copy(slot, part).wait_send()

    join.wait()


def chain(initial, starts, gain, keep, own, other, sqkv0, sqkv1, sout0, sout1, output_grad):
    count, width = initial.shape
    half = sout0.shape[0]
    heads = half // HEAD_DIM
    bf16, f32 = jnp.bfloat16, jnp.float32
    vmem, anywhere = pl.BlockSpec(memory_space=pltpu.VMEM), pl.BlockSpec(memory_space=pl.ANY)
    dma = pltpu.SemaphoreType.DMA
    parts = count // CHUNK
    return pl.pallas_call(
        chain_kernel,
        in_specs=[vmem] * 10 + [anywhere],
        out_specs=[vmem] * 9 + [anywhere],
        out_shape=[
            jax.ShapeDtypeStruct((count, width), f32),
            jax.ShapeDtypeStruct((count, width), bf16),
            jax.ShapeDtypeStruct((count, 3 * half), bf16),
            jax.ShapeDtypeStruct((count, 3 * half), bf16),
            jax.ShapeDtypeStruct((count, half), bf16),
            jax.ShapeDtypeStruct((count, half), bf16),
            jax.ShapeDtypeStruct((2, heads, count, 1), f32),
            jax.ShapeDtypeStruct((count, width), f32),
            jax.ShapeDtypeStruct((count, width), bf16),
            jax.ShapeDtypeStruct((2 * output_grad.shape[2], width), bf16),
        ],
        scratch_shapes=[
            pltpu.VMEM((CHAIN - 1, count, width), bf16),
            pltpu.VMEM((CHAIN - 1, count, width), bf16),
            dma((CHAIN - 1, parts)), dma((CHAIN - 1, parts)),
            dma((1,)), dma((1,)), dma((1,)),
        ],
        compiler_params=params(collective_id=1, has_side_effects=True),
        cost_estimate=pl.CostEstimate(
            flops=CHAIN * count * width * (8 * width + 8 * count),
            bytes_accessed=25 * 1024 * 1024,
            transcendentals=CHAIN * count * count * 4 * heads,
        ),
    )(initial, starts, gain, keep, own, other, sqkv0, sqkv1, sout0, sout1, output_grad)


LATE = 10


def chain_back_kernel(
    starts, ends, gain, keep, own, other, ps0, ps1, os0, os1, lse, *refs,
):
    distant, refs = refs[:LATE], refs[LATE:]
    result, ending, first_grad, gproj0, gproj1, gtok0, gtok1, gup, small, scattered = refs[:10]
    fetched, refs = refs[10 : 10 + LATE], refs[10 + LATE :]
    state, update, tok_k0, tok_v0, tok_k1, tok_v1, sqkv0, sqkv1, sout0, sout1 = fetched
    (
        grad_state, weights, grad_os0, grad_os1, sent, landed, send_sem, recv_sem, piece_send, piece_recv, piece_sem, late_sem
    ) = refs
    fetches = [
        pltpu.make_async_copy(source, target, late_sem.at[i])
        for i, (source, target) in enumerate(zip(distant, fetched))
    ]
    for fetch in fetches:
        fetch.start()
    prior, following = neighbours()
    scatter = Scatter((result, ending), scattered, piece_send, piece_recv, piece_sem)
    meet([prior, following] + scatter.members)
    scatter.start()
    count, width = state.shape
    half = os0.shape[1]
    heads = half // HEAD_DIM
    parts = count // CHUNK
    sides = (
        (own, ps0, os0, tok_k0, tok_v0, gproj0, gtok0, grad_os0),
        (other, ps1, os1, tok_k1, tok_v1, gproj1, gtok1, grad_os1),
    )

    def lanes(h):
        return [pl.ds(pl.multiple_of(i * half + h * HEAD_DIM, HEAD_DIM), HEAD_DIM) for i in range(3)]

    def copy(slot, part):
        return pass_on(sent, landed, send_sem, recv_sem, slot, part, prior)

    def prepare(h, carry):
        at = lanes(h)
        for which, (tok, st, *_) in enumerate(sides):
            tok_key, key = tok[:, at[1]], st[:, at[1]]
            for part in range(parts):
                rows = slice(part * CHUNK, (part + 1) * CHUNK)
                query, log_total = st[rows, at[0]], lse[which, h, rows]
                weights[which, h, rows, :count] = bf(
                    jnp.exp2(nt(query, tok_key) * LOG2_SCALE - log_total)
                )
                weights[which, h, rows, count:] = bf(
                    jnp.exp2(nt(query, key) * LOG2_SCALE - log_total)
                )
        return carry

    lax.fori_loop(0, heads, prepare, 0)
    for fetch in fetches:
        fetch.wait()
    grad_state[...] = jnp.zeros_like(grad_state)

    def work(turn):
        for part in range(parts):
            rows = slice(part * CHUNK, (part + 1) * CHUNK)

            @pl.when(turn > 0)
            def _():
                slot = turn - 1
                copy(slot, part).wait_recv()
                grad_state[rows] = jnp.where(
                    ends[...] > 0.0, 0.0, landed[slot, rows].astype(jnp.float32)
                )

            out = bf((1.0 - keep[...]) * grad_state[rows])
            gup[rows] = out
            grad_os0[rows] = bf(nt(out, sout0[...]))
            grad_os1[rows] = bf(nt(out, sout1[...]))

        def one_head(h, carry):
            at = lanes(h)
            for which, (tok, st, mixed, given_k, given_v, gproj, gtok, grad_os) in enumerate(sides):
                tok_key, tok_value = tok[:, at[1]], tok[:, at[2]]
                key, value = st[:, at[1]], st[:, at[2]]
                for part in range(parts):
                    rows = slice(part * CHUNK, (part + 1) * CHUNK)
                    query, grad = st[rows, at[0]], grad_os[rows, at[0]]
                    inner = jnp.sum(
                        grad.astype(jnp.float32) * mixed[rows, at[0]].astype(jnp.float32),
                        axis=-1, keepdims=True,
                    )
                    p_tok, p = weights[which, h, rows, :count], weights[which, h, rows, count:]
                    s_tok = bf(p_tok.astype(jnp.float32) * (nt(grad, tok_value) - inner))
                    s = bf(p.astype(jnp.float32) * (nt(grad, value) - inner))
                    gproj[rows, at[0]] = bf((nn(s_tok, tok_key) + nn(s, key)) * SCALE)
                    gk, gv = tn(s, query) * SCALE, tn(p, grad)
                    if part == 0:
                        total_k, total_v = gk + given_k[:, at[0]], gv + given_v[:, at[0]]
                    else:
                        total_k, total_v = total_k + gk, total_v + gv

                    @pl.when(turn >= CHAIN - 2)
                    def _():
                        gtk, gtv = tn(s_tok, query) * SCALE, tn(p_tok, grad)
                        if part == 0:
                            gtok[:, at[0]], gtok[:, at[1]] = gtk, gtv
                        else:
                            gtok[:, at[0]] += gtk
                            gtok[:, at[1]] += gtv

                gproj[:, at[1]], gproj[:, at[2]] = bf(total_k), bf(total_v)
            return carry

        lax.fori_loop(0, heads, one_head, 0, unroll=True)
        for part in range(parts):
            rows = slice(part * CHUNK, (part + 1) * CHUNK)
            back = nt(gproj0[rows], sqkv0[...]) + nt(gproj1[rows], sqkv1[...])
            value, new = state[rows], grad_state[rows]
            factor = inverse_rms(value)
            scaled = value * factor
            through = back * gain[...]
            leaving = keep[...] * new + factor * (
                through - scaled * jnp.mean(through * scaled, axis=-1, keepdims=True)
            )

            @pl.when(turn < CHAIN - 1)
            def _():
                sent[turn, rows] = bf(leaving)
                copy(turn, part).start()

            @pl.when(turn >= CHAIN - 2)
            def _():
                gain_term = jnp.sum(back * scaled, axis=0, keepdims=True)
                bias_term = jnp.sum(new * (value - update[rows]), axis=0, keepdims=True) * (
                    keep[...] * (1.0 - keep[...])
                )
                if part == 0:
                    small[0:1, :], small[1:2, :] = gain_term, bias_term
                else:
                    small[0:1, :] += gain_term
                    small[1:2, :] += bias_term
                first_grad[rows] = bf(jnp.where(starts[...] > 0.0, leaving, 0.0))

    parity = 1 - block_of(lax.axis_index(SECTION), lax.axis_index(TENSOR)) % 2

    def one_round(turn, nothing):
        pl.when(parity == turn % 2)(lambda: work(turn))
        return nothing

    lax.fori_loop(0, CHAIN, one_round, 0)
    for slot in range(CHAIN - 1):

        @pl.when(parity == slot % 2)
        def _():
            for part in range(parts):
                copy(slot, part).wait_send()

    scatter.wait()


def chain_back(
    starts, ends, state, update, gain, keep, own, other, ps0, ps1, os0, os1, lse,
    tok_k0, tok_v0, tok_k1, tok_v1, sqkv0, sqkv1, sout0, sout1, result, ending,
):
    count, width = state.shape
    half = sout0.shape[0]
    heads = half // HEAD_DIM
    bf16, f32 = jnp.bfloat16, jnp.float32
    vmem, anywhere = pl.BlockSpec(memory_space=pltpu.VMEM), pl.BlockSpec(memory_space=pl.ANY)
    dma = pltpu.SemaphoreType.DMA
    parts = count // CHUNK
    rows = own.shape[0]
    distant = (state, update, tok_k0, tok_v0, tok_k1, tok_v1, sqkv0, sqkv1, sout0, sout1)
    return pl.pallas_call(
        chain_back_kernel,
        in_specs=[vmem] * 11 + [anywhere] * (LATE + 2),
        out_specs=[vmem] * 7 + [anywhere],
        out_shape=[
            jax.ShapeDtypeStruct((count, width), bf16),
            jax.ShapeDtypeStruct((count, 3 * half), bf16),
            jax.ShapeDtypeStruct((count, 3 * half), bf16),
            jax.ShapeDtypeStruct((rows, 2 * half), f32),
            jax.ShapeDtypeStruct((rows, 2 * half), f32),
            jax.ShapeDtypeStruct((count, width), bf16),
            jax.ShapeDtypeStruct((2, width), f32),
            jax.ShapeDtypeStruct((2, 8, rows // 2, width // 4), bf16),
        ],
        scratch_shapes=[pltpu.VMEM(late.shape, late.dtype) for late in distant]
        + [
            pltpu.VMEM((count, width), f32),
            pltpu.VMEM((2, heads, count, rows + count), bf16),
            pltpu.VMEM((count, half), bf16),
            pltpu.VMEM((count, half), bf16),
            pltpu.VMEM((CHAIN - 1, count, width), bf16),
            pltpu.VMEM((CHAIN - 1, count, width), bf16),
            dma((CHAIN - 1, parts)), dma((CHAIN - 1, parts)), dma((14,)), dma((14,)), dma((2,)), dma((LATE,)),
        ],
        compiler_params=params(collective_id=2, has_side_effects=True),
        cost_estimate=pl.CostEstimate(
            flops=CHAIN * count * width * (16 * width + 16 * count),
            bytes_accessed=45 * 1024 * 1024,
            transcendentals=count * count * 4 * heads,
        ),
    )(starts, ends, gain, keep, own, other, ps0, ps1, os0, os1, lse, *distant, result, ending)


RING = 8
SHORT_RING = 4
TILE = 256
TAIL = 12
LAGS = (0, 1, 2, 4, 6, 7, 8, 9, 10)
UP_D, DOWN_D, UP_B, DOWN_B, OUT_C, QKV_C, SOUT_C, SQKV_C, QKV_A, OUT_A = range(10)
WEIGHTS = (
    (UP_D, True, 8), (DOWN_D, False, 8), (UP_B, True, 8), (DOWN_B, False, 8), (OUT_C, False, 2),
    (QKV_C, True, 6), (SOUT_C, False, 2), (SQKV_C, True, 6), (QKV_A, True, 6), (OUT_A, False, 2),
)
STARTS = [sum(w[2] for w in WEIGHTS[:i]) for i in range(len(WEIGHTS))]
PLAIN = sum(w[2] for w in WEIGHTS)
TAIL_WEIGHT = [w[0] for w in WEIGHTS].index(QKV_A)
TAIL_INPUTS = 10
TILES = PLAIN + 2


def grads_kernel(*refs):
    count = len(WEIGHTS)
    lefts, refs = refs[:count], refs[count:]
    panels_own, panels_other, refs = list(refs[: count - 1]), list(refs[count - 1 : 2 * count - 2]), refs[2 * count - 2 :]
    first, small, leaving_keys, refs = refs[0], refs[1], refs[2:6], refs[6:]
    distant, gain, refs = refs[:TAIL_INPUTS], refs[TAIL_INPUTS], refs[TAIL_INPUTS + 1 :]
    outs, last_out, landed = refs[:count], refs[count], refs[count + 1]
    refs = refs[count + 2 :]
    (
        left, panel, pair, core_in, kept1, first_in, kept2, second_in, kept3, third_in, kept4, fourth_in, result,
        left_sem, panel_sem, last_sem, core_send, core_recv, first_send, first_recv, second_send, second_recv,
        send_sem, recv_sem, piece_send, piece_recv, piece_sem,
        halo, ga0, ga1, rows_out, small_rows, gain_sum, tail_sem, halo_send, halo_recv,
    ) = refs[:-TAIL_INPUTS]
    fetched = refs[-TAIL_INPUTS:]
    panels_own.insert(TAIL_WEIGHT, ga0)
    panels_other.insert(TAIL_WEIGHT, ga1)
    section, tensor, group = (lax.axis_index(a) for a in (SECTION, TENSOR, DP))
    core, high = section % 2, section // 2
    near, far = group % 2, group // 2
    half, quarter = TILE // 2, TILE // 4
    other_core = {SECTION: section + 1 - 2 * core}
    near_group = {DP: group + 1 - 2 * near}
    far_group = {DP: (group + 2) % 4}
    scatter = Scatter((rows_out,), landed, piece_send, piece_recv, piece_sem)
    tail_fetches = [
        pltpu.make_async_copy(source, target, tail_sem.at[i])
        for i, (source, target) in enumerate(zip(distant + (small,), fetched + (small_rows,)))
    ]
    for fetch in tail_fetches:
        fetch.start()
    prior, _ = neighbours()
    meet(scatter.members + [near_group, far_group])

    def halo_copy(i):
        to = 2 * ((tensor + prior[TENSOR] + i // 2) % 2) + i % 2
        return pltpu.make_async_remote_copy(
            src_ref=leaving_keys[i], dst_ref=halo.at[to], send_sem=halo_send.at[i],
            recv_sem=halo_recv.at[to], device_id=prior, device_id_type=MESH,
        )

    for i in range(4):
        halo_copy(i).start()

    def remote(source, target, sems, recvs, where, partner):
        return pltpu.make_async_remote_copy(
            src_ref=source, dst_ref=target, send_sem=sems.at[where], recv_sem=recvs.at[where],
            device_id=partner, device_id_type=MESH,
        )

    def left_copy(w):
        return pltpu.make_async_copy(lefts[w], left.at[w % 3], left_sem.at[w % 3])

    left_copy(0).start()

    def panel_copies(w, k):
        slot = k % SHORT_RING
        columns = pl.ds(pl.multiple_of((k - STARTS[w]) * TILE, TILE), TILE)
        return [
            pltpu.make_async_copy(source[w].at[:, columns], panel.at[slot, j], panel_sem.at[2 * slot + j])
            for j, source in enumerate((panels_own, panels_other))
        ]

    def last_copies(which):
        slot = (PLAIN + which) % SHORT_RING
        for i in range(8):
            s, t = i // 2, i % 2
            columns = slice(s * TILE, (s + 1) * TILE)
            source = small_rows.at[:, columns] if which else first.at[t * TILE : (t + 1) * TILE, columns]
            yield pltpu.make_async_copy(source, pair.at[slot, s % 2, s // 2, t], last_sem.at[i])

    def core_copy(k):
        slot = k % SHORT_RING
        return remote(
            pair.at[slot, 1 - core], core_in.at[slot], core_send, core_recv, slot, other_core
        )

    def order(k):
        turn = k % 2
        send = (
            (1 - turn) * (1 - tensor) + turn * (2 - 2 * high),
            (1 - turn) * (3 - tensor) + turn * (3 - 2 * high),
        )
        keep = (
            (1 - turn) * tensor + turn * 2 * high,
            (1 - turn) * (2 + tensor) + turn * (2 * high + 1),
        )
        return send, keep, (1 - turn) * high + turn * tensor

    def partner_of(turn):
        return {
            SECTION: section * (1 - turn) + ((section + 2) % 4) * turn,
            TENSOR: tensor + (1 - turn) * (1 - 2 * tensor),
        }

    def first_copy(k, i):
        slot = k % RING
        return remote(
            kept1.at[k % SHORT_RING, order(k)[0][i]], first_in.at[slot, i], first_send, first_recv,
            2 * slot + i, partner_of(k % 2),
        )

    def second_copy(k):
        slot = k % RING
        return remote(
            kept2.at[slot, 1 - order(k)[2]], second_in.at[slot], second_send, second_recv,
            slot, partner_of(1 - k % 2),
        )

    def third_copy(k):
        slot = k % RING
        return remote(
            kept3.at[slot, pl.ds((1 - near) * half, half)], third_in.at[slot], send_sem, recv_sem,
            slot, near_group,
        )

    def fourth_copy(k):
        slot = k % RING
        return remote(
            kept4.at[slot, pl.ds((1 - far) * quarter, quarter)], fourth_in.at[slot], send_sem, recv_sem,
            RING + slot, far_group,
        )

    def back_far(k):
        rows = pl.ds(near * half + far * quarter, quarter)
        return remote(
            result.at[k, rows], result.at[k, rows], send_sem, recv_sem, 2 * RING + k % RING, far_group
        )

    def back_near(k):
        rows = pl.ds(near * half, half)
        return remote(
            result.at[k, rows], result.at[k, rows], send_sem, recv_sem, 3 * RING + k % RING, near_group
        )

    def add(a, b):
        return bf(a.astype(jnp.float32) + b.astype(jnp.float32))

    def fetch(k):
        for w in range(count):

            @pl.when((k >= STARTS[w]) & (k < STARTS[w] + WEIGHTS[w][2]))
            def _():
                for copy in panel_copies(w, k):
                    copy.start()

            if w + 1 < count:

                @pl.when(k == STARTS[w])
                def _():
                    left_copy(w + 1).start()

    def multiply(k):
        slot = k % SHORT_RING

        @pl.when(k < PLAIN)
        def _():
            at = 0
            for w in range(count):
                if w:
                    at = at + jnp.where(k >= STARTS[w], 1, 0)

                @pl.when(k == STARTS[w])
                def _():
                    left_copy(w).wait()

            for j, place in enumerate((tensor, 1 - tensor)):
                pltpu.make_async_copy(
                    panels_own[0].at[:, :TILE], panel.at[slot, j], panel_sem.at[2 * slot + j]
                ).wait()
                product = bf(tn(panel[slot, j], left[at % 3]))
                for s in range(4):
                    pair[slot, s % 2, s // 2, place] = product[:, s * TILE : (s + 1) * TILE]

        for which in range(2):

            @pl.when(k == PLAIN + which)
            def _():
                for copy in last_copies(which):
                    copy.start()
                for copy in last_copies(which):
                    copy.wait()

        core_copy(k).start()

    def over_cores(k):
        core_copy(k).wait()
        for i in range(4):
            kept1[k % SHORT_RING, i] = add(
                pair[k % SHORT_RING, core, i // 2, i % 2], core_in[k % SHORT_RING, i // 2, i % 2]
            )
        for i in range(2):
            first_copy(k, i).start()

    def over_first(k):
        slot = k % RING
        for i in range(2):
            first_copy(k, i).wait()
        for i in range(2):
            kept2[slot, i] = add(kept1[k % SHORT_RING, order(k)[1][i]], first_in[slot, i])
        second_copy(k).start()

    def over_second(k):
        slot = k % RING
        second_copy(k).wait()
        kept3[slot] = add(kept2[slot, order(k)[2]], second_in[slot])
        third_copy(k).start()

    def over_near(k):
        slot = k % RING
        third_copy(k).wait()
        kept4[slot] = add(kept3[slot, pl.ds(near * half, half)], third_in[slot])
        fourth_copy(k).start()

    def over_far(k):
        slot = k % RING
        fourth_copy(k).wait()
        result[k, pl.ds(near * half + far * quarter, quarter)] = add(
            kept4[slot, pl.ds(far * quarter, quarter)], fourth_in[slot]
        )
        back_far(k).start()

    def from_far(k):
        back_far(k).wait()
        back_near(k).start()

    def from_near(k):
        back_near(k).wait()
        for w in range(count):

            @pl.when((k >= STARTS[w]) & (k < STARTS[w] + WEIGHTS[w][2]))
            def _():
                at = pl.ds(pl.multiple_of((k - STARTS[w]) * TILE, TILE), TILE)
                if WEIGHTS[w][1]:
                    outs[w][:, at] = bf(result[k].astype(jnp.float32).T)
                else:
                    outs[w][at, :] = result[k]

        @pl.when(k >= PLAIN)
        def _():
            last_out[k - PLAIN] = result[k]

    gq0, gk0, gv0, gq1, gk1, gv1, w0, w1, tokens, grad = fetched
    wide = gq0.shape[1]

    def tail_begin():
        for copy in tail_fetches:
            copy.wait()
        for i in range(4):
            halo_copy(i).wait_send()
            pltpu.make_async_remote_copy(
                src_ref=leaving_keys[i], dst_ref=halo.at[i], send_sem=halo_send.at[i],
                recv_sem=halo_recv.at[i], device_id=prior, device_id_type=MESH,
            ).wait_recv()
        gain_sum[...] = jnp.zeros_like(gain_sum)

    def tail_rows(start):
        rows = slice(start, start + CHUNK)
        for side, (to, q, k, v) in enumerate(((ga0, gq0, gk0, gv0), (ga1, gq1, gk1, gv1))):
            to[rows, :wide] = q[rows]
            to[rows, wide : 2 * wide] = bf(k[rows] + halo[2 * side, rows].astype(jnp.float32))
            to[rows, 2 * wide :] = bf(v[rows] + halo[2 * side + 1, rows].astype(jnp.float32))
        back = nt(ga0[rows], w0[...]) + nt(ga1[rows], w1[...])
        value = tokens[rows].astype(jnp.float32)
        factor = inverse_rms(value)
        scaled = value * factor
        through = back * gain[...]
        rows_out[rows] = bf(
            grad[rows]
            + factor * (through - scaled * jnp.mean(through * scaled, axis=-1, keepdims=True))
        )
        gain_sum[0:1] += jnp.sum(back * scaled, axis=0, keepdims=True)

    def tail_end():
        top = small_rows[:16].astype(jnp.float32)
        row = lax.broadcasted_iota(jnp.int32, top.shape, 0)
        small_rows[:16] = bf(jnp.where(row == 0, gain_sum[0:1], top))
        scatter.start()

    stages = (
        fetch, multiply, over_cores, over_first, over_second, over_near, over_far, from_far, from_near
    )

    def step(i, nothing):
        pl.when(i == TAIL)(tail_begin)
        for part in range(grad.shape[0] // CHUNK):
            pl.when(i == TAIL + 2 + 2 * part)(functools.partial(tail_rows, part * CHUNK))
        pl.when(i == TAIL + 3 + 2 * (grad.shape[0] // CHUNK))(tail_end)
        for stage, lag in zip(stages, LAGS):
            k = i - lag

            @pl.when((k >= 0) & (k < TILES))
            def _():
                stage(k)

        return nothing

    lax.fori_loop(0, TILES + LAGS[-1], step, 0)
    scatter.wait()


def weight_grads(operands, first, small, leaving_keys, tail, gain):
    bf16 = jnp.bfloat16
    dma = pltpu.SemaphoreType.DMA
    anywhere, vmem = pl.BlockSpec(memory_space=pl.ANY), pl.BlockSpec(memory_space=pltpu.VMEM)
    count = len(WEIGHTS)
    rows, width = operands[WEIGHTS[0][0]][0].shape
    shapes = [(TILE, n * TILE) if by_rows else (n * TILE, TILE) for _, by_rows, n in WEIGHTS]
    shapes += [(2, TILE, TILE)]
    results = pl.pallas_call(
        grads_kernel,
        in_specs=[anywhere] * (3 * count + 4 + TAIL_INPUTS) + [vmem],
        out_specs=[vmem] * (count + 1) + [anywhere],
        out_shape=[jax.ShapeDtypeStruct(s, bf16) for s in shapes + [(1, 8, TILE, TILE)]],
        scratch_shapes=[
            pltpu.VMEM((3, rows, width), bf16),
            pltpu.VMEM((SHORT_RING, 2, rows, TILE), bf16),
            pltpu.VMEM((SHORT_RING, 2, 2, 2, TILE, TILE), bf16),
            pltpu.VMEM((SHORT_RING, 2, 2, TILE, TILE), bf16),
            pltpu.VMEM((SHORT_RING, 4, TILE, TILE), bf16),
            pltpu.VMEM((RING, 2, TILE, TILE), bf16),
            pltpu.VMEM((RING, 2, TILE, TILE), bf16),
            pltpu.VMEM((RING, TILE, TILE), bf16),
            pltpu.VMEM((RING, TILE, TILE), bf16),
            pltpu.VMEM((RING, TILE // 2, TILE), bf16),
            pltpu.VMEM((RING, TILE // 2, TILE), bf16),
            pltpu.VMEM((RING, TILE // 4, TILE), bf16),
            pltpu.VMEM((TILES, TILE, TILE), bf16),
            dma((3,)), dma((2 * SHORT_RING,)), dma((8,)),
            dma((SHORT_RING,)), dma((SHORT_RING,)),
            dma((2 * RING,)), dma((2 * RING,)), dma((RING,)), dma((RING,)),
            dma((4 * RING,)), dma((4 * RING,)), dma((7,)), dma((7,)), dma((1,)),
            pltpu.VMEM((4, rows, width // 2), bf16),
            pltpu.VMEM((rows, 3 * width // 2), bf16),
            pltpu.VMEM((rows, 3 * width // 2), bf16),
            pltpu.VMEM((rows, width), bf16),
            pltpu.VMEM((TILE, width), bf16),
            pltpu.VMEM((8, width), jnp.float32),
            dma((TAIL_INPUTS + 1,)), dma((4,)), dma((4,)),
        ]
        + [pltpu.VMEM(value.shape, value.dtype) for value in tail],
        compiler_params=params(collective_id=3, has_side_effects=True),
        cost_estimate=pl.CostEstimate(
            flops=2 * 8 * TILES * TILE * TILE * rows,
            bytes_accessed=40 * TILES * TILE * TILE,
            transcendentals=0,
        ),
    )(
        *(operands[w[0]][0] for w in WEIGHTS),
        *(operands[w[0]][i] for i in (1, 2) for w in WEIGHTS if w[0] != QKV_A),
        first, small, *leaving_keys, *tail, gain,
    )
    shares = {w[0]: r for w, r in zip(WEIGHTS, results)}
    return shares, results[count], results[count + 1]


def last_layer_kernel(
    alive, h, gy, r, up0, up1, down0, down1, a0, a1, g0, g1, result, through, total, back
):
    step, steps = pl.program_id(0), pl.num_programs(0)

    @pl.when(step == 0)
    def _():
        total[...] = jnp.zeros_like(total)
        back[...] = jnp.zeros_like(back)

    def chunk(up, down, a_out, g_out):
        u = nn(h[...], up[...])
        square = u * u
        slope = math.sqrt(2.0 / math.pi)
        t = jnp.tanh(slope * (u + 0.044715 * (square * u)))
        a = bf(0.5 * u * (1.0 + t))
        a_out[...] = a
        total[...] += nn(a, down[...])
        rise = 0.5 * (1.0 + t) + 0.5 * u * (1.0 - t * t) * (slope + (3.0 * 0.044715 * slope) * square)
        g = bf(nt(gy[...], down[...]) * rise)
        g_out[...] = g
        back[...] += nt(g, up[...])

    pl.when(step < steps // 2)(lambda: chunk(up0, down0, a0, g0))
    pl.when(step >= steps // 2)(lambda: chunk(up1, down1, a1, g1))

    @pl.when(step == steps - 1)
    def _():
        result[...] = bf(jnp.where(alive[0] > 0, r[...] + total[...], 0.0))
        through[...] = back[...]


def last_layer(alive, h, gy, r, up0, up1, down0, down1):
    rows, width = h.shape
    hidden = up0.shape[1]
    wide = 512
    half = hidden // wide

    def first(i):
        return jnp.minimum(i, half - 1)

    def second(i):
        return jnp.maximum(i - half, 0)

    ups = [pl.BlockSpec((width, wide), lambda i, of=of: (0, of(i))) for of in (first, second)]
    downs = [pl.BlockSpec((wide, width), lambda i, of=of: (of(i), 0)) for of in (first, second)]
    hiddens = [pl.BlockSpec((rows, wide), lambda i, of=of: (0, of(i))) for of in (first, second)]
    kept = pl.BlockSpec((rows, width), lambda i: (0, 0))
    return pl.pallas_call(
        last_layer_kernel,
        grid=(2 * half,),
        in_specs=[pl.BlockSpec(memory_space=pltpu.SMEM), kept, kept, kept] + ups + downs,
        out_specs=hiddens + hiddens + [kept, kept],
        out_shape=[jax.ShapeDtypeStruct((rows, hidden), jnp.bfloat16)] * 4
        + [
            jax.ShapeDtypeStruct((rows, width), jnp.bfloat16),
            jax.ShapeDtypeStruct((rows, width), jnp.float32),
        ],
        scratch_shapes=[pltpu.VMEM((rows, width), jnp.float32)] * 2,
        compiler_params=params(),
        cost_estimate=pl.CostEstimate(
            flops=16 * rows * width * hidden,
            bytes_accessed=8 * width * hidden + 16 * rows * hidden,
            transcendentals=2 * rows * hidden,
        ),
    )(alive, h, gy, r, up0, up1, down0, down1)


def gelu_back(values, grad):
    return jax.vjp(smooth, values)[1](grad)[0]


def block_body(
    layer_input, output_grad, seg_blocks, seg_group, gain_a, wqkv_a, wout_a, gain_b, up_b, down_b,
    gain_c, gain_s, wqkv_c, sqkv_c, wout_c, sout_c, gate_bias, init_states, gain_d, up_d, down_d,
):
    sections, tensors = lax.axis_size(SECTION), lax.axis_size(TENSOR)
    block_count, shard_rows, width = layer_input.shape[1:]
    rows = shard_rows * tensors
    section, tensor = lax.axis_index(SECTION), lax.axis_index(TENSOR)
    block = block_of(section, tensor)
    begins, closes, lively, numbers = layout(
        seg_blocks, seg_group, lax.axis_index(DP), block_count
    )
    alive = lively[block]
    starts = begins[block] | jnp.logical_not(alive)
    ends = closes[block] | jnp.logical_not(alive)
    opening = starts.astype(jnp.int32)[None]
    f32 = jnp.float32
    ga, gb, gc, gd = (v.astype(f32) for v in (gain_a, gain_b, gain_c, gain_d))

    def in_order(own, other):
        low = jnp.where(tensor == 0, own, other)
        high = jnp.where(tensor == 0, other, own)
        return low, high

    def crossed(weight):
        size = weight.shape[0] // sections
        piece = lax.dynamic_slice_in_dim(weight, section * size, size, 0)
        return lax.ppermute(piece, TENSOR, SWAP)

    def flat(weight):
        return jnp.concatenate([weight[:, i] for i in range(3)], axis=1)

    wqkv_a0, wqkv_c0, sqkv_c0 = flat(wqkv_a), flat(wqkv_c), flat(sqkv_c)
    (tokens, before, initial), others = gather(
        layer_input, init_states,
        (wout_a, sout_c, wout_c, wqkv_a0, wqkv_c0, sqkv_c0, up_b, down_b),
    )
    wout_a1, sout_c1, wout_c1, wqkv_a1, wqkv_c1, sqkv_c1, up_b1, down_b1 = others
    tokens, late_up, late_down = lax.optimization_barrier((tokens, up_d, down_d))
    pieces = crossed(late_up), crossed(late_down)

    def normed(values, gain):
        return bf(values * inverse_rms(values) * gain)

    def dot(a, b):
        return jnp.dot(a, b, preferred_element_type=f32)

    def dot_t(a, b):
        return lax.dot_general(a, b, (((1,), (1,)), ((), ())), preferred_element_type=f32)

    half = wout_a.shape[0]
    r0 = tokens.astype(f32)
    h0 = normed(r0, ga)
    h_before = normed(before.astype(f32), ga)
    pa0, pa1 = bf(dot(h0, wqkv_a0)), bf(dot(h0, wqkv_a1))
    prior_a0 = bf(dot(h_before, wqkv_a0[:, half:]))
    prior_a1 = bf(dot(h_before, wqkv_a1[:, half:]))
    oa0, lse_a0, oa1, lse_a1 = attend(opening, (pa0, pa1), (prior_a0, prior_a1))
    r1 = r0 + (dot(oa0, wout_a) + dot(oa1, wout_a1))

    h1 = normed(r1, gb)
    ub0, ub1 = dot(h1, up_b), dot(h1, up_b1)
    ab0, ab1 = bf(smooth(ub0)), bf(smooth(ub1))
    ab0, *pieces = lax.optimization_barrier((ab0, *pieces))
    up_d1, down_d1 = (lax.all_gather(piece, SECTION, axis=0, tiled=True) for piece in pieces)
    r2 = r1 + (dot(ab0, down_b) + dot(ab1, down_b1))

    h2 = normed(r2, gc)
    pc0, pc1 = bf(dot(h2, wqkv_c0)), bf(dot(h2, wqkv_c1))
    halo = lax.ppermute(jnp.stack(in_order(pc0[:, half:], pc1[:, half:])), GROUP, TO_NEXT)
    prior_c0, prior_c1 = in_order(halo[0], halo[1])

    retain = jax.nn.sigmoid(gate_bias.astype(f32))[None, :]
    state_gain = gain_s.astype(f32)[None, :]

    def flag(value):
        return jnp.broadcast_to(value.astype(f32), (1, width))

    (
        state_in, hs, ps0, ps1, os0, os1, lse_s, update, state_new, cotangent
    ) = chain(
        initial, flag(starts), state_gain, retain, pc0, pc1,
        sqkv_c0, sqkv_c1, sout_c, sout_c1, output_grad,
    )
    oc0, lse_c0, oc1, lse_c1 = attend(opening, (pc0, pc1), (prior_c0, prior_c1), (ps0, ps1))
    r3 = r2 + (dot(oc0, wout_c) + dot(oc1, wout_c1))

    h3 = normed(r3, gd)
    def feed_back(up_name, down_name, grad, values, h, gain, u0, u1, a0, a1, up0, up1, down0, down1):
        gy = bf(grad)
        g0 = bf(gelu_back(u0, dot_t(gy, down0)))
        g1 = bf(gelu_back(u1, dot_t(gy, down1)))
        operands[down_name] = (gy, a0, a1)
        operands[up_name] = (h, g0, g1)
        through = dot_t(g0, up0) + dot_t(g1, up1)
        back, gain_grad = norm_back(values, gain, through)
        return grad + back, gain_grad

    operands = {}
    grad4 = jnp.where(alive, cotangent.astype(f32), 0.0)
    gy4 = bf(grad4)
    ad0, ad1, gd0, gd1, result, through_d = last_layer(
        alive.astype(jnp.int32)[None], h3, gy4, r3, up_d, up_d1, down_d, down_d1
    )
    operands[DOWN_D] = (gy4, ad0, ad1)
    operands[UP_D] = (h3, gd0, gd1)
    back_d, gain_d_grad = norm_back(r3, gd, through_d)
    grad3 = grad4 + back_d

    gy3 = bf(grad3)
    tok0, tok1 = attend_back(
        opening, (pc0, pc1), (prior_c0, prior_c1), (bf(dot_t(gy3, wout_c)), bf(dot_t(gy3, wout_c1))),
        (oc0, oc1), (lse_c0, lse_c1), (ps0, ps1),
    )

    def halo_back(one, two):
        pair = in_order(
            jnp.concatenate([one[3], one[4]], axis=1), jnp.concatenate([two[3], two[4]], axis=1)
        )
        back = lax.ppermute(jnp.stack(pair), GROUP, TO_PRIOR)
        return in_order(back[0], back[1])

    halo_c0, halo_c1 = halo_back(tok0, tok1)
    first_grad, gs0, gs1, gtok0, gtok1, gup, small, landed = chain_back(
        flag(starts), flag(ends), state_in, update, state_gain, retain, pc0, pc1, ps0, ps1, os0, os1, lse_s,
        tok0[5], tok0[6], tok1[5], tok1[6], sqkv_c0, sqkv_c1, sout_c, sout_c1, result, state_new,
    )

    def projected_back(parts, halo_part, extra=None):
        pair = jnp.concatenate([parts[1], parts[2]], axis=1) + halo_part.astype(f32)
        if extra is not None:
            pair = pair + extra
        return jnp.concatenate([parts[0], bf(pair)], axis=1)

    gc0 = projected_back(tok0, halo_c0, gtok0)
    gc1 = projected_back(tok1, halo_c1, gtok1)
    operands[QKV_C] = (h2, gc0, gc1)
    operands[SQKV_C] = (hs, gs0, gs1)
    operands[OUT_C] = (gy3, oc0, oc1)
    operands[SOUT_C] = (gup, os0, os1)
    def through_qkv(g, w):
        return dot_t(g, w)

    back_c, gain_c_grad = norm_back(
        r2, gc, through_qkv(gc0, wqkv_c0) + through_qkv(gc1, wqkv_c1)
    )
    grad2 = grad3 + back_c

    grad1, gain_b_grad = feed_back(
        UP_B, DOWN_B, grad2, r1, h1, gb, ub0, ub1, ab0, ab1, up_b, up_b1, down_b, down_b1
    )

    gy1 = bf(grad1)
    att0, att1 = attend_back(
        opening, (pa0, pa1), (prior_a0, prior_a1), (bf(dot_t(gy1, wout_a)), bf(dot_t(gy1, wout_a1))),
        (oa0, oa1), (lse_a0, lse_a1),
    )
    operands[QKV_A] = (h0,)
    operands[OUT_A] = (gy1, oa0, oa1)
    smalls = jnp.stack(
        [jnp.zeros_like(gain_b_grad), gain_b_grad, gain_c_grad, small[0], gain_d_grad, small[1]]
    )
    shares, last_share, landed_input = weight_grads(
        operands, first_grad, jnp.pad(bf(smalls), ((0, TILE - 6), (0, 0))), (*att0[3:5], *att1[3:5]),
        (*att0[:3], *att1[:3], wqkv_a0, wqkv_a1, tokens, grad1), ga[None, :],
    )
    small_share = last_share[1].astype(f32)
    chosen = (
        (numbers[:, None] == jnp.arange(SLOTS, dtype=jnp.int32)[None, :])
        & (closes & lively)[:, None]
    )
    state_tiles = landed[1].astype(f32)
    final_share = jnp.stack(
        [
            jnp.sum(jnp.where(chosen[:, i, None, None], state_tiles, 0.0), axis=0)
            for i in range(SLOTS)
        ],
        axis=1,
    )

    def share(name):
        value = shares[name].astype(f32)
        return value.reshape(value.shape[0], 3, -1) if name in (QKV_A, QKV_C, SQKV_C) else value

    return (
        landed[0][None],
        final_share[None],
        landed_input.astype(f32),
        small_share[0],
        share(QKV_A),
        share(OUT_A),
        small_share[1],
        share(UP_B),
        share(DOWN_B),
        small_share[2],
        small_share[3],
        share(QKV_C),
        share(SQKV_C),
        share(OUT_C),
        share(SOUT_C),
        small_share[5],
        last_share[0].astype(f32),
        small_share[4],
        share(UP_D),
        share(DOWN_D),
    )


def chosen(*arrays):
    devices = (lax.axis_size(SECTION), lax.axis_size(TENSOR), lax.axis_size(DP))
    if devices == (4, 2, 4) and arrays[0].shape[1] == 8:
        return block_body(*arrays)
    return relay_body(*arrays)


def solution(mesh):
    in_specs = (
        P(DP, None, TENSOR, None),
        P(DP, None, TENSOR, None),
        P(),
        P(),
        P(),
        P(None, None, TENSOR),
        P(TENSOR, None),
        P(),
        P(None, TENSOR),
        P(TENSOR, None),
        P(),
        P(),
        P(None, None, TENSOR),
        P(None, None, TENSOR),
        P(TENSOR, None),
        P(TENSOR, None),
        P(),
        P(TENSOR, None),
        P(),
        P(None, TENSOR),
        P(TENSOR, None),
    )
    out_specs = (
        P(DP, None, TENSOR, SECTION),
        P(DP, TENSOR, None, SECTION),
        P(DP, None, TENSOR, SECTION),
        P(SECTION),
        P(SECTION, None, TENSOR),
        P(TENSOR, SECTION),
        P(SECTION),
        P(SECTION, TENSOR),
        P(TENSOR, SECTION),
        P(SECTION),
        P(SECTION),
        P(SECTION, None, TENSOR),
        P(SECTION, None, TENSOR),
        P(TENSOR, SECTION),
        P(TENSOR, SECTION),
        P(SECTION),
        P(TENSOR, SECTION),
        P(SECTION),
        P(SECTION, TENSOR),
        P(TENSOR, SECTION),
    )
    return jax.shard_map(chosen, mesh=mesh, in_specs=in_specs, out_specs=out_specs, check_vma=False)
```

```python
import functools
import math

import jax
import jax.numpy as jnp
from jax import lax
from jax.experimental import pallas as pl
from jax.experimental.pallas import tpu as pltpu
from jax.sharding import PartitionSpec as P

SECTION, DP, TENSOR = "section", "dp", "tensor"
HEAD_DIM = 128
SLOTS = 3


EPSILON = 1e-06
NEGATIVE = -1e30


def shifted(value, axis, by):
    devices = lax.axis_size(axis)
    pairs = [(i, i + by) for i in range(devices) if 0 <= i + by < devices]
    return lax.ppermute(value, axis, pairs)


def for_sending(value):
    return jax.tree.map(lambda a: a.astype(jnp.bfloat16) if a.dtype == jnp.float32 else a, value)


def layout(seg_blocks, seg_group, group_index, block_count):
    mine = seg_group == group_index
    lengths = jnp.where(mine, seg_blocks, 0)
    offsets = jnp.cumsum(lengths) - lengths
    ranking = jnp.cumsum(mine.astype(jnp.int32)) - mine.astype(jnp.int32)
    blocks = jnp.arange(block_count, dtype=jnp.int32)[None, :]
    inside = mine[:, None] & (blocks >= offsets[:, None]) & (blocks < (offsets + lengths)[:, None])
    begins = jnp.any(inside & (blocks == offsets[:, None]), axis=0)
    closes = jnp.any(inside & (blocks == (offsets + lengths - 1)[:, None]), axis=0)
    lively = jnp.any(inside, axis=0)
    numbers = jnp.sum(jnp.where(inside, ranking[:, None], 0), axis=0)
    return (begins, closes, lively, numbers)


def inverse_rms(values):
    return lax.rsqrt(jnp.mean(values * values, axis=-1, keepdims=True) + EPSILON)


def norm_back(values, gain, grad_normed):
    factor = inverse_rms(values)
    scaled = values * factor
    grad_scaled = grad_normed * gain
    grad_values = factor * (
        grad_scaled - scaled * jnp.mean(grad_scaled * scaled, axis=-1, keepdims=True)
    )
    return (grad_values, jnp.sum(grad_normed * scaled, axis=0))


def smooth(values):
    return jax.nn.gelu(values, approximate=True)


def split_heads(rows_in):
    return rows_in.reshape(rows_in.shape[0], -1, HEAD_DIM)


def attend_forward(queries, key_rows, value_rows, allowed):
    score_scale = 1.0 / math.sqrt(HEAD_DIM)
    scores = (
        jnp.einsum("rhd,khd->hrk", queries, key_rows, preferred_element_type=jnp.float32)
        * score_scale
    )
    scores = jnp.where(allowed[None], scores, NEGATIVE)
    largest = jnp.max(scores, axis=-1, keepdims=True)
    totals = jnp.sum(jnp.exp(scores - largest), axis=-1, keepdims=True)
    log_total = largest + jnp.log(totals)
    weights = jnp.exp(scores - log_total).astype(jnp.bfloat16)
    mixture_output = jnp.einsum(
        "hrk,khd->rhd", weights, value_rows, preferred_element_type=jnp.float32
    )
    return (mixture_output, log_total[..., 0])


def attend_backward(queries, key_rows, value_rows, allowed, log_total, grad_mixture):
    score_scale = 1.0 / math.sqrt(HEAD_DIM)
    scores = (
        jnp.einsum("rhd,khd->hrk", queries, key_rows, preferred_element_type=jnp.float32)
        * score_scale
    )
    scores = jnp.where(allowed[None], scores, NEGATIVE)
    weights = jnp.exp(scores - log_total[..., None])
    rounded = weights.astype(jnp.bfloat16)
    grad_weights = jnp.einsum(
        "rhd,khd->hrk", grad_mixture, value_rows, preferred_element_type=jnp.float32
    )
    grad_values = jnp.einsum(
        "hrk,rhd->khd", rounded, grad_mixture, preferred_element_type=jnp.float32
    )
    inner_sum = jnp.sum(weights * grad_weights, axis=-1, keepdims=True)
    grad_scores = (weights * (grad_weights - inner_sum)).astype(jnp.bfloat16)
    grad_queries = (
        jnp.einsum("hrk,khd->rhd", grad_scores, key_rows, preferred_element_type=jnp.float32)
        * score_scale
    )
    grad_keys = (
        jnp.einsum("hrk,rhd->khd", grad_scores, queries, preferred_element_type=jnp.float32)
        * score_scale
    )
    return (grad_queries, grad_keys, grad_values)


def place_row(store, position, value, active_tick):
    previous = lax.dynamic_index_in_dim(store, position, 0, False)
    return lax.dynamic_update_index_in_dim(
        store, jnp.where(active_tick, value, previous), position, 0
    )


def renewed(grad_sums, active_tick, changes):
    return tuple(
        (
            total + jnp.where(active_tick, changes[position], 0.0) if position in changes else total
            for position, total in enumerate(grad_sums)
        )
    )


def relay_body(
    layer_input,
    output_grad,
    seg_blocks,
    seg_group,
    gain_a,
    wqkv_a,
    wout_a,
    gain_b,
    up_b,
    down_b,
    gain_c,
    gain_s,
    wqkv_c,
    sqkv_c,
    wout_c,
    sout_c,
    gate_bias,
    init_states,
    gain_d,
    up_d,
    down_d,
):
    block_count = layer_input.shape[1]
    shard_rows = layer_input.shape[2]
    model_width = layer_input.shape[3]
    tensor_count = lax.axis_size(TENSOR)
    token_rows = shard_rows * tensor_count
    state_shard = init_states.shape[0]
    state_count = state_shard * tensor_count
    local_width = wqkv_a.shape[2]
    local_heads = local_width // HEAD_DIM
    section_index = lax.axis_index(SECTION)
    group_index = lax.axis_index(DP)
    on_cell_section = section_index == 2
    begins, closes, lively, numbers = layout(seg_blocks, seg_group, group_index, block_count)
    token_gains = jnp.stack([gain_a, gain_b, gain_c, gain_d]).astype(jnp.float32)
    state_gain = gain_s.astype(jnp.float32)
    retain = jax.nn.sigmoid(gate_bias.astype(jnp.float32))
    initial = init_states.astype(jnp.float32)
    empty_state = jnp.zeros((state_count, model_width), jnp.float32)
    empty_token_store = jnp.zeros((token_rows, 4, local_width), jnp.bfloat16)
    empty_state_store = jnp.zeros((state_count, 4, local_width), jnp.bfloat16)
    empty_token_lse = jnp.zeros((local_heads, token_rows), jnp.float32)
    empty_state_lse = jnp.zeros((local_heads, state_count), jnp.float32)
    empty_carry = jnp.zeros((token_rows, local_width), jnp.float32)
    every_key = jnp.ones((state_count, token_rows + state_count), bool)
    state_keys_all = jnp.ones((token_rows, state_count), bool)

    def token_masks(opening):
        later_keys = lax.broadcasted_iota(
            jnp.int32, (token_rows, token_rows), 1
        ) > lax.broadcasted_iota(jnp.int32, (token_rows, token_rows), 0)
        return (jnp.logical_and(later_keys, jnp.logical_not(opening)), jnp.logical_not(later_keys))

    def plain_forward(normed_tok, normed_st, prior_block, opening):
        projected = jnp.einsum(
            "rd,dcn->rcn", normed_tok, wqkv_a, preferred_element_type=jnp.float32
        ).astype(jnp.bfloat16)
        reach_prior, reach_current = token_masks(opening)
        allowed = jnp.concatenate([reach_prior, reach_current], axis=1)
        key_rows = jnp.concatenate([prior_block[:, 1], projected[:, 1]], axis=0)
        value_rows = jnp.concatenate([prior_block[:, 2], projected[:, 2]], axis=0)
        mixture_output, token_lse = attend_forward(
            split_heads(projected[:, 0]), split_heads(key_rows), split_heads(value_rows), allowed
        )
        mixture_output = mixture_output.reshape(token_rows, local_width).astype(jnp.bfloat16)
        branch = jnp.dot(mixture_output, wout_a, preferred_element_type=jnp.float32)
        stored = jnp.concatenate([projected, mixture_output[:, None]], axis=1)
        return (branch, empty_state, stored, empty_state_store, token_lse, empty_state_lse)

    def feed_forward(up_projection_weight, down_projection_weight):

        def forward_fn(normed_tok, normed_st, prior_block, opening):
            hidden_rows = jnp.dot(
                normed_tok, up_projection_weight, preferred_element_type=jnp.float32
            )
            active_flags = smooth(hidden_rows).astype(jnp.bfloat16)
            branch = jnp.dot(
                active_flags, down_projection_weight, preferred_element_type=jnp.float32
            )
            return (
                branch,
                empty_state,
                empty_token_store,
                empty_state_store,
                empty_token_lse,
                empty_state_lse,
            )

        return forward_fn

    def recurrent_forward(normed_tok, normed_st, prior_block, opening):
        projected = jnp.einsum(
            "rd,dcn->rcn", normed_tok, wqkv_c, preferred_element_type=jnp.float32
        ).astype(jnp.bfloat16)
        state_proj = jnp.einsum(
            "sd,dcn->scn", normed_st, sqkv_c, preferred_element_type=jnp.float32
        ).astype(jnp.bfloat16)
        reach_prior, reach_current = token_masks(opening)
        allowed = jnp.concatenate([reach_prior, reach_current, state_keys_all], axis=1)
        token_keys = jnp.concatenate([prior_block[:, 1], projected[:, 1], state_proj[:, 1]], axis=0)
        token_values = jnp.concatenate(
            [prior_block[:, 2], projected[:, 2], state_proj[:, 2]], axis=0
        )
        token_mixture, token_lse = attend_forward(
            split_heads(projected[:, 0]),
            split_heads(token_keys),
            split_heads(token_values),
            allowed,
        )
        state_keys = jnp.concatenate([projected[:, 1], state_proj[:, 1]], axis=0)
        state_values = jnp.concatenate([projected[:, 2], state_proj[:, 2]], axis=0)
        state_mixture, state_lse = attend_forward(
            split_heads(state_proj[:, 0]),
            split_heads(state_keys),
            split_heads(state_values),
            every_key,
        )
        token_mixture = token_mixture.reshape(token_rows, local_width).astype(jnp.bfloat16)
        state_mixture = state_mixture.reshape(state_count, local_width).astype(jnp.bfloat16)
        branch = jnp.dot(token_mixture, wout_c, preferred_element_type=jnp.float32)
        update_term = jnp.dot(state_mixture, sout_c, preferred_element_type=jnp.float32)
        stored = jnp.concatenate([projected, token_mixture[:, None]], axis=1)
        state_stored = jnp.concatenate([state_proj, state_mixture[:, None]], axis=1)
        return (branch, update_term, stored, state_stored, token_lse, state_lse)

    def plain_backward(
        grad_tok,
        grad_st,
        normed_tok,
        normed_st,
        tok_block,
        st_block,
        prior_block,
        token_lse,
        state_lse,
        opening,
        carry_keys,
        carry_values,
        grad_sums,
        active_tick,
    ):
        reach_prior, reach_current = token_masks(opening)
        allowed = jnp.concatenate([reach_prior, reach_current], axis=1)
        key_rows = jnp.concatenate([prior_block[:, 1], tok_block[:, 1]], axis=0)
        value_rows = jnp.concatenate([prior_block[:, 2], tok_block[:, 2]], axis=0)
        weight_out = jnp.einsum(
            "rn,rd->nd", tok_block[:, 3], grad_tok, preferred_element_type=jnp.float32
        )
        grad_mixture = jnp.einsum(
            "rd,nd->rn", grad_tok, wout_a, preferred_element_type=jnp.float32
        ).astype(jnp.bfloat16)
        grad_query, grad_keys, grad_values = attend_backward(
            split_heads(tok_block[:, 0]),
            split_heads(key_rows),
            split_heads(value_rows),
            allowed,
            token_lse,
            split_heads(grad_mixture),
        )
        grad_query = grad_query.reshape(token_rows, local_width)
        grad_keys = grad_keys.reshape(2 * token_rows, local_width)
        grad_values = grad_values.reshape(2 * token_rows, local_width)
        grad_proj = jnp.stack(
            [
                grad_query,
                grad_keys[token_rows:] + carry_keys,
                grad_values[token_rows:] + carry_values,
            ],
            axis=1,
        ).astype(jnp.bfloat16)
        weight_in = jnp.einsum(
            "rd,rcn->dcn", normed_tok, grad_proj, preferred_element_type=jnp.float32
        )
        grad_normed = jnp.einsum(
            "rcn,dcn->rd", grad_proj, wqkv_a, preferred_element_type=jnp.float32
        )
        return (
            grad_normed,
            empty_state,
            grad_keys[:token_rows],
            grad_values[:token_rows],
            renewed(grad_sums, active_tick, {0: weight_in, 1: weight_out}),
        )

    def feed_backward(up_projection_weight, down_projection_weight, up_slot, down_slot):

        def backward_fn(
            grad_tok,
            grad_st,
            normed_tok,
            normed_st,
            tok_block,
            st_block,
            prior_block,
            token_lse,
            state_lse,
            opening,
            carry_keys,
            carry_values,
            grad_sums,
            active_tick,
        ):
            hidden_rows = jnp.dot(
                normed_tok, up_projection_weight, preferred_element_type=jnp.float32
            )
            active_flags, gelu_back = jax.vjp(smooth, hidden_rows)
            weight_down = jnp.einsum(
                "rf,rd->fd",
                active_flags.astype(jnp.bfloat16),
                grad_tok,
                preferred_element_type=jnp.float32,
            )
            grad_active = jnp.einsum(
                "rd,fd->rf", grad_tok, down_projection_weight, preferred_element_type=jnp.float32
            )
            grad_hidden = gelu_back(grad_active)[0].astype(jnp.bfloat16)
            weight_up = jnp.einsum(
                "rd,rf->df", normed_tok, grad_hidden, preferred_element_type=jnp.float32
            )
            grad_normed = jnp.einsum(
                "rf,df->rd", grad_hidden, up_projection_weight, preferred_element_type=jnp.float32
            )
            return (
                grad_normed,
                empty_state,
                empty_carry,
                empty_carry,
                renewed(grad_sums, active_tick, {up_slot: weight_up, down_slot: weight_down}),
            )

        return backward_fn

    def recurrent_backward(
        grad_tok,
        grad_st,
        normed_tok,
        normed_st,
        tok_block,
        st_block,
        prior_block,
        token_lse,
        state_lse,
        opening,
        carry_keys,
        carry_values,
        grad_sums,
        active_tick,
    ):
        reach_prior, reach_current = token_masks(opening)
        allowed = jnp.concatenate([reach_prior, reach_current, state_keys_all], axis=1)
        token_keys = jnp.concatenate([prior_block[:, 1], tok_block[:, 1], st_block[:, 1]], axis=0)
        token_values = jnp.concatenate([prior_block[:, 2], tok_block[:, 2], st_block[:, 2]], axis=0)
        state_keys = jnp.concatenate([tok_block[:, 1], st_block[:, 1]], axis=0)
        state_values = jnp.concatenate([tok_block[:, 2], st_block[:, 2]], axis=0)
        weight_out = jnp.einsum(
            "rn,rd->nd", tok_block[:, 3], grad_tok, preferred_element_type=jnp.float32
        )
        weight_state_out = jnp.einsum(
            "sn,sd->nd", st_block[:, 3], grad_st, preferred_element_type=jnp.float32
        )
        grad_token_mixture = jnp.einsum(
            "rd,nd->rn", grad_tok, wout_c, preferred_element_type=jnp.float32
        ).astype(jnp.bfloat16)
        grad_state_mixture = jnp.einsum(
            "sd,nd->sn", grad_st, sout_c, preferred_element_type=jnp.float32
        ).astype(jnp.bfloat16)
        grad_query, grad_keys, grad_values = attend_backward(
            split_heads(tok_block[:, 0]),
            split_heads(token_keys),
            split_heads(token_values),
            allowed,
            token_lse,
            split_heads(grad_token_mixture),
        )
        state_query, state_grad_keys, state_grad_values = attend_backward(
            split_heads(st_block[:, 0]),
            split_heads(state_keys),
            split_heads(state_values),
            every_key,
            state_lse,
            split_heads(grad_state_mixture),
        )
        grad_query = grad_query.reshape(token_rows, local_width)
        grad_keys = grad_keys.reshape(2 * token_rows + state_count, local_width)
        grad_values = grad_values.reshape(2 * token_rows + state_count, local_width)
        state_query = state_query.reshape(state_count, local_width)
        state_grad_keys = state_grad_keys.reshape(token_rows + state_count, local_width)
        state_grad_values = state_grad_values.reshape(token_rows + state_count, local_width)
        own_keys = (
            grad_keys[token_rows : 2 * token_rows] + state_grad_keys[:token_rows] + carry_keys
        )
        own_values = (
            grad_values[token_rows : 2 * token_rows] + state_grad_values[:token_rows] + carry_values
        )
        cell_keys = grad_keys[2 * token_rows :] + state_grad_keys[token_rows:]
        cell_values = grad_values[2 * token_rows :] + state_grad_values[token_rows:]
        grad_proj = jnp.stack([grad_query, own_keys, own_values], axis=1).astype(jnp.bfloat16)
        grad_state_proj = jnp.stack([state_query, cell_keys, cell_values], axis=1).astype(
            jnp.bfloat16
        )
        weight_in = jnp.einsum(
            "rd,rcn->dcn", normed_tok, grad_proj, preferred_element_type=jnp.float32
        )
        weight_state_in = jnp.einsum(
            "sd,scn->dcn", normed_st, grad_state_proj, preferred_element_type=jnp.float32
        )
        grad_normed = jnp.einsum(
            "rcn,dcn->rd", grad_proj, wqkv_c, preferred_element_type=jnp.float32
        )
        grad_state_normed = jnp.einsum(
            "scn,dcn->sd", grad_state_proj, sqkv_c, preferred_element_type=jnp.float32
        )
        changes = {4: weight_in, 5: weight_state_in, 6: weight_out, 7: weight_state_out}
        return (
            grad_normed,
            grad_state_normed,
            grad_keys[:token_rows],
            grad_values[:token_rows],
            renewed(grad_sums, active_tick, changes),
        )

    forward_branches = [
        plain_forward,
        feed_forward(up_b, down_b),
        recurrent_forward,
        feed_forward(up_d, down_d),
    ]
    backward_branches = [
        plain_backward,
        feed_backward(up_b, down_b, 2, 3),
        recurrent_backward,
        feed_backward(up_d, down_d, 8, 9),
    ]

    def forward_tick(tick_number, carried):
        (
            received,
            state_carry,
            tok_normed,
            st_normed,
            tok_stored,
            st_stored,
            tok_lse_all,
            st_lse_all,
            entered,
            state_entered,
            updates,
            leaving_rows,
            finals,
        ) = carried
        block_number = tick_number - section_index
        active_tick = (block_number >= 0) & (block_number < block_count)
        block_index = jnp.clip(block_number, 0, block_count - 1)
        opening = begins[block_index]
        entering = jnp.where(
            section_index == 0, layer_input[0, block_index].astype(jnp.float32), received
        )
        state_in = jnp.where(opening, initial, state_carry)
        token_gain = token_gains[section_index]
        normed_shard = (entering * inverse_rms(entering) * token_gain).astype(jnp.bfloat16)
        state_normed_shard = (state_in * inverse_rms(state_in) * state_gain).astype(jnp.bfloat16)
        normed_tok, normed_st = (
            lax.all_gather(normed_shard, TENSOR, axis=0, tiled=True),
            lax.all_gather(state_normed_shard, TENSOR, axis=0, tiled=True),
        )
        prior_block = tok_stored[jnp.maximum(block_index - 1, 0)]
        branch, update_term, stored, state_stored, token_lse, state_lse = lax.switch(
            section_index, forward_branches, normed_tok, normed_st, prior_block, opening
        )
        branch_shard, update_shard = (
            lax.psum_scatter(
                branch.astype(jnp.bfloat16), TENSOR, scatter_dimension=0, tiled=True
            ).astype(jnp.float32),
            lax.psum_scatter(
                update_term.astype(jnp.bfloat16), TENSOR, scatter_dimension=0, tiled=True
            ).astype(jnp.float32),
        )
        leaving = entering + branch_shard
        state_new = retain * state_in + (1.0 - retain) * update_shard
        tok_normed = place_row(tok_normed, block_index, normed_tok, active_tick)
        st_normed = place_row(st_normed, block_index, normed_st, active_tick)
        tok_stored = place_row(tok_stored, block_index, stored, active_tick)
        st_stored = place_row(st_stored, block_index, state_stored, active_tick)
        tok_lse_all = place_row(tok_lse_all, block_index, token_lse, active_tick)
        st_lse_all = place_row(st_lse_all, block_index, state_lse, active_tick)
        entered = place_row(entered, block_index, entering, active_tick)
        state_entered = place_row(state_entered, block_index, state_in, active_tick)
        updates = place_row(updates, block_index, update_shard, active_tick)
        leaving_rows = place_row(leaving_rows, block_index, leaving, active_tick)
        on_cell = active_tick & on_cell_section
        state_carry = jnp.where(on_cell, state_new, state_carry)
        keep_final = on_cell & closes[block_index] & lively[block_index]
        slot_hit = (jnp.arange(SLOTS, dtype=jnp.int32) == numbers[block_index])[
            None, :, None
        ] & keep_final
        finals = jnp.where(slot_hit, state_new[:, None, :], finals)
        received = shifted(leaving.astype(jnp.bfloat16), SECTION, 1).astype(leaving.dtype)
        return (
            received,
            state_carry,
            tok_normed,
            st_normed,
            tok_stored,
            st_stored,
            tok_lse_all,
            st_lse_all,
            entered,
            state_entered,
            updates,
            leaving_rows,
            finals,
        )

    forward_start = (
        jnp.zeros((shard_rows, model_width), jnp.float32),
        jnp.zeros((state_shard, model_width), jnp.float32),
        jnp.zeros((block_count, token_rows, model_width), jnp.bfloat16),
        jnp.zeros((block_count, state_count, model_width), jnp.bfloat16),
        jnp.zeros((block_count, token_rows, 4, local_width), jnp.bfloat16),
        jnp.zeros((block_count, state_count, 4, local_width), jnp.bfloat16),
        jnp.zeros((block_count, local_heads, token_rows), jnp.float32),
        jnp.zeros((block_count, local_heads, state_count), jnp.float32),
        jnp.zeros((block_count, shard_rows, model_width), jnp.float32),
        jnp.zeros((block_count, state_shard, model_width), jnp.float32),
        jnp.zeros((block_count, state_shard, model_width), jnp.float32),
        jnp.zeros((block_count, shard_rows, model_width), jnp.float32),
        jnp.zeros((state_shard, SLOTS, model_width), jnp.float32),
    )
    (
        _,
        _,
        tok_normed,
        st_normed,
        tok_stored,
        st_stored,
        tok_lse_all,
        st_lse_all,
        entered,
        state_entered,
        updates,
        leaving_rows,
        finals,
    ) = lax.fori_loop(0, block_count + 3, forward_tick, forward_start)
    gain_rows_of_section = jnp.array([0, 1, 2, 4], dtype=jnp.int32)
    small_rows = jnp.arange(6, dtype=jnp.int32)[:, None]

    def backward_tick(tick_number, carried):
        (
            received,
            state_grad,
            carry_keys,
            carry_values,
            grad_sums,
            smalls,
            initial_grad,
            input_rows,
        ) = carried
        block_number = block_count - 1 - tick_number + 3 - section_index
        active_tick = (block_number >= 0) & (block_number < block_count)
        block_index = jnp.clip(block_number, 0, block_count - 1)
        opening = begins[block_index]
        arriving = jnp.where(
            section_index == 3,
            output_grad[0, block_index].astype(jnp.float32)
            * lively[block_index].astype(jnp.float32),
            received,
        )
        update_grad = (1.0 - retain) * state_grad
        grad_tok, grad_st = (
            lax.all_gather(arriving.astype(jnp.bfloat16), TENSOR, axis=0, tiled=True),
            lax.all_gather(update_grad.astype(jnp.bfloat16), TENSOR, axis=0, tiled=True),
        )
        grad_normed_tok, grad_normed_st, prior_keys, prior_values, grad_sums = lax.switch(
            section_index,
            backward_branches,
            grad_tok,
            grad_st,
            tok_normed[block_index],
            st_normed[block_index],
            tok_stored[block_index],
            st_stored[block_index],
            tok_stored[jnp.maximum(block_index - 1, 0)],
            tok_lse_all[block_index],
            st_lse_all[block_index],
            opening,
            carry_keys,
            carry_values,
            grad_sums,
            active_tick,
        )
        tok_shard, st_shard = (
            lax.psum_scatter(
                grad_normed_tok.astype(jnp.bfloat16), TENSOR, scatter_dimension=0, tiled=True
            ).astype(jnp.float32),
            lax.psum_scatter(
                grad_normed_st.astype(jnp.bfloat16), TENSOR, scatter_dimension=0, tiled=True
            ).astype(jnp.float32),
        )
        grad_entering, token_gain_term = norm_back(
            entered[block_index], token_gains[section_index], tok_shard
        )
        leaving_grad = arriving + grad_entering
        state_in = state_entered[block_index]
        grad_state_norm, state_gain_term = norm_back(state_in, state_gain, st_shard)
        grad_state_in = retain * state_grad + grad_state_norm
        bias_term = (
            jnp.sum(state_grad * (state_in - updates[block_index]), axis=0)
            * retain
            * (1.0 - retain)
        )
        on_cell = active_tick & on_cell_section
        gain_part = (small_rows == gain_rows_of_section[section_index]).astype(
            jnp.float32
        ) * token_gain_term[None, :]
        cell_part = (small_rows == 3).astype(jnp.float32) * state_gain_term[None, :] + (
            small_rows == 5
        ).astype(jnp.float32) * bias_term[None, :]
        smalls = (
            smalls + jnp.where(active_tick, gain_part, 0.0) + jnp.where(on_cell, cell_part, 0.0)
        )
        initial_grad = initial_grad + jnp.where(on_cell & opening, grad_state_in, 0.0)
        state_grad = jnp.where(on_cell, jnp.where(opening, 0.0, grad_state_in), state_grad)
        carry_keys = jnp.where(active_tick, prior_keys, carry_keys)
        carry_values = jnp.where(active_tick, prior_values, carry_values)
        input_rows = place_row(input_rows, block_index, leaving_grad, active_tick)
        received = shifted(for_sending(leaving_grad), SECTION, -1).astype(leaving_grad.dtype)
        return (
            received,
            state_grad,
            carry_keys,
            carry_values,
            grad_sums,
            smalls,
            initial_grad,
            input_rows,
        )

    zero_grads = (
        jnp.zeros(wqkv_a.shape, jnp.float32),
        jnp.zeros(wout_a.shape, jnp.float32),
        jnp.zeros(up_b.shape, jnp.float32),
        jnp.zeros(down_b.shape, jnp.float32),
        jnp.zeros(wqkv_c.shape, jnp.float32),
        jnp.zeros(sqkv_c.shape, jnp.float32),
        jnp.zeros(wout_c.shape, jnp.float32),
        jnp.zeros(sout_c.shape, jnp.float32),
        jnp.zeros(up_d.shape, jnp.float32),
        jnp.zeros(down_d.shape, jnp.float32),
    )
    backward_start = (
        jnp.zeros((shard_rows, model_width), jnp.float32),
        jnp.zeros((state_shard, model_width), jnp.float32),
        empty_carry,
        empty_carry,
        zero_grads,
        jnp.zeros((6, model_width), jnp.float32),
        jnp.zeros((state_shard, model_width), jnp.float32),
        jnp.zeros((block_count, shard_rows, model_width), jnp.float32),
    )
    _, _, _, _, grad_sums, smalls, initial_grad, input_rows = lax.fori_loop(
        0, block_count + 3, backward_tick, backward_start
    )
    out_term = jnp.where(
        section_index == 3, leaving_rows * lively[:, None, None].astype(jnp.float32), 0.0
    )[None]
    input_term = jnp.where(section_index == 0, input_rows, 0.0)[None]
    final_term = jnp.where(section_index == 2, finals, 0.0)[None]
    out_share, input_share, final_share = (
        lax.psum_scatter(
            out_term.astype(jnp.bfloat16), SECTION, scatter_dimension=3, tiled=True
        ).astype(jnp.float32),
        lax.psum_scatter(
            input_term.astype(jnp.bfloat16), SECTION, scatter_dimension=3, tiled=True
        ).astype(jnp.float32),
        lax.psum_scatter(
            final_term.astype(jnp.bfloat16), SECTION, scatter_dimension=3, tiled=True
        ).astype(jnp.float32),
    )
    (
        grad_qkv_a,
        grad_out_a,
        grad_upper_b,
        grad_lower_b,
        grad_qkv_c,
        grad_state_qkv,
        grad_out_c,
        grad_state_out,
        grad_upper_d,
        grad_lower_d,
    ) = grad_sums
    totals = (
        lax.psum(grad_qkv_a.astype(jnp.bfloat16), DP).astype(jnp.float32),
        lax.psum(grad_out_a.astype(jnp.bfloat16), DP).astype(jnp.float32),
        lax.psum(grad_upper_b.astype(jnp.bfloat16), DP).astype(jnp.float32),
        lax.psum(grad_lower_b.astype(jnp.bfloat16), DP).astype(jnp.float32),
        lax.psum(grad_qkv_c.astype(jnp.bfloat16), DP).astype(jnp.float32),
        lax.psum(grad_state_qkv.astype(jnp.bfloat16), DP).astype(jnp.float32),
        lax.psum(grad_out_c.astype(jnp.bfloat16), DP).astype(jnp.float32),
        lax.psum(grad_state_out.astype(jnp.bfloat16), DP).astype(jnp.float32),
        lax.psum(grad_upper_d.astype(jnp.bfloat16), DP).astype(jnp.float32),
        lax.psum(grad_lower_d.astype(jnp.bfloat16), DP).astype(jnp.float32),
        lax.psum(initial_grad.astype(jnp.bfloat16), DP).astype(jnp.float32),
    )
    small_total = lax.psum(smalls, (DP, TENSOR))
    shares = (
        lax.psum_scatter(
            totals[0].astype(jnp.bfloat16), SECTION, scatter_dimension=0, tiled=True
        ).astype(jnp.float32),
        lax.psum_scatter(
            totals[1].astype(jnp.bfloat16), SECTION, scatter_dimension=1, tiled=True
        ).astype(jnp.float32),
        lax.psum_scatter(
            totals[2].astype(jnp.bfloat16), SECTION, scatter_dimension=0, tiled=True
        ).astype(jnp.float32),
        lax.psum_scatter(
            totals[3].astype(jnp.bfloat16), SECTION, scatter_dimension=1, tiled=True
        ).astype(jnp.float32),
        lax.psum_scatter(
            totals[4].astype(jnp.bfloat16), SECTION, scatter_dimension=0, tiled=True
        ).astype(jnp.float32),
        lax.psum_scatter(
            totals[5].astype(jnp.bfloat16), SECTION, scatter_dimension=0, tiled=True
        ).astype(jnp.float32),
        lax.psum_scatter(
            totals[6].astype(jnp.bfloat16), SECTION, scatter_dimension=1, tiled=True
        ).astype(jnp.float32),
        lax.psum_scatter(
            totals[7].astype(jnp.bfloat16), SECTION, scatter_dimension=1, tiled=True
        ).astype(jnp.float32),
        lax.psum_scatter(
            totals[8].astype(jnp.bfloat16), SECTION, scatter_dimension=0, tiled=True
        ).astype(jnp.float32),
        lax.psum_scatter(
            totals[9].astype(jnp.bfloat16), SECTION, scatter_dimension=1, tiled=True
        ).astype(jnp.float32),
        lax.psum_scatter(
            totals[10].astype(jnp.bfloat16), SECTION, scatter_dimension=1, tiled=True
        ).astype(jnp.float32),
        lax.psum_scatter(
            small_total.astype(jnp.bfloat16), SECTION, scatter_dimension=1, tiled=True
        ).astype(jnp.float32),
    )
    small_share = shares[11]
    return (
        out_share.astype(jnp.bfloat16),
        final_share,
        input_share,
        small_share[0],
        shares[0],
        shares[1],
        small_share[1],
        shares[2],
        shares[3],
        small_share[2],
        small_share[3],
        shares[4],
        shares[5],
        shares[6],
        shares[7],
        small_share[5],
        shares[10],
        small_share[4],
        shares[8],
        shares[9],
    )


CHAIN = 4
MESH = pl.DeviceIdType.MESH
SCALE = 1.0 / math.sqrt(HEAD_DIM)
LOG2_SCALE = SCALE * math.log2(math.e)
ALL_AXES = (SECTION, DP, TENSOR)
GROUP = (SECTION, TENSOR)
VMEM_BYTES = 60 * 1024 * 1024
CHUNK = 256


def block_of(section, tensor):
    high = section // 2
    return 2 * (2 * high + (tensor + high) % 2) + section % 2


DEVICE_OF_BLOCK = [0] * 8
for _section in range(4):
    for _tensor in range(2):
        DEVICE_OF_BLOCK[block_of(_section, _tensor)] = 2 * _section + _tensor
TO_NEXT = [(DEVICE_OF_BLOCK[b], DEVICE_OF_BLOCK[b + 1]) for b in range(7)]
TO_PRIOR = [(there, here) for here, there in TO_NEXT]
SWAP = [(0, 1), (1, 0)]


def params(**extra):
    return pltpu.CompilerParams(vmem_limit_bytes=VMEM_BYTES, **extra)


def nt(a, b):
    return lax.dot_general(a, b, (((1,), (1,)), ((), ())), preferred_element_type=jnp.float32)


def nn(a, b):
    return lax.dot_general(a, b, (((1,), (0,)), ((), ())), preferred_element_type=jnp.float32)


def tn(a, b):
    return lax.dot_general(a, b, (((0,), (0,)), ((), ())), preferred_element_type=jnp.float32)


def bf(a):
    return a.astype(jnp.bfloat16)


def with_ones(values):
    return jnp.concatenate([values, jnp.ones_like(values)], axis=1)


def later_mask(rows):
    return lax.broadcasted_iota(jnp.int32, (rows, rows), 1) > lax.broadcasted_iota(
        jnp.int32, (rows, rows), 0
    )


def window_scores(query, k, pk, start, rows, bar):
    stop = start + query.shape[0]
    own = nt(query, k[:stop])
    prior = nt(query, pk[start:]) + bar
    later = later_mask(query.shape[0])
    pieces = [jnp.where(later, prior[:, : stop - start], own[:, start:])]
    if start:
        pieces = [own[:, :start]] + pieces
    if stop < rows:
        pieces = pieces + [prior[:, stop - start :]]
    return jnp.concatenate(pieces, axis=1) if len(pieces) > 1 else pieces[0]


def window_parts(values, start):
    size = values.shape[0]
    later = later_mask(size)
    middle = values[:, start : start + size]
    zero = jnp.zeros_like(middle)
    own, prior = jnp.where(later, zero, middle), jnp.where(later, middle, zero)
    if start:
        own = jnp.concatenate([values[:, :start], own], axis=1)
    if start + size < values.shape[1]:
        prior = jnp.concatenate([prior, values[:, start + size :]], axis=1)
    return own, prior


def attend_kernel(with_states, *refs):
    if with_states:
        open_ref, q, k, v, pk, pv, sk, sv, out, lse = refs
    else:
        open_ref, q, k, v, pk, pv, out, lse = refs
    rows = q.shape[0]
    bar = jnp.where(open_ref[0] > 0, NEGATIVE, 0.0)
    keys, prior_keys = k[...], pk[...]
    values, prior_values = with_ones(v[...]), with_ones(pv[...])
    if with_states:
        state_keys, state_values = sk[...], with_ones(sv[...])
    for start in range(0, rows, CHUNK):
        query = q[start : start + CHUNK]
        scores = window_scores(query, keys, prior_keys, start, rows, bar)
        top = jnp.max(scores, axis=-1, keepdims=True)
        if with_states:
            more = nt(query, state_keys)
            top = jnp.maximum(top, jnp.max(more, axis=-1, keepdims=True))
        own, prior = window_parts(bf(jnp.exp2((scores - top) * LOG2_SCALE)), start)
        mixed = nn(own, values[: start + CHUNK]) + nn(prior, prior_values[start:])
        if with_states:
            mixed = mixed + nn(bf(jnp.exp2((more - top) * LOG2_SCALE)), state_values)
        total = mixed[:, HEAD_DIM:]
        out[start : start + CHUNK] = bf(mixed[:, :HEAD_DIM] / total)
        lse[0, start : start + CHUNK] = top * LOG2_SCALE + jnp.log2(total[:, :1])


def side_blocks(rows, offset, heads):
    return (
        pl.BlockSpec((rows, HEAD_DIM), lambda h: (0, offset + jnp.minimum(h, heads - 1))),
        pl.BlockSpec((rows, HEAD_DIM), lambda h: (0, offset + jnp.maximum(h - heads, 0))),
    )


def lse_blocks(rows, heads):
    return (
        pl.BlockSpec((1, rows, 1), lambda h: (jnp.minimum(h, heads - 1), 0, 0)),
        pl.BlockSpec((1, rows, 1), lambda h: (jnp.maximum(h - heads, 0), 0, 0)),
    )


def both_sides(kernel, inputs, outputs, open_ref, *refs):
    ins, outs, scratch = refs[: 2 * inputs], refs[2 * inputs : 2 * (inputs + outputs)], refs[2 * (inputs + outputs) :]
    own = pl.program_id(0) < pl.num_programs(0) // 2
    pl.when(own)(lambda: kernel(open_ref, *ins[:inputs], *outs[:outputs], *scratch))
    pl.when(jnp.logical_not(own))(lambda: kernel(open_ref, *ins[inputs:], *outs[outputs:], *scratch))


def attend(opening, projs, priors, states=None):
    rows, width = projs[0].shape[0], projs[0].shape[1] // 3
    heads = width // HEAD_DIM
    columns = [side_blocks(rows, i * heads, heads) for i in (0, 1, 2, 0, 1)]
    arrays = [projs, projs, projs, priors, priors]
    keys = 2 * rows
    if states is not None:
        columns += [side_blocks(states[0].shape[0], i * heads, heads) for i in (1, 2)]
        arrays += [states, states]
        keys += states[0].shape[0]
    outs = [side_blocks(rows, 0, heads), lse_blocks(rows, heads)]
    mixed0, lse0, mixed1, lse1 = pl.pallas_call(
        functools.partial(
            both_sides, functools.partial(attend_kernel, states is not None), len(arrays), 2
        ),
        grid=(2 * heads,),
        in_specs=[pl.BlockSpec(memory_space=pltpu.SMEM)]
        + [pair[side] for side in range(2) for pair in columns],
        out_specs=[pair[side] for side in range(2) for pair in outs],
        out_shape=[
            jax.ShapeDtypeStruct((rows, width), jnp.bfloat16),
            jax.ShapeDtypeStruct((heads, rows, 1), jnp.float32),
        ]
        * 2,
        compiler_params=params(),
        cost_estimate=pl.CostEstimate(
            flops=8 * rows * keys * width,
            bytes_accessed=4 * rows * width * 8,
            transcendentals=rows * keys * heads,
        ),
    )(opening, *(pair[side] for side in range(2) for pair in arrays))
    return mixed0, lse0, mixed1, lse1


def attend_back_kernel(with_states, *refs):
    if with_states:
        (open_ref, q, k, v, pk, pv, sk, sv, gmix, mix, lse) = refs[:11]
        (gq, gk, gv, gpk, gpv, gsk, gsv) = refs[11:18]
    else:
        (open_ref, q, k, v, pk, pv, gmix, mix, lse) = refs[:9]
        (gq, gk, gv, gpk, gpv) = refs[9:14]
    gpk_sum, gpv_sum = refs[-2:]
    rows = q.shape[0]
    bar = jnp.where(open_ref[0] > 0, NEGATIVE, 0.0)
    keys, prior_keys, values, prior_values = k[...], pk[...], v[...], pv[...]
    if with_states:
        state_keys, state_values = sk[...], sv[...]
    for start in range(0, rows, CHUNK):
        stop = start + CHUNK
        query, grad, log_total = q[start:stop], gmix[start:stop], lse[0, start:stop]
        inner = jnp.sum(
            grad.astype(jnp.float32) * mix[start:stop].astype(jnp.float32), axis=-1, keepdims=True
        )
        scores = window_scores(query, keys, prior_keys, start, rows, bar)
        weights = jnp.exp2(scores * LOG2_SCALE - log_total)
        grad_weights = window_scores(grad, values, prior_values, start, rows, 0.0)
        own, prior = window_parts(bf(weights), start)
        own_scores, prior_scores = window_parts(bf(weights * (grad_weights - inner)), start)
        grad_query = nn(own_scores, keys[:stop]) + nn(prior_scores, prior_keys[start:])
        add_own_v, add_own_k = tn(own, grad), tn(own_scores, query)
        add_prior_v, add_prior_k = tn(prior, grad), tn(prior_scores, query)
        if with_states:
            more = jnp.exp2(nt(query, state_keys) * LOG2_SCALE - log_total)
            from_states = bf(more * (nt(grad, state_values) - inner))
            grad_query = grad_query + nn(from_states, state_keys)
            add_sv, add_sk = tn(bf(more), grad), tn(from_states, query)
        gq[start:stop] = bf(grad_query * SCALE)
        if start == 0:
            gv[:stop], gk[:stop] = add_own_v, add_own_k * SCALE
            gpv_sum[...], gpk_sum[...] = add_prior_v, add_prior_k
            if with_states:
                gsv[...], gsk[...] = add_sv, add_sk * SCALE
        else:
            gv[:start] += add_own_v[:start]
            gk[:start] += add_own_k[:start] * SCALE
            gv[start:stop], gk[start:stop] = add_own_v[start:], add_own_k[start:] * SCALE
            gpv_sum[start:] += add_prior_v
            gpk_sum[start:] += add_prior_k
            if with_states:
                gsv[...] += add_sv
                gsk[...] += add_sk * SCALE
    gpv[...] = bf(gpv_sum[...])
    gpk[...] = bf(gpk_sum[...] * SCALE)


def attend_back(opening, projs, priors, grads, mixed, lse, states=None):
    rows, width = projs[0].shape[0], projs[0].shape[1] // 3
    heads = width // HEAD_DIM
    columns = [side_blocks(rows, i * heads, heads) for i in (0, 1, 2, 0, 1)]
    arrays = [projs, projs, projs, priors, priors]
    kinds = [jnp.bfloat16, jnp.float32, jnp.float32, jnp.bfloat16, jnp.bfloat16]
    keys = 2 * rows
    if states is not None:
        columns += [side_blocks(states[0].shape[0], i * heads, heads) for i in (1, 2)]
        arrays += [states, states]
        kinds += [jnp.float32, jnp.float32]
        keys += states[0].shape[0]
    columns += [side_blocks(rows, 0, heads)] * 2 + [lse_blocks(rows, heads)]
    arrays += [grads, mixed, lse]
    results = pl.pallas_call(
        functools.partial(
            both_sides, functools.partial(attend_back_kernel, states is not None), len(arrays), len(kinds)
        ),
        grid=(2 * heads,),
        in_specs=[pl.BlockSpec(memory_space=pltpu.SMEM)]
        + [pair[side] for side in range(2) for pair in columns],
        out_specs=[side_blocks(rows, 0, heads)[side] for side in range(2) for _ in kinds],
        out_shape=[jax.ShapeDtypeStruct((rows, width), kind) for kind in kinds] * 2,
        scratch_shapes=[pltpu.VMEM((rows, HEAD_DIM), jnp.float32)] * 2,
        compiler_params=params(),
        cost_estimate=pl.CostEstimate(
            flops=20 * rows * keys * width,
            bytes_accessed=4 * rows * width * 24,
            transcendentals=rows * keys * heads,
        ),
    )(opening, *(pair[side] for side in range(2) for pair in arrays))
    return results[: len(kinds)], results[len(kinds) :]


KINDS = 9
FLIGHT = 4


class Spread:
    def __init__(self, sources, targets, send, recv):
        section, tensor, group = (lax.axis_index(a) for a in (SECTION, TENSOR, DP))
        self.sources, self.targets, self.send, self.recv = sources, targets, send, recv
        self.core, self.high, self.near = section % 2, section // 2, group % 2
        self.across = {TENSOR: 1 - tensor}
        self.along = {SECTION: (section + 2) % 4}
        self.beside = {DP: group + 1 - 2 * self.near}
        self.other = {SECTION: section + 1 - 2 * self.core}

    def partners(self):
        return [self.across, self.along, self.beside, self.other]

    def copy(self, kind, w):
        size = self.targets[w].shape[0] // 8
        y, z = self.high, self.near
        high, near, first, rows, to = (
            (y, z, 0, size, self.across),
            (y, z, 0, size, self.along),
            (y, z, 0, size, self.beside),
            (y, 1 - z, 0, size // 2, self.along),
            (1 - y, z, size // 2, size // 2, self.beside),
            (y, z, 0, size, self.other),
            (1 - y, z, 0, size, self.other),
            (y, 1 - z, 0, size, self.other),
            (1 - y, 1 - z, 0, size, self.other),
        )[kind]
        part = (near * 2 + high) * 2 + self.core
        where = pl.ds(pl.multiple_of(part * size + first, rows), rows)
        source = self.sources[w] if kind == 0 else self.targets[w]
        return pltpu.make_async_remote_copy(
            src_ref=source.at[where], dst_ref=self.targets[w].at[where],
            send_sem=self.send.at[kind * len(self.targets) + w],
            recv_sem=self.recv.at[kind * len(self.targets) + w],
            device_id=to, device_id_type=MESH,
        )

    def begin(self, w):
        self.copy(0, w).start()

    def hop(self, w):
        self.copy(0, w).wait_recv()
        for kind in (1, 2, 5):
            self.copy(kind, w).start()

    def cross(self, w):
        for kind in (1, 2):
            self.copy(kind, w).wait_recv()
        for kind in (3, 4, 6, 7):
            self.copy(kind, w).start()

    def close(self, w):
        for kind in (3, 4):
            self.copy(kind, w).wait_recv()
        self.copy(8, w).start()

    def end(self, w):
        for kind in (5, 6, 7, 8):
            self.copy(kind, w).wait_recv()
        for kind in range(KINDS):
            self.copy(kind, w).wait_send()


class Join:
    def __init__(self, source, theirs, mine, target, local, send, recv, i):
        tensor = lax.axis_index(TENSOR)
        rows = source.shape[-2]
        where = pl.ds(pl.multiple_of(tensor * rows, rows), rows)

        def of(index):
            return source if index is None else source.at[0, index]

        self.own = pltpu.make_async_copy(of(mine), target.at[where], local.at[i])
        self.remote = pltpu.make_async_remote_copy(
            src_ref=of(theirs), dst_ref=target.at[where], send_sem=send.at[i], recv_sem=recv.at[i],
            device_id={TENSOR: 1 - tensor}, device_id_type=MESH,
        )

    def start(self):
        self.remote.start()
        self.own.start()

    def wait(self):
        self.remote.wait()
        self.own.wait()


def meet(partners):
    barrier = pltpu.get_barrier_semaphore()
    for partner in partners:
        pl.semaphore_signal(barrier, inc=1, device_id=partner, device_id_type=MESH)
    pl.semaphore_wait(barrier, len(partners))


def gather_kernel(count, layer_input, init_states, *refs):
    sources, refs = refs[:count], refs[count:]
    tokens, before, initial = refs[:3]
    targets = refs[3 : 3 + count]
    send, recv, local, join_send, join_recv = refs[3 + count :]
    spread = Spread(sources, targets, send, recv)
    section, tensor = lax.axis_index(SECTION), lax.axis_index(TENSOR)
    block, partner = block_of(section, tensor), block_of(section, 1 - tensor)
    joins = [
        Join(layer_input, partner, block, tokens, local, join_send, join_recv, 0),
        Join(
            layer_input, jnp.maximum(partner - 1, 0), jnp.maximum(block - 1, 0),
            before, local, join_send, join_recv, 1,
        ),
        Join(init_states, None, None, initial, local, join_send, join_recv, 2),
    ]
    meet(spread.partners())
    def begin(i):
        if i < count:
            spread.begin(i)
        elif i < count + len(joins):
            joins[i - count].start()

    for i in range(FLIGHT):
        begin(i)
    for w in range(count + 2):
        if w < count:
            spread.hop(w)
        begin(w + FLIGHT)
        if 0 <= w - 1 < count:
            spread.cross(w - 1)
        if 0 <= w - 2 < count:
            spread.close(w - 2)
    for w in range(count):
        spread.end(w)
    for join in joins:
        join.wait()


def gather(layer_input, init_states, weights):
    count = len(weights)
    rows, width = 2 * layer_input.shape[2], layer_input.shape[3]
    dma = pltpu.SemaphoreType.DMA
    anywhere = pl.BlockSpec(memory_space=pl.ANY)
    shapes = [(rows, width)] * 2 + [(2 * init_states.shape[0], width)] + [w.shape for w in weights]
    results = pl.pallas_call(
        functools.partial(gather_kernel, count),
        in_specs=[anywhere] * (2 + count),
        out_specs=[anywhere] * (3 + count),
        out_shape=[jax.ShapeDtypeStruct(s, jnp.bfloat16) for s in shapes],
        scratch_shapes=[dma((KINDS * count,))] * 2 + [dma((3,))] * 3,
        compiler_params=params(collective_id=4, has_side_effects=True),
        cost_estimate=pl.CostEstimate(flops=0, bytes_accessed=200 * 1024 * 1024, transcendentals=0),
    )(layer_input, init_states, *weights)
    return results[:3], results[3:]


def neighbours():
    section, tensor = lax.axis_index(SECTION), lax.axis_index(TENSOR)
    block = block_of(section, tensor)

    return place_of((block + 7) % 8), place_of((block + 1) % 8)


def place_of(block):
    pair = block // 2
    high = pair // 2
    return {SECTION: 2 * high + block % 2, TENSOR: (pair + high) % 2}


class Scatter:
    def __init__(self, values, landed, send, recv, local):
        section, tensor = lax.axis_index(SECTION), lax.axis_index(TENSOR)
        block = block_of(section, tensor)
        self.members = [place_of((block + i) % 8) for i in range(1, 8)]
        rows, width = values[0].shape[0] // 2, values[0].shape[1] // 4

        def piece(value, to):
            high = pl.multiple_of(to[TENSOR] * rows, rows)
            left = pl.multiple_of(to[SECTION] * width, width)
            return value.at[pl.ds(high, rows), pl.ds(left, width)]

        self.copies = [
            pltpu.make_async_remote_copy(
                src_ref=piece(value, to), dst_ref=landed.at[j, block],
                send_sem=send.at[j * 7 + i], recv_sem=recv.at[j * 7 + i],
                device_id=to, device_id_type=MESH,
            )
            for j, value in enumerate(values)
            for i, to in enumerate(self.members)
        ]
        self.own = [
            pltpu.make_async_copy(
                piece(value, {SECTION: section, TENSOR: tensor}), landed.at[j, block], local.at[j]
            )
            for j, value in enumerate(values)
        ]

    def start(self):
        for copy in self.copies + self.own:
            copy.start()

    def wait(self):
        for copy in self.copies + self.own:
            copy.wait()


def pass_on(sent, landed, send_sem, recv_sem, slot, part, target):
    rows = pl.ds(part * CHUNK, CHUNK)
    return pltpu.make_async_remote_copy(
        src_ref=sent.at[slot, rows],
        dst_ref=landed.at[slot, rows],
        send_sem=send_sem.at[slot, part],
        recv_sem=recv_sem.at[slot, part],
        device_id=target,
        device_id_type=MESH,
    )


def chain_kernel(
    initial, starts, gain, keep, own, other, sqkv0, sqkv1, sout0, sout1, output_grad,
    state, hs, ps0, ps1, os0, os1, lse, update, fresh, cotangent,
    sent, landed, send_sem, recv_sem, local, join_send, join_recv,
):
    prior, following = neighbours()
    section, tensor = lax.axis_index(SECTION), lax.axis_index(TENSOR)
    join = Join(
        output_grad, block_of(section, 1 - tensor), block_of(section, tensor),
        cotangent, local, join_send, join_recv, 0,
    )
    meet([prior, following, {TENSOR: 1 - tensor}])
    join.start()
    count, width = initial.shape
    half = os0.shape[1]
    parts = count // CHUNK
    state[...] = initial[...].astype(jnp.float32)

    def copy(slot, part):
        return pass_on(sent, landed, send_sem, recv_sem, slot, part, following)

    def work(turn):
        for part in range(parts):
            rows = slice(part * CHUNK, (part + 1) * CHUNK)

            @pl.when(turn > 0)
            def _():
                slot = turn - 1
                copy(slot, part).wait_recv()
                state[rows] = jnp.where(
                    starts[...] > 0.0, initial[rows].astype(jnp.float32), landed[slot, rows].astype(jnp.float32)
                )

            value = state[rows]
            hidden = bf(value * inverse_rms(value) * gain[...])
            hs[rows] = hidden
            ps0[rows] = bf(nn(hidden, sqkv0[...]))
            ps1[rows] = bf(nn(hidden, sqkv1[...]))

        def one_head(h, carry):
            at = [pl.ds(pl.multiple_of(i * half + h * HEAD_DIM, HEAD_DIM), HEAD_DIM) for i in range(3)]
            for which, (tok, st, mixed) in enumerate(((own, ps0, os0), (other, ps1, os1))):
                tok_key, tok_value = tok[:, at[1]], with_ones(tok[:, at[2]])
                key, value = st[:, at[1]], with_ones(st[:, at[2]])
                for part in range(parts):
                    rows = slice(part * CHUNK, (part + 1) * CHUNK)
                    query = st[rows, at[0]]
                    score_tok, score = nt(query, tok_key), nt(query, key)
                    top = jnp.maximum(
                        jnp.max(score_tok, axis=-1, keepdims=True),
                        jnp.max(score, axis=-1, keepdims=True),
                    )
                    mix = nn(bf(jnp.exp2((score_tok - top) * LOG2_SCALE)), tok_value) + nn(
                        bf(jnp.exp2((score - top) * LOG2_SCALE)), value
                    )
                    total = mix[:, HEAD_DIM:]
                    mixed[rows, at[0]] = bf(mix[:, :HEAD_DIM] / total)
                    lse[which, h, rows] = top * LOG2_SCALE + jnp.log2(total[:, :1])
            return carry

        lax.fori_loop(0, half // HEAD_DIM, one_head, 0, unroll=True)
        for part in range(parts):
            rows = slice(part * CHUNK, (part + 1) * CHUNK)
            term = nn(os0[rows], sout0[...]) + nn(os1[rows], sout1[...])
            update[rows] = term
            renewed_state = bf(keep[...] * state[rows] + (1.0 - keep[...]) * term)
            fresh[rows] = renewed_state

            @pl.when(turn < CHAIN - 1)
            def _():
                sent[turn, rows] = renewed_state
                copy(turn, part).start()

    parity = block_of(section, tensor) % 2

    def one_round(turn, nothing):
        pl.when(parity == turn % 2)(lambda: work(turn))
        return nothing

    lax.fori_loop(0, CHAIN, one_round, 0)
    for slot in range(CHAIN - 1):

        @pl.when(parity == slot % 2)
        def _():
            for part in range(parts):
                copy(slot, part).wait_send()

    join.wait()


def chain(initial, starts, gain, keep, own, other, sqkv0, sqkv1, sout0, sout1, output_grad):
    count, width = initial.shape
    half = sout0.shape[0]
    heads = half // HEAD_DIM
    bf16, f32 = jnp.bfloat16, jnp.float32
    vmem, anywhere = pl.BlockSpec(memory_space=pltpu.VMEM), pl.BlockSpec(memory_space=pl.ANY)
    dma = pltpu.SemaphoreType.DMA
    parts = count // CHUNK
    return pl.pallas_call(
        chain_kernel,
        in_specs=[vmem] * 10 + [anywhere],
        out_specs=[vmem] * 9 + [anywhere],
        out_shape=[
            jax.ShapeDtypeStruct((count, width), f32),
            jax.ShapeDtypeStruct((count, width), bf16),
            jax.ShapeDtypeStruct((count, 3 * half), bf16),
            jax.ShapeDtypeStruct((count, 3 * half), bf16),
            jax.ShapeDtypeStruct((count, half), bf16),
            jax.ShapeDtypeStruct((count, half), bf16),
            jax.ShapeDtypeStruct((2, heads, count, 1), f32),
            jax.ShapeDtypeStruct((count, width), f32),
            jax.ShapeDtypeStruct((count, width), bf16),
            jax.ShapeDtypeStruct((2 * output_grad.shape[2], width), bf16),
        ],
        scratch_shapes=[
            pltpu.VMEM((CHAIN - 1, count, width), bf16),
            pltpu.VMEM((CHAIN - 1, count, width), bf16),
            dma((CHAIN - 1, parts)), dma((CHAIN - 1, parts)),
            dma((1,)), dma((1,)), dma((1,)),
        ],
        compiler_params=params(collective_id=1, has_side_effects=True),
        cost_estimate=pl.CostEstimate(
            flops=CHAIN * count * width * (8 * width + 8 * count),
            bytes_accessed=25 * 1024 * 1024,
            transcendentals=CHAIN * count * count * 4 * heads,
        ),
    )(initial, starts, gain, keep, own, other, sqkv0, sqkv1, sout0, sout1, output_grad)


LATE = 10


def chain_back_kernel(
    starts, ends, gain, keep, own, other, ps0, ps1, os0, os1, lse, *refs,
):
    distant, refs = refs[:LATE], refs[LATE:]
    result, ending, first_grad, gproj0, gproj1, gtok0, gtok1, gup, small, scattered = refs[:10]
    fetched, refs = refs[10 : 10 + LATE], refs[10 + LATE :]
    state, update, tok_k0, tok_v0, tok_k1, tok_v1, sqkv0, sqkv1, sout0, sout1 = fetched
    (
        grad_state, weights, grad_os0, grad_os1, sent, landed, send_sem, recv_sem, piece_send, piece_recv, piece_sem, late_sem
    ) = refs
    fetches = [
        pltpu.make_async_copy(source, target, late_sem.at[i])
        for i, (source, target) in enumerate(zip(distant, fetched))
    ]
    for fetch in fetches:
        fetch.start()
    prior, following = neighbours()
    scatter = Scatter((result, ending), scattered, piece_send, piece_recv, piece_sem)
    meet([prior, following] + scatter.members)
    scatter.start()
    count, width = state.shape
    half = os0.shape[1]
    heads = half // HEAD_DIM
    parts = count // CHUNK
    sides = (
        (own, ps0, os0, tok_k0, tok_v0, gproj0, gtok0, grad_os0),
        (other, ps1, os1, tok_k1, tok_v1, gproj1, gtok1, grad_os1),
    )

    def lanes(h):
        return [pl.ds(pl.multiple_of(i * half + h * HEAD_DIM, HEAD_DIM), HEAD_DIM) for i in range(3)]

    def copy(slot, part):
        return pass_on(sent, landed, send_sem, recv_sem, slot, part, prior)

    def prepare(h, carry):
        at = lanes(h)
        for which, (tok, st, *_) in enumerate(sides):
            tok_key, key = tok[:, at[1]], st[:, at[1]]
            for part in range(parts):
                rows = slice(part * CHUNK, (part + 1) * CHUNK)
                query, log_total = st[rows, at[0]], lse[which, h, rows]
                weights[which, h, rows, :count] = bf(
                    jnp.exp2(nt(query, tok_key) * LOG2_SCALE - log_total)
                )
                weights[which, h, rows, count:] = bf(
                    jnp.exp2(nt(query, key) * LOG2_SCALE - log_total)
                )
        return carry

    lax.fori_loop(0, heads, prepare, 0)
    for fetch in fetches:
        fetch.wait()
    grad_state[...] = jnp.zeros_like(grad_state)

    def work(turn):
        for part in range(parts):
            rows = slice(part * CHUNK, (part + 1) * CHUNK)

            @pl.when(turn > 0)
            def _():
                slot = turn - 1
                copy(slot, part).wait_recv()
                grad_state[rows] = jnp.where(
                    ends[...] > 0.0, 0.0, landed[slot, rows].astype(jnp.float32)
                )

            out = bf((1.0 - keep[...]) * grad_state[rows])
            gup[rows] = out
            grad_os0[rows] = bf(nt(out, sout0[...]))
            grad_os1[rows] = bf(nt(out, sout1[...]))

        def one_head(h, carry):
            at = lanes(h)
            for which, (tok, st, mixed, given_k, given_v, gproj, gtok, grad_os) in enumerate(sides):
                tok_key, tok_value = tok[:, at[1]], tok[:, at[2]]
                key, value = st[:, at[1]], st[:, at[2]]
                for part in range(parts):
                    rows = slice(part * CHUNK, (part + 1) * CHUNK)
                    query, grad = st[rows, at[0]], grad_os[rows, at[0]]
                    inner = jnp.sum(
                        grad.astype(jnp.float32) * mixed[rows, at[0]].astype(jnp.float32),
                        axis=-1, keepdims=True,
                    )
                    p_tok, p = weights[which, h, rows, :count], weights[which, h, rows, count:]
                    s_tok = bf(p_tok.astype(jnp.float32) * (nt(grad, tok_value) - inner))
                    s = bf(p.astype(jnp.float32) * (nt(grad, value) - inner))
                    gproj[rows, at[0]] = bf((nn(s_tok, tok_key) + nn(s, key)) * SCALE)
                    gk, gv = tn(s, query) * SCALE, tn(p, grad)
                    if part == 0:
                        total_k, total_v = gk + given_k[:, at[0]], gv + given_v[:, at[0]]
                    else:
                        total_k, total_v = total_k + gk, total_v + gv

                    @pl.when(turn >= CHAIN - 2)
                    def _():
                        gtk, gtv = tn(s_tok, query) * SCALE, tn(p_tok, grad)
                        if part == 0:
                            gtok[:, at[0]], gtok[:, at[1]] = gtk, gtv
                        else:
                            gtok[:, at[0]] += gtk
                            gtok[:, at[1]] += gtv

                gproj[:, at[1]], gproj[:, at[2]] = bf(total_k), bf(total_v)
            return carry

        lax.fori_loop(0, heads, one_head, 0, unroll=True)
        for part in range(parts):
            rows = slice(part * CHUNK, (part + 1) * CHUNK)
            back = nt(gproj0[rows], sqkv0[...]) + nt(gproj1[rows], sqkv1[...])
            value, new = state[rows], grad_state[rows]
            factor = inverse_rms(value)
            scaled = value * factor
            through = back * gain[...]
            leaving = keep[...] * new + factor * (
                through - scaled * jnp.mean(through * scaled, axis=-1, keepdims=True)
            )

            @pl.when(turn < CHAIN - 1)
            def _():
                sent[turn, rows] = bf(leaving)
                copy(turn, part).start()

            @pl.when(turn >= CHAIN - 2)
            def _():
                gain_term = jnp.sum(back * scaled, axis=0, keepdims=True)
                bias_term = jnp.sum(new * (value - update[rows]), axis=0, keepdims=True) * (
                    keep[...] * (1.0 - keep[...])
                )
                if part == 0:
                    small[0:1, :], small[1:2, :] = gain_term, bias_term
                else:
                    small[0:1, :] += gain_term
                    small[1:2, :] += bias_term
                first_grad[rows] = bf(jnp.where(starts[...] > 0.0, leaving, 0.0))

    parity = 1 - block_of(lax.axis_index(SECTION), lax.axis_index(TENSOR)) % 2

    def one_round(turn, nothing):
        pl.when(parity == turn % 2)(lambda: work(turn))
        return nothing

    lax.fori_loop(0, CHAIN, one_round, 0)
    for slot in range(CHAIN - 1):

        @pl.when(parity == slot % 2)
        def _():
            for part in range(parts):
                copy(slot, part).wait_send()

    scatter.wait()


def chain_back(
    starts, ends, state, update, gain, keep, own, other, ps0, ps1, os0, os1, lse,
    tok_k0, tok_v0, tok_k1, tok_v1, sqkv0, sqkv1, sout0, sout1, result, ending,
):
    count, width = state.shape
    half = sout0.shape[0]
    heads = half // HEAD_DIM
    bf16, f32 = jnp.bfloat16, jnp.float32
    vmem, anywhere = pl.BlockSpec(memory_space=pltpu.VMEM), pl.BlockSpec(memory_space=pl.ANY)
    dma = pltpu.SemaphoreType.DMA
    parts = count // CHUNK
    rows = own.shape[0]
    distant = (state, update, tok_k0, tok_v0, tok_k1, tok_v1, sqkv0, sqkv1, sout0, sout1)
    return pl.pallas_call(
        chain_back_kernel,
        in_specs=[vmem] * 11 + [anywhere] * (LATE + 2),
        out_specs=[vmem] * 7 + [anywhere],
        out_shape=[
            jax.ShapeDtypeStruct((count, width), bf16),
            jax.ShapeDtypeStruct((count, 3 * half), bf16),
            jax.ShapeDtypeStruct((count, 3 * half), bf16),
            jax.ShapeDtypeStruct((rows, 2 * half), f32),
            jax.ShapeDtypeStruct((rows, 2 * half), f32),
            jax.ShapeDtypeStruct((count, width), bf16),
            jax.ShapeDtypeStruct((2, width), f32),
            jax.ShapeDtypeStruct((2, 8, rows // 2, width // 4), bf16),
        ],
        scratch_shapes=[pltpu.VMEM(late.shape, late.dtype) for late in distant]
        + [
            pltpu.VMEM((count, width), f32),
            pltpu.VMEM((2, heads, count, rows + count), bf16),
            pltpu.VMEM((count, half), bf16),
            pltpu.VMEM((count, half), bf16),
            pltpu.VMEM((CHAIN - 1, count, width), bf16),
            pltpu.VMEM((CHAIN - 1, count, width), bf16),
            dma((CHAIN - 1, parts)), dma((CHAIN - 1, parts)), dma((14,)), dma((14,)), dma((2,)), dma((LATE,)),
        ],
        compiler_params=params(collective_id=2, has_side_effects=True),
        cost_estimate=pl.CostEstimate(
            flops=CHAIN * count * width * (16 * width + 16 * count),
            bytes_accessed=45 * 1024 * 1024,
            transcendentals=count * count * 4 * heads,
        ),
    )(starts, ends, gain, keep, own, other, ps0, ps1, os0, os1, lse, *distant, result, ending)


RING = 8
SHORT_RING = 4
TILE = 256
TAIL = 12
LAGS = (0, 1, 2, 4, 6, 7, 8, 9, 10)
UP_D, DOWN_D, UP_B, DOWN_B, OUT_C, QKV_C, SOUT_C, SQKV_C, QKV_A, OUT_A = range(10)
WEIGHTS = (
    (UP_D, True, 8), (DOWN_D, False, 8), (UP_B, True, 8), (DOWN_B, False, 8), (OUT_C, False, 2),
    (QKV_C, True, 6), (SOUT_C, False, 2), (SQKV_C, True, 6), (QKV_A, True, 6), (OUT_A, False, 2),
)
STARTS = [sum(w[2] for w in WEIGHTS[:i]) for i in range(len(WEIGHTS))]
PLAIN = sum(w[2] for w in WEIGHTS)
TAIL_WEIGHT = [w[0] for w in WEIGHTS].index(QKV_A)
TAIL_INPUTS = 10
TILES = PLAIN + 2


def grads_kernel(*refs):
    count = len(WEIGHTS)
    lefts, refs = refs[:count], refs[count:]
    panels_own, panels_other, refs = list(refs[: count - 1]), list(refs[count - 1 : 2 * count - 2]), refs[2 * count - 2 :]
    first, small, leaving_keys, refs = refs[0], refs[1], refs[2:6], refs[6:]
    distant, gain, refs = refs[:TAIL_INPUTS], refs[TAIL_INPUTS], refs[TAIL_INPUTS + 1 :]
    outs, last_out, landed = refs[:count], refs[count], refs[count + 1]
    refs = refs[count + 2 :]
    (
        left, panel, pair, core_in, kept1, first_in, kept2, second_in, kept3, third_in, kept4, fourth_in, result,
        left_sem, panel_sem, last_sem, core_send, core_recv, first_send, first_recv, second_send, second_recv,
        send_sem, recv_sem, piece_send, piece_recv, piece_sem,
        halo, ga0, ga1, rows_out, small_rows, gain_sum, tail_sem, halo_send, halo_recv,
    ) = refs[:-TAIL_INPUTS]
    fetched = refs[-TAIL_INPUTS:]
    panels_own.insert(TAIL_WEIGHT, ga0)
    panels_other.insert(TAIL_WEIGHT, ga1)
    section, tensor, group = (lax.axis_index(a) for a in (SECTION, TENSOR, DP))
    core, high = section % 2, section // 2
    near, far = group % 2, group // 2
    half, quarter = TILE // 2, TILE // 4
    other_core = {SECTION: section + 1 - 2 * core}
    near_group = {DP: group + 1 - 2 * near}
    far_group = {DP: (group + 2) % 4}
    scatter = Scatter((rows_out,), landed, piece_send, piece_recv, piece_sem)
    tail_fetches = [
        pltpu.make_async_copy(source, target, tail_sem.at[i])
        for i, (source, target) in enumerate(zip(distant + (small,), fetched + (small_rows,)))
    ]
    for fetch in tail_fetches:
        fetch.start()
    prior, _ = neighbours()
    meet(scatter.members + [near_group, far_group])

    def halo_copy(i):
        to = 2 * ((tensor + prior[TENSOR] + i // 2) % 2) + i % 2
        return pltpu.make_async_remote_copy(
            src_ref=leaving_keys[i], dst_ref=halo.at[to], send_sem=halo_send.at[i],
            recv_sem=halo_recv.at[to], device_id=prior, device_id_type=MESH,
        )

    for i in range(4):
        halo_copy(i).start()

    def remote(source, target, sems, recvs, where, partner):
        return pltpu.make_async_remote_copy(
            src_ref=source, dst_ref=target, send_sem=sems.at[where], recv_sem=recvs.at[where],
            device_id=partner, device_id_type=MESH,
        )

    def left_copy(w):
        return pltpu.make_async_copy(lefts[w], left.at[w % 3], left_sem.at[w % 3])

    left_copy(0).start()

    def panel_copies(w, k):
        slot = k % SHORT_RING
        columns = pl.ds(pl.multiple_of((k - STARTS[w]) * TILE, TILE), TILE)
        return [
            pltpu.make_async_copy(source[w].at[:, columns], panel.at[slot, j], panel_sem.at[2 * slot + j])
            for j, source in enumerate((panels_own, panels_other))
        ]

    def last_copies(which):
        slot = (PLAIN + which) % SHORT_RING
        for i in range(8):
            s, t = i // 2, i % 2
            columns = slice(s * TILE, (s + 1) * TILE)
            source = small_rows.at[:, columns] if which else first.at[t * TILE : (t + 1) * TILE, columns]
            yield pltpu.make_async_copy(source, pair.at[slot, s % 2, s // 2, t], last_sem.at[i])

    def core_copy(k):
        slot = k % SHORT_RING
        return remote(
            pair.at[slot, 1 - core], core_in.at[slot], core_send, core_recv, slot, other_core
        )

    def order(k):
        turn = k % 2
        send = (
            (1 - turn) * (1 - tensor) + turn * (2 - 2 * high),
            (1 - turn) * (3 - tensor) + turn * (3 - 2 * high),
        )
        keep = (
            (1 - turn) * tensor + turn * 2 * high,
            (1 - turn) * (2 + tensor) + turn * (2 * high + 1),
        )
        return send, keep, (1 - turn) * high + turn * tensor

    def partner_of(turn):
        return {
            SECTION: section * (1 - turn) + ((section + 2) % 4) * turn,
            TENSOR: tensor + (1 - turn) * (1 - 2 * tensor),
        }

    def first_copy(k, i):
        slot = k % RING
        return remote(
            kept1.at[k % SHORT_RING, order(k)[0][i]], first_in.at[slot, i], first_send, first_recv,
            2 * slot + i, partner_of(k % 2),
        )

    def second_copy(k):
        slot = k % RING
        return remote(
            kept2.at[slot, 1 - order(k)[2]], second_in.at[slot], second_send, second_recv,
            slot, partner_of(1 - k % 2),
        )

    def third_copy(k):
        slot = k % RING
        return remote(
            kept3.at[slot, pl.ds((1 - near) * half, half)], third_in.at[slot], send_sem, recv_sem,
            slot, near_group,
        )

    def fourth_copy(k):
        slot = k % RING
        return remote(
            kept4.at[slot, pl.ds((1 - far) * quarter, quarter)], fourth_in.at[slot], send_sem, recv_sem,
            RING + slot, far_group,
        )

    def back_far(k):
        rows = pl.ds(near * half + far * quarter, quarter)
        return remote(
            result.at[k, rows], result.at[k, rows], send_sem, recv_sem, 2 * RING + k % RING, far_group
        )

    def back_near(k):
        rows = pl.ds(near * half, half)
        return remote(
            result.at[k, rows], result.at[k, rows], send_sem, recv_sem, 3 * RING + k % RING, near_group
        )

    def add(a, b):
        return bf(a.astype(jnp.float32) + b.astype(jnp.float32))

    def fetch(k):
        for w in range(count):

            @pl.when((k >= STARTS[w]) & (k < STARTS[w] + WEIGHTS[w][2]))
            def _():
                for copy in panel_copies(w, k):
                    copy.start()

            if w + 1 < count:

                @pl.when(k == STARTS[w])
                def _():
                    left_copy(w + 1).start()

    def multiply(k):
        slot = k % SHORT_RING

        @pl.when(k < PLAIN)
        def _():
            at = 0
            for w in range(count):
                if w:
                    at = at + jnp.where(k >= STARTS[w], 1, 0)

                @pl.when(k == STARTS[w])
                def _():
                    left_copy(w).wait()

            for j, place in enumerate((tensor, 1 - tensor)):
                pltpu.make_async_copy(
                    panels_own[0].at[:, :TILE], panel.at[slot, j], panel_sem.at[2 * slot + j]
                ).wait()
                product = bf(tn(panel[slot, j], left[at % 3]))
                for s in range(4):
                    pair[slot, s % 2, s // 2, place] = product[:, s * TILE : (s + 1) * TILE]

        for which in range(2):

            @pl.when(k == PLAIN + which)
            def _():
                for copy in last_copies(which):
                    copy.start()
                for copy in last_copies(which):
                    copy.wait()

        core_copy(k).start()

    def over_cores(k):
        core_copy(k).wait()
        for i in range(4):
            kept1[k % SHORT_RING, i] = add(
                pair[k % SHORT_RING, core, i // 2, i % 2], core_in[k % SHORT_RING, i // 2, i % 2]
            )
        for i in range(2):
            first_copy(k, i).start()

    def over_first(k):
        slot = k % RING
        for i in range(2):
            first_copy(k, i).wait()
        for i in range(2):
            kept2[slot, i] = add(kept1[k % SHORT_RING, order(k)[1][i]], first_in[slot, i])
        second_copy(k).start()

    def over_second(k):
        slot = k % RING
        second_copy(k).wait()
        kept3[slot] = add(kept2[slot, order(k)[2]], second_in[slot])
        third_copy(k).start()

    def over_near(k):
        slot = k % RING
        third_copy(k).wait()
        kept4[slot] = add(kept3[slot, pl.ds(near * half, half)], third_in[slot])
        fourth_copy(k).start()

    def over_far(k):
        slot = k % RING
        fourth_copy(k).wait()
        result[k, pl.ds(near * half + far * quarter, quarter)] = add(
            kept4[slot, pl.ds(far * quarter, quarter)], fourth_in[slot]
        )
        back_far(k).start()

    def from_far(k):
        back_far(k).wait()
        back_near(k).start()

    def from_near(k):
        back_near(k).wait()
        for w in range(count):

            @pl.when((k >= STARTS[w]) & (k < STARTS[w] + WEIGHTS[w][2]))
            def _():
                at = pl.ds(pl.multiple_of((k - STARTS[w]) * TILE, TILE), TILE)
                if WEIGHTS[w][1]:
                    outs[w][:, at] = bf(result[k].astype(jnp.float32).T)
                else:
                    outs[w][at, :] = result[k]

        @pl.when(k >= PLAIN)
        def _():
            last_out[k - PLAIN] = result[k]

    gq0, gk0, gv0, gq1, gk1, gv1, w0, w1, tokens, grad = fetched
    wide = gq0.shape[1]

    def tail_begin():
        for copy in tail_fetches:
            copy.wait()
        for i in range(4):
            halo_copy(i).wait_send()
            pltpu.make_async_remote_copy(
                src_ref=leaving_keys[i], dst_ref=halo.at[i], send_sem=halo_send.at[i],
                recv_sem=halo_recv.at[i], device_id=prior, device_id_type=MESH,
            ).wait_recv()
        gain_sum[...] = jnp.zeros_like(gain_sum)

    def tail_rows(start):
        rows = slice(start, start + CHUNK)
        for side, (to, q, k, v) in enumerate(((ga0, gq0, gk0, gv0), (ga1, gq1, gk1, gv1))):
            to[rows, :wide] = q[rows]
            to[rows, wide : 2 * wide] = bf(k[rows] + halo[2 * side, rows].astype(jnp.float32))
            to[rows, 2 * wide :] = bf(v[rows] + halo[2 * side + 1, rows].astype(jnp.float32))
        back = nt(ga0[rows], w0[...]) + nt(ga1[rows], w1[...])
        value = tokens[rows].astype(jnp.float32)
        factor = inverse_rms(value)
        scaled = value * factor
        through = back * gain[...]
        rows_out[rows] = bf(
            grad[rows]
            + factor * (through - scaled * jnp.mean(through * scaled, axis=-1, keepdims=True))
        )
        gain_sum[0:1] += jnp.sum(back * scaled, axis=0, keepdims=True)

    def tail_end():
        top = small_rows[:16].astype(jnp.float32)
        row = lax.broadcasted_iota(jnp.int32, top.shape, 0)
        small_rows[:16] = bf(jnp.where(row == 0, gain_sum[0:1], top))
        scatter.start()

    stages = (
        fetch, multiply, over_cores, over_first, over_second, over_near, over_far, from_far, from_near
    )

    def step(i, nothing):
        pl.when(i == TAIL)(tail_begin)
        for part in range(grad.shape[0] // CHUNK):
            pl.when(i == TAIL + 2 + 2 * part)(functools.partial(tail_rows, part * CHUNK))
        pl.when(i == TAIL + 3 + 2 * (grad.shape[0] // CHUNK))(tail_end)
        for stage, lag in zip(stages, LAGS):
            k = i - lag

            @pl.when((k >= 0) & (k < TILES))
            def _():
                stage(k)

        return nothing

    lax.fori_loop(0, TILES + LAGS[-1], step, 0)
    scatter.wait()


def weight_grads(operands, first, small, leaving_keys, tail, gain):
    bf16 = jnp.bfloat16
    dma = pltpu.SemaphoreType.DMA
    anywhere, vmem = pl.BlockSpec(memory_space=pl.ANY), pl.BlockSpec(memory_space=pltpu.VMEM)
    count = len(WEIGHTS)
    rows, width = operands[WEIGHTS[0][0]][0].shape
    shapes = [(TILE, n * TILE) if by_rows else (n * TILE, TILE) for _, by_rows, n in WEIGHTS]
    shapes += [(2, TILE, TILE)]
    results = pl.pallas_call(
        grads_kernel,
        in_specs=[anywhere] * (3 * count + 4 + TAIL_INPUTS) + [vmem],
        out_specs=[vmem] * (count + 1) + [anywhere],
        out_shape=[jax.ShapeDtypeStruct(s, bf16) for s in shapes + [(1, 8, TILE, TILE)]],
        scratch_shapes=[
            pltpu.VMEM((3, rows, width), bf16),
            pltpu.VMEM((SHORT_RING, 2, rows, TILE), bf16),
            pltpu.VMEM((SHORT_RING, 2, 2, 2, TILE, TILE), bf16),
            pltpu.VMEM((SHORT_RING, 2, 2, TILE, TILE), bf16),
            pltpu.VMEM((SHORT_RING, 4, TILE, TILE), bf16),
            pltpu.VMEM((RING, 2, TILE, TILE), bf16),
            pltpu.VMEM((RING, 2, TILE, TILE), bf16),
            pltpu.VMEM((RING, TILE, TILE), bf16),
            pltpu.VMEM((RING, TILE, TILE), bf16),
            pltpu.VMEM((RING, TILE // 2, TILE), bf16),
            pltpu.VMEM((RING, TILE // 2, TILE), bf16),
            pltpu.VMEM((RING, TILE // 4, TILE), bf16),
            pltpu.VMEM((TILES, TILE, TILE), bf16),
            dma((3,)), dma((2 * SHORT_RING,)), dma((8,)),
            dma((SHORT_RING,)), dma((SHORT_RING,)),
            dma((2 * RING,)), dma((2 * RING,)), dma((RING,)), dma((RING,)),
            dma((4 * RING,)), dma((4 * RING,)), dma((7,)), dma((7,)), dma((1,)),
            pltpu.VMEM((4, rows, width // 2), bf16),
            pltpu.VMEM((rows, 3 * width // 2), bf16),
            pltpu.VMEM((rows, 3 * width // 2), bf16),
            pltpu.VMEM((rows, width), bf16),
            pltpu.VMEM((TILE, width), bf16),
            pltpu.VMEM((8, width), jnp.float32),
            dma((TAIL_INPUTS + 1,)), dma((4,)), dma((4,)),
        ]
        + [pltpu.VMEM(value.shape, value.dtype) for value in tail],
        compiler_params=params(collective_id=3, has_side_effects=True),
        cost_estimate=pl.CostEstimate(
            flops=2 * 8 * TILES * TILE * TILE * rows,
            bytes_accessed=40 * TILES * TILE * TILE,
            transcendentals=0,
        ),
    )(
        *(operands[w[0]][0] for w in WEIGHTS),
        *(operands[w[0]][i] for i in (1, 2) for w in WEIGHTS if w[0] != QKV_A),
        first, small, *leaving_keys, *tail, gain,
    )
    shares = {w[0]: r for w, r in zip(WEIGHTS, results)}
    return shares, results[count], results[count + 1]


def last_layer_kernel(
    alive, h, gy, r, up0, up1, down0, down1, a0, a1, g0, g1, result, through, total, back
):
    step, steps = pl.program_id(0), pl.num_programs(0)

    @pl.when(step == 0)
    def _():
        total[...] = jnp.zeros_like(total)
        back[...] = jnp.zeros_like(back)

    def chunk(up, down, a_out, g_out):
        u = nn(h[...], up[...])
        square = u * u
        slope = math.sqrt(2.0 / math.pi)
        t = jnp.tanh(slope * (u + 0.044715 * (square * u)))
        a = bf(0.5 * u * (1.0 + t))
        a_out[...] = a
        total[...] += nn(a, down[...])
        rise = 0.5 * (1.0 + t) + 0.5 * u * (1.0 - t * t) * (slope + (3.0 * 0.044715 * slope) * square)
        g = bf(nt(gy[...], down[...]) * rise)
        g_out[...] = g
        back[...] += nt(g, up[...])

    pl.when(step < steps // 2)(lambda: chunk(up0, down0, a0, g0))
    pl.when(step >= steps // 2)(lambda: chunk(up1, down1, a1, g1))

    @pl.when(step == steps - 1)
    def _():
        result[...] = bf(jnp.where(alive[0] > 0, r[...] + total[...], 0.0))
        through[...] = back[...]


def last_layer(alive, h, gy, r, up0, up1, down0, down1):
    rows, width = h.shape
    hidden = up0.shape[1]
    wide = 512
    half = hidden // wide

    def first(i):
        return jnp.minimum(i, half - 1)

    def second(i):
        return jnp.maximum(i - half, 0)

    ups = [pl.BlockSpec((width, wide), lambda i, of=of: (0, of(i))) for of in (first, second)]
    downs = [pl.BlockSpec((wide, width), lambda i, of=of: (of(i), 0)) for of in (first, second)]
    hiddens = [pl.BlockSpec((rows, wide), lambda i, of=of: (0, of(i))) for of in (first, second)]
    kept = pl.BlockSpec((rows, width), lambda i: (0, 0))
    return pl.pallas_call(
        last_layer_kernel,
        grid=(2 * half,),
        in_specs=[pl.BlockSpec(memory_space=pltpu.SMEM), kept, kept, kept] + ups + downs,
        out_specs=hiddens + hiddens + [kept, kept],
        out_shape=[jax.ShapeDtypeStruct((rows, hidden), jnp.bfloat16)] * 4
        + [
            jax.ShapeDtypeStruct((rows, width), jnp.bfloat16),
            jax.ShapeDtypeStruct((rows, width), jnp.float32),
        ],
        scratch_shapes=[pltpu.VMEM((rows, width), jnp.float32)] * 2,
        compiler_params=params(),
        cost_estimate=pl.CostEstimate(
            flops=16 * rows * width * hidden,
            bytes_accessed=8 * width * hidden + 16 * rows * hidden,
            transcendentals=2 * rows * hidden,
        ),
    )(alive, h, gy, r, up0, up1, down0, down1)


def gelu_back(values, grad):
    return jax.vjp(smooth, values)[1](grad)[0]


def block_body(
    layer_input, output_grad, seg_blocks, seg_group, gain_a, wqkv_a, wout_a, gain_b, up_b, down_b,
    gain_c, gain_s, wqkv_c, sqkv_c, wout_c, sout_c, gate_bias, init_states, gain_d, up_d, down_d,
):
    sections, tensors = lax.axis_size(SECTION), lax.axis_size(TENSOR)
    block_count, shard_rows, width = layer_input.shape[1:]
    rows = shard_rows * tensors
    section, tensor = lax.axis_index(SECTION), lax.axis_index(TENSOR)
    block = block_of(section, tensor)
    begins, closes, lively, numbers = layout(
        seg_blocks, seg_group, lax.axis_index(DP), block_count
    )
    alive = lively[block]
    starts = begins[block] | jnp.logical_not(alive)
    ends = closes[block] | jnp.logical_not(alive)
    opening = starts.astype(jnp.int32)[None]
    f32 = jnp.float32
    ga, gb, gc, gd = (v.astype(f32) for v in (gain_a, gain_b, gain_c, gain_d))

    def in_order(own, other):
        low = jnp.where(tensor == 0, own, other)
        high = jnp.where(tensor == 0, other, own)
        return low, high

    def crossed(weight):
        size = weight.shape[0] // sections
        piece = lax.dynamic_slice_in_dim(weight, section * size, size, 0)
        return lax.ppermute(piece, TENSOR, SWAP)

    def flat(weight):
        return jnp.concatenate([weight[:, i] for i in range(3)], axis=1)

    wqkv_a0, wqkv_c0, sqkv_c0 = flat(wqkv_a), flat(wqkv_c), flat(sqkv_c)
    (tokens, before, initial), others = gather(
        layer_input, init_states,
        (wout_a, sout_c, wout_c, wqkv_a0, wqkv_c0, sqkv_c0, up_b, down_b),
    )
    wout_a1, sout_c1, wout_c1, wqkv_a1, wqkv_c1, sqkv_c1, up_b1, down_b1 = others
    tokens, late_up, late_down = lax.optimization_barrier((tokens, up_d, down_d))
    pieces = crossed(late_up), crossed(late_down)

    def normed(values, gain):
        return bf(values * inverse_rms(values) * gain)

    def dot(a, b):
        return jnp.dot(a, b, preferred_element_type=f32)

    def dot_t(a, b):
        return lax.dot_general(a, b, (((1,), (1,)), ((), ())), preferred_element_type=f32)

    half = wout_a.shape[0]
    r0 = tokens.astype(f32)
    h0 = normed(r0, ga)
    h_before = normed(before.astype(f32), ga)
    pa0, pa1 = bf(dot(h0, wqkv_a0)), bf(dot(h0, wqkv_a1))
    prior_a0 = bf(dot(h_before, wqkv_a0[:, half:]))
    prior_a1 = bf(dot(h_before, wqkv_a1[:, half:]))
    oa0, lse_a0, oa1, lse_a1 = attend(opening, (pa0, pa1), (prior_a0, prior_a1))
    r1 = r0 + (dot(oa0, wout_a) + dot(oa1, wout_a1))

    h1 = normed(r1, gb)
    ub0, ub1 = dot(h1, up_b), dot(h1, up_b1)
    ab0, ab1 = bf(smooth(ub0)), bf(smooth(ub1))
    ab1, *pieces = lax.optimization_barrier((ab1, *pieces))
    up_d1, down_d1 = (lax.all_gather(piece, SECTION, axis=0, tiled=True) for piece in pieces)
    r2 = r1 + (dot(ab0, down_b) + dot(ab1, down_b1))

    h2 = normed(r2, gc)
    pc0, pc1 = bf(dot(h2, wqkv_c0)), bf(dot(h2, wqkv_c1))
    halo = lax.ppermute(jnp.stack(in_order(pc0[:, half:], pc1[:, half:])), GROUP, TO_NEXT)
    prior_c0, prior_c1 = in_order(halo[0], halo[1])

    retain = jax.nn.sigmoid(gate_bias.astype(f32))[None, :]
    state_gain = gain_s.astype(f32)[None, :]

    def flag(value):
        return jnp.broadcast_to(value.astype(f32), (1, width))

    (
        state_in, hs, ps0, ps1, os0, os1, lse_s, update, state_new, cotangent
    ) = chain(
        initial, flag(starts), state_gain, retain, pc0, pc1,
        sqkv_c0, sqkv_c1, sout_c, sout_c1, output_grad,
    )
    oc0, lse_c0, oc1, lse_c1 = attend(opening, (pc0, pc1), (prior_c0, prior_c1), (ps0, ps1))
    r3 = r2 + (dot(oc0, wout_c) + dot(oc1, wout_c1))

    h3 = normed(r3, gd)
    def feed_back(up_name, down_name, grad, values, h, gain, u0, u1, a0, a1, up0, up1, down0, down1):
        gy = bf(grad)
        g0 = bf(gelu_back(u0, dot_t(gy, down0)))
        g1 = bf(gelu_back(u1, dot_t(gy, down1)))
        operands[down_name] = (gy, a0, a1)
        operands[up_name] = (h, g0, g1)
        through = dot_t(g0, up0) + dot_t(g1, up1)
        back, gain_grad = norm_back(values, gain, through)
        return grad + back, gain_grad

    operands = {}
    grad4 = jnp.where(alive, cotangent.astype(f32), 0.0)
    gy4 = bf(grad4)
    ad0, ad1, gd0, gd1, result, through_d = last_layer(
        alive.astype(jnp.int32)[None], h3, gy4, r3, up_d, up_d1, down_d, down_d1
    )
    operands[DOWN_D] = (gy4, ad0, ad1)
    operands[UP_D] = (h3, gd0, gd1)
    back_d, gain_d_grad = norm_back(r3, gd, through_d)
    grad3 = grad4 + back_d

    gy3 = bf(grad3)
    tok0, tok1 = attend_back(
        opening, (pc0, pc1), (prior_c0, prior_c1), (bf(dot_t(gy3, wout_c)), bf(dot_t(gy3, wout_c1))),
        (oc0, oc1), (lse_c0, lse_c1), (ps0, ps1),
    )

    def halo_back(one, two):
        pair = in_order(
            jnp.concatenate([one[3], one[4]], axis=1), jnp.concatenate([two[3], two[4]], axis=1)
        )
        back = lax.ppermute(jnp.stack(pair), GROUP, TO_PRIOR)
        return in_order(back[0], back[1])

    halo_c0, halo_c1 = halo_back(tok0, tok1)
    first_grad, gs0, gs1, gtok0, gtok1, gup, small, landed = chain_back(
        flag(starts), flag(ends), state_in, update, state_gain, retain, pc0, pc1, ps0, ps1, os0, os1, lse_s,
        tok0[5], tok0[6], tok1[5], tok1[6], sqkv_c0, sqkv_c1, sout_c, sout_c1, result, state_new,
    )

    def projected_back(parts, halo_part, extra=None):
        pair = jnp.concatenate([parts[1], parts[2]], axis=1) + halo_part.astype(f32)
        if extra is not None:
            pair = pair + extra
        return jnp.concatenate([parts[0], bf(pair)], axis=1)

    gc0 = projected_back(tok0, halo_c0, gtok0)
    gc1 = projected_back(tok1, halo_c1, gtok1)
    operands[QKV_C] = (h2, gc0, gc1)
    operands[SQKV_C] = (hs, gs0, gs1)
    operands[OUT_C] = (gy3, oc0, oc1)
    operands[SOUT_C] = (gup, os0, os1)
    def through_qkv(g, w):
        return dot_t(g, w)

    back_c, gain_c_grad = norm_back(
        r2, gc, through_qkv(gc0, wqkv_c0) + through_qkv(gc1, wqkv_c1)
    )
    grad2 = grad3 + back_c

    grad1, gain_b_grad = feed_back(
        UP_B, DOWN_B, grad2, r1, h1, gb, ub0, ub1, ab0, ab1, up_b, up_b1, down_b, down_b1
    )

    gy1 = bf(grad1)
    att0, att1 = attend_back(
        opening, (pa0, pa1), (prior_a0, prior_a1), (bf(dot_t(gy1, wout_a)), bf(dot_t(gy1, wout_a1))),
        (oa0, oa1), (lse_a0, lse_a1),
    )
    operands[QKV_A] = (h0,)
    operands[OUT_A] = (gy1, oa0, oa1)
    smalls = jnp.stack(
        [jnp.zeros_like(gain_b_grad), gain_b_grad, gain_c_grad, small[0], gain_d_grad, small[1]]
    )
    shares, last_share, landed_input = weight_grads(
        operands, first_grad, jnp.pad(bf(smalls), ((0, TILE - 6), (0, 0))), (*att0[3:5], *att1[3:5]),
        (*att0[:3], *att1[:3], wqkv_a0, wqkv_a1, tokens, grad1), ga[None, :],
    )
    small_share = last_share[1].astype(f32)
    chosen = (
        (numbers[:, None] == jnp.arange(SLOTS, dtype=jnp.int32)[None, :])
        & (closes & lively)[:, None]
    )
    state_tiles = landed[1].astype(f32)
    final_share = jnp.stack(
        [
            jnp.sum(jnp.where(chosen[:, i, None, None], state_tiles, 0.0), axis=0)
            for i in range(SLOTS)
        ],
        axis=1,
    )

    def share(name):
        value = shares[name].astype(f32)
        return value.reshape(value.shape[0], 3, -1) if name in (QKV_A, QKV_C, SQKV_C) else value

    return (
        landed[0][None],
        final_share[None],
        landed_input.astype(f32),
        small_share[0],
        share(QKV_A),
        share(OUT_A),
        small_share[1],
        share(UP_B),
        share(DOWN_B),
        small_share[2],
        small_share[3],
        share(QKV_C),
        share(SQKV_C),
        share(OUT_C),
        share(SOUT_C),
        small_share[5],
        last_share[0].astype(f32),
        small_share[4],
        share(UP_D),
        share(DOWN_D),
    )


def chosen(*arrays):
    devices = (lax.axis_size(SECTION), lax.axis_size(TENSOR), lax.axis_size(DP))
    if devices == (4, 2, 4) and arrays[0].shape[1] == 8:
        return block_body(*arrays)
    return relay_body(*arrays)


def solution(mesh):
    in_specs = (
        P(DP, None, TENSOR, None),
        P(DP, None, TENSOR, None),
        P(),
        P(),
        P(),
        P(None, None, TENSOR),
        P(TENSOR, None),
        P(),
        P(None, TENSOR),
        P(TENSOR, None),
        P(),
        P(),
        P(None, None, TENSOR),
        P(None, None, TENSOR),
        P(TENSOR, None),
        P(TENSOR, None),
        P(),
        P(TENSOR, None),
        P(),
        P(None, TENSOR),
        P(TENSOR, None),
    )
    out_specs = (
        P(DP, None, TENSOR, SECTION),
        P(DP, TENSOR, None, SECTION),
        P(DP, None, TENSOR, SECTION),
        P(SECTION),
        P(SECTION, None, TENSOR),
        P(TENSOR, SECTION),
        P(SECTION),
        P(SECTION, TENSOR),
        P(TENSOR, SECTION),
        P(SECTION),
        P(SECTION),
        P(SECTION, None, TENSOR),
        P(SECTION, None, TENSOR),
        P(TENSOR, SECTION),
        P(TENSOR, SECTION),
        P(SECTION),
        P(TENSOR, SECTION),
        P(SECTION),
        P(SECTION, TENSOR),
        P(TENSOR, SECTION),
    )
    return jax.shard_map(chosen, mesh=mesh, in_specs=in_specs, out_specs=out_specs, check_vma=False)
```
